32 devices in a mesh: fsdp: 4 (over x, core), sp: 8 (over z, y).
Axes of the slice: x: 2, y: 2, z: 4, core: 2. Of those that a mesh axis runs over, the one named last changes fastest.
Arguments:
- tokens: bfloat16 [2, 2048, 2048], P(None, ('fsdp', 'sp')), may hold values from -6 to 6
- cotangent: bfloat16 [2, 2048, 2048], P(None, ('fsdp', 'sp')), may hold values from -6 to 6
- seq_len: int32 [16], replicated, may hold values from 0 to 512, as said below
- slot_order: int32 [16], replicated, may hold values from 0 to 15, as said below
- norm1_gain: bfloat16 [2048], P('fsdp'), may hold values from 0.5 to 1.5
- query_weight: bfloat16 [2048, 2048], P('fsdp'), may hold values from -0.125 to 0.125
- key_weight: bfloat16 [2048, 256], P('fsdp'), may hold values from -0.125 to 0.125
- value_weight: bfloat16 [2048, 256], P('fsdp'), may hold values from -0.125 to 0.125
- output_weight: bfloat16 [2048, 2048], P('fsdp'), may hold values from -2 to 2
- norm2_gain: bfloat16 [2048], P('fsdp'), may hold values from 0.5 to 1.5
- gate_weight: bfloat16 [2048, 5632], P('fsdp'), may hold values from -0.125 to 0.125
- up_weight: bfloat16 [2048, 5632], P('fsdp'), may hold values from -0.125 to 0.125
- down_weight: bfloat16 [2048, 5632], P('fsdp'), may hold values from -0.078125 to 0.078125
Outputs:
- block_out: float32 [2, 2048, 2048], P(None, ('fsdp', 'sp'))
- input_grad: float32 [2, 2048, 2048], P(None, ('fsdp', 'sp'))
- norm1_grad: float32 [2048], P(('fsdp', 'sp'))
- query_grad: float32 [2048, 2048], P(('fsdp', 'sp'))
- key_grad: float32 [2048, 256], P(('fsdp', 'sp'))
- value_grad: float32 [2048, 256], P(('fsdp', 'sp'))
- output_grad: float32 [2048, 2048], P(('fsdp', 'sp'))
- norm2_grad: float32 [2048], P(('fsdp', 'sp'))
- gate_grad: float32 [2048, 5632], P(('fsdp', 'sp'))
- up_grad: float32 [2048, 5632], P(('fsdp', 'sp'))
- down_grad: float32 [2048, 5632], P(('fsdp', 'sp'))
The draws below stay inside these ranges and needn't reach their ends.
Inputs may be any that keep to these rules, and one draw needn't show every extreme that they name: `seq_len`: window w = f * 2 + m holds from its first row sequence slot_order[2w], then sequence slot_order[2w + 1], then padding. For every fsdp index f one of its 2 windows holds one sequence of 512 tokens and one of length 0; every other window holds two sequences of 128 to 256 tokens. `slot_order`: A permutation of the 16 sequences.
All inputs are finite; a program needn't handle non-finite values.
Results may differ from the reference program's by a relative error of at most 0.013.
The reference program's roundings to bfloat16 on the way count: a program that leaves them out, or rounds other values in their place, can miss the bound.
Values may be sent and summed in bfloat16 or wider, within the bound.
A program may use at most 288 MiB of HBM per device.

```python
import jax
import jax.numpy as jnp
from jax import lax

D = 2048
HEADS = 32
KV = 4
HDIM = 64
FF = 5632
TOK_DEV = 64
MB = 2
TOKW = 2048
N_FSDP = 4
N_SP = 8


def layout_draw(key):
    window = N_SP * TOK_DEV
    window_count = N_FSDP * MB
    key_full, key_length, key_order = jax.random.split(key, 3)
    full_micro = jax.random.randint(key_full, (N_FSDP,), 0, MB)
    lengths = jax.random.randint(key_length, (window_count, 2), window // 4, window // 2 + 1)
    window_ids = jnp.arange(window_count, dtype=jnp.int32)
    is_full = window_ids % MB == full_micro[window_ids // MB]
    first_len = jnp.where(is_full, window, lengths[:, 0])
    second_len = jnp.where(is_full, 0, lengths[:, 1])
    slot_len = jnp.stack([first_len, second_len], axis=1).reshape(-1).astype(jnp.int32)
    order = jax.random.permutation(key_order, 2 * window_count).astype(jnp.int32)
    seq_len = jnp.zeros((2 * window_count,), jnp.int32).at[order].set(slot_len)
    return (seq_len, order)


def draw_seq_len(key, part):
    return layout_draw(key)[0]


def draw_slot_order(key, part):
    return layout_draw(key)[1]


def steps_of(rng, extent, pieces, smallest, high):
    def one(dim, blocks):
        steps = jax.random.uniform(jax.random.fold_in(jax.random.fold_in(rng, 6), dim), (blocks,), jnp.float32, smallest / len(pieces), high / len(pieces))
        return jnp.repeat(jnp.exp(steps), extent[dim] // blocks).reshape((-1,) + (1,) * (len(extent) - dim - 1))

    gain = one(*pieces[0])
    for cut in pieces[1:]:
        gain = gain * one(*cut)
    return gain


def scatter_about(stream_key, extent, width, most, pieces=(), kind=jnp.bfloat16):
    level = steps_of(stream_key, extent, pieces, -0.22, 0.18) if pieces else 1.0
    array = jax.random.normal(stream_key, extent, jnp.float32) * width * level
    return jnp.minimum(jnp.maximum(array, -most), most).astype(kind)


def setup_inputs(seed: int = 0) -> dict:
    key_list = jax.random.split(jax.random.key(seed), 14)
    tokens = scatter_about(key_list[0], (MB, TOKW, D), 1.0, 6.0, ((1, 32),))
    cotangent = scatter_about(key_list[1], (MB, TOKW, D), 1.0, 6.0, ((1, 32),))
    seq_len = draw_seq_len(jax.random.fold_in(key_list[13], 71), 0)
    slot_order = draw_slot_order(jax.random.fold_in(key_list[13], 71), 0)
    norm1_gain = jnp.clip(1.0 + 0.1 * jax.random.normal(key_list[4], (D,), jnp.float32), 0.5, 1.5).astype(jnp.bfloat16)
    query_weight = scatter_about(key_list[5], (D, D), D ** -0.5, 0.125, ((0, 4),))
    key_weight = scatter_about(key_list[6], (D, KV * HDIM), D ** -0.5, 0.125, ((0, 4),))
    value_weight = scatter_about(key_list[7], (D, KV * HDIM), D ** -0.5, 0.125, ((0, 4),))
    output_weight = scatter_about(key_list[8], (D, D), (max(D // 256, 4)) ** -0.5, 2.0, ((0, 4),))
    norm2_gain = jnp.clip(1.0 + 0.1 * jax.random.normal(key_list[9], (D,), jnp.float32), 0.5, 1.5).astype(jnp.bfloat16)
    gate_weight = scatter_about(key_list[10], (D, FF), D ** -0.5, 0.125, ((0, 4),))
    up_weight = scatter_about(key_list[11], (D, FF), D ** -0.5, 0.125, ((0, 4),))
    down_weight = scatter_about(key_list[12], (D, FF), FF ** -0.5, 0.078125, ((0, 4),))
    return {"tokens": tokens, "cotangent": cotangent, "seq_len": seq_len, "slot_order": slot_order, "norm1_gain": norm1_gain, "query_weight": query_weight, "key_weight": key_weight, "value_weight": value_weight, "output_weight": output_weight, "norm2_gain": norm2_gain, "gate_weight": gate_weight, "up_weight": up_weight, "down_weight": down_weight}


EPSILON = 1e-05
ROPE_BASE = 10000.0
HIGHEST = lax.Precision.HIGHEST

@jax.custom_vjp
def low(v):
    return lax.optimization_barrier(v.astype(jnp.bfloat16)).astype(jnp.float32)

@jax.custom_vjp
def low_back(v):
    return v

def low_keep(v):
    return (low(v), None)

def low_pass(kept, grad):
    return (grad,)

def back_keep(v):
    return (v, None)

def back_low(kept, grad):
    return (low(grad),)
low.defvjp(low_keep, low_pass)
low_back.defvjp(back_keep, back_low)

def window_layout(seq_len, slot_order, window_index, window):
    first_len = seq_len[slot_order[2 * window_index]]
    second_len = seq_len[slot_order[2 * window_index + 1]]
    places = jnp.arange(window, dtype=jnp.int32)
    segment = jnp.where(places < first_len, 0, jnp.where(places < first_len + second_len, 1, 2)).astype(jnp.int32)
    anchor = jnp.where(segment == 0, 0, jnp.where(segment == 1, first_len, first_len + second_len)).astype(jnp.int32)
    return (segment, (places - anchor).astype(jnp.int32))

def rope_tables(position, head_size):
    half_size = head_size // 2
    inverse = ROPE_BASE ** (-2.0 * jnp.arange(half_size, dtype=jnp.float32) / head_size)
    angles = position.astype(jnp.float32)[:, None] * inverse[None, :]
    angles = jnp.concatenate([angles, angles], axis=1)
    return (jnp.cos(angles)[:, None, :], jnp.sin(angles)[:, None, :])

def apply_rope(vectors, cosine, sine):
    half_size = vectors.shape[-1] // 2
    turned = jnp.concatenate([-vectors[..., half_size:], vectors[..., :half_size]], axis=-1)
    return vectors * cosine + turned * sine

def rms_scale(inputs):
    return lax.rsqrt(lax.optimization_barrier(jnp.mean(inputs * inputs, axis=-1, keepdims=True)) + EPSILON)

def product(left_side, right_side):
    return jnp.dot(left_side, right_side, precision=HIGHEST)

def attention(query_rot, key_rep, value_rep, segment):
    window = query_rot.shape[0]
    block_rows = min(512, window)
    scale_factor = HDIM ** (-0.5)
    places = jnp.arange(window, dtype=jnp.int32)

    def one_block(row_start):
        query_block = lax.dynamic_slice_in_dim(query_rot, row_start, block_rows, 0)
        block_segment = lax.dynamic_slice_in_dim(segment, row_start, block_rows, 0)
        row_place = row_start + jnp.arange(block_rows, dtype=jnp.int32)
        raw_scores = jnp.einsum('qhd,khd->hqk', query_block, key_rep, precision=HIGHEST) * scale_factor
        scores = low_back(raw_scores)
        allowed = (block_segment[:, None] == segment[None, :]) & (places[None, :] <= row_place[:, None])
        scores = jnp.where(allowed[None], scores, -1e+30)
        row_top = lax.optimization_barrier(jnp.max(scores, axis=-1, keepdims=True))
        weights_exp = jnp.exp(scores - row_top)
        probs = weights_exp / lax.optimization_barrier(jnp.sum(weights_exp, axis=-1, keepdims=True))
        return jnp.einsum('hqk,khd->qhd', low(probs), value_rep, precision=HIGHEST)
    starts = jnp.arange(window // block_rows, dtype=jnp.int32) * block_rows
    outputs = lax.map(jax.checkpoint(one_block), starts)
    return outputs.reshape(window, query_rot.shape[1], query_rot.shape[2])

def layer(inputs, norm1_gain, query_weight, key_weight, value_weight, output_weight, norm2_gain, gate_weight, up_weight, down_weight, segment, position):
    window = inputs.shape[0]
    normed = low(inputs * rms_scale(inputs) * norm1_gain)
    query_proj = low(low_back(product(normed, query_weight))).reshape(window, HEADS, HDIM)
    key_proj = low(low_back(product(normed, key_weight))).reshape(window, KV, HDIM)
    value_proj = low(low_back(product(normed, value_weight))).reshape(window, KV, HDIM)
    cosine, sine = rope_tables(position, HDIM)
    query_rot = low(apply_rope(query_proj, cosine, sine))
    key_rot = low(apply_rope(key_proj, cosine, sine))
    group_size = HEADS // KV
    attention_mix = attention(query_rot, jnp.repeat(key_rot, group_size, axis=1), jnp.repeat(value_proj, group_size, axis=1), segment)
    attended = low(low_back(attention_mix.reshape(window, D)))
    middle = inputs + low_back(product(attended, output_weight))
    normed_two = low(middle * rms_scale(middle) * norm2_gain)
    gate_proj = low_back(product(normed_two, gate_weight))
    up_proj = low_back(product(normed_two, up_weight))
    hidden = low(jax.nn.silu(gate_proj) * up_proj)
    return middle + low_back(product(hidden, down_weight.T))

def reference(tokens, cotangent, seq_len, slot_order, norm1_gain, query_weight, key_weight, value_weight, output_weight, norm2_gain, gate_weight, up_weight, down_weight):
    window = N_SP * TOK_DEV
    window_count = N_FSDP * MB
    weights = tuple((matrix.astype(jnp.float32) for matrix in (norm1_gain, query_weight, key_weight, value_weight, output_weight, norm2_gain, gate_weight, up_weight, down_weight)))

    def arrange(tensor):
        return tensor.astype(jnp.float32).reshape(MB, N_FSDP, window, D).transpose(1, 0, 2, 3).reshape(window_count, window, D)

    def restore(tensor):
        return tensor.reshape(N_FSDP, MB, window, D).transpose(1, 0, 2, 3).reshape(MB, N_FSDP * window, D)

    def one_window(totals, inputs_all):
        window_tokens, window_cot, window_index = inputs_all
        segment, position = window_layout(seq_len, slot_order, window_index, window)
        valid_rows = (segment < 2).astype(jnp.float32)

        def forward(block_in, *params):
            return layer(block_in, *params, segment, position)
        output, pullback = jax.vjp(forward, window_tokens, *weights)
        gradients = pullback(window_cot * valid_rows[:, None])
        totals = tuple((total + grad_part for total, grad_part in zip(totals, gradients[1:])))
        return (totals, (output, gradients[0]))
    start_totals = tuple((jnp.zeros_like(matrix) for matrix in weights))
    window_ids = jnp.arange(window_count, dtype=jnp.int32)
    totals, (outputs, input_grads) = lax.scan(one_window, start_totals, (arrange(tokens), arrange(cotangent), window_ids))
    return (restore(outputs), restore(input_grads), totals[0], totals[1], totals[2], totals[3], totals[4], totals[5], totals[6], totals[7], totals[8])
```

```python
import jax
import jax.numpy as jnp
from jax import lax
from jax.sharding import PartitionSpec as P

D = 2048
HEADS = 32
KV = 4
HDIM = 64
FF = 5632
MB = 2


EPSILON = 1e-05
ROPE_BASE = 10000.0


def plain_dot(left_side, right_side):
    return jnp.dot(left_side, right_side, preferred_element_type=jnp.float32)


def contract_rows(left_side, right_side):
    return lax.dot_general(
        left_side, right_side, (((0,), (0,)), ((), ())), preferred_element_type=jnp.float32
    )


def contract_cols(left_side, right_side):
    return lax.dot_general(
        left_side, right_side, (((1,), (1,)), ((), ())), preferred_element_type=jnp.float32
    )


def window_layout(seq_len, slot_order, window_index, window):
    first_len = seq_len[slot_order[2 * window_index]]
    second_len = seq_len[slot_order[2 * window_index + 1]]
    places = jnp.arange(window, dtype=jnp.int32)
    segment = jnp.where(
        places < first_len, 0, jnp.where(places < first_len + second_len, 1, 2)
    ).astype(jnp.int32)
    anchor = jnp.where(segment == 0, 0, jnp.where(segment == 1, first_len, first_len + second_len))
    return (segment, places - anchor)


def rope_tables(position, head_size):
    half_size = head_size // 2
    inverse = ROPE_BASE ** (-2.0 * jnp.arange(half_size, dtype=jnp.float32) / head_size)
    angles = position.astype(jnp.float32)[:, None] * inverse[None, :]
    angles = jnp.concatenate([angles, angles], axis=1)
    return (jnp.cos(angles)[:, None, :], jnp.sin(angles)[:, None, :])


def apply_rope(vectors, cosine, sine):
    half_size = vectors.shape[-1] // 2
    turned = jnp.concatenate([-vectors[..., half_size:], vectors[..., :half_size]], axis=-1)
    return vectors * cosine + turned * sine


def rope_back(grad_in, cosine, sine):
    half_size = grad_in.shape[-1] // 2
    rotated = grad_in * sine
    return grad_in * cosine + jnp.concatenate(
        [rotated[..., half_size:], -rotated[..., :half_size]], axis=-1
    )


def rms_scale(inputs):
    return lax.rsqrt(jnp.mean(inputs * inputs, axis=-1, keepdims=True) + EPSILON)


def norm_back(inputs, scale_rows, gain_full, upstream):
    through = upstream * gain_full
    gain_term = jnp.sum(upstream * inputs * scale_rows, axis=0)
    grad_in = scale_rows * through - inputs * scale_rows**3 * jnp.mean(
        through * inputs, axis=-1, keepdims=True
    )
    return (grad_in, gain_term)


def score_block(query_block, key_rot, segment, row_start):
    block_rows = query_block.shape[0]
    places = jnp.arange(key_rot.shape[0], dtype=jnp.int32)
    row_place = row_start + jnp.arange(block_rows, dtype=jnp.int32)
    block_segment = lax.dynamic_slice_in_dim(segment, row_start, block_rows, 0)
    allowed = (block_segment[:, None] == segment[None, :]) & (places[None, :] <= row_place[:, None])
    raw_scores = jnp.einsum(
        "qhd,khd->hqk", query_block, key_rot, preferred_element_type=jnp.float32
    ) * query_block.shape[2] ** (-0.5)
    return jnp.where(allowed[None], raw_scores, -1e30)


def attend_forward(query_rot, key_rot, value_heads, segment):
    window = query_rot.shape[0]
    block_rows = min(512, window)

    def step(carry, block_index):
        row_start = block_index * block_rows
        query_block = lax.dynamic_slice_in_dim(query_rot, row_start, block_rows, 0)
        scores = score_block(query_block, key_rot, segment, row_start)
        row_top = jnp.max(scores, axis=-1, keepdims=True)
        weights_exp = jnp.exp(scores - row_top)
        row_total = jnp.sum(weights_exp, axis=-1, keepdims=True)
        probs = (weights_exp / row_total).astype(jnp.bfloat16)
        block_out = jnp.einsum(
            "hqk,khd->qhd", probs, value_heads, preferred_element_type=jnp.float32
        )
        log_total = (row_top + jnp.log(row_total))[:, :, 0].T
        return (carry, (block_out, log_total))

    block_ids = jnp.arange(window // block_rows, dtype=jnp.int32)
    _, (outputs, log_totals) = lax.scan(step, jnp.zeros((), jnp.int32), block_ids)
    return (outputs.reshape(query_rot.shape), log_totals.reshape(window, query_rot.shape[1]))


def attend_backward(query_rot, key_rot, value_heads, grad_heads, log_totals, segment):
    window = query_rot.shape[0]
    block_rows = min(512, window)
    scale_factor = query_rot.shape[2] ** (-0.5)

    def step(carry, block_index):
        key_acc, value_acc = carry
        row_start = block_index * block_rows
        query_block = lax.dynamic_slice_in_dim(query_rot, row_start, block_rows, 0)
        grad_block = lax.dynamic_slice_in_dim(grad_heads, row_start, block_rows, 0)
        total_block = lax.dynamic_slice_in_dim(log_totals, row_start, block_rows, 0)
        scores = score_block(query_block, key_rot, segment, row_start)
        probs = jnp.exp(scores - total_block.T[:, :, None])
        grad_probs = jnp.einsum(
            "qhd,khd->hqk", grad_block, value_heads, preferred_element_type=jnp.float32
        )
        inner_sum = jnp.sum(probs * grad_probs, axis=-1, keepdims=True)
        grad_scores = (probs * (grad_probs - inner_sum)).astype(jnp.bfloat16)
        query_part = (
            jnp.einsum("hqk,khd->qhd", grad_scores, key_rot, preferred_element_type=jnp.float32)
            * scale_factor
        )
        key_acc = (
            key_acc
            + jnp.einsum(
                "hqk,qhd->khd", grad_scores, query_block, preferred_element_type=jnp.float32
            )
            * scale_factor
        )
        value_acc = value_acc + jnp.einsum(
            "hqk,qhd->khd",
            probs.astype(jnp.bfloat16),
            grad_block,
            preferred_element_type=jnp.float32,
        )
        return ((key_acc, value_acc), query_part)

    start_acc = (jnp.zeros(key_rot.shape, jnp.float32), jnp.zeros(value_heads.shape, jnp.float32))
    block_ids = jnp.arange(window // block_rows, dtype=jnp.int32)
    (key_acc, value_acc), query_parts = lax.scan(step, start_acc, block_ids)
    return (query_parts.reshape(query_rot.shape), key_acc, value_acc)


def weight_terms(stored):
    joined = [jnp.concatenate(pieces, axis=0) for pieces in zip(*stored)]
    (
        normed,
        query_low,
        key_low,
        value_low,
        attn_rows,
        middle_low,
        normed_two,
        gate_low,
        up_low,
        upstream_low,
        hidden,
    ) = joined
    return jnp.concatenate(
        [
            contract_rows(normed, query_low),
            contract_rows(normed, key_low),
            contract_rows(normed, value_low),
            contract_rows(attn_rows, middle_low),
            contract_rows(normed_two, gate_low),
            contract_rows(normed_two, up_low),
            contract_rows(upstream_low, hidden),
        ],
        axis=1,
    )


def body(
    tokens,
    cotangent,
    seq_len,
    slot_order,
    norm1_gain,
    query_weight,
    key_weight,
    value_weight,
    output_weight,
    norm2_gain,
    gate_weight,
    up_weight,
    down_weight,
):
    seq_devices = lax.axis_size("sp")
    seq_rank = lax.axis_index("sp")
    shard_rank = lax.axis_index("fsdp")
    tok_rows = tokens.shape[1]
    window = seq_devices * tok_rows
    group_size = HEADS // KV
    kept = []
    outputs = []
    input_grads = []
    gain_sum = jnp.zeros((2, D), jnp.float32)
    grad_shards = None
    for micro_step in range(MB):
        gathered = (
            lax.all_gather(norm1_gain, "fsdp", axis=0, tiled=True),
            lax.all_gather(query_weight, "fsdp", axis=0, tiled=True),
            lax.all_gather(key_weight, "fsdp", axis=0, tiled=True),
            lax.all_gather(value_weight, "fsdp", axis=0, tiled=True),
            lax.all_gather(output_weight, "fsdp", axis=0, tiled=True),
            lax.all_gather(norm2_gain, "fsdp", axis=0, tiled=True),
            lax.all_gather(gate_weight, "fsdp", axis=0, tiled=True),
            lax.all_gather(up_weight, "fsdp", axis=0, tiled=True),
            lax.all_gather(down_weight, "fsdp", axis=0, tiled=True),
        )
        gain_one, w_query, w_key, w_value, w_output, gain_two, w_gate, w_up, w_down = gathered
        gain_one = gain_one.astype(jnp.float32)
        gain_two = gain_two.astype(jnp.float32)
        inputs = tokens[micro_step].astype(jnp.float32)
        window_index = shard_rank * MB + micro_step
        segment, position = window_layout(seq_len, slot_order, window_index, window)
        own_segment = lax.dynamic_slice_in_dim(segment, seq_rank * tok_rows, tok_rows, 0)
        valid_rows = (own_segment < 2).astype(jnp.float32)
        scale_one = rms_scale(inputs)
        normed = (inputs * scale_one * gain_one).astype(jnp.bfloat16)
        query_proj = plain_dot(normed, w_query).astype(jnp.bfloat16).reshape(tok_rows, HEADS, HDIM)
        key_proj = plain_dot(normed, w_key).astype(jnp.bfloat16).reshape(tok_rows, KV, HDIM)
        value_proj = plain_dot(normed, w_value).astype(jnp.bfloat16).reshape(tok_rows, KV, HDIM)
        packed = jnp.concatenate(
            [
                query_proj,
                jnp.repeat(key_proj, group_size, axis=1),
                jnp.repeat(value_proj, group_size, axis=1),
            ],
            axis=2,
        )
        head_side = lax.all_to_all(packed, "sp", split_axis=1, concat_axis=0, tiled=True)
        cosine, sine = rope_tables(position, HDIM)
        query_rot = apply_rope(head_side[:, :, :HDIM].astype(jnp.float32), cosine, sine).astype(
            jnp.bfloat16
        )
        key_rot = apply_rope(
            head_side[:, :, HDIM : 2 * HDIM].astype(jnp.float32), cosine, sine
        ).astype(jnp.bfloat16)
        value_heads = head_side[:, :, 2 * HDIM :]
        attended, log_totals = attend_forward(query_rot, key_rot, value_heads, segment)
        token_side = lax.all_to_all(
            attended.astype(jnp.bfloat16), "sp", split_axis=0, concat_axis=1, tiled=True
        )
        attn_rows = token_side.reshape(tok_rows, D)
        middle = inputs + plain_dot(attn_rows, w_output)
        scale_two = rms_scale(middle)
        normed_two = (middle * scale_two * gain_two).astype(jnp.bfloat16)
        gate_proj = plain_dot(normed_two, w_gate)
        up_proj = plain_dot(normed_two, w_up)
        gate_sig = jax.nn.sigmoid(gate_proj)
        hidden = (gate_proj * gate_sig * up_proj).astype(jnp.bfloat16)
        outputs.append(middle + contract_cols(hidden, w_down))
        upstream = cotangent[micro_step].astype(jnp.float32) * valid_rows[:, None]
        upstream_low = upstream.astype(jnp.bfloat16)
        hidden_grad = plain_dot(upstream_low, w_down)
        up_low = (hidden_grad * gate_proj * gate_sig).astype(jnp.bfloat16)
        gate_low = (hidden_grad * up_proj * gate_sig * (1.0 + gate_proj * (1.0 - gate_sig))).astype(
            jnp.bfloat16
        )
        normed_two_grad = contract_cols(gate_low, w_gate) + contract_cols(up_low, w_up)
        middle_grad, gain_two_term = norm_back(middle, scale_two, gain_two, normed_two_grad)
        middle_grad = middle_grad + upstream
        middle_low = middle_grad.astype(jnp.bfloat16)
        attn_grad = (
            contract_cols(middle_low, w_output).astype(jnp.bfloat16).reshape(tok_rows, HEADS, HDIM)
        )
        grad_heads = lax.all_to_all(attn_grad, "sp", split_axis=1, concat_axis=0, tiled=True)
        query_part, key_acc, value_acc = attend_backward(
            query_rot, key_rot, value_heads, grad_heads, log_totals, segment
        )
        packed_grad = jnp.concatenate(
            [rope_back(query_part, cosine, sine), rope_back(key_acc, cosine, sine), value_acc],
            axis=2,
        )
        grad_tokens = lax.all_to_all(packed_grad, "sp", split_axis=0, concat_axis=1, tiled=True)
        query_low = grad_tokens[:, :, :HDIM].reshape(tok_rows, D).astype(jnp.bfloat16)
        key_low = (
            grad_tokens[:, :, HDIM : 2 * HDIM]
            .reshape(tok_rows, KV, group_size, HDIM)
            .sum(axis=2)
            .reshape(tok_rows, KV * HDIM)
            .astype(jnp.bfloat16)
        )
        value_low = (
            grad_tokens[:, :, 2 * HDIM :]
            .reshape(tok_rows, KV, group_size, HDIM)
            .sum(axis=2)
            .reshape(tok_rows, KV * HDIM)
            .astype(jnp.bfloat16)
        )
        normed_grad = (
            contract_cols(query_low, w_query)
            + contract_cols(key_low, w_key)
            + contract_cols(value_low, w_value)
        )
        inputs_grad, gain_one_term = norm_back(inputs, scale_one, gain_one, normed_grad)
        input_grads.append(inputs_grad + middle_grad)
        gain_sum = gain_sum + jnp.stack([gain_one_term, gain_two_term])
        kept.append(
            (
                normed,
                query_low,
                key_low,
                value_low,
                attn_rows,
                middle_low,
                normed_two,
                gate_low,
                up_low,
                upstream_low,
                hidden,
            )
        )
        grad_shards = None
    grad_shards = lax.psum_scatter(
        weight_terms(kept), ("fsdp", "sp"), scatter_dimension=0, tiled=True
    )
    gain_shards = lax.psum_scatter(gain_sum, ("fsdp", "sp"), scatter_dimension=1, tiled=True)
    kv_width = KV * HDIM
    edges = [
        0,
        D,
        D + kv_width,
        D + 2 * kv_width,
        2 * D + 2 * kv_width,
        2 * D + 2 * kv_width + FF,
        2 * D + 2 * kv_width + 2 * FF,
        2 * D + 2 * kv_width + 3 * FF,
    ]
    pieces = [grad_shards[:, edges[slot] : edges[slot + 1]] for slot in range(7)]
    return (
        jnp.stack(outputs),
        jnp.stack(input_grads),
        gain_shards[0],
        pieces[0],
        pieces[1],
        pieces[2],
        pieces[3],
        gain_shards[1],
        pieces[4],
        pieces[5],
        pieces[6],
    )


def silu_parts(gate_proj):
    gate_sig = jax.nn.sigmoid(gate_proj)
    return gate_sig, gate_proj * gate_sig


def turned(vectors):
    half_size = vectors.shape[-1] // 2
    return jnp.concatenate([-vectors[..., half_size:], vectors[..., :half_size]], axis=-1)


def group_body(
    tokens,
    cotangent,
    seq_len,
    slot_order,
    norm1_gain,
    query_weight,
    key_weight,
    value_weight,
    output_weight,
    norm2_gain,
    gate_weight,
    up_weight,
    down_weight,
):
    n_sp = lax.axis_size("sp")
    n_fsdp = lax.axis_size("fsdp")
    group = n_sp // MB
    rank = lax.axis_index("sp")
    shard = lax.axis_index("fsdp")
    micro = rank // group
    member = rank % group
    tok_rows = tokens.shape[1]
    window = n_sp * tok_rows
    own_rows = MB * tok_rows
    groups = [[m * group + t for t in range(group)] for m in range(MB)]
    flat = lambda f, s: f * n_sp + s

    def swap(array):
        return lax.ppermute(array, "sp", [(s, (s + group) % n_sp) for s in range(n_sp)])

    def pick(pair, index):
        return lax.dynamic_index_in_dim(pair, index, 0, keepdims=False)

    def in_order(mine, theirs):
        return jnp.where(micro == 0, jnp.concatenate([mine, theirs]), jnp.concatenate([theirs, mine]))

    def gather_rows(array):
        return lax.all_gather(array, "sp", axis=0, tiled=True, axis_index_groups=groups)

    def sum_rows(partial):
        pieces = lax.all_to_all(
            partial.astype(jnp.bfloat16).reshape(group, own_rows, D),
            "sp", split_axis=0, concat_axis=0, tiled=True, axis_index_groups=groups,
        )
        return jnp.sum(pieces.astype(jnp.float32), axis=0)

    def gather_weight(weight):
        width = weight.shape[1] // group
        part = lax.dynamic_slice_in_dim(weight, member * width, width, 1)
        return lax.all_gather(part, "fsdp", axis=0, tiled=True)

    def reduce_weight(partial):
        width = partial.shape[1]
        rows = partial.reshape(2, 2, MB, group, tok_rows, width)

        def halve(array, axis, index, axis_name, perm):
            keep = lax.dynamic_index_in_dim(array, index, axis, keepdims=False)
            send = lax.dynamic_index_in_dim(array, 1 - index, axis, keepdims=False)
            got = lax.ppermute(send.astype(jnp.bfloat16), axis_name, perm)
            return keep + got.astype(jnp.float32)

        rows = halve(rows, 1, shard % 2, "fsdp", [(f, f ^ 1) for f in range(n_fsdp)])
        rows = halve(rows, 0, shard // 2, "fsdp", [(f, f ^ 2) for f in range(n_fsdp)])
        rows = halve(rows, 0, micro, "sp", [(s, (s + group) % n_sp) for s in range(n_sp)])
        rows = lax.all_to_all(
            rows.astype(jnp.bfloat16), "sp", split_axis=0, concat_axis=0, tiled=True, axis_index_groups=groups
        )
        return rows.astype(jnp.float32).transpose(1, 0, 2).reshape(tok_rows, group * width)

    w_query = gather_weight(query_weight)
    w_key = gather_weight(key_weight)
    w_value = gather_weight(value_weight)
    both = ("fsdp", "sp")
    members = [(m * group + t, t) for m in range(MB) for t in range(group)]
    over_x = lax.ppermute(output_weight, both, [(flat(t, s), flat(t ^ 2, s)) for s, t in members])
    held = jnp.where(shard == member, output_weight, over_x)
    over_core = lax.ppermute(
        held, both, [(flat(t ^ k, s), flat(t ^ k ^ 1, s)) for s, t in members for k in (0, 2)]
    )
    w_output = jnp.where((shard & 1) == (member & 1), held, over_core)
    w_gate = gather_weight(gate_weight)
    w_up = gather_weight(up_weight)
    w_down = gather_weight(down_weight)
    gain_one = lax.all_gather(norm1_gain, "fsdp", axis=0, tiled=True).astype(jnp.float32)
    gain_two = lax.all_gather(norm2_gain, "fsdp", axis=0, tiled=True).astype(jnp.float32)

    ids = jnp.arange(window, dtype=jnp.int32)
    owner, half, inner = ids // own_rows, (ids // tok_rows) % MB, ids % tok_rows
    place = (half * group + owner) * tok_rows + inner
    window_index = shard * MB + micro
    first_len = seq_len[slot_order[2 * window_index]]
    second_len = seq_len[slot_order[2 * window_index + 1]]
    segment = jnp.where(place < first_len, 0, jnp.where(place < first_len + second_len, 1, 2))
    anchor = jnp.where(segment == 0, 0, jnp.where(segment == 1, first_len, first_len + second_len))
    position = place - anchor
    allowed = (segment[:, None] == segment[None, :]) & (place[None, :] <= place[:, None])
    valid = (segment < 2).astype(jnp.float32)
    own_valid = lax.dynamic_slice_in_dim(valid, member * own_rows, own_rows, 0)
    cosine, sine = rope_tables(position, HDIM)

    own_tokens = in_order(pick(tokens, micro), swap(pick(tokens, 1 - micro)))
    own_cot = in_order(pick(cotangent, micro), swap(pick(cotangent, 1 - micro)))
    inputs = own_tokens.astype(jnp.float32)
    upstream = own_cot.astype(jnp.float32) * own_valid[:, None]
    upstream_low = gather_rows(upstream.astype(jnp.bfloat16))

    scale_one = rms_scale(inputs)
    normed = gather_rows((inputs * scale_one * gain_one).astype(jnp.bfloat16))
    heads = HEADS // group
    query = plain_dot(normed, w_query).astype(jnp.bfloat16).astype(jnp.float32).reshape(window, heads, HDIM)
    key = plain_dot(normed, w_key).astype(jnp.bfloat16).astype(jnp.float32).reshape(window, 1, HDIM)
    value = plain_dot(normed, w_value).astype(jnp.bfloat16)
    query_rot = apply_rope(query, cosine, sine).astype(jnp.bfloat16)
    key_rot = apply_rope(key, cosine, sine).astype(jnp.bfloat16)[:, 0]

    scale = HDIM**-0.5
    scores = jnp.einsum("qhd,kd->hqk", query_rot, key_rot, preferred_element_type=jnp.float32) * scale
    scores = jnp.where(allowed[None], scores, -1e30)
    top = jnp.max(scores, axis=-1, keepdims=True)
    weights_exp = jnp.exp(scores - top)
    probs = weights_exp / jnp.sum(weights_exp, axis=-1, keepdims=True)
    probs_low = probs.astype(jnp.bfloat16)
    attended = jnp.einsum("hqk,kd->qhd", probs_low, value, preferred_element_type=jnp.float32)
    attended = attended.astype(jnp.bfloat16).reshape(window, heads * HDIM)

    middle = inputs + sum_rows(plain_dot(attended, w_output))
    scale_two = rms_scale(middle)
    normed_two = gather_rows((middle * scale_two * gain_two).astype(jnp.bfloat16))
    gate = plain_dot(normed_two, w_gate)
    up = plain_dot(normed_two, w_up)
    sig, silu = silu_parts(gate)
    hidden = (silu * up).astype(jnp.bfloat16)
    block = middle + sum_rows(contract_cols(hidden, w_down))
    d_hidden = plain_dot(upstream_low, w_down)
    d_up = (d_hidden * silu).astype(jnp.bfloat16)
    d_gate = (d_hidden * up * sig * (1.0 + gate * (1.0 - sig))).astype(jnp.bfloat16)
    d_normed_two = sum_rows(contract_cols(d_gate, w_gate) + contract_cols(d_up, w_up))
    d_middle, gain_two_term = norm_back(middle, scale_two, gain_two, d_normed_two)
    d_middle = d_middle + upstream
    middle_low = gather_rows(d_middle.astype(jnp.bfloat16))

    d_attended = contract_cols(middle_low, w_output).astype(jnp.bfloat16).reshape(window, heads, HDIM)
    d_probs = jnp.einsum("qhd,kd->hqk", d_attended, value, preferred_element_type=jnp.float32)
    inner_sum = jnp.sum(probs * d_probs, axis=-1, keepdims=True)
    d_scores = (probs * (d_probs - inner_sum)).astype(jnp.bfloat16)
    d_query_rot = jnp.einsum("hqk,kd->qhd", d_scores, key_rot, preferred_element_type=jnp.float32) * scale
    d_key_rot = jnp.einsum("hqk,qhd->kd", d_scores, query_rot, preferred_element_type=jnp.float32) * scale
    d_value = jnp.einsum("hqk,qhd->kd", probs_low, d_attended, preferred_element_type=jnp.float32)
    d_query = rope_back(d_query_rot, cosine, sine).astype(jnp.bfloat16).reshape(window, heads * HDIM)
    d_key = rope_back(d_key_rot[:, None], cosine, sine)[:, 0].astype(jnp.bfloat16)
    d_value = d_value.astype(jnp.bfloat16)
    d_normed = sum_rows(
        contract_cols(d_query, w_query) + contract_cols(d_key, w_key) + contract_cols(d_value, w_value)
    )
    d_inputs, gain_one_term = norm_back(inputs, scale_one, gain_one, d_normed)
    d_inputs = d_inputs + d_middle

    def to_owner(rows):
        halves = rows.reshape(MB, tok_rows, D)
        mine, theirs = pick(halves, micro), swap(pick(halves, 1 - micro))
        return jnp.where(micro == 0, jnp.stack([mine, theirs]), jnp.stack([theirs, mine]))

    gate_grad = reduce_weight(contract_rows(normed_two, d_gate))
    up_grad = reduce_weight(contract_rows(normed_two, d_up))
    down_grad = reduce_weight(contract_rows(upstream_low, hidden))
    query_grad = reduce_weight(contract_rows(normed, d_query))
    key_grad = reduce_weight(contract_rows(normed, d_key))
    value_grad = reduce_weight(contract_rows(normed, d_value))

    output_part = contract_rows(attended, middle_low)
    got = lax.ppermute(
        output_part.astype(jnp.bfloat16), both,
        [(flat(t ^ k ^ 1, s), flat(t ^ k, s)) for s, t in members for k in (0, 2)],
    )
    output_part = output_part + got.astype(jnp.float32)
    got = lax.ppermute(
        output_part.astype(jnp.bfloat16), both, [(flat(t ^ 2, s), flat(t, s)) for s, t in members]
    )
    output_part = (output_part + got.astype(jnp.float32)).reshape(MB, group * tok_rows, D)
    got = swap(pick(output_part, 1 - micro).astype(jnp.bfloat16))
    output_part = pick(output_part, micro) + got.astype(jnp.float32)
    pieces = lax.all_to_all(
        output_part.astype(jnp.bfloat16).reshape(group, tok_rows, D),
        "sp", split_axis=0, concat_axis=0, tiled=True, axis_index_groups=groups,
    )
    output_grad = pick(pieces, shard).astype(jnp.float32)

    gains = lax.psum_scatter(
        jnp.stack([gain_one_term, gain_two_term]), both, scatter_dimension=1, tiled=True
    )
    return (
        to_owner(block),
        to_owner(d_inputs),
        gains[0],
        query_grad,
        key_grad,
        value_grad,
        output_grad,
        gains[1],
        gate_grad,
        up_grad,
        down_grad,
    )


def solution(mesh):
    fits = mesh.shape["fsdp"] == KV and mesh.shape["sp"] == MB * KV
    placed = (
        P(None, ("fsdp", "sp"), None),
        P(None, ("fsdp", "sp"), None),
        P(),
        P(),
        P("fsdp"),
        P("fsdp", None),
        P("fsdp", None),
        P("fsdp", None),
        P("fsdp", None),
        P("fsdp"),
        P("fsdp", None),
        P("fsdp", None),
        P("fsdp", None),
    )
    return jax.shard_map(
        group_body if fits else body,
        mesh=mesh,
        in_specs=placed,
        out_specs=(
            P(None, ("fsdp", "sp"), None),
            P(None, ("fsdp", "sp"), None),
            P(("fsdp", "sp")),
            P(("fsdp", "sp"), None),
            P(("fsdp", "sp"), None),
            P(("fsdp", "sp"), None),
            P(("fsdp", "sp"), None),
            P(("fsdp", "sp")),
            P(("fsdp", "sp"), None),
            P(("fsdp", "sp"), None),
            P(("fsdp", "sp"), None),
        ),
        check_vma=False,
    )
```

```python
import functools

import jax
import jax.numpy as jnp
import numpy as np
from jax import lax
from jax.experimental import pallas as pl
from jax.experimental.pallas import tpu as pltpu
from jax.sharding import PartitionSpec as P

D = 2048
HEADS = 32
KV = 4
HDIM = 64
FF = 5632
MB = 2
MESH = pl.DeviceIdType.MESH
VMEM_BYTES = 56 * 2**20


EPSILON = 1e-05
ROPE_BASE = 10000.0


def plain_dot(left_side, right_side):
    return jnp.dot(left_side, right_side, preferred_element_type=jnp.float32)


def contract_rows(left_side, right_side):
    return lax.dot_general(
        left_side, right_side, (((0,), (0,)), ((), ())), preferred_element_type=jnp.float32
    )


def contract_cols(left_side, right_side):
    return lax.dot_general(
        left_side, right_side, (((1,), (1,)), ((), ())), preferred_element_type=jnp.float32
    )


def window_layout(seq_len, slot_order, window_index, window):
    first_len = seq_len[slot_order[2 * window_index]]
    second_len = seq_len[slot_order[2 * window_index + 1]]
    places = jnp.arange(window, dtype=jnp.int32)
    segment = jnp.where(
        places < first_len, 0, jnp.where(places < first_len + second_len, 1, 2)
    ).astype(jnp.int32)
    anchor = jnp.where(segment == 0, 0, jnp.where(segment == 1, first_len, first_len + second_len))
    return (segment, places - anchor)


def rope_tables(position, head_size):
    half_size = head_size // 2
    inverse = ROPE_BASE ** (-2.0 * jnp.arange(half_size, dtype=jnp.float32) / head_size)
    angles = position.astype(jnp.float32)[:, None] * inverse[None, :]
    angles = jnp.concatenate([angles, angles], axis=1)
    return (jnp.cos(angles)[:, None, :], jnp.sin(angles)[:, None, :])


def apply_rope(vectors, cosine, sine):
    half_size = vectors.shape[-1] // 2
    turned = jnp.concatenate([-vectors[..., half_size:], vectors[..., :half_size]], axis=-1)
    return vectors * cosine + turned * sine


def rope_back(grad_in, cosine, sine):
    half_size = grad_in.shape[-1] // 2
    rotated = grad_in * sine
    return grad_in * cosine + jnp.concatenate(
        [rotated[..., half_size:], -rotated[..., :half_size]], axis=-1
    )


def rms_scale(inputs):
    return lax.rsqrt(jnp.mean(inputs * inputs, axis=-1, keepdims=True) + EPSILON)


def norm_back(inputs, scale_rows, gain_full, upstream):
    through = upstream * gain_full
    gain_term = jnp.sum(upstream * inputs * scale_rows, axis=0)
    grad_in = scale_rows * through - inputs * scale_rows**3 * jnp.mean(
        through * inputs, axis=-1, keepdims=True
    )
    return (grad_in, gain_term)


def score_block(query_block, key_rot, segment, row_start):
    block_rows = query_block.shape[0]
    places = jnp.arange(key_rot.shape[0], dtype=jnp.int32)
    row_place = row_start + jnp.arange(block_rows, dtype=jnp.int32)
    block_segment = lax.dynamic_slice_in_dim(segment, row_start, block_rows, 0)
    allowed = (block_segment[:, None] == segment[None, :]) & (places[None, :] <= row_place[:, None])
    raw_scores = jnp.einsum(
        "qhd,khd->hqk", query_block, key_rot, preferred_element_type=jnp.float32
    ) * query_block.shape[2] ** (-0.5)
    return jnp.where(allowed[None], raw_scores, -1e30)


def attend_forward(query_rot, key_rot, value_heads, segment):
    window = query_rot.shape[0]
    block_rows = min(512, window)

    def step(carry, block_index):
        row_start = block_index * block_rows
        query_block = lax.dynamic_slice_in_dim(query_rot, row_start, block_rows, 0)
        scores = score_block(query_block, key_rot, segment, row_start)
        row_top = jnp.max(scores, axis=-1, keepdims=True)
        weights_exp = jnp.exp(scores - row_top)
        row_total = jnp.sum(weights_exp, axis=-1, keepdims=True)
        probs = (weights_exp / row_total).astype(jnp.bfloat16)
        block_out = jnp.einsum(
            "hqk,khd->qhd", probs, value_heads, preferred_element_type=jnp.float32
        )
        log_total = (row_top + jnp.log(row_total))[:, :, 0].T
        return (carry, (block_out, log_total))

    block_ids = jnp.arange(window // block_rows, dtype=jnp.int32)
    _, (outputs, log_totals) = lax.scan(step, jnp.zeros((), jnp.int32), block_ids)
    return (outputs.reshape(query_rot.shape), log_totals.reshape(window, query_rot.shape[1]))


def attend_backward(query_rot, key_rot, value_heads, grad_heads, log_totals, segment):
    window = query_rot.shape[0]
    block_rows = min(512, window)
    scale_factor = query_rot.shape[2] ** (-0.5)

    def step(carry, block_index):
        key_acc, value_acc = carry
        row_start = block_index * block_rows
        query_block = lax.dynamic_slice_in_dim(query_rot, row_start, block_rows, 0)
        grad_block = lax.dynamic_slice_in_dim(grad_heads, row_start, block_rows, 0)
        total_block = lax.dynamic_slice_in_dim(log_totals, row_start, block_rows, 0)
        scores = score_block(query_block, key_rot, segment, row_start)
        probs = jnp.exp(scores - total_block.T[:, :, None])
        grad_probs = jnp.einsum(
            "qhd,khd->hqk", grad_block, value_heads, preferred_element_type=jnp.float32
        )
        inner_sum = jnp.sum(probs * grad_probs, axis=-1, keepdims=True)
        grad_scores = (probs * (grad_probs - inner_sum)).astype(jnp.bfloat16)
        query_part = (
            jnp.einsum("hqk,khd->qhd", grad_scores, key_rot, preferred_element_type=jnp.float32)
            * scale_factor
        )
        key_acc = (
            key_acc
            + jnp.einsum(
                "hqk,qhd->khd", grad_scores, query_block, preferred_element_type=jnp.float32
            )
            * scale_factor
        )
        value_acc = value_acc + jnp.einsum(
            "hqk,qhd->khd",
            probs.astype(jnp.bfloat16),
            grad_block,
            preferred_element_type=jnp.float32,
        )
        return ((key_acc, value_acc), query_part)

    start_acc = (jnp.zeros(key_rot.shape, jnp.float32), jnp.zeros(value_heads.shape, jnp.float32))
    block_ids = jnp.arange(window // block_rows, dtype=jnp.int32)
    (key_acc, value_acc), query_parts = lax.scan(step, start_acc, block_ids)
    return (query_parts.reshape(query_rot.shape), key_acc, value_acc)


def weight_terms(stored):
    joined = [jnp.concatenate(pieces, axis=0) for pieces in zip(*stored)]
    (
        normed,
        query_low,
        key_low,
        value_low,
        attn_rows,
        middle_low,
        normed_two,
        gate_low,
        up_low,
        upstream_low,
        hidden,
    ) = joined
    return jnp.concatenate(
        [
            contract_rows(normed, query_low),
            contract_rows(normed, key_low),
            contract_rows(normed, value_low),
            contract_rows(attn_rows, middle_low),
            contract_rows(normed_two, gate_low),
            contract_rows(normed_two, up_low),
            contract_rows(upstream_low, hidden),
        ],
        axis=1,
    )


def body(
    tokens,
    cotangent,
    seq_len,
    slot_order,
    norm1_gain,
    query_weight,
    key_weight,
    value_weight,
    output_weight,
    norm2_gain,
    gate_weight,
    up_weight,
    down_weight,
):
    seq_devices = lax.axis_size("sp")
    seq_rank = lax.axis_index("sp")
    shard_rank = lax.axis_index("fsdp")
    tok_rows = tokens.shape[1]
    window = seq_devices * tok_rows
    group_size = HEADS // KV
    kept = []
    outputs = []
    input_grads = []
    gain_sum = jnp.zeros((2, D), jnp.float32)
    grad_shards = None
    for micro_step in range(MB):
        gathered = (
            lax.all_gather(norm1_gain, "fsdp", axis=0, tiled=True),
            lax.all_gather(query_weight, "fsdp", axis=0, tiled=True),
            lax.all_gather(key_weight, "fsdp", axis=0, tiled=True),
            lax.all_gather(value_weight, "fsdp", axis=0, tiled=True),
            lax.all_gather(output_weight, "fsdp", axis=0, tiled=True),
            lax.all_gather(norm2_gain, "fsdp", axis=0, tiled=True),
            lax.all_gather(gate_weight, "fsdp", axis=0, tiled=True),
            lax.all_gather(up_weight, "fsdp", axis=0, tiled=True),
            lax.all_gather(down_weight, "fsdp", axis=0, tiled=True),
        )
        gain_one, w_query, w_key, w_value, w_output, gain_two, w_gate, w_up, w_down = gathered
        gain_one = gain_one.astype(jnp.float32)
        gain_two = gain_two.astype(jnp.float32)
        inputs = tokens[micro_step].astype(jnp.float32)
        window_index = shard_rank * MB + micro_step
        segment, position = window_layout(seq_len, slot_order, window_index, window)
        own_segment = lax.dynamic_slice_in_dim(segment, seq_rank * tok_rows, tok_rows, 0)
        valid_rows = (own_segment < 2).astype(jnp.float32)
        scale_one = rms_scale(inputs)
        normed = (inputs * scale_one * gain_one).astype(jnp.bfloat16)
        query_proj = plain_dot(normed, w_query).astype(jnp.bfloat16).reshape(tok_rows, HEADS, HDIM)
        key_proj = plain_dot(normed, w_key).astype(jnp.bfloat16).reshape(tok_rows, KV, HDIM)
        value_proj = plain_dot(normed, w_value).astype(jnp.bfloat16).reshape(tok_rows, KV, HDIM)
        packed = jnp.concatenate(
            [
                query_proj,
                jnp.repeat(key_proj, group_size, axis=1),
                jnp.repeat(value_proj, group_size, axis=1),
            ],
            axis=2,
        )
        head_side = lax.all_to_all(packed, "sp", split_axis=1, concat_axis=0, tiled=True)
        cosine, sine = rope_tables(position, HDIM)
        query_rot = apply_rope(head_side[:, :, :HDIM].astype(jnp.float32), cosine, sine).astype(
            jnp.bfloat16
        )
        key_rot = apply_rope(
            head_side[:, :, HDIM : 2 * HDIM].astype(jnp.float32), cosine, sine
        ).astype(jnp.bfloat16)
        value_heads = head_side[:, :, 2 * HDIM :]
        attended, log_totals = attend_forward(query_rot, key_rot, value_heads, segment)
        token_side = lax.all_to_all(
            attended.astype(jnp.bfloat16), "sp", split_axis=0, concat_axis=1, tiled=True
        )
        attn_rows = token_side.reshape(tok_rows, D)
        middle = inputs + plain_dot(attn_rows, w_output)
        scale_two = rms_scale(middle)
        normed_two = (middle * scale_two * gain_two).astype(jnp.bfloat16)
        gate_proj = plain_dot(normed_two, w_gate)
        up_proj = plain_dot(normed_two, w_up)
        gate_sig = jax.nn.sigmoid(gate_proj)
        hidden = (gate_proj * gate_sig * up_proj).astype(jnp.bfloat16)
        outputs.append(middle + contract_cols(hidden, w_down))
        upstream = cotangent[micro_step].astype(jnp.float32) * valid_rows[:, None]
        upstream_low = upstream.astype(jnp.bfloat16)
        hidden_grad = plain_dot(upstream_low, w_down)
        up_low = (hidden_grad * gate_proj * gate_sig).astype(jnp.bfloat16)
        gate_low = (hidden_grad * up_proj * gate_sig * (1.0 + gate_proj * (1.0 - gate_sig))).astype(
            jnp.bfloat16
        )
        normed_two_grad = contract_cols(gate_low, w_gate) + contract_cols(up_low, w_up)
        middle_grad, gain_two_term = norm_back(middle, scale_two, gain_two, normed_two_grad)
        middle_grad = middle_grad + upstream
        middle_low = middle_grad.astype(jnp.bfloat16)
        attn_grad = (
            contract_cols(middle_low, w_output).astype(jnp.bfloat16).reshape(tok_rows, HEADS, HDIM)
        )
        grad_heads = lax.all_to_all(attn_grad, "sp", split_axis=1, concat_axis=0, tiled=True)
        query_part, key_acc, value_acc = attend_backward(
            query_rot, key_rot, value_heads, grad_heads, log_totals, segment
        )
        packed_grad = jnp.concatenate(
            [rope_back(query_part, cosine, sine), rope_back(key_acc, cosine, sine), value_acc],
            axis=2,
        )
        grad_tokens = lax.all_to_all(packed_grad, "sp", split_axis=0, concat_axis=1, tiled=True)
        query_low = grad_tokens[:, :, :HDIM].reshape(tok_rows, D).astype(jnp.bfloat16)
        key_low = (
            grad_tokens[:, :, HDIM : 2 * HDIM]
            .reshape(tok_rows, KV, group_size, HDIM)
            .sum(axis=2)
            .reshape(tok_rows, KV * HDIM)
            .astype(jnp.bfloat16)
        )
        value_low = (
            grad_tokens[:, :, 2 * HDIM :]
            .reshape(tok_rows, KV, group_size, HDIM)
            .sum(axis=2)
            .reshape(tok_rows, KV * HDIM)
            .astype(jnp.bfloat16)
        )
        normed_grad = (
            contract_cols(query_low, w_query)
            + contract_cols(key_low, w_key)
            + contract_cols(value_low, w_value)
        )
        inputs_grad, gain_one_term = norm_back(inputs, scale_one, gain_one, normed_grad)
        input_grads.append(inputs_grad + middle_grad)
        gain_sum = gain_sum + jnp.stack([gain_one_term, gain_two_term])
        kept.append(
            (
                normed,
                query_low,
                key_low,
                value_low,
                attn_rows,
                middle_low,
                normed_two,
                gate_low,
                up_low,
                upstream_low,
                hidden,
            )
        )
        grad_shards = None
    grad_shards = lax.psum_scatter(
        weight_terms(kept), ("fsdp", "sp"), scatter_dimension=0, tiled=True
    )
    gain_shards = lax.psum_scatter(gain_sum, ("fsdp", "sp"), scatter_dimension=1, tiled=True)
    kv_width = KV * HDIM
    edges = [
        0,
        D,
        D + kv_width,
        D + 2 * kv_width,
        2 * D + 2 * kv_width,
        2 * D + 2 * kv_width + FF,
        2 * D + 2 * kv_width + 2 * FF,
        2 * D + 2 * kv_width + 3 * FF,
    ]
    pieces = [grad_shards[:, edges[slot] : edges[slot + 1]] for slot in range(7)]
    return (
        jnp.stack(outputs),
        jnp.stack(input_grads),
        gain_shards[0],
        pieces[0],
        pieces[1],
        pieces[2],
        pieces[3],
        gain_shards[1],
        pieces[4],
        pieces[5],
        pieces[6],
    )


def mesh_place(n_sp):
    shard = lax.axis_index("fsdp")
    rank = lax.axis_index("sp")
    group = n_sp // MB
    chip, core = shard // 2, shard % 2
    micro, member = rank // group, rank % group
    high, low = member // 2, member % 2
    base = micro * group
    peers = (
        (shard, base + high * 2 + (1 - low)),
        (shard, base + (1 - high) * 2 + low),
        (shard, base + (1 - high) * 2 + (1 - low)),
    )
    members = (high * 2 + (1 - low), (1 - high) * 2 + low, (1 - high) * 2 + (1 - low))
    partner = (shard, (1 - micro) * group + member)
    core_mate = (chip * 2 + (1 - core), rank)
    chip_mate = ((1 - chip) * 2 + core, rank)
    far_mate = ((1 - chip) * 2 + (1 - core), rank)
    return shard, rank, micro, member, peers, members, partner, core_mate, chip_mate, far_mate


def greet(devices):
    barrier = pltpu.get_barrier_semaphore()
    for device in devices:
        pl.semaphore_signal(barrier, inc=1, device_id=device, device_id_type=MESH)
    pl.semaphore_wait(barrier, len(devices))


def lane_ids(shape):
    return lax.broadcasted_iota(jnp.int32, shape, len(shape) - 1)


def turn(vectors):
    width = vectors.shape[-1]
    ahead = pltpu.roll(vectors, width - HDIM // 2, 1)
    behind = pltpu.roll(vectors, HDIM // 2, 1)
    first = lane_ids(vectors.shape) % HDIM < HDIM // 2
    return jnp.where(first, -ahead, behind)


def turn_back(vectors):
    return -turn(vectors)


def softmax_rows(query_pair, key_twice, bias, lower):
    lanes = lane_ids(query_pair.shape)
    query = jnp.where((lanes < HDIM) == lower, query_pair, jnp.zeros_like(query_pair))
    scores = contract_cols(query, key_twice) * HDIM**-0.5 + bias
    top = jnp.max(scores, axis=-1, keepdims=True)
    weights_exp = jnp.exp(scores - top)
    return weights_exp * (1.0 / jnp.sum(weights_exp, axis=-1, keepdims=True))


def row_places(shape, dim, group, tok_rows):
    ids = lax.broadcasted_iota(jnp.int32, shape, dim)
    own_rows = MB * tok_rows
    return ((ids % own_rows) // tok_rows) * (group * tok_rows) + (ids // own_rows) * tok_rows + ids % tok_rows


def pair_bias(window, group, tok_rows, first_len, both_len):
    place = row_places((window, 1), 0, group, tok_rows)
    key_place = row_places((1, window), 1, group, tok_rows)
    anchor = jnp.where(place < first_len, 0, jnp.where(place < both_len, first_len, both_len))
    return jnp.where((key_place <= place) & (key_place >= anchor), 0.0, -1e30)


def front_kernel(
    n_sp,
    tokens,
    cotangent,
    seq_len,
    slot_order,
    gains,
    wq_in,
    wkv_in,
    wo_in,
    wg_in,
    wu_in,
    wd_in,
    cosine,
    sine,
    xs,
    upstream,
    normed,
    query_rot,
    keys,
    values,
    attended,
    middle,
    normed_two,
    wq,
    wkv,
    wo,
    wg,
    wu,
    wd,
    gains_all,
    gs,
    sent,
    got,
    bias,
    local_sem,
    send_sem,
    recv_sem,
):
    place = mesh_place(n_sp)
    shard, rank, micro, member, peers, members, partner, core_mate, chip_mate, far_mate = place
    group = n_sp // MB
    tok_rows = tokens.shape[1]
    own_rows = MB * tok_rows
    window = group * own_rows
    greet((*peers, partner, core_mate, chip_mate, far_mate))

    def send(index, source, target, device):
        copy = pltpu.make_async_remote_copy(
            src_ref=source,
            dst_ref=target,
            send_sem=send_sem.at[index],
            recv_sem=recv_sem.at[index],
            device_id=device,
            device_id_type=MESH,
        )
        copy.start()
        return copy

    def move(index, source, target):
        copy = pltpu.make_async_copy(source, target, local_sem.at[index])
        copy.start()
        return copy

    swap_x = send(0, tokens.at[1 - micro], xs.at[micro], partner)
    swap_g = send(1, cotangent.at[1 - micro], gs.at[micro], partner)
    own_x = move(0, tokens.at[micro], xs.at[micro])
    own_g = move(1, cotangent.at[micro], gs.at[micro])
    gain_sends = [
        send(2 + i, gains, gains_all.at[shard], device) for i, device in enumerate((core_mate, chip_mate, far_mate))
    ]
    own_gain = move(2, gains, gains_all.at[shard])

    def columns(ref, width):
        return ref.at[:, pl.ds(pl.multiple_of(member * width, 128), width)]

    chip_shard = (1 - shard // 2) * 2 + shard % 2
    width_q, width_f = wq.shape[2], wg.shape[2]
    parts = (
        (columns(wq_in, width_q), wq),
        (wkv_in, wkv),
        (columns(wg_in, width_f), wg),
        (columns(wu_in, width_f), wu),
        (columns(wd_in, width_f), wd),
    )

    def weight_out(i):
        source, target = parts[i]
        over_chip = send(5 + 3 * i, source, target.at[shard], chip_mate)
        over_core = send(6 + 3 * i, source, target.at[shard], core_mate)
        here = move(3 + i, source, target.at[shard])
        return over_chip, over_core, here

    def weight_on(i):
        target = parts[i][1]
        return send(7 + 3 * i, target.at[chip_shard], target.at[chip_shard], core_mate)

    started = {i: weight_out(i) for i in (0, 1)}
    wo_x, wo_core, wo_on = 20, 21, 22

    def wo_copy(index, source, device):
        return pltpu.make_async_remote_copy(
            src_ref=source,
            dst_ref=wo,
            send_sem=send_sem.at[index],
            recv_sem=recv_sem.at[index],
            device_id=device,
            device_id_type=MESH,
        )

    same_chip = shard // 2 == member // 2
    same_core = shard % 2 == member % 2
    wo_here = pltpu.make_async_copy(wo_in, wo, local_sem.at[8])

    @pl.when(same_chip & same_core)
    def _():
        wo_copy(wo_x, wo_in, chip_mate).start()
        wo_copy(wo_core, wo_in, core_mate).start()
        wo_here.start()

    first_len = seq_len[slot_order[2 * (shard * MB + micro)]]
    both_len = first_len + seq_len[slot_order[2 * (shard * MB + micro) + 1]]

    own_gain.wait()
    for copy in gain_sends:
        copy.wait()
    gain_one = jnp.concatenate([gains_all[f, 0:1, :] for f in range(KV)], axis=1)
    gain_two = jnp.concatenate([gains_all[f, 1:2, :] for f in range(KV)], axis=1)
    own_x.wait()
    swap_x.wait()
    inputs = xs[...].reshape(own_rows, D).astype(jnp.float32)
    normed[member] = (inputs * rms_scale(inputs) * gain_one).astype(jnp.bfloat16)
    gather = [send(23 + i, normed.at[member], normed.at[member], device) for i, device in enumerate(peers)]

    own_g.wait()
    swap_g.wait()
    ids = lax.broadcasted_iota(jnp.int32, (own_rows, 1), 0)
    own_place = (ids // tok_rows) * (group * tok_rows) + member * tok_rows + ids % tok_rows
    valid = jnp.where(own_place < both_len, 1.0, 0.0)
    upstream[member] = (gs[...].reshape(own_rows, D).astype(jnp.float32) * valid).astype(jnp.bfloat16)

    on = []
    for i in (0, 1):
        started[i][0].wait()
        on.append(weight_on(i))
    for i in (2, 3, 4):
        started[i] = weight_out(i)
    for i in (0, 1):
        started[i][1].wait()
        started[i][2].wait()
    for copy in on:
        copy.wait()

    def project(rows):
        block = normed[rows]
        place_rows = pl.ds(pl.multiple_of(rows * own_rows, own_rows), own_rows)
        query = jnp.zeros((own_rows, width_q), jnp.float32)
        pair = jnp.zeros((own_rows, 2 * HDIM), jnp.float32)
        for f in range(KV):
            part = block[:, f * (D // KV) : (f + 1) * (D // KV)]
            query += plain_dot(part, wq[f])
            pair += plain_dot(part, wkv[f])
        cos, sin = cosine[place_rows, :], sine[place_rows, :]
        for j in range(width_q // 128):
            lanes = slice(j * 128, (j + 1) * 128)
            head = query[:, lanes].astype(jnp.bfloat16).astype(jnp.float32)
            query_rot[place_rows, lanes] = (head * cos + turn(head) * sin).astype(jnp.bfloat16)
        pair = pair.astype(jnp.bfloat16).astype(jnp.float32)
        turned_key = pair * cos + turn(pair) * sin
        lower = lane_ids(pair.shape) < HDIM
        keys[place_rows, :] = jnp.where(lower, turned_key, pltpu.roll(turned_key, HDIM, 1)).astype(jnp.bfloat16)
        values[place_rows, :] = jnp.where(lower, pltpu.roll(pair, HDIM, 1), pair).astype(jnp.bfloat16)

    project(member)
    for i, copy in enumerate(gather):
        copy.wait()
        project(members[i])
    gather_g = [send(26 + i, upstream.at[member], upstream.at[member], device) for i, device in enumerate(peers)]

    bias[...] = pair_bias(window, group, tok_rows, first_len, both_len)
    key_twice = keys[...]
    value_twice = values[...]
    lower = lane_ids(value_twice.shape) < HDIM
    value_low = jnp.where(lower, value_twice, jnp.zeros_like(value_twice))
    value_high = jnp.where(lower, jnp.zeros_like(value_twice), value_twice)

    @pl.loop(0, width_q // 128)
    def _(j):
        lanes = pl.ds(pl.multiple_of(j * 128, 128), 128)
        pair = query_rot[:, lanes]
        low_probs = softmax_rows(pair, key_twice, bias[...], True).astype(jnp.bfloat16)
        total = plain_dot(low_probs, value_low)
        high_probs = softmax_rows(pair, key_twice, bias[...], False).astype(jnp.bfloat16)
        total += plain_dot(high_probs, value_high)
        attended[:, lanes] = total.astype(jnp.bfloat16)

    @pl.when(same_chip & same_core)
    def _():
        wo_copy(wo_x, wo_in, chip_mate).wait_send()
        wo_copy(wo_core, wo_in, core_mate).wait_send()
        wo_here.wait()

    @pl.when(jnp.logical_not(same_chip) & same_core)
    def _():
        wo_copy(wo_x, wo_in, chip_mate).wait_recv()
        forward = wo_copy(wo_on, wo, core_mate)
        forward.start()
        forward.wait_send()

    @pl.when(same_chip & jnp.logical_not(same_core))
    def _():
        wo_copy(wo_core, wo_in, core_mate).wait_recv()

    @pl.when(jnp.logical_not(same_chip) & jnp.logical_not(same_core))
    def _():
        wo_copy(wo_on, wo, core_mate).wait_recv()

    def project_out(rows):
        place_rows = pl.ds(pl.multiple_of(rows * own_rows, own_rows), own_rows)
        return plain_dot(attended[place_rows, :], wo[...])

    sums = {}
    for i in (2, 0, 1):
        sent[i] = project_out(members[i]).astype(jnp.bfloat16)
        sums[i] = send(29 + i, sent.at[i], got.at[i], peers[i])
    total = inputs + project_out(member)
    for i in (0, 1, 2):
        sums[i].wait()
        total += got[i].astype(jnp.float32)
    middle[...] = total
    normed_two[member] = (total * rms_scale(total) * gain_two).astype(jnp.bfloat16)
    gather_two = [
        send(32 + i, normed_two.at[member], normed_two.at[member], device) for i, device in enumerate(peers)
    ]
    on = []
    for i in (2, 3, 4):
        started[i][0].wait()
        on.append(weight_on(i))
        started[i][1].wait()
        started[i][2].wait()
    for copy in (*on, *gather_g, *gather_two):
        copy.wait()


def front(n_sp, tok_rows, heads, *operands):
    group = n_sp // MB
    own_rows = MB * tok_rows
    window = group * own_rows
    width_q = heads * HDIM
    width_f = FF // group
    low = jnp.bfloat16
    vmem = pl.BlockSpec(memory_space=pltpu.VMEM)
    anywhere = pl.BlockSpec(memory_space=pl.ANY)
    smem = pl.BlockSpec(memory_space=pltpu.SMEM)
    shape = jax.ShapeDtypeStruct
    return pl.pallas_call(
        functools.partial(front_kernel, n_sp),
        out_shape=(
            shape((MB, tok_rows, D), low),
            shape((group, own_rows, D), low),
            shape((group, own_rows, D), low),
            shape((window, width_q), low),
            shape((window, 2 * HDIM), low),
            shape((window, 2 * HDIM), low),
            shape((window, width_q), low),
            shape((own_rows, D), jnp.float32),
            shape((group, own_rows, D), low),
            shape((KV, D // KV, width_q), low),
            shape((KV, D // KV, 2 * HDIM), low),
            shape((width_q, D), low),
            shape((KV, D // KV, width_f), low),
            shape((KV, D // KV, width_f), low),
            shape((KV, D // KV, width_f), low),
            shape((KV, 8, D // KV), jnp.float32),
        ),
        in_specs=[anywhere, anywhere, smem, smem, vmem, anywhere, anywhere, anywhere, anywhere, anywhere, anywhere, vmem, vmem],
        out_specs=tuple([vmem] * 12 + [anywhere] * 3 + [vmem]),
        scratch_shapes=[
            pltpu.VMEM((MB, tok_rows, D), low),
            pltpu.VMEM((group - 1, own_rows, D), low),
            pltpu.VMEM((group - 1, own_rows, D), low),
            pltpu.VMEM((window, window), jnp.float32),
            pltpu.SemaphoreType.DMA((9,)),
            pltpu.SemaphoreType.DMA((35,)),
            pltpu.SemaphoreType.DMA((35,)),
        ],
        compiler_params=pltpu.CompilerParams(
            collective_id=0, has_side_effects=True, vmem_limit_bytes=VMEM_BYTES
        ),
        cost_estimate=pl.CostEstimate(flops=8 * 10**9, bytes_accessed=40 * 10**6, transcendentals=2 * 10**6),
        name="front",
    )(*operands)


def group_body(
    tokens,
    cotangent,
    seq_len,
    slot_order,
    norm1_gain,
    query_weight,
    key_weight,
    value_weight,
    output_weight,
    norm2_gain,
    gate_weight,
    up_weight,
    down_weight,
):
    n_sp = lax.axis_size("sp")
    n_fsdp = lax.axis_size("fsdp")
    group = n_sp // MB
    rank = lax.axis_index("sp")
    shard = lax.axis_index("fsdp")
    micro = rank // group
    member = rank % group
    tok_rows = tokens.shape[1]
    window = n_sp * tok_rows
    own_rows = MB * tok_rows
    groups = [[m * group + t for t in range(group)] for m in range(MB)]
    both = ("fsdp", "sp")
    members = [(m * group + t, t) for m in range(MB) for t in range(group)]
    flat = lambda f, s: f * n_sp + s

    def swap(array):
        return lax.ppermute(array, "sp", [(s, (s + group) % n_sp) for s in range(n_sp)])

    def pick(pair, index):
        return lax.dynamic_index_in_dim(pair, index, 0, keepdims=False)

    def in_order(mine, theirs):
        return jnp.where(micro == 0, jnp.concatenate([mine, theirs]), jnp.concatenate([theirs, mine]))

    def gather_rows(array):
        return lax.all_gather(array, "sp", axis=0, tiled=True, axis_index_groups=groups)

    def sum_rows(partial):
        pieces = lax.all_to_all(
            partial.astype(jnp.bfloat16).reshape(group, own_rows, D),
            "sp", split_axis=0, concat_axis=0, tiled=True, axis_index_groups=groups,
        )
        return jnp.sum(pieces.astype(jnp.float32), axis=0)

    def gather_weight(weight):
        width = weight.shape[1] // group
        part = lax.dynamic_slice_in_dim(weight, member * width, width, 1)
        return lax.all_gather(part, "fsdp", axis=0, tiled=True)

    def reduce_weight(partial):
        width = partial.shape[1]
        rows = partial.reshape(2, 2, MB, group, tok_rows, width)

        def halve(array, axis, index, axis_name, perm):
            keep = lax.dynamic_index_in_dim(array, index, axis, keepdims=False)
            send = lax.dynamic_index_in_dim(array, 1 - index, axis, keepdims=False)
            got = lax.ppermute(send.astype(jnp.bfloat16), axis_name, perm)
            return keep + got.astype(jnp.float32)

        rows = halve(rows, 1, shard % 2, "fsdp", [(f, f ^ 1) for f in range(n_fsdp)])
        rows = halve(rows, 0, shard // 2, "fsdp", [(f, f ^ 2) for f in range(n_fsdp)])
        rows = halve(rows, 0, micro, "sp", [(s, (s + group) % n_sp) for s in range(n_sp)])
        rows = lax.all_to_all(
            rows.astype(jnp.bfloat16), "sp", split_axis=0, concat_axis=0, tiled=True, axis_index_groups=groups
        )
        return rows.astype(jnp.float32).transpose(1, 0, 2).reshape(tok_rows, group * width)

    first_len = seq_len[slot_order[2 * (shard * MB + micro)]]
    second_len = seq_len[slot_order[2 * (shard * MB + micro) + 1]]
    place = row_places((window,), 0, group, tok_rows)
    anchor = jnp.where(place < first_len, 0, jnp.where(place < first_len + second_len, first_len, first_len + second_len))
    inverse = ROPE_BASE ** (-2.0 * jnp.arange(HDIM // 2, dtype=jnp.float32) / HDIM)
    angles = (place - anchor).astype(jnp.float32)[:, None] * jnp.tile(inverse, 4)[None, :]
    cosine, sine = jnp.cos(angles), jnp.sin(angles)

    def columns(weight):
        width = weight.shape[1] // group
        return lax.dynamic_slice_in_dim(weight, member * width, width, 1)

    gains = jnp.concatenate(
        [norm1_gain[None], norm2_gain[None], jnp.zeros((6, norm1_gain.shape[0]), jnp.bfloat16)]
    ).astype(jnp.float32)
    kv_weight = jnp.concatenate([columns(key_weight), columns(value_weight)], axis=1)
    heads = HEADS // group
    (
        own_tokens,
        upstream_low,
        normed,
        query_rot,
        keys,
        values,
        attended,
        middle,
        normed_two,
        w_query,
        w_kv,
        w_output,
        w_gate,
        w_up,
        w_down,
        gains,
    ) = front(
        n_sp, tok_rows, heads,
        tokens, cotangent, seq_len, slot_order, gains,
        query_weight, kv_weight, output_weight, gate_weight, up_weight, down_weight, cosine, sine,
    )
    gain_one, gain_two = gains[:, 0].reshape(D), gains[:, 1].reshape(D)
    upstream_low, normed, normed_two = (rows.reshape(window, D) for rows in (upstream_low, normed, normed_two))
    w_query, w_kv, w_gate, w_up, w_down = (w.reshape(D, -1) for w in (w_query, w_kv, w_gate, w_up, w_down))
    w_key, w_value = w_kv[:, :HDIM], w_kv[:, HDIM:]
    inputs = own_tokens.reshape(own_rows, D).astype(jnp.float32)
    upstream = lax.dynamic_slice_in_dim(upstream_low, member * own_rows, own_rows, 0).astype(jnp.float32)
    scale_one = rms_scale(inputs)
    scale_two = rms_scale(middle)
    cosine, sine = cosine[:, None, :HDIM], sine[:, None, :HDIM]
    query_rot = query_rot.reshape(window, heads, HDIM)
    key_rot, value = keys[:, :HDIM], values[:, :HDIM]
    scale = HDIM**-0.5
    scores = jnp.einsum("qhd,kd->hqk", query_rot, key_rot, preferred_element_type=jnp.float32) * scale
    scores = scores + pair_bias(window, group, tok_rows, first_len, first_len + second_len)[None]
    probs = jax.nn.softmax(scores, axis=-1)
    probs_low = probs.astype(jnp.bfloat16)
    gate = plain_dot(normed_two, w_gate)
    up = plain_dot(normed_two, w_up)
    sig = jax.nn.sigmoid(gate)
    silu = gate * sig
    hidden = (silu * up).astype(jnp.bfloat16)
    block = middle + sum_rows(contract_cols(hidden, w_down))
    d_hidden = plain_dot(upstream_low, w_down)
    d_up = (d_hidden * silu).astype(jnp.bfloat16)
    d_gate = (d_hidden * up * sig * (1.0 + gate * (1.0 - sig))).astype(jnp.bfloat16)
    d_normed_two = sum_rows(contract_cols(d_gate, w_gate) + contract_cols(d_up, w_up))
    d_middle, gain_two_term = norm_back(middle, scale_two, gain_two, d_normed_two)
    d_middle = d_middle + upstream
    middle_low = gather_rows(d_middle.astype(jnp.bfloat16))

    d_attended = contract_cols(middle_low, w_output).astype(jnp.bfloat16).reshape(window, heads, HDIM)
    d_probs = jnp.einsum("qhd,kd->hqk", d_attended, value, preferred_element_type=jnp.float32)
    inner_sum = jnp.sum(probs * d_probs, axis=-1, keepdims=True)
    d_scores = (probs * (d_probs - inner_sum)).astype(jnp.bfloat16)
    d_query_rot = jnp.einsum("hqk,kd->qhd", d_scores, key_rot, preferred_element_type=jnp.float32) * scale
    d_key_rot = jnp.einsum("hqk,qhd->kd", d_scores, query_rot, preferred_element_type=jnp.float32) * scale
    d_value = jnp.einsum("hqk,qhd->kd", probs_low, d_attended, preferred_element_type=jnp.float32)
    d_query = rope_back(d_query_rot, cosine, sine).astype(jnp.bfloat16).reshape(window, heads * HDIM)
    d_key = rope_back(d_key_rot[:, None], cosine, sine)[:, 0].astype(jnp.bfloat16)
    d_value = d_value.astype(jnp.bfloat16)
    d_normed = sum_rows(
        contract_cols(d_query, w_query) + contract_cols(d_key, w_key) + contract_cols(d_value, w_value)
    )
    d_inputs, gain_one_term = norm_back(inputs, scale_one, gain_one, d_normed)
    d_inputs = d_inputs + d_middle

    def to_owner(rows):
        halves = rows.reshape(MB, tok_rows, D)
        mine, theirs = pick(halves, micro), swap(pick(halves, 1 - micro))
        return jnp.where(micro == 0, jnp.stack([mine, theirs]), jnp.stack([theirs, mine]))

    gate_grad = reduce_weight(contract_rows(normed_two, d_gate))
    up_grad = reduce_weight(contract_rows(normed_two, d_up))
    down_grad = reduce_weight(contract_rows(upstream_low, hidden))
    query_grad = reduce_weight(contract_rows(normed, d_query))
    key_grad = reduce_weight(contract_rows(normed, d_key))
    value_grad = reduce_weight(contract_rows(normed, d_value))

    output_part = contract_rows(attended, middle_low)
    got = lax.ppermute(
        output_part.astype(jnp.bfloat16), both,
        [(flat(t ^ k ^ 1, s), flat(t ^ k, s)) for s, t in members for k in (0, 2)],
    )
    output_part = output_part + got.astype(jnp.float32)
    got = lax.ppermute(
        output_part.astype(jnp.bfloat16), both, [(flat(t ^ 2, s), flat(t, s)) for s, t in members]
    )
    output_part = (output_part + got.astype(jnp.float32)).reshape(MB, group * tok_rows, D)
    got = swap(pick(output_part, 1 - micro).astype(jnp.bfloat16))
    output_part = pick(output_part, micro) + got.astype(jnp.float32)
    pieces = lax.all_to_all(
        output_part.astype(jnp.bfloat16).reshape(group, tok_rows, D),
        "sp", split_axis=0, concat_axis=0, tiled=True, axis_index_groups=groups,
    )
    output_grad = pick(pieces, shard).astype(jnp.float32)

    gains = lax.psum_scatter(
        jnp.stack([gain_one_term, gain_two_term]), both, scatter_dimension=1, tiled=True
    )
    return (
        to_owner(block),
        to_owner(d_inputs),
        gains[0],
        query_grad,
        key_grad,
        value_grad,
        output_grad,
        gains[1],
        gate_grad,
        up_grad,
        down_grad,
    )


def solution(mesh):
    fits = mesh.shape["fsdp"] == KV and mesh.shape["sp"] == MB * KV
    placed = (
        P(None, ("fsdp", "sp"), None),
        P(None, ("fsdp", "sp"), None),
        P(),
        P(),
        P("fsdp"),
        P("fsdp", None),
        P("fsdp", None),
        P("fsdp", None),
        P("fsdp", None),
        P("fsdp"),
        P("fsdp", None),
        P("fsdp", None),
        P("fsdp", None),
    )
    return jax.shard_map(
        group_body if fits else body,
        mesh=mesh,
        in_specs=placed,
        out_specs=(
            P(None, ("fsdp", "sp"), None),
            P(None, ("fsdp", "sp"), None),
            P(("fsdp", "sp")),
            P(("fsdp", "sp"), None),
            P(("fsdp", "sp"), None),
            P(("fsdp", "sp"), None),
            P(("fsdp", "sp"), None),
            P(("fsdp", "sp")),
            P(("fsdp", "sp"), None),
            P(("fsdp", "sp"), None),
            P(("fsdp", "sp"), None),
        ),
        check_vma=False,
    )
```

```python
import functools

import jax
import jax.numpy as jnp
import numpy as np
from jax import lax
from jax.experimental import pallas as pl
from jax.experimental.pallas import tpu as pltpu
from jax.sharding import PartitionSpec as P

D = 2048
HEADS = 32
KV = 4
HDIM = 64
FF = 5632
MB = 2
MESH = pl.DeviceIdType.MESH
VMEM_BYTES = 60 * 2**20


EPSILON = 1e-05
ROPE_BASE = 10000.0


def plain_dot(left_side, right_side):
    return jnp.dot(left_side, right_side, preferred_element_type=jnp.float32)


def contract_rows(left_side, right_side):
    return lax.dot_general(
        left_side, right_side, (((0,), (0,)), ((), ())), preferred_element_type=jnp.float32
    )


def contract_cols(left_side, right_side):
    return lax.dot_general(
        left_side, right_side, (((1,), (1,)), ((), ())), preferred_element_type=jnp.float32
    )


def window_layout(seq_len, slot_order, window_index, window):
    first_len = seq_len[slot_order[2 * window_index]]
    second_len = seq_len[slot_order[2 * window_index + 1]]
    places = jnp.arange(window, dtype=jnp.int32)
    segment = jnp.where(
        places < first_len, 0, jnp.where(places < first_len + second_len, 1, 2)
    ).astype(jnp.int32)
    anchor = jnp.where(segment == 0, 0, jnp.where(segment == 1, first_len, first_len + second_len))
    return (segment, places - anchor)


def rope_tables(position, head_size):
    half_size = head_size // 2
    inverse = ROPE_BASE ** (-2.0 * jnp.arange(half_size, dtype=jnp.float32) / head_size)
    angles = position.astype(jnp.float32)[:, None] * inverse[None, :]
    angles = jnp.concatenate([angles, angles], axis=1)
    return (jnp.cos(angles)[:, None, :], jnp.sin(angles)[:, None, :])


def apply_rope(vectors, cosine, sine):
    half_size = vectors.shape[-1] // 2
    turned = jnp.concatenate([-vectors[..., half_size:], vectors[..., :half_size]], axis=-1)
    return vectors * cosine + turned * sine


def rope_back(grad_in, cosine, sine):
    half_size = grad_in.shape[-1] // 2
    rotated = grad_in * sine
    return grad_in * cosine + jnp.concatenate(
        [rotated[..., half_size:], -rotated[..., :half_size]], axis=-1
    )


def rms_scale(inputs):
    return lax.rsqrt(jnp.mean(inputs * inputs, axis=-1, keepdims=True) + EPSILON)


def norm_back(inputs, scale_rows, gain_full, upstream):
    through = upstream * gain_full
    gain_term = jnp.sum(upstream * inputs * scale_rows, axis=0)
    grad_in = scale_rows * through - inputs * scale_rows**3 * jnp.mean(
        through * inputs, axis=-1, keepdims=True
    )
    return (grad_in, gain_term)


def score_block(query_block, key_rot, segment, row_start):
    block_rows = query_block.shape[0]
    places = jnp.arange(key_rot.shape[0], dtype=jnp.int32)
    row_place = row_start + jnp.arange(block_rows, dtype=jnp.int32)
    block_segment = lax.dynamic_slice_in_dim(segment, row_start, block_rows, 0)
    allowed = (block_segment[:, None] == segment[None, :]) & (places[None, :] <= row_place[:, None])
    raw_scores = jnp.einsum(
        "qhd,khd->hqk", query_block, key_rot, preferred_element_type=jnp.float32
    ) * query_block.shape[2] ** (-0.5)
    return jnp.where(allowed[None], raw_scores, -1e30)


def attend_forward(query_rot, key_rot, value_heads, segment):
    window = query_rot.shape[0]
    block_rows = min(512, window)

    def step(carry, block_index):
        row_start = block_index * block_rows
        query_block = lax.dynamic_slice_in_dim(query_rot, row_start, block_rows, 0)
        scores = score_block(query_block, key_rot, segment, row_start)
        row_top = jnp.max(scores, axis=-1, keepdims=True)
        weights_exp = jnp.exp(scores - row_top)
        row_total = jnp.sum(weights_exp, axis=-1, keepdims=True)
        probs = (weights_exp / row_total).astype(jnp.bfloat16)
        block_out = jnp.einsum(
            "hqk,khd->qhd", probs, value_heads, preferred_element_type=jnp.float32
        )
        log_total = (row_top + jnp.log(row_total))[:, :, 0].T
        return (carry, (block_out, log_total))

    block_ids = jnp.arange(window // block_rows, dtype=jnp.int32)
    _, (outputs, log_totals) = lax.scan(step, jnp.zeros((), jnp.int32), block_ids)
    return (outputs.reshape(query_rot.shape), log_totals.reshape(window, query_rot.shape[1]))


def attend_backward(query_rot, key_rot, value_heads, grad_heads, log_totals, segment):
    window = query_rot.shape[0]
    block_rows = min(512, window)
    scale_factor = query_rot.shape[2] ** (-0.5)

    def step(carry, block_index):
        key_acc, value_acc = carry
        row_start = block_index * block_rows
        query_block = lax.dynamic_slice_in_dim(query_rot, row_start, block_rows, 0)
        grad_block = lax.dynamic_slice_in_dim(grad_heads, row_start, block_rows, 0)
        total_block = lax.dynamic_slice_in_dim(log_totals, row_start, block_rows, 0)
        scores = score_block(query_block, key_rot, segment, row_start)
        probs = jnp.exp(scores - total_block.T[:, :, None])
        grad_probs = jnp.einsum(
            "qhd,khd->hqk", grad_block, value_heads, preferred_element_type=jnp.float32
        )
        inner_sum = jnp.sum(probs * grad_probs, axis=-1, keepdims=True)
        grad_scores = (probs * (grad_probs - inner_sum)).astype(jnp.bfloat16)
        query_part = (
            jnp.einsum("hqk,khd->qhd", grad_scores, key_rot, preferred_element_type=jnp.float32)
            * scale_factor
        )
        key_acc = (
            key_acc
            + jnp.einsum(
                "hqk,qhd->khd", grad_scores, query_block, preferred_element_type=jnp.float32
            )
            * scale_factor
        )
        value_acc = value_acc + jnp.einsum(
            "hqk,qhd->khd",
            probs.astype(jnp.bfloat16),
            grad_block,
            preferred_element_type=jnp.float32,
        )
        return ((key_acc, value_acc), query_part)

    start_acc = (jnp.zeros(key_rot.shape, jnp.float32), jnp.zeros(value_heads.shape, jnp.float32))
    block_ids = jnp.arange(window // block_rows, dtype=jnp.int32)
    (key_acc, value_acc), query_parts = lax.scan(step, start_acc, block_ids)
    return (query_parts.reshape(query_rot.shape), key_acc, value_acc)


def weight_terms(stored):
    joined = [jnp.concatenate(pieces, axis=0) for pieces in zip(*stored)]
    (
        normed,
        query_low,
        key_low,
        value_low,
        attn_rows,
        middle_low,
        normed_two,
        gate_low,
        up_low,
        upstream_low,
        hidden,
    ) = joined
    return jnp.concatenate(
        [
            contract_rows(normed, query_low),
            contract_rows(normed, key_low),
            contract_rows(normed, value_low),
            contract_rows(attn_rows, middle_low),
            contract_rows(normed_two, gate_low),
            contract_rows(normed_two, up_low),
            contract_rows(upstream_low, hidden),
        ],
        axis=1,
    )


def body(
    tokens,
    cotangent,
    seq_len,
    slot_order,
    norm1_gain,
    query_weight,
    key_weight,
    value_weight,
    output_weight,
    norm2_gain,
    gate_weight,
    up_weight,
    down_weight,
):
    seq_devices = lax.axis_size("sp")
    seq_rank = lax.axis_index("sp")
    shard_rank = lax.axis_index("fsdp")
    tok_rows = tokens.shape[1]
    window = seq_devices * tok_rows
    group_size = HEADS // KV
    kept = []
    outputs = []
    input_grads = []
    gain_sum = jnp.zeros((2, D), jnp.float32)
    grad_shards = None
    for micro_step in range(MB):
        gathered = (
            lax.all_gather(norm1_gain, "fsdp", axis=0, tiled=True),
            lax.all_gather(query_weight, "fsdp", axis=0, tiled=True),
            lax.all_gather(key_weight, "fsdp", axis=0, tiled=True),
            lax.all_gather(value_weight, "fsdp", axis=0, tiled=True),
            lax.all_gather(output_weight, "fsdp", axis=0, tiled=True),
            lax.all_gather(norm2_gain, "fsdp", axis=0, tiled=True),
            lax.all_gather(gate_weight, "fsdp", axis=0, tiled=True),
            lax.all_gather(up_weight, "fsdp", axis=0, tiled=True),
            lax.all_gather(down_weight, "fsdp", axis=0, tiled=True),
        )
        gain_one, w_query, w_key, w_value, w_output, gain_two, w_gate, w_up, w_down = gathered
        gain_one = gain_one.astype(jnp.float32)
        gain_two = gain_two.astype(jnp.float32)
        inputs = tokens[micro_step].astype(jnp.float32)
        window_index = shard_rank * MB + micro_step
        segment, position = window_layout(seq_len, slot_order, window_index, window)
        own_segment = lax.dynamic_slice_in_dim(segment, seq_rank * tok_rows, tok_rows, 0)
        valid_rows = (own_segment < 2).astype(jnp.float32)
        scale_one = rms_scale(inputs)
        normed = (inputs * scale_one * gain_one).astype(jnp.bfloat16)
        query_proj = plain_dot(normed, w_query).astype(jnp.bfloat16).reshape(tok_rows, HEADS, HDIM)
        key_proj = plain_dot(normed, w_key).astype(jnp.bfloat16).reshape(tok_rows, KV, HDIM)
        value_proj = plain_dot(normed, w_value).astype(jnp.bfloat16).reshape(tok_rows, KV, HDIM)
        packed = jnp.concatenate(
            [
                query_proj,
                jnp.repeat(key_proj, group_size, axis=1),
                jnp.repeat(value_proj, group_size, axis=1),
            ],
            axis=2,
        )
        head_side = lax.all_to_all(packed, "sp", split_axis=1, concat_axis=0, tiled=True)
        cosine, sine = rope_tables(position, HDIM)
        query_rot = apply_rope(head_side[:, :, :HDIM].astype(jnp.float32), cosine, sine).astype(
            jnp.bfloat16
        )
        key_rot = apply_rope(
            head_side[:, :, HDIM : 2 * HDIM].astype(jnp.float32), cosine, sine
        ).astype(jnp.bfloat16)
        value_heads = head_side[:, :, 2 * HDIM :]
        attended, log_totals = attend_forward(query_rot, key_rot, value_heads, segment)
        token_side = lax.all_to_all(
            attended.astype(jnp.bfloat16), "sp", split_axis=0, concat_axis=1, tiled=True
        )
        attn_rows = token_side.reshape(tok_rows, D)
        middle = inputs + plain_dot(attn_rows, w_output)
        scale_two = rms_scale(middle)
        normed_two = (middle * scale_two * gain_two).astype(jnp.bfloat16)
        gate_proj = plain_dot(normed_two, w_gate)
        up_proj = plain_dot(normed_two, w_up)
        gate_sig = jax.nn.sigmoid(gate_proj)
        hidden = (gate_proj * gate_sig * up_proj).astype(jnp.bfloat16)
        outputs.append(middle + contract_cols(hidden, w_down))
        upstream = cotangent[micro_step].astype(jnp.float32) * valid_rows[:, None]
        upstream_low = upstream.astype(jnp.bfloat16)
        hidden_grad = plain_dot(upstream_low, w_down)
        up_low = (hidden_grad * gate_proj * gate_sig).astype(jnp.bfloat16)
        gate_low = (hidden_grad * up_proj * gate_sig * (1.0 + gate_proj * (1.0 - gate_sig))).astype(
            jnp.bfloat16
        )
        normed_two_grad = contract_cols(gate_low, w_gate) + contract_cols(up_low, w_up)
        middle_grad, gain_two_term = norm_back(middle, scale_two, gain_two, normed_two_grad)
        middle_grad = middle_grad + upstream
        middle_low = middle_grad.astype(jnp.bfloat16)
        attn_grad = (
            contract_cols(middle_low, w_output).astype(jnp.bfloat16).reshape(tok_rows, HEADS, HDIM)
        )
        grad_heads = lax.all_to_all(attn_grad, "sp", split_axis=1, concat_axis=0, tiled=True)
        query_part, key_acc, value_acc = attend_backward(
            query_rot, key_rot, value_heads, grad_heads, log_totals, segment
        )
        packed_grad = jnp.concatenate(
            [rope_back(query_part, cosine, sine), rope_back(key_acc, cosine, sine), value_acc],
            axis=2,
        )
        grad_tokens = lax.all_to_all(packed_grad, "sp", split_axis=0, concat_axis=1, tiled=True)
        query_low = grad_tokens[:, :, :HDIM].reshape(tok_rows, D).astype(jnp.bfloat16)
        key_low = (
            grad_tokens[:, :, HDIM : 2 * HDIM]
            .reshape(tok_rows, KV, group_size, HDIM)
            .sum(axis=2)
            .reshape(tok_rows, KV * HDIM)
            .astype(jnp.bfloat16)
        )
        value_low = (
            grad_tokens[:, :, 2 * HDIM :]
            .reshape(tok_rows, KV, group_size, HDIM)
            .sum(axis=2)
            .reshape(tok_rows, KV * HDIM)
            .astype(jnp.bfloat16)
        )
        normed_grad = (
            contract_cols(query_low, w_query)
            + contract_cols(key_low, w_key)
            + contract_cols(value_low, w_value)
        )
        inputs_grad, gain_one_term = norm_back(inputs, scale_one, gain_one, normed_grad)
        input_grads.append(inputs_grad + middle_grad)
        gain_sum = gain_sum + jnp.stack([gain_one_term, gain_two_term])
        kept.append(
            (
                normed,
                query_low,
                key_low,
                value_low,
                attn_rows,
                middle_low,
                normed_two,
                gate_low,
                up_low,
                upstream_low,
                hidden,
            )
        )
        grad_shards = None
    grad_shards = lax.psum_scatter(
        weight_terms(kept), ("fsdp", "sp"), scatter_dimension=0, tiled=True
    )
    gain_shards = lax.psum_scatter(gain_sum, ("fsdp", "sp"), scatter_dimension=1, tiled=True)
    kv_width = KV * HDIM
    edges = [
        0,
        D,
        D + kv_width,
        D + 2 * kv_width,
        2 * D + 2 * kv_width,
        2 * D + 2 * kv_width + FF,
        2 * D + 2 * kv_width + 2 * FF,
        2 * D + 2 * kv_width + 3 * FF,
    ]
    pieces = [grad_shards[:, edges[slot] : edges[slot + 1]] for slot in range(7)]
    return (
        jnp.stack(outputs),
        jnp.stack(input_grads),
        gain_shards[0],
        pieces[0],
        pieces[1],
        pieces[2],
        pieces[3],
        gain_shards[1],
        pieces[4],
        pieces[5],
        pieces[6],
    )


def mesh_place(n_sp):
    shard = lax.axis_index("fsdp")
    rank = lax.axis_index("sp")
    group = n_sp // MB
    chip, core = shard // 2, shard % 2
    micro, member = rank // group, rank % group
    high, low = member // 2, member % 2
    base = micro * group
    peers = (
        (shard, base + high * 2 + (1 - low)),
        (shard, base + (1 - high) * 2 + low),
        (shard, base + (1 - high) * 2 + (1 - low)),
    )
    members = (high * 2 + (1 - low), (1 - high) * 2 + low, (1 - high) * 2 + (1 - low))
    partner = (shard, (1 - micro) * group + member)
    core_mate = (chip * 2 + (1 - core), rank)
    chip_mate = ((1 - chip) * 2 + core, rank)
    far_mate = ((1 - chip) * 2 + (1 - core), rank)
    return shard, rank, micro, member, peers, members, partner, core_mate, chip_mate, far_mate


def greet(devices):
    barrier = pltpu.get_barrier_semaphore()
    for device in devices:
        pl.semaphore_signal(barrier, inc=1, device_id=device, device_id_type=MESH)
    pl.semaphore_wait(barrier, len(devices))


def lane_ids(shape):
    return lax.broadcasted_iota(jnp.int32, shape, len(shape) - 1)


def turn(vectors):
    width = vectors.shape[-1]
    ahead = pltpu.roll(vectors, width - HDIM // 2, 1)
    behind = pltpu.roll(vectors, HDIM // 2, 1)
    first = lane_ids(vectors.shape) % HDIM < HDIM // 2
    return jnp.where(first, -ahead, behind)


def turn_back(vectors):
    return -turn(vectors)


def softmax_columns(key_side, query_pair, bias):
    scores = contract_cols(key_side, query_pair) + bias
    weights_exp = jnp.exp(scores - jnp.max(scores, axis=0, keepdims=True))
    return weights_exp * (1.0 / jnp.sum(weights_exp, axis=0, keepdims=True))


def row_places(shape, dim, group, tok_rows):
    ids = lax.broadcasted_iota(jnp.int32, shape, dim)
    own_rows = MB * tok_rows
    return ((ids % own_rows) // tok_rows) * (group * tok_rows) + (ids // own_rows) * tok_rows + ids % tok_rows


def pair_bias(window, group, tok_rows, first_len, both_len):
    place = row_places((1, window), 1, group, tok_rows)
    key_place = row_places((window, 1), 0, group, tok_rows)
    anchor = jnp.where(place < first_len, 0, jnp.where(place < both_len, first_len, both_len))
    return jnp.where((key_place <= place) & (key_place >= anchor), 0.0, -1e30)


def front_kernel(
    n_sp,
    tokens,
    cotangent,
    seq_len,
    slot_order,
    gains,
    wq_in,
    wkv_in,
    wo_in,
    wg_in,
    wu_in,
    wd_in,
    cosine,
    sine,
    xs,
    upstream,
    normed,
    query_rot,
    keys,
    values,
    attended,
    middle,
    normed_two,
    wq,
    wkv,
    wo,
    wg,
    wu,
    wd,
    gains_all,
    gs,
    sent,
    got,
    bias,
    local_sem,
    send_sem,
    recv_sem,
):
    place = mesh_place(n_sp)
    shard, rank, micro, member, peers, members, partner, core_mate, chip_mate, far_mate = place
    group = n_sp // MB
    tok_rows = tokens.shape[1]
    own_rows = MB * tok_rows
    window = group * own_rows
    greet((*peers, partner, core_mate, chip_mate, far_mate))

    def send(index, source, target, device):
        copy = pltpu.make_async_remote_copy(
            src_ref=source,
            dst_ref=target,
            send_sem=send_sem.at[index],
            recv_sem=recv_sem.at[index],
            device_id=device,
            device_id_type=MESH,
        )
        copy.start()
        return copy

    def move(index, source, target):
        copy = pltpu.make_async_copy(source, target, local_sem.at[index])
        copy.start()
        return copy

    swap_x = send(0, tokens.at[1 - micro], xs.at[micro], partner)
    swap_g = send(1, cotangent.at[1 - micro], gs.at[micro], partner)
    own_x = move(0, tokens.at[micro], xs.at[micro])
    own_g = move(1, cotangent.at[micro], gs.at[micro])
    gain_sends = [
        send(2 + i, gains, gains_all.at[shard], device) for i, device in enumerate((core_mate, chip_mate, far_mate))
    ]
    own_gain = move(2, gains, gains_all.at[shard])

    def columns(ref, width):
        return ref.at[:, pl.ds(pl.multiple_of(member * width, 128), width)]

    chip_shard = (1 - shard // 2) * 2 + shard % 2
    width_q, width_f = wq.shape[2], wg.shape[2]
    parts = (
        (columns(wq_in, width_q), wq),
        (wkv_in, wkv),
        (columns(wg_in, width_f), wg),
        (columns(wu_in, width_f), wu),
        (columns(wd_in, width_f), wd),
    )

    def weight_out(i):
        source, target = parts[i]
        over_chip = send(5 + 3 * i, source, target.at[shard], chip_mate)
        over_core = send(6 + 3 * i, source, target.at[shard], core_mate)
        here = move(3 + i, source, target.at[shard])
        return over_chip, over_core, here

    def weight_on(i):
        target = parts[i][1]
        return send(7 + 3 * i, target.at[chip_shard], target.at[chip_shard], core_mate)

    started = {i: weight_out(i) for i in (0, 1)}
    wo_x, wo_core, wo_on = 20, 21, 22

    def wo_copy(index, source, device):
        return pltpu.make_async_remote_copy(
            src_ref=source,
            dst_ref=wo,
            send_sem=send_sem.at[index],
            recv_sem=recv_sem.at[index],
            device_id=device,
            device_id_type=MESH,
        )

    same_chip = shard // 2 == member // 2
    same_core = shard % 2 == member % 2
    wo_here = pltpu.make_async_copy(wo_in, wo, local_sem.at[8])

    @pl.when(same_chip & same_core)
    def _():
        wo_copy(wo_x, wo_in, chip_mate).start()
        wo_copy(wo_core, wo_in, core_mate).start()
        wo_here.start()

    first_len = seq_len[slot_order[2 * (shard * MB + micro)]]
    both_len = first_len + seq_len[slot_order[2 * (shard * MB + micro) + 1]]

    own_gain.wait()
    for copy in gain_sends:
        copy.wait()
    gain_one = jnp.concatenate([gains_all[f, 0:1, :] for f in range(KV)], axis=1)
    gain_two = jnp.concatenate([gains_all[f, 1:2, :] for f in range(KV)], axis=1)
    own_x.wait()
    swap_x.wait()
    inputs = xs[...].reshape(own_rows, D).astype(jnp.float32)
    normed[member] = (inputs * rms_scale(inputs) * gain_one).astype(jnp.bfloat16)
    gather = [send(23 + i, normed.at[member], normed.at[member], device) for i, device in enumerate(peers)]

    own_g.wait()
    swap_g.wait()
    ids = lax.broadcasted_iota(jnp.int32, (own_rows, 1), 0)
    own_place = (ids // tok_rows) * (group * tok_rows) + member * tok_rows + ids % tok_rows
    valid = jnp.where(own_place < both_len, 1.0, 0.0)
    upstream[member] = (gs[...].reshape(own_rows, D).astype(jnp.float32) * valid).astype(jnp.bfloat16)

    on = []
    for i in (0, 1):
        started[i][0].wait()
        on.append(weight_on(i))
    for i in (2, 3, 4):
        started[i] = weight_out(i)
    for i in (0, 1):
        started[i][1].wait()
        started[i][2].wait()
    for copy in on:
        copy.wait()

    def project(rows):
        block = normed[rows]
        place_rows = pl.ds(pl.multiple_of(rows * own_rows, own_rows), own_rows)
        query = jnp.zeros((own_rows, width_q), jnp.float32)
        pair = jnp.zeros((own_rows, 2 * HDIM), jnp.float32)
        for f in range(KV):
            part = block[:, f * (D // KV) : (f + 1) * (D // KV)]
            query += plain_dot(part, wq[f])
            pair += plain_dot(part, wkv[f])
        cos, sin = cosine[place_rows, :], sine[place_rows, :]
        for j in range(width_q // 128):
            lanes = slice(j * 128, (j + 1) * 128)
            head = query[:, lanes].astype(jnp.bfloat16).astype(jnp.float32)
            head = (head * cos + turn(head) * sin).astype(jnp.bfloat16)
            query_rot[place_rows, lanes] = head * HDIM**-0.5
        pair = pair.astype(jnp.bfloat16).astype(jnp.float32)
        turned_key = pair * cos + turn(pair) * sin
        lower = lane_ids(pair.shape) < HDIM
        keys[place_rows, :] = jnp.where(lower, turned_key, pltpu.roll(turned_key, HDIM, 1)).astype(jnp.bfloat16)
        values[place_rows, :] = jnp.where(lower, pltpu.roll(pair, HDIM, 1), pair).astype(jnp.bfloat16)

    project(member)
    for i, copy in enumerate(gather):
        copy.wait()
        project(members[i])
    gather_g = [send(26 + i, upstream.at[member], upstream.at[member], device) for i, device in enumerate(peers)]

    bias[...] = pair_bias(window, group, tok_rows, first_len, both_len)
    key_twice = keys[...]
    value_twice = values[...]
    lower = lane_ids(value_twice.shape) < HDIM
    zero = jnp.zeros_like(key_twice)
    key_low, key_high = jnp.where(lower, key_twice, zero), jnp.where(lower, zero, key_twice)
    value_low, value_high = jnp.where(lower, value_twice, zero).T, jnp.where(lower, zero, value_twice).T

    @pl.loop(0, width_q // 128)
    def _(j):
        lanes = pl.ds(pl.multiple_of(j * 128, 128), 128)
        pair = query_rot[:, lanes]
        total = plain_dot(value_low, softmax_columns(key_low, pair, bias[...]).astype(jnp.bfloat16))
        total += plain_dot(value_high, softmax_columns(key_high, pair, bias[...]).astype(jnp.bfloat16))
        attended[:, lanes] = total.T.astype(jnp.bfloat16)

    @pl.when(same_chip & same_core)
    def _():
        wo_copy(wo_x, wo_in, chip_mate).wait_send()
        wo_copy(wo_core, wo_in, core_mate).wait_send()
        wo_here.wait()

    @pl.when(jnp.logical_not(same_chip) & same_core)
    def _():
        wo_copy(wo_x, wo_in, chip_mate).wait_recv()
        forward = wo_copy(wo_on, wo, core_mate)
        forward.start()
        forward.wait_send()

    @pl.when(same_chip & jnp.logical_not(same_core))
    def _():
        wo_copy(wo_core, wo_in, core_mate).wait_recv()

    @pl.when(jnp.logical_not(same_chip) & jnp.logical_not(same_core))
    def _():
        wo_copy(wo_on, wo, core_mate).wait_recv()

    def project_out(rows):
        place_rows = pl.ds(pl.multiple_of(rows * own_rows, own_rows), own_rows)
        return plain_dot(attended[place_rows, :], wo[...])

    sums = {}
    for i in (2, 0, 1):
        sent[i] = project_out(members[i]).astype(jnp.bfloat16)
        sums[i] = send(29 + i, sent.at[i], got.at[i], peers[i])
    total = inputs + project_out(member)
    for i in (0, 1, 2):
        sums[i].wait()
        total += got[i].astype(jnp.float32)
    middle[...] = total
    normed_two[member] = (total * rms_scale(total) * gain_two).astype(jnp.bfloat16)
    gather_two = [
        send(32 + i, normed_two.at[member], normed_two.at[member], device) for i, device in enumerate(peers)
    ]
    on = []
    for i in (2, 3, 4):
        started[i][0].wait()
        on.append(weight_on(i))
        started[i][1].wait()
        started[i][2].wait()
    for copy in (*on, *gather_g, *gather_two):
        copy.wait()


def front(n_sp, tok_rows, heads, *operands):
    group = n_sp // MB
    own_rows = MB * tok_rows
    window = group * own_rows
    width_q = heads * HDIM
    width_f = FF // group
    low = jnp.bfloat16
    vmem = pl.BlockSpec(memory_space=pltpu.VMEM)
    anywhere = pl.BlockSpec(memory_space=pl.ANY)
    smem = pl.BlockSpec(memory_space=pltpu.SMEM)
    shape = jax.ShapeDtypeStruct
    return pl.pallas_call(
        functools.partial(front_kernel, n_sp),
        out_shape=(
            shape((MB, tok_rows, D), low),
            shape((group, own_rows, D), low),
            shape((group, own_rows, D), low),
            shape((window, width_q), low),
            shape((window, 2 * HDIM), low),
            shape((window, 2 * HDIM), low),
            shape((window, width_q), low),
            shape((own_rows, D), jnp.float32),
            shape((group, own_rows, D), low),
            shape((KV, D // KV, width_q), low),
            shape((KV, D // KV, 2 * HDIM), low),
            shape((width_q, D), low),
            shape((KV, D // KV, width_f), low),
            shape((KV, D // KV, width_f), low),
            shape((KV, D // KV, width_f), low),
            shape((KV, 8, D // KV), jnp.float32),
        ),
        in_specs=[anywhere, anywhere, smem, smem, vmem, anywhere, anywhere, anywhere, anywhere, anywhere, anywhere, vmem, vmem],
        out_specs=tuple([vmem] * 12 + [anywhere] * 3 + [vmem]),
        scratch_shapes=[
            pltpu.VMEM((MB, tok_rows, D), low),
            pltpu.VMEM((group - 1, own_rows, D), low),
            pltpu.VMEM((group - 1, own_rows, D), low),
            pltpu.VMEM((window, window), jnp.float32),
            pltpu.SemaphoreType.DMA((9,)),
            pltpu.SemaphoreType.DMA((35,)),
            pltpu.SemaphoreType.DMA((35,)),
        ],
        compiler_params=pltpu.CompilerParams(
            collective_id=0, has_side_effects=True, vmem_limit_bytes=VMEM_BYTES
        ),
        cost_estimate=pl.CostEstimate(flops=8 * 10**9, bytes_accessed=40 * 10**6, transcendentals=2 * 10**6),
        name="front",
    )(*operands)


def back_kernel(
    n_sp,
    d_two_part,
    block_part,
    gate_part,
    up_part,
    down_part,
    middle_in,
    tokens_in,
    upstream_in,
    normed_in,
    query_in,
    keys_in,
    values_in,
    attended_in,
    wq_in,
    wkv_in,
    wo_in,
    seq_len,
    slot_order,
    gains,
    cosine,
    sine,
    block_out,
    input_grad,
    ffn_grad,
    qkv_grad,
    out_grad,
    gain_sum,
    own_two,
    own_block,
    own_one,
    middle,
    xs,
    upstream,
    normed,
    query_rot,
    keys,
    values,
    attended,
    wq,
    wkv,
    wo,
    d_middle,
    d_full,
    d_attended,
    d_query,
    d_pair,
    key_sum,
    value_sum,
    bias,
    sent,
    got_two,
    got_one,
    rows_out,
    rows_got,
    from_core,
    from_chip,
    from_half,
    unit_stage,
    late,
    late_core,
    late_chip,
    late_half,
    out_part,
    out_core,
    out_chip,
    out_half,
    gain_part,
    gain_got,
    local_sem,
    send_sem,
    recv_sem,
):
    place = mesh_place(n_sp)
    shard, rank, micro, member, peers, members, partner, core_mate, chip_mate, far_mate = place
    chip, core = shard // 2, shard % 2
    group = n_sp // MB
    own_rows = middle.shape[0]
    tok_rows = own_rows // MB
    window = group * own_rows
    width_q = query_rot.shape[1]
    greet((*peers, partner, core_mate, chip_mate))

    def copy_to(index, source, target, device):
        return pltpu.make_async_remote_copy(
            src_ref=source,
            dst_ref=target,
            send_sem=send_sem.at[index],
            recv_sem=recv_sem.at[index],
            device_id=device,
            device_id_type=MESH,
        )

    def send(index, source, target, device):
        copy = copy_to(index, source, target, device)
        copy.start()
        return copy

    def move(index, source, target):
        copy = pltpu.make_async_copy(source, target, local_sem.at[index])
        copy.start()
        return copy

    ffn_parts = (gate_part, up_part, down_part)
    sums_two = {i: send(6 + i, d_two_part.at[members[i]], got_two.at[i], peers[i]) for i in (2, 0, 1)}
    own_load = move(0, d_two_part.at[member], own_two)
    core_copies = {}
    for w in range(3):
        for x in range(2):
            core_copies[w, x] = send(
                2 * w + x, ffn_parts[w].at[x, 1 - core], from_core.at[w, x], core_mate
            )
    inputs_in = (
        (middle_in, middle),
        (upstream_in.at[member], upstream),
        (wo_in, wo),
        (attended_in, attended),
        (query_in, query_rot),
        (keys_in, keys),
        (values_in, values),
        (wq_in, wq),
        (wkv_in, wkv),
        (normed_in, normed),
        (tokens_in, xs),
    )
    kept = [move(4 + i, source, target) for i, (source, target) in enumerate(inputs_in)]

    units = []
    for w in range(3):
        units.append((w, 1 - chip, 1 - micro))
    for w in (0, 1):
        units.append((w, chip, 1 - micro))
        units.append((w, 1 - chip, micro))
    units.append((2, chip, 1 - micro))
    units.append((2, 1 - chip, micro))
    for w in range(3):
        units.append((w, chip, micro))
    turn_of = {"next": 0, "load": None}

    def load_unit(number):
        w, x, m = units[number]
        return move(15 + number % 2, ffn_parts[w].at[x, core, m], unit_stage.at[number % 2])

    def next_unit():
        number = turn_of["next"]
        turn_of["load"].wait()
        if number + 1 < len(units):
            turn_of["load"] = load_unit(number + 1)
        turn_of["next"] = number + 1
        return unit_stage.at[number % 2]

    turn_of["load"] = load_unit(0)
    chip_copies, half_copies, last_copies, here_copies = {}, {}, [], []

    def chip_unit(w, m, index):
        part = next_unit()
        if (w, "core") not in turn_of:
            turn_of[w, "core"] = True
            core_copies[w, 0].wait()
            core_copies[w, 1].wait()

        @pl.loop(0, group)
        def _(t):
            total = from_core[w, 1 - chip, m, t].astype(jnp.float32) + part[t].astype(jnp.float32)
            from_core[w, 1 - chip, m, t] = total.astype(jnp.bfloat16)

        chip_copies[w, index] = send(
            9 + 2 * w + index, from_core.at[w, 1 - chip, m], from_chip.at[w, m], chip_mate
        )

    def half_unit(w):
        part = next_unit()
        chip_copies[w, 0].wait()

        @pl.loop(0, group)
        def _(t):
            total = from_core[w, chip, 1 - micro, t].astype(jnp.float32) + part[t].astype(jnp.float32)
            total += from_chip[w, 1 - micro, t].astype(jnp.float32)
            from_chip[w, 1 - micro, t] = total.astype(jnp.bfloat16)

        half_copies[w] = send(15 + w, from_chip.at[w, 1 - micro], from_half.at[w], partner)

    def last_unit(w):
        part = next_unit()
        chip_copies[w, 1].wait()
        half_copies[w].wait()

        @pl.loop(0, group)
        def _(t):
            total = from_core[w, chip, micro, t].astype(jnp.float32) + part[t].astype(jnp.float32)
            total += from_chip[w, micro, t].astype(jnp.float32) + from_half[w, t].astype(jnp.float32)
            from_chip[w, micro, t] = total.astype(jnp.bfloat16)

        for i in range(group - 1):
            last_copies.append(
                send(18 + 3 * w + i, from_chip.at[w, micro, members[i]], ffn_grad.at[w, member], peers[i])
            )
        here_copies.append(move(17 + w, from_chip.at[w, micro, member], ffn_grad.at[w, member]))

    chip_unit(0, 1 - micro, 0)
    chip_unit(1, 1 - micro, 0)

    kept[0].wait()
    kept[1].wait()
    gain_one = jnp.concatenate([gains[f, 0:1, :] for f in range(KV)], axis=1)
    gain_two = jnp.concatenate([gains[f, 1:2, :] for f in range(KV)], axis=1)
    own_load.wait()
    upstream_rows = own_two[...].astype(jnp.float32)
    for i in range(group - 1):
        sums_two[i].wait()
        upstream_rows += got_two[i].astype(jnp.float32)
    middle_rows = middle[...]
    grad, two_term = norm_back(middle_rows, rms_scale(middle_rows), gain_two, upstream_rows)
    grad += upstream[...].astype(jnp.float32)
    d_middle[...] = grad
    d_full[member] = grad.astype(jnp.bfloat16)
    gather = [send(27 + i, d_full.at[member], d_full.at[member], device) for i, device in enumerate(peers)]
    block_load = move(1, block_part.at[member], own_block)

    first_len = seq_len[slot_order[2 * (shard * MB + micro)]]
    both_len = first_len + seq_len[slot_order[2 * (shard * MB + micro) + 1]]
    bias[...] = pair_bias(window, group, tok_rows, first_len, both_len)
    chip_unit(2, 1 - micro, 0)

    for i in (2, 3, 4, 5, 6):
        kept[i].wait()

    def attention_grad(rows):
        place_rows = pl.ds(pl.multiple_of(rows * own_rows, own_rows), own_rows)
        d_attended[place_rows, :] = contract_cols(d_full[rows], wo[...]).astype(jnp.bfloat16)

    attention_grad(member)
    for i, copy in enumerate(gather):
        copy.wait()
        attention_grad(members[i])

    sums_block = {i: send(30 + i, block_part.at[members[i]], got_two.at[i], peers[i]) for i in (2, 0, 1)}

    same_chip = chip == member // 2
    same_core = core == member % 2
    d_rows = d_full[...].reshape(window, D)
    for j in range(width_q // 128):
        part = contract_rows(attended[:, j * 128 : (j + 1) * 128], d_rows)
        for k in range(128 // tok_rows):
            out_part[j * (128 // tok_rows) + k] = part[k * tok_rows : (k + 1) * tok_rows].astype(jnp.bfloat16)
    out_by_core = copy_to(33, out_part, out_core, core_mate)
    out_by_chip = copy_to(34, out_part, out_chip, chip_mate)
    out_by_half = copy_to(35, out_part.at[pl.ds((1 - micro) * group, group)], out_half, partner)

    @pl.when(jnp.logical_not(same_core))
    def _():
        out_by_core.start()

    half_unit(0)
    chip_unit(0, micro, 1)
    half_unit(1)
    chip_unit(1, micro, 1)

    @pl.when(jnp.logical_not(same_core))
    def _():
        out_by_core.wait_send()

    @pl.when(same_core)
    def _():
        out_by_core.wait_recv()

        @pl.loop(0, MB * group)
        def _(t):
            total = out_part[t].astype(jnp.float32) + out_core[t].astype(jnp.float32)
            out_part[t] = total.astype(jnp.bfloat16)

    @pl.when(same_core & jnp.logical_not(same_chip))
    def _():
        out_by_chip.start()

    key_twice, value_twice = keys[...], values[...]
    lower = lane_ids(key_twice.shape) < HDIM
    zero = jnp.zeros_like(key_twice)
    key_low, key_high = jnp.where(lower, key_twice, zero), jnp.where(lower, zero, key_twice)
    value_low, value_high = jnp.where(lower, value_twice, zero), jnp.where(lower, zero, value_twice)
    key_low_turned, key_high_turned = key_low.T, key_high.T
    key_sum[...] = jnp.zeros_like(key_sum)
    value_sum[...] = jnp.zeros_like(value_sum)

    def attention_pair(j):
        lanes = pl.ds(pl.multiple_of(j * 128, 128), 128)
        query_pair, grad_pair = query_rot[:, lanes], d_attended[:, lanes]
        total = jnp.zeros((2 * HDIM, window), jnp.float32)
        for side, (key_side, value_side, key_turned) in enumerate(
            ((key_low, value_low, key_low_turned), (key_high, value_high, key_high_turned))
        ):
            probs = softmax_columns(key_side, query_pair, bias[...])
            d_probs = contract_cols(value_side, grad_pair)
            inner = jnp.sum(probs * d_probs, axis=0, keepdims=True)
            d_scores = (probs * (d_probs - inner)).astype(jnp.bfloat16)
            total += plain_dot(key_turned, d_scores)
            key_sum[side] += plain_dot(d_scores, query_pair)
            value_sum[side] += plain_dot(probs.astype(jnp.bfloat16), grad_pair)
        grad_rot = total.T * HDIM**-0.5
        d_query[:, lanes] = (grad_rot * cosine[...] + turn_back(grad_rot * sine[...])).astype(jnp.bfloat16)

    pl.loop(0, width_q // 256)(attention_pair)
    half_unit(2)
    chip_unit(2, micro, 1)
    pl.loop(width_q // 256, width_q // 128)(attention_pair)

    fold = lambda sums: jnp.where(lower, sums[0] + pltpu.roll(sums[1], HDIM, 1), 0.0)
    key_grad, value_grad = fold(key_sum), fold(value_sum)
    key_grad = key_grad * cosine[...] + turn_back(key_grad * sine[...])
    d_pair[...] = jnp.where(lower, key_grad, pltpu.roll(value_grad, HDIM, 1)).astype(jnp.bfloat16)

    block_load.wait()
    block = middle[...] + own_block[...].astype(jnp.float32)
    for i in range(group - 1):
        sums_block[i].wait()
        block += got_two[i].astype(jnp.float32)

    for i in (7, 8, 9, 10):
        kept[i].wait()

    def project_back(rows):
        place_rows = pl.ds(pl.multiple_of(rows * own_rows, own_rows), own_rows)
        grad_rows, pair_rows = d_query[place_rows, :], d_pair[place_rows, :]
        return jnp.concatenate(
            [contract_cols(grad_rows, wq[f]) + contract_cols(pair_rows, wkv[f]) for f in range(KV)], axis=1
        )

    sums_one = {}
    for i in (2, 0, 1):
        sent[i] = project_back(members[i]).astype(jnp.bfloat16)
        sums_one[i] = send(36 + i, sent.at[i], got_one.at[i], peers[i])
    own_one[...] = project_back(member)

    def give(slot, rows, target):
        rows_out[slot] = jnp.where(micro == 0, rows[tok_rows:], rows[:tok_rows]).astype(jnp.bfloat16)
        target[micro] = jnp.where(micro == 0, rows[:tok_rows], rows[tok_rows:])
        return send(39 + slot, rows_out.at[slot], rows_got.at[slot], partner)

    def take(slot, copy, target):
        copy.wait()
        target[1 - micro] = rows_got[slot].astype(jnp.float32)

    give_block = give(0, block, block_out)

    normed_rows = normed
    d_all = jnp.concatenate([d_query[...], d_pair[...]], axis=1)
    late_core_copies = []

    def late_part(x, c):
        for m in range(MB):
            first = ((x * 2 + c) * MB + m) * (group * tok_rows)
            columns = pl.ds(pl.multiple_of(first, group * tok_rows), group * tok_rows)
            rows = normed_rows[:, :, columns].reshape(window, group * tok_rows)
            part = contract_rows(rows, d_all)
            late[x, c, m] = part.astype(jnp.bfloat16).reshape(group, tok_rows, -1)

    for x in range(2):
        late_part(x, 1 - core)
        late_core_copies.append(send(41 + x, late.at[x, 1 - core], late_core.at[x], core_mate))
    for x in range(2):
        late_part(x, core)

    last_unit(0)
    for copy in late_core_copies:
        copy.wait()

    @pl.loop(0, MB * group)
    def _(k):
        m, t = k // group, k % group
        total = late[1 - chip, core, m, t].astype(jnp.float32) + late_core[1 - chip, m, t].astype(jnp.float32)
        late[1 - chip, core, m, t] = total.astype(jnp.bfloat16)

    late_to_chip = send(43, late.at[1 - chip, core], late_chip, chip_mate)

    @pl.when(same_core & jnp.logical_not(same_chip))
    def _():
        out_by_chip.wait_send()

    @pl.when(same_core & same_chip)
    def _():
        out_by_chip.wait_recv()

        @pl.loop(0, MB * group)
        def _(t):
            total = out_part[t].astype(jnp.float32) + out_chip[t].astype(jnp.float32)
            out_part[t] = total.astype(jnp.bfloat16)

        out_by_half.start()

    inputs = xs[...].reshape(own_rows, D).astype(jnp.float32)
    upstream_rows = own_one[...]
    for i in range(group - 1):
        sums_one[i].wait()
        upstream_rows += got_one[i].astype(jnp.float32)
    grad, one_term = norm_back(inputs, rms_scale(inputs), gain_one, upstream_rows)
    give_grad = give(1, grad + d_middle[...], input_grad)
    gain_part[...] = jnp.concatenate([one_term[None], two_term[None], jnp.zeros((6, D), jnp.float32)], axis=0)

    gain_core = send(44, gain_part, gain_got.at[0], core_mate)
    last_unit(1)
    gain_core.wait()
    gain_part[...] = gain_part[...] + gain_got[0]
    gain_chip = send(45, gain_part, gain_got.at[1], chip_mate)

    late_to_chip.wait()

    @pl.loop(0, group)
    def _(t):
        total = late[chip, core, 1 - micro, t].astype(jnp.float32) + late_core[chip, 1 - micro, t].astype(jnp.float32)
        total += late_chip[1 - micro, t].astype(jnp.float32)
        late_chip[1 - micro, t] = total.astype(jnp.bfloat16)

    late_to_half = send(46, late_chip.at[1 - micro], late_half, partner)
    gain_chip.wait()
    gain_part[...] = gain_part[...] + gain_got[1]
    gain_half = send(47, gain_part, gain_got.at[2], partner)

    last_unit(2)
    take(0, give_block, block_out)

    out_here = pltpu.make_async_copy(out_part.at[micro * group + member], out_grad, local_sem.at[24])

    def out_to(i):
        return pltpu.make_async_remote_copy(
            src_ref=out_part.at[micro * group + members[i]],
            dst_ref=out_grad,
            send_sem=send_sem.at[48 + i],
            recv_sem=recv_sem.at[48],
            device_id=peers[i],
            device_id_type=MESH,
        )

    @pl.when(same_core & same_chip)
    def _():
        out_by_half.wait()

        @pl.loop(0, group)
        def _(t):
            total = out_part[micro * group + t].astype(jnp.float32) + out_half[t].astype(jnp.float32)
            out_part[micro * group + t] = total.astype(jnp.bfloat16)

        for i in range(group - 1):
            out_to(i).start()
        out_here.start()

    gain_half.wait()
    gain_part[...] = gain_part[...] + gain_got[2]
    gain_all = [send(51 + i, gain_part, gain_got.at[3 + i], device) for i, device in enumerate(peers)]

    late_to_half.wait()

    @pl.loop(0, group)
    def _(t):
        total = late[chip, core, micro, t].astype(jnp.float32) + late_core[chip, micro, t].astype(jnp.float32)
        total += late_chip[micro, t].astype(jnp.float32) + late_half[t].astype(jnp.float32)
        late_chip[micro, t] = total.astype(jnp.bfloat16)

    for i in range(group - 1):
        last_copies.append(send(54 + i, late_chip.at[micro, members[i]], qkv_grad.at[member], peers[i]))
    here_copies.append(move(25, late_chip.at[micro, member], qkv_grad.at[member]))
    take(1, give_grad, input_grad)
    for copy in gain_all:
        copy.wait()
    gain_sum[...] = gain_part[...] + gain_got[3] + gain_got[4] + gain_got[5]

    @pl.when(same_core & same_chip)
    def _():
        for i in range(group - 1):
            out_to(i).wait_send()
        out_here.wait()

    @pl.when(jnp.logical_not(same_core & same_chip))
    def _():
        out_to(0).wait_recv()

    for copy in (*last_copies, *here_copies):
        copy.wait()


def back(n_sp, tok_rows, heads, *operands):
    group = n_sp // MB
    own_rows = MB * tok_rows
    window = group * own_rows
    width_q = heads * HDIM
    width_f = FF // group
    width_l = width_q + 2 * HDIM
    low, full = jnp.bfloat16, jnp.float32
    vmem = pl.BlockSpec(memory_space=pltpu.VMEM)
    anywhere = pl.BlockSpec(memory_space=pl.ANY)
    smem = pl.BlockSpec(memory_space=pltpu.SMEM)
    shape = jax.ShapeDtypeStruct
    return pl.pallas_call(
        functools.partial(back_kernel, n_sp),
        out_shape=(
            shape((MB, tok_rows, D), full),
            shape((MB, tok_rows, D), full),
            shape((3, group, tok_rows, width_f), low),
            shape((group, tok_rows, width_l), low),
            shape((tok_rows, D), low),
            shape((8, D), full),
        ),
        in_specs=[anywhere] * 16 + [smem] * 2 + [vmem] * 3,
        out_specs=(vmem, vmem, anywhere, anywhere, anywhere, vmem),
        scratch_shapes=[
            pltpu.VMEM((own_rows, D), low),
            pltpu.VMEM((own_rows, D), low),
            pltpu.VMEM((own_rows, D), full),
            pltpu.VMEM((own_rows, D), full),
            pltpu.VMEM((MB, tok_rows, D), low),
            pltpu.VMEM((own_rows, D), low),
            pltpu.VMEM((group, own_rows, D), low),
            pltpu.VMEM((window, width_q), low),
            pltpu.VMEM((window, 2 * HDIM), low),
            pltpu.VMEM((window, 2 * HDIM), low),
            pltpu.VMEM((window, width_q), low),
            pltpu.VMEM((KV, D // KV, width_q), low),
            pltpu.VMEM((KV, D // KV, 2 * HDIM), low),
            pltpu.VMEM((width_q, D), low),
            pltpu.VMEM((own_rows, D), full),
            pltpu.VMEM((group, own_rows, D), low),
            pltpu.VMEM((window, width_q), low),
            pltpu.VMEM((window, width_q), low),
            pltpu.VMEM((window, 2 * HDIM), low),
            pltpu.VMEM((2, window, 2 * HDIM), full),
            pltpu.VMEM((2, window, 2 * HDIM), full),
            pltpu.VMEM((window, window), full),
            pltpu.VMEM((group - 1, own_rows, D), low),
            pltpu.VMEM((group - 1, own_rows, D), low),
            pltpu.VMEM((group - 1, own_rows, D), low),
            pltpu.VMEM((2, tok_rows, D), low),
            pltpu.VMEM((2, tok_rows, D), low),
            pltpu.VMEM((3, 2, MB, group, tok_rows, width_f), low),
            pltpu.VMEM((3, MB, group, tok_rows, width_f), low),
            pltpu.VMEM((3, group, tok_rows, width_f), low),
            pltpu.VMEM((2, group, tok_rows, width_f), low),
            pltpu.VMEM((2, 2, MB, group, tok_rows, width_l), low),
            pltpu.VMEM((2, MB, group, tok_rows, width_l), low),
            pltpu.VMEM((MB, group, tok_rows, width_l), low),
            pltpu.VMEM((group, tok_rows, width_l), low),
            pltpu.VMEM((MB * group, tok_rows, D), low),
            pltpu.VMEM((MB * group, tok_rows, D), low),
            pltpu.VMEM((MB * group, tok_rows, D), low),
            pltpu.VMEM((group, tok_rows, D), low),
            pltpu.VMEM((8, D), full),
            pltpu.VMEM((6, 8, D), full),
            pltpu.SemaphoreType.DMA((26,)),
            pltpu.SemaphoreType.DMA((57,)),
            pltpu.SemaphoreType.DMA((57,)),
        ],
        compiler_params=pltpu.CompilerParams(
            collective_id=1, has_side_effects=True, vmem_limit_bytes=VMEM_BYTES
        ),
        cost_estimate=pl.CostEstimate(flops=14 * 10**9, bytes_accessed=60 * 10**6, transcendentals=2 * 10**6),
        name="back",
    )(*operands)


def group_body(
    tokens,
    cotangent,
    seq_len,
    slot_order,
    norm1_gain,
    query_weight,
    key_weight,
    value_weight,
    output_weight,
    norm2_gain,
    gate_weight,
    up_weight,
    down_weight,
):
    n_sp = lax.axis_size("sp")
    n_fsdp = lax.axis_size("fsdp")
    group = n_sp // MB
    rank = lax.axis_index("sp")
    shard = lax.axis_index("fsdp")
    micro = rank // group
    member = rank % group
    tok_rows = tokens.shape[1]
    window = n_sp * tok_rows
    own_rows = MB * tok_rows
    first_len = seq_len[slot_order[2 * (shard * MB + micro)]]
    second_len = seq_len[slot_order[2 * (shard * MB + micro) + 1]]
    place = row_places((window,), 0, group, tok_rows)
    anchor = jnp.where(place < first_len, 0, jnp.where(place < first_len + second_len, first_len, first_len + second_len))
    inverse = ROPE_BASE ** (-2.0 * jnp.arange(HDIM // 2, dtype=jnp.float32) / HDIM)
    angles = (place - anchor).astype(jnp.float32)[:, None] * jnp.tile(inverse, 4)[None, :]
    cosine, sine = jnp.cos(angles), jnp.sin(angles)

    def columns(weight):
        width = weight.shape[1] // group
        return lax.dynamic_slice_in_dim(weight, member * width, width, 1)

    gains = jnp.concatenate(
        [norm1_gain[None], norm2_gain[None], jnp.zeros((6, norm1_gain.shape[0]), jnp.bfloat16)]
    ).astype(jnp.float32)
    kv_weight = jnp.concatenate([columns(key_weight), columns(value_weight)], axis=1)
    heads = HEADS // group
    (
        own_tokens,
        upstream_low,
        normed,
        query_rot,
        keys,
        values,
        attended,
        middle,
        normed_two,
        w_query,
        w_kv,
        w_output,
        w_gate,
        w_up,
        w_down,
        gains,
    ) = front(
        n_sp, tok_rows, heads,
        tokens, cotangent, seq_len, slot_order, gains,
        query_weight, kv_weight, output_weight, gate_weight, up_weight, down_weight, cosine, sine,
    )
    upstream_rows, normed_rows = upstream_low.reshape(window, D), normed_two.reshape(window, D)
    gate_full, up_full, down_full = (w.reshape(D, -1) for w in (w_gate, w_up, w_down))
    gate = plain_dot(normed_rows, gate_full)
    up = plain_dot(normed_rows, up_full)
    d_hidden = plain_dot(upstream_rows, down_full)
    sig = jax.nn.sigmoid(gate)
    silu = gate * sig
    hidden = (silu * up).astype(jnp.bfloat16)
    d_up = (d_hidden * silu).astype(jnp.bfloat16)
    d_gate = (d_hidden * up * sig * (1.0 + gate * (1.0 - sig))).astype(jnp.bfloat16)
    d_two_part = contract_cols(d_gate, gate_full) + contract_cols(d_up, up_full)
    block_part = contract_cols(hidden, down_full)
    gate_part = contract_rows(normed_rows, d_gate).astype(jnp.bfloat16)
    up_part = contract_rows(normed_rows, d_up).astype(jnp.bfloat16)
    down_part = contract_rows(upstream_rows, hidden).astype(jnp.bfloat16)
    by_owner = lambda part: part.reshape(2, 2, MB, group, tok_rows, -1)
    by_member = lambda part: part.reshape(group, own_rows, D).astype(jnp.bfloat16)
    block, d_inputs, ffn_grad, qkv_grad, output_grad, gain_sum = back(
        n_sp, tok_rows, heads,
        by_member(d_two_part), by_member(block_part), by_owner(gate_part), by_owner(up_part), by_owner(down_part),
        middle, own_tokens, upstream_low, normed, query_rot, keys, values, attended,
        w_query, w_kv, w_output, seq_len, slot_order, gains, cosine, sine,
    )
    gain_own = lax.dynamic_slice_in_dim(gain_sum, (shard * n_sp + rank) * tok_rows, tok_rows, 1)

    def side_by_side(pieces):
        return jnp.swapaxes(pieces, 0, 1).reshape(tok_rows, -1).astype(jnp.float32)

    width_q = heads * HDIM
    return (
        block,
        d_inputs,
        gain_own[0],
        side_by_side(qkv_grad[:, :, :width_q]),
        side_by_side(qkv_grad[:, :, width_q : width_q + HDIM]),
        side_by_side(qkv_grad[:, :, width_q + HDIM :]),
        output_grad.astype(jnp.float32),
        gain_own[1],
        side_by_side(ffn_grad[0]),
        side_by_side(ffn_grad[1]),
        side_by_side(ffn_grad[2]),
    )


def solution(mesh):
    fits = mesh.shape["fsdp"] == KV and mesh.shape["sp"] == MB * KV
    placed = (
        P(None, ("fsdp", "sp"), None),
        P(None, ("fsdp", "sp"), None),
        P(),
        P(),
        P("fsdp"),
        P("fsdp", None),
        P("fsdp", None),
        P("fsdp", None),
        P("fsdp", None),
        P("fsdp"),
        P("fsdp", None),
        P("fsdp", None),
        P("fsdp", None),
    )
    return jax.shard_map(
        group_body if fits else body,
        mesh=mesh,
        in_specs=placed,
        out_specs=(
            P(None, ("fsdp", "sp"), None),
            P(None, ("fsdp", "sp"), None),
            P(("fsdp", "sp")),
            P(("fsdp", "sp"), None),
            P(("fsdp", "sp"), None),
            P(("fsdp", "sp"), None),
            P(("fsdp", "sp"), None),
            P(("fsdp", "sp")),
            P(("fsdp", "sp"), None),
            P(("fsdp", "sp"), None),
            P(("fsdp", "sp"), None),
        ),
        check_vma=False,
    )
```

```python
import functools

import jax
import jax.numpy as jnp
import numpy as np
from jax import lax
from jax.experimental import pallas as pl
from jax.experimental.pallas import tpu as pltpu
from jax.sharding import PartitionSpec as P

D = 2048
HEADS = 32
KV = 4
HDIM = 64
FF = 5632
MB = 2
MESH = pl.DeviceIdType.MESH
VMEM_BYTES = 60 * 2**20


EPSILON = 1e-05
ROPE_BASE = 10000.0


def plain_dot(left_side, right_side):
    return jnp.dot(left_side, right_side, preferred_element_type=jnp.float32)


def contract_rows(left_side, right_side):
    return lax.dot_general(
        left_side, right_side, (((0,), (0,)), ((), ())), preferred_element_type=jnp.float32
    )


def contract_cols(left_side, right_side):
    return lax.dot_general(
        left_side, right_side, (((1,), (1,)), ((), ())), preferred_element_type=jnp.float32
    )


def window_layout(seq_len, slot_order, window_index, window):
    first_len = seq_len[slot_order[2 * window_index]]
    second_len = seq_len[slot_order[2 * window_index + 1]]
    places = jnp.arange(window, dtype=jnp.int32)
    segment = jnp.where(
        places < first_len, 0, jnp.where(places < first_len + second_len, 1, 2)
    ).astype(jnp.int32)
    anchor = jnp.where(segment == 0, 0, jnp.where(segment == 1, first_len, first_len + second_len))
    return (segment, places - anchor)


def rope_tables(position, head_size):
    half_size = head_size // 2
    inverse = ROPE_BASE ** (-2.0 * jnp.arange(half_size, dtype=jnp.float32) / head_size)
    angles = position.astype(jnp.float32)[:, None] * inverse[None, :]
    angles = jnp.concatenate([angles, angles], axis=1)
    return (jnp.cos(angles)[:, None, :], jnp.sin(angles)[:, None, :])


def apply_rope(vectors, cosine, sine):
    half_size = vectors.shape[-1] // 2
    turned = jnp.concatenate([-vectors[..., half_size:], vectors[..., :half_size]], axis=-1)
    return vectors * cosine + turned * sine


def rope_back(grad_in, cosine, sine):
    half_size = grad_in.shape[-1] // 2
    rotated = grad_in * sine
    return grad_in * cosine + jnp.concatenate(
        [rotated[..., half_size:], -rotated[..., :half_size]], axis=-1
    )


def rms_scale(inputs):
    return lax.rsqrt(jnp.mean(inputs * inputs, axis=-1, keepdims=True) + EPSILON)


def norm_back(inputs, scale_rows, gain_full, upstream):
    through = upstream * gain_full
    gain_term = jnp.sum(upstream * inputs * scale_rows, axis=0)
    grad_in = scale_rows * through - inputs * scale_rows**3 * jnp.mean(
        through * inputs, axis=-1, keepdims=True
    )
    return (grad_in, gain_term)


def score_block(query_block, key_rot, segment, row_start):
    block_rows = query_block.shape[0]
    places = jnp.arange(key_rot.shape[0], dtype=jnp.int32)
    row_place = row_start + jnp.arange(block_rows, dtype=jnp.int32)
    block_segment = lax.dynamic_slice_in_dim(segment, row_start, block_rows, 0)
    allowed = (block_segment[:, None] == segment[None, :]) & (places[None, :] <= row_place[:, None])
    raw_scores = jnp.einsum(
        "qhd,khd->hqk", query_block, key_rot, preferred_element_type=jnp.float32
    ) * query_block.shape[2] ** (-0.5)
    return jnp.where(allowed[None], raw_scores, -1e30)


def attend_forward(query_rot, key_rot, value_heads, segment):
    window = query_rot.shape[0]
    block_rows = min(512, window)

    def step(carry, block_index):
        row_start = block_index * block_rows
        query_block = lax.dynamic_slice_in_dim(query_rot, row_start, block_rows, 0)
        scores = score_block(query_block, key_rot, segment, row_start)
        row_top = jnp.max(scores, axis=-1, keepdims=True)
        weights_exp = jnp.exp(scores - row_top)
        row_total = jnp.sum(weights_exp, axis=-1, keepdims=True)
        probs = (weights_exp / row_total).astype(jnp.bfloat16)
        block_out = jnp.einsum(
            "hqk,khd->qhd", probs, value_heads, preferred_element_type=jnp.float32
        )
        log_total = (row_top + jnp.log(row_total))[:, :, 0].T
        return (carry, (block_out, log_total))

    block_ids = jnp.arange(window // block_rows, dtype=jnp.int32)
    _, (outputs, log_totals) = lax.scan(step, jnp.zeros((), jnp.int32), block_ids)
    return (outputs.reshape(query_rot.shape), log_totals.reshape(window, query_rot.shape[1]))


def attend_backward(query_rot, key_rot, value_heads, grad_heads, log_totals, segment):
    window = query_rot.shape[0]
    block_rows = min(512, window)
    scale_factor = query_rot.shape[2] ** (-0.5)

    def step(carry, block_index):
        key_acc, value_acc = carry
        row_start = block_index * block_rows
        query_block = lax.dynamic_slice_in_dim(query_rot, row_start, block_rows, 0)
        grad_block = lax.dynamic_slice_in_dim(grad_heads, row_start, block_rows, 0)
        total_block = lax.dynamic_slice_in_dim(log_totals, row_start, block_rows, 0)
        scores = score_block(query_block, key_rot, segment, row_start)
        probs = jnp.exp(scores - total_block.T[:, :, None])
        grad_probs = jnp.einsum(
            "qhd,khd->hqk", grad_block, value_heads, preferred_element_type=jnp.float32
        )
        inner_sum = jnp.sum(probs * grad_probs, axis=-1, keepdims=True)
        grad_scores = (probs * (grad_probs - inner_sum)).astype(jnp.bfloat16)
        query_part = (
            jnp.einsum("hqk,khd->qhd", grad_scores, key_rot, preferred_element_type=jnp.float32)
            * scale_factor
        )
        key_acc = (
            key_acc
            + jnp.einsum(
                "hqk,qhd->khd", grad_scores, query_block, preferred_element_type=jnp.float32
            )
            * scale_factor
        )
        value_acc = value_acc + jnp.einsum(
            "hqk,qhd->khd",
            probs.astype(jnp.bfloat16),
            grad_block,
            preferred_element_type=jnp.float32,
        )
        return ((key_acc, value_acc), query_part)

    start_acc = (jnp.zeros(key_rot.shape, jnp.float32), jnp.zeros(value_heads.shape, jnp.float32))
    block_ids = jnp.arange(window // block_rows, dtype=jnp.int32)
    (key_acc, value_acc), query_parts = lax.scan(step, start_acc, block_ids)
    return (query_parts.reshape(query_rot.shape), key_acc, value_acc)


def weight_terms(stored):
    joined = [jnp.concatenate(pieces, axis=0) for pieces in zip(*stored)]
    (
        normed,
        query_low,
        key_low,
        value_low,
        attn_rows,
        middle_low,
        normed_two,
        gate_low,
        up_low,
        upstream_low,
        hidden,
    ) = joined
    return jnp.concatenate(
        [
            contract_rows(normed, query_low),
            contract_rows(normed, key_low),
            contract_rows(normed, value_low),
            contract_rows(attn_rows, middle_low),
            contract_rows(normed_two, gate_low),
            contract_rows(normed_two, up_low),
            contract_rows(upstream_low, hidden),
        ],
        axis=1,
    )


def body(
    tokens,
    cotangent,
    seq_len,
    slot_order,
    norm1_gain,
    query_weight,
    key_weight,
    value_weight,
    output_weight,
    norm2_gain,
    gate_weight,
    up_weight,
    down_weight,
):
    seq_devices = lax.axis_size("sp")
    seq_rank = lax.axis_index("sp")
    shard_rank = lax.axis_index("fsdp")
    tok_rows = tokens.shape[1]
    window = seq_devices * tok_rows
    group_size = HEADS // KV
    kept = []
    outputs = []
    input_grads = []
    gain_sum = jnp.zeros((2, D), jnp.float32)
    grad_shards = None
    for micro_step in range(MB):
        gathered = (
            lax.all_gather(norm1_gain, "fsdp", axis=0, tiled=True),
            lax.all_gather(query_weight, "fsdp", axis=0, tiled=True),
            lax.all_gather(key_weight, "fsdp", axis=0, tiled=True),
            lax.all_gather(value_weight, "fsdp", axis=0, tiled=True),
            lax.all_gather(output_weight, "fsdp", axis=0, tiled=True),
            lax.all_gather(norm2_gain, "fsdp", axis=0, tiled=True),
            lax.all_gather(gate_weight, "fsdp", axis=0, tiled=True),
            lax.all_gather(up_weight, "fsdp", axis=0, tiled=True),
            lax.all_gather(down_weight, "fsdp", axis=0, tiled=True),
        )
        gain_one, w_query, w_key, w_value, w_output, gain_two, w_gate, w_up, w_down = gathered
        gain_one = gain_one.astype(jnp.float32)
        gain_two = gain_two.astype(jnp.float32)
        inputs = tokens[micro_step].astype(jnp.float32)
        window_index = shard_rank * MB + micro_step
        segment, position = window_layout(seq_len, slot_order, window_index, window)
        own_segment = lax.dynamic_slice_in_dim(segment, seq_rank * tok_rows, tok_rows, 0)
        valid_rows = (own_segment < 2).astype(jnp.float32)
        scale_one = rms_scale(inputs)
        normed = (inputs * scale_one * gain_one).astype(jnp.bfloat16)
        query_proj = plain_dot(normed, w_query).astype(jnp.bfloat16).reshape(tok_rows, HEADS, HDIM)
        key_proj = plain_dot(normed, w_key).astype(jnp.bfloat16).reshape(tok_rows, KV, HDIM)
        value_proj = plain_dot(normed, w_value).astype(jnp.bfloat16).reshape(tok_rows, KV, HDIM)
        packed = jnp.concatenate(
            [
                query_proj,
                jnp.repeat(key_proj, group_size, axis=1),
                jnp.repeat(value_proj, group_size, axis=1),
            ],
            axis=2,
        )
        head_side = lax.all_to_all(packed, "sp", split_axis=1, concat_axis=0, tiled=True)
        cosine, sine = rope_tables(position, HDIM)
        query_rot = apply_rope(head_side[:, :, :HDIM].astype(jnp.float32), cosine, sine).astype(
            jnp.bfloat16
        )
        key_rot = apply_rope(
            head_side[:, :, HDIM : 2 * HDIM].astype(jnp.float32), cosine, sine
        ).astype(jnp.bfloat16)
        value_heads = head_side[:, :, 2 * HDIM :]
        attended, log_totals = attend_forward(query_rot, key_rot, value_heads, segment)
        token_side = lax.all_to_all(
            attended.astype(jnp.bfloat16), "sp", split_axis=0, concat_axis=1, tiled=True
        )
        attn_rows = token_side.reshape(tok_rows, D)
        middle = inputs + plain_dot(attn_rows, w_output)
        scale_two = rms_scale(middle)
        normed_two = (middle * scale_two * gain_two).astype(jnp.bfloat16)
        gate_proj = plain_dot(normed_two, w_gate)
        up_proj = plain_dot(normed_two, w_up)
        gate_sig = jax.nn.sigmoid(gate_proj)
        hidden = (gate_proj * gate_sig * up_proj).astype(jnp.bfloat16)
        outputs.append(middle + contract_cols(hidden, w_down))
        upstream = cotangent[micro_step].astype(jnp.float32) * valid_rows[:, None]
        upstream_low = upstream.astype(jnp.bfloat16)
        hidden_grad = plain_dot(upstream_low, w_down)
        up_low = (hidden_grad * gate_proj * gate_sig).astype(jnp.bfloat16)
        gate_low = (hidden_grad * up_proj * gate_sig * (1.0 + gate_proj * (1.0 - gate_sig))).astype(
            jnp.bfloat16
        )
        normed_two_grad = contract_cols(gate_low, w_gate) + contract_cols(up_low, w_up)
        middle_grad, gain_two_term = norm_back(middle, scale_two, gain_two, normed_two_grad)
        middle_grad = middle_grad + upstream
        middle_low = middle_grad.astype(jnp.bfloat16)
        attn_grad = (
            contract_cols(middle_low, w_output).astype(jnp.bfloat16).reshape(tok_rows, HEADS, HDIM)
        )
        grad_heads = lax.all_to_all(attn_grad, "sp", split_axis=1, concat_axis=0, tiled=True)
        query_part, key_acc, value_acc = attend_backward(
            query_rot, key_rot, value_heads, grad_heads, log_totals, segment
        )
        packed_grad = jnp.concatenate(
            [rope_back(query_part, cosine, sine), rope_back(key_acc, cosine, sine), value_acc],
            axis=2,
        )
        grad_tokens = lax.all_to_all(packed_grad, "sp", split_axis=0, concat_axis=1, tiled=True)
        query_low = grad_tokens[:, :, :HDIM].reshape(tok_rows, D).astype(jnp.bfloat16)
        key_low = (
            grad_tokens[:, :, HDIM : 2 * HDIM]
            .reshape(tok_rows, KV, group_size, HDIM)
            .sum(axis=2)
            .reshape(tok_rows, KV * HDIM)
            .astype(jnp.bfloat16)
        )
        value_low = (
            grad_tokens[:, :, 2 * HDIM :]
            .reshape(tok_rows, KV, group_size, HDIM)
            .sum(axis=2)
            .reshape(tok_rows, KV * HDIM)
            .astype(jnp.bfloat16)
        )
        normed_grad = (
            contract_cols(query_low, w_query)
            + contract_cols(key_low, w_key)
            + contract_cols(value_low, w_value)
        )
        inputs_grad, gain_one_term = norm_back(inputs, scale_one, gain_one, normed_grad)
        input_grads.append(inputs_grad + middle_grad)
        gain_sum = gain_sum + jnp.stack([gain_one_term, gain_two_term])
        kept.append(
            (
                normed,
                query_low,
                key_low,
                value_low,
                attn_rows,
                middle_low,
                normed_two,
                gate_low,
                up_low,
                upstream_low,
                hidden,
            )
        )
        grad_shards = None
    grad_shards = lax.psum_scatter(
        weight_terms(kept), ("fsdp", "sp"), scatter_dimension=0, tiled=True
    )
    gain_shards = lax.psum_scatter(gain_sum, ("fsdp", "sp"), scatter_dimension=1, tiled=True)
    kv_width = KV * HDIM
    edges = [
        0,
        D,
        D + kv_width,
        D + 2 * kv_width,
        2 * D + 2 * kv_width,
        2 * D + 2 * kv_width + FF,
        2 * D + 2 * kv_width + 2 * FF,
        2 * D + 2 * kv_width + 3 * FF,
    ]
    pieces = [grad_shards[:, edges[slot] : edges[slot + 1]] for slot in range(7)]
    return (
        jnp.stack(outputs),
        jnp.stack(input_grads),
        gain_shards[0],
        pieces[0],
        pieces[1],
        pieces[2],
        pieces[3],
        gain_shards[1],
        pieces[4],
        pieces[5],
        pieces[6],
    )


def mesh_place(n_sp):
    shard = lax.axis_index("fsdp")
    rank = lax.axis_index("sp")
    group = n_sp // MB
    chip, core = shard // 2, shard % 2
    micro, member = rank // group, rank % group
    high, low = member // 2, member % 2
    base = micro * group
    peers = (
        (shard, base + high * 2 + (1 - low)),
        (shard, base + (1 - high) * 2 + low),
        (shard, base + (1 - high) * 2 + (1 - low)),
    )
    members = (high * 2 + (1 - low), (1 - high) * 2 + low, (1 - high) * 2 + (1 - low))
    partner = (shard, (1 - micro) * group + member)
    core_mate = (chip * 2 + (1 - core), rank)
    chip_mate = ((1 - chip) * 2 + core, rank)
    far_mate = ((1 - chip) * 2 + (1 - core), rank)
    return shard, rank, micro, member, peers, members, partner, core_mate, chip_mate, far_mate


def greet(devices):
    barrier = pltpu.get_barrier_semaphore()
    for device in devices:
        pl.semaphore_signal(barrier, inc=1, device_id=device, device_id_type=MESH)
    pl.semaphore_wait(barrier, len(devices))


def lane_ids(shape):
    return lax.broadcasted_iota(jnp.int32, shape, len(shape) - 1)


def turn(vectors):
    width = vectors.shape[-1]
    ahead = pltpu.roll(vectors, width - HDIM // 2, 1)
    behind = pltpu.roll(vectors, HDIM // 2, 1)
    first = lane_ids(vectors.shape) % HDIM < HDIM // 2
    return jnp.where(first, -ahead, behind)


def turn_back(vectors):
    return -turn(vectors)


def softmax_columns(key_side, query_pair, bias):
    scores = contract_cols(key_side, query_pair) + bias
    weights_exp = jnp.exp(scores - jnp.max(scores, axis=0, keepdims=True))
    return weights_exp * (1.0 / jnp.sum(weights_exp, axis=0, keepdims=True))


def row_places(shape, dim, group, tok_rows):
    ids = lax.broadcasted_iota(jnp.int32, shape, dim)
    own_rows = MB * tok_rows
    return ((ids % own_rows) // tok_rows) * (group * tok_rows) + (ids // own_rows) * tok_rows + ids % tok_rows


def row_positions(window, dim, group, tok_rows, first_len, both_len):
    shape = (window, 1) if dim == 0 else (1, window)
    place = row_places(shape, dim, group, tok_rows)
    anchor = jnp.where(place < first_len, 0, jnp.where(place < both_len, first_len, both_len))
    return place, place - anchor


def pair_bias(window, group, tok_rows, first_len, both_len):
    place, position = row_positions(window, 1, group, tok_rows, first_len, both_len)
    key_place = row_places((window, 1), 0, group, tok_rows)
    return jnp.where((key_place <= place) & (key_place >= place - position), 0.0, -1e30)


def front_kernel(
    n_sp,
    tokens,
    cotangent,
    seq_len,
    slot_order,
    norm1_gain,
    norm2_gain,
    inverse,
    key_in,
    value_in,
    wq_in,
    wo_in,
    wg_in,
    wu_in,
    wd_in,
    xs,
    upstream,
    normed,
    query_rot,
    keys,
    values,
    attended,
    middle,
    normed_two,
    wq,
    wkv,
    wo,
    wg,
    wu,
    wd,
    gains_all,
    cosine,
    sine,
    gains,
    wkv_in,
    gs,
    sent,
    got,
    bias,
    local_sem,
    send_sem,
    recv_sem,
):
    place = mesh_place(n_sp)
    shard, rank, micro, member, peers, members, partner, core_mate, chip_mate, far_mate = place
    group = n_sp // MB
    tok_rows = tokens.shape[1]
    own_rows = MB * tok_rows
    window = group * own_rows
    greet((*peers, partner, core_mate, chip_mate, far_mate))

    def send(index, source, target, device):
        copy = pltpu.make_async_remote_copy(
            src_ref=source,
            dst_ref=target,
            send_sem=send_sem.at[index],
            recv_sem=recv_sem.at[index],
            device_id=device,
            device_id_type=MESH,
        )
        copy.start()
        return copy

    def move(index, source, target):
        copy = pltpu.make_async_copy(source, target, local_sem.at[index])
        copy.start()
        return copy

    swap_x = send(0, tokens.at[1 - micro], xs.at[micro], partner)
    swap_g = send(1, cotangent.at[1 - micro], gs.at[micro], partner)
    own_x = move(0, tokens.at[micro], xs.at[micro])
    own_g = move(1, cotangent.at[micro], gs.at[micro])
    gains[0:1, :] = norm1_gain[...].astype(jnp.float32)
    gains[1:2, :] = norm2_gain[...].astype(jnp.float32)
    gain_sends = [
        send(2 + i, gains, gains_all.at[shard], device) for i, device in enumerate((core_mate, chip_mate, far_mate))
    ]
    own_gain = move(2, gains, gains_all.at[shard])

    def columns(ref, width):
        return ref.at[:, pl.ds(pl.multiple_of(member * width, 128), width)]

    own_pair = pl.ds(pl.multiple_of(member // 2 * 128, 128), 128)
    key_pair = key_in[:, own_pair].astype(jnp.float32)
    value_pair = value_in[:, own_pair].astype(jnp.float32)
    key_pair = jnp.where(member % 2 == 0, key_pair, pltpu.roll(key_pair, HDIM, 1))
    value_pair = jnp.where(member % 2 == 0, pltpu.roll(value_pair, HDIM, 1), value_pair)
    wkv_in[...] = jnp.where(lane_ids(key_pair.shape) < HDIM, key_pair, value_pair).astype(jnp.bfloat16)

    chip_shard = (1 - shard // 2) * 2 + shard % 2
    width_q, width_f = wq.shape[2], wg.shape[2]
    parts = (
        (columns(wq_in, width_q), wq),
        (wkv_in, wkv),
        (columns(wd_in, width_f), wd),
        (columns(wg_in, width_f), wg),
        (columns(wu_in, width_f), wu),
    )

    def weight_out(i):
        source, target = parts[i]
        over_chip = send(5 + 3 * i, source, target.at[shard], chip_mate)
        over_core = send(6 + 3 * i, source, target.at[shard], core_mate)
        here = move(3 + i, source, target.at[shard])
        return over_chip, over_core, here

    def weight_on(i):
        target = parts[i][1]
        return send(7 + 3 * i, target.at[chip_shard], target.at[chip_shard], core_mate)

    started = {i: weight_out(i) for i in (0, 1)}
    wo_x, wo_core, wo_on = 20, 21, 22

    def wo_copy(index, source, device):
        return pltpu.make_async_remote_copy(
            src_ref=source,
            dst_ref=wo,
            send_sem=send_sem.at[index],
            recv_sem=recv_sem.at[index],
            device_id=device,
            device_id_type=MESH,
        )

    same_chip = shard // 2 == member // 2
    same_core = shard % 2 == member % 2
    wo_here = pltpu.make_async_copy(wo_in, wo, local_sem.at[8])

    @pl.when(same_chip & same_core)
    def _():
        wo_copy(wo_x, wo_in, chip_mate).start()
        wo_copy(wo_core, wo_in, core_mate).start()
        wo_here.start()

    for i in (2, 3, 4):
        started[i] = weight_out(i)

    first_len = seq_len[slot_order[2 * (shard * MB + micro)]]
    both_len = first_len + seq_len[slot_order[2 * (shard * MB + micro) + 1]]
    angles = row_positions(window, 0, group, tok_rows, first_len, both_len)[1].astype(jnp.float32) * inverse[...]
    cosine[...] = jnp.cos(angles)
    sine[...] = jnp.sin(angles)
    bias[...] = pair_bias(window, group, tok_rows, first_len, both_len)

    own_gain.wait()
    for copy in gain_sends:
        copy.wait()
    gain_one = jnp.concatenate([gains_all[f, 0:1, :] for f in range(KV)], axis=1)
    gain_two = jnp.concatenate([gains_all[f, 1:2, :] for f in range(KV)], axis=1)
    own_x.wait()
    swap_x.wait()
    inputs = xs[...].reshape(own_rows, D).astype(jnp.float32)
    normed[member] = (inputs * rms_scale(inputs) * gain_one).astype(jnp.bfloat16)
    gather = [send(23 + i, normed.at[member], normed.at[member], device) for i, device in enumerate(peers)]

    own_g.wait()
    swap_g.wait()
    ids = lax.broadcasted_iota(jnp.int32, (own_rows, 1), 0)
    own_place = (ids // tok_rows) * (group * tok_rows) + member * tok_rows + ids % tok_rows
    valid = jnp.where(own_place < both_len, 1.0, 0.0)
    upstream[member] = (gs[...].reshape(own_rows, D).astype(jnp.float32) * valid).astype(jnp.bfloat16)

    on = []
    for i in (0, 1):
        started[i][0].wait()
        on.append(weight_on(i))
    for i in (0, 1):
        started[i][1].wait()
        started[i][2].wait()
    for copy in on:
        copy.wait()

    def project(rows):
        block = normed[rows]
        place_rows = pl.ds(pl.multiple_of(rows * own_rows, own_rows), own_rows)
        query = jnp.zeros((own_rows, width_q), jnp.float32)
        pair = jnp.zeros((own_rows, 2 * HDIM), jnp.float32)
        for f in range(KV):
            part = block[:, f * (D // KV) : (f + 1) * (D // KV)]
            query += plain_dot(part, wq[f])
            pair += plain_dot(part, wkv[f])
        cos, sin = cosine[place_rows, :], sine[place_rows, :]
        for j in range(width_q // 128):
            lanes = slice(j * 128, (j + 1) * 128)
            head = query[:, lanes].astype(jnp.bfloat16).astype(jnp.float32)
            head = (head * cos + turn(head) * sin).astype(jnp.bfloat16)
            query_rot[place_rows, lanes] = head * HDIM**-0.5
        pair = pair.astype(jnp.bfloat16).astype(jnp.float32)
        turned_key = pair * cos + turn(pair) * sin
        lower = lane_ids(pair.shape) < HDIM
        keys[place_rows, :] = jnp.where(lower, turned_key, pltpu.roll(turned_key, HDIM, 1)).astype(jnp.bfloat16)
        values[place_rows, :] = jnp.where(lower, pltpu.roll(pair, HDIM, 1), pair).astype(jnp.bfloat16)

    project(member)
    for i, copy in enumerate(gather):
        copy.wait()
        project(members[i])
    gather_g = [send(26 + i, upstream.at[member], upstream.at[member], device) for i, device in enumerate(peers)]

    key_twice = keys[...]
    value_twice = values[...]
    lower = lane_ids(value_twice.shape) < HDIM
    zero = jnp.zeros_like(key_twice)
    key_low, key_high = jnp.where(lower, key_twice, zero), jnp.where(lower, zero, key_twice)
    value_low, value_high = jnp.where(lower, value_twice, zero).T, jnp.where(lower, zero, value_twice).T

    @pl.loop(0, width_q // 128)
    def _(j):
        lanes = pl.ds(pl.multiple_of(j * 128, 128), 128)
        pair = query_rot[:, lanes]
        total = plain_dot(value_low, softmax_columns(key_low, pair, bias[...]).astype(jnp.bfloat16))
        total += plain_dot(value_high, softmax_columns(key_high, pair, bias[...]).astype(jnp.bfloat16))
        attended[:, lanes] = total.T.astype(jnp.bfloat16)

    on = []

    def pass_on(i):
        started[i][0].wait()
        on.append(weight_on(i))

    @pl.when(same_chip & same_core)
    def _():
        wo_copy(wo_x, wo_in, chip_mate).wait_send()
        wo_copy(wo_core, wo_in, core_mate).wait_send()
        wo_here.wait()

    @pl.when(jnp.logical_not(same_chip) & same_core)
    def _():
        wo_copy(wo_x, wo_in, chip_mate).wait_recv()
        forward = wo_copy(wo_on, wo, core_mate)
        forward.start()
        forward.wait_send()

    @pl.when(same_chip & jnp.logical_not(same_core))
    def _():
        wo_copy(wo_core, wo_in, core_mate).wait_recv()

    @pl.when(jnp.logical_not(same_chip) & jnp.logical_not(same_core))
    def _():
        wo_copy(wo_on, wo, core_mate).wait_recv()

    def project_out(rows):
        place_rows = pl.ds(pl.multiple_of(rows * own_rows, own_rows), own_rows)
        return plain_dot(attended[place_rows, :], wo[...])

    sums = {}
    for i in (2, 0, 1):
        sent[i] = project_out(members[i]).astype(jnp.bfloat16)
        sums[i] = send(29 + i, sent.at[i], got.at[i], peers[i])
    total = inputs + project_out(member)
    pass_on(2)
    for i in (0, 1, 2):
        sums[i].wait()
        total += got[i].astype(jnp.float32)
    middle[...] = total
    normed_two[member] = (total * rms_scale(total) * gain_two).astype(jnp.bfloat16)
    gather_two = [
        send(32 + i, normed_two.at[member], normed_two.at[member], device) for i, device in enumerate(peers)
    ]
    for i in (3, 4):
        pass_on(i)
    for i in (2, 3, 4):
        started[i][1].wait()
        started[i][2].wait()
    for copy in (*on, *gather_g, *gather_two):
        copy.wait()


def front(n_sp, tok_rows, heads, *operands):
    group = n_sp // MB
    own_rows = MB * tok_rows
    window = group * own_rows
    width_q = heads * HDIM
    width_f = FF // group
    low = jnp.bfloat16
    vmem = pl.BlockSpec(memory_space=pltpu.VMEM)
    anywhere = pl.BlockSpec(memory_space=pl.ANY)
    smem = pl.BlockSpec(memory_space=pltpu.SMEM)
    shape = jax.ShapeDtypeStruct
    return pl.pallas_call(
        functools.partial(front_kernel, n_sp),
        out_shape=(
            shape((MB, tok_rows, D), low),
            shape((group, own_rows, D), low),
            shape((group, own_rows, D), low),
            shape((window, width_q), low),
            shape((window, 2 * HDIM), low),
            shape((window, 2 * HDIM), low),
            shape((window, width_q), low),
            shape((own_rows, D), jnp.float32),
            shape((group, own_rows, D), low),
            shape((KV, D // KV, width_q), low),
            shape((KV, D // KV, 2 * HDIM), low),
            shape((width_q, D), low),
            shape((KV, D // KV, width_f), low),
            shape((KV, D // KV, width_f), low),
            shape((KV, D // KV, width_f), low),
            shape((KV, 8, D // KV), jnp.float32),
            shape((window, 2 * HDIM), jnp.float32),
            shape((window, 2 * HDIM), jnp.float32),
        ),
        in_specs=[anywhere] * 2 + [smem] * 2 + [vmem] * 5 + [anywhere] * 5,
        out_specs=tuple([vmem] * 12 + [anywhere] * 3 + [vmem] * 3),
        scratch_shapes=[
            pltpu.VMEM((8, D // KV), jnp.float32),
            pltpu.VMEM((D // KV, 2 * HDIM), low),
            pltpu.VMEM((MB, tok_rows, D), low),
            pltpu.VMEM((group - 1, own_rows, D), low),
            pltpu.VMEM((group - 1, own_rows, D), low),
            pltpu.VMEM((window, window), jnp.float32),
            pltpu.SemaphoreType.DMA((9,)),
            pltpu.SemaphoreType.DMA((35,)),
            pltpu.SemaphoreType.DMA((35,)),
        ],
        compiler_params=pltpu.CompilerParams(
            collective_id=0, has_side_effects=True, vmem_limit_bytes=VMEM_BYTES
        ),
        cost_estimate=pl.CostEstimate(flops=8 * 10**9, bytes_accessed=40 * 10**6, transcendentals=2 * 10**6),
        name="front",
    )(*operands)


def back_kernel(
    n_sp,
    d_two_part,
    block_part,
    gate_part,
    up_part,
    down_part,
    middle_in,
    tokens_in,
    upstream_in,
    normed_in,
    query_in,
    keys_in,
    values_in,
    attended_in,
    wq_in,
    wkv_in,
    wo_in,
    seq_len,
    slot_order,
    gains,
    cosine,
    sine,
    block_out,
    input_grad,
    ffn_grad,
    qkv_grad,
    out_grad,
    gain_sum,
    own_two,
    own_block,
    own_one,
    middle,
    xs,
    upstream,
    normed,
    query_rot,
    keys,
    values,
    attended,
    wq,
    wkv,
    wo,
    d_middle,
    d_full,
    d_attended,
    d_query,
    d_pair,
    key_sum,
    value_sum,
    bias,
    sent,
    got_two,
    got_one,
    rows_out,
    rows_got,
    from_core,
    from_chip,
    from_half,
    unit_stage,
    late,
    late_core,
    late_chip,
    late_half,
    out_part,
    out_core,
    out_chip,
    out_half,
    gain_part,
    gain_got,
    local_sem,
    send_sem,
    recv_sem,
):
    place = mesh_place(n_sp)
    shard, rank, micro, member, peers, members, partner, core_mate, chip_mate, far_mate = place
    chip, core = shard // 2, shard % 2
    group = n_sp // MB
    own_rows = middle.shape[0]
    tok_rows = own_rows // MB
    window = group * own_rows
    width_q = query_rot.shape[1]
    greet((*peers, partner, core_mate, chip_mate))

    def copy_to(index, source, target, device):
        return pltpu.make_async_remote_copy(
            src_ref=source,
            dst_ref=target,
            send_sem=send_sem.at[index],
            recv_sem=recv_sem.at[index],
            device_id=device,
            device_id_type=MESH,
        )

    def send(index, source, target, device):
        copy = copy_to(index, source, target, device)
        copy.start()
        return copy

    def move(index, source, target):
        copy = pltpu.make_async_copy(source, target, local_sem.at[index])
        copy.start()
        return copy

    ffn_parts = (gate_part, up_part, down_part)
    width_f = from_half.shape[-1]
    own_ffn = pl.ds(pl.multiple_of(member * width_f, 128), width_f)
    sums_two = {i: send(6 + i, d_two_part.at[members[i]], got_two.at[i], peers[i]) for i in (2, 0, 1)}
    own_load = move(0, d_two_part.at[member], own_two)
    core_copies = {}
    for w in range(3):
        for x in range(2):
            core_copies[w, x] = send(
                2 * w + x, ffn_parts[w].at[x, 1 - core], from_core.at[w, x], core_mate
            )
    inputs_in = (
        (middle_in, middle),
        (upstream_in.at[member], upstream),
        (wo_in, wo),
        (attended_in, attended),
        (query_in, query_rot),
        (keys_in, keys),
        (values_in, values),
        (wq_in, wq),
        (wkv_in, wkv),
        (normed_in, normed),
        (tokens_in, xs),
    )
    kept = [move(4 + i, source, target) for i, (source, target) in enumerate(inputs_in)]

    units = [(w, 1 - chip, 1 - micro) for w in range(3)]
    units += [(w, chip, 1 - micro) for w in range(3)]
    units += [(w, 1 - chip, micro) for w in range(3)]
    units += [(w, chip, micro) for w in range(3)]
    turn_of = {"next": 0, "load": None}

    def load_unit(number):
        w, x, m = units[number]
        return move(15 + number % 2, ffn_parts[w].at[x, core, m], unit_stage.at[number % 2])

    def next_unit():
        number = turn_of["next"]
        turn_of["load"].wait()
        if number + 1 < len(units):
            turn_of["load"] = load_unit(number + 1)
        turn_of["next"] = number + 1
        return unit_stage.at[number % 2]

    turn_of["load"] = load_unit(0)
    chip_copies, half_copies, last_copies, here_copies = {}, {}, [], []

    def chip_unit(w, m, index):
        part = next_unit()
        if (w, "core") not in turn_of:
            turn_of[w, "core"] = True
            core_copies[w, 0].wait()
            core_copies[w, 1].wait()

        @pl.loop(0, group)
        def _(t):
            total = from_core[w, 1 - chip, m, t].astype(jnp.float32) + part[t].astype(jnp.float32)
            from_core[w, 1 - chip, m, t] = total.astype(jnp.bfloat16)

        chip_copies[w, index] = send(
            9 + 2 * w + index, from_core.at[w, 1 - chip, m], from_chip.at[w, m], chip_mate
        )

    def half_unit(w):
        part = next_unit()
        chip_copies[w, 0].wait()

        @pl.loop(0, group)
        def _(t):
            total = from_core[w, chip, 1 - micro, t].astype(jnp.float32) + part[t].astype(jnp.float32)
            total += from_chip[w, 1 - micro, t].astype(jnp.float32)
            from_chip[w, 1 - micro, t] = total.astype(jnp.bfloat16)

        half_copies[w] = send(15 + w, from_chip.at[w, 1 - micro], from_half.at[w], partner)

    def last_unit(w):
        part = next_unit()
        chip_copies[w, 1].wait()
        half_copies[w].wait()

        @pl.loop(0, group)
        def _(t):
            total = from_core[w, chip, micro, t].astype(jnp.float32) + part[t].astype(jnp.float32)
            total += from_chip[w, micro, t].astype(jnp.float32) + from_half[w, t].astype(jnp.float32)
            from_chip[w, micro, t] = total.astype(jnp.bfloat16)

        for i in range(group - 1):
            last_copies.append(
                send(18 + 3 * w + i, from_chip.at[w, micro, members[i]], ffn_grad.at[w, :, own_ffn], peers[i])
            )
        here_copies.append(move(17 + w, from_chip.at[w, micro, member], ffn_grad.at[w, :, own_ffn]))

    for w in range(3):
        chip_unit(w, 1 - micro, 0)

    kept[0].wait()
    kept[1].wait()
    gain_one = jnp.concatenate([gains[f, 0:1, :] for f in range(KV)], axis=1)
    gain_two = jnp.concatenate([gains[f, 1:2, :] for f in range(KV)], axis=1)
    own_load.wait()
    upstream_rows = own_two[...].astype(jnp.float32)
    for i in range(group - 1):
        sums_two[i].wait()
        upstream_rows += got_two[i].astype(jnp.float32)
    middle_rows = middle[...]
    grad, two_term = norm_back(middle_rows, rms_scale(middle_rows), gain_two, upstream_rows)
    grad += upstream[...].astype(jnp.float32)
    d_middle[...] = grad
    d_full[member] = grad.astype(jnp.bfloat16)
    gather = [send(27 + i, d_full.at[member], d_full.at[member], device) for i, device in enumerate(peers)]
    block_load = move(1, block_part.at[member], own_block)

    first_len = seq_len[slot_order[2 * (shard * MB + micro)]]
    both_len = first_len + seq_len[slot_order[2 * (shard * MB + micro) + 1]]
    bias[...] = pair_bias(window, group, tok_rows, first_len, both_len)
    half_unit(0)

    for i in (2, 3, 4, 5, 6):
        kept[i].wait()

    def attention_grad(rows):
        place_rows = pl.ds(pl.multiple_of(rows * own_rows, own_rows), own_rows)
        d_attended[place_rows, :] = contract_cols(d_full[rows], wo[...]).astype(jnp.bfloat16)

    attention_grad(member)
    half_unit(1)
    for i, copy in enumerate(gather):
        copy.wait()
        attention_grad(members[i])

    sums_block = {i: send(30 + i, block_part.at[members[i]], got_two.at[i], peers[i]) for i in (2, 0, 1)}

    same_chip = chip == member // 2
    same_core = core == member % 2
    d_rows = d_full[...].reshape(window, D)
    for j in range(width_q // 128):
        part = contract_rows(attended[:, j * 128 : (j + 1) * 128], d_rows)
        for k in range(128 // tok_rows):
            out_part[j * (128 // tok_rows) + k] = part[k * tok_rows : (k + 1) * tok_rows].astype(jnp.bfloat16)
    out_by_core = copy_to(33, out_part, out_core, core_mate)
    out_by_chip = copy_to(34, out_part, out_chip, chip_mate)
    out_by_half = copy_to(35, out_part.at[pl.ds((1 - micro) * group, group)], out_half, partner)

    @pl.when(jnp.logical_not(same_core))
    def _():
        out_by_core.start()

    @pl.when(jnp.logical_not(same_core))
    def _():
        out_by_core.wait_send()

    @pl.when(same_core)
    def _():
        out_by_core.wait_recv()

        @pl.loop(0, MB * group)
        def _(t):
            total = out_part[t].astype(jnp.float32) + out_core[t].astype(jnp.float32)
            out_part[t] = total.astype(jnp.bfloat16)

    @pl.when(same_core & jnp.logical_not(same_chip))
    def _():
        out_by_chip.start()

    half_unit(2)
    for w in range(3):
        chip_unit(w, micro, 1)

    key_twice, value_twice = keys[...], values[...]
    lower = lane_ids(key_twice.shape) < HDIM
    zero = jnp.zeros_like(key_twice)
    key_low, key_high = jnp.where(lower, key_twice, zero), jnp.where(lower, zero, key_twice)
    value_low, value_high = jnp.where(lower, value_twice, zero), jnp.where(lower, zero, value_twice)
    key_low_turned, key_high_turned = key_low.T, key_high.T
    key_sum[...] = jnp.zeros_like(key_sum)
    value_sum[...] = jnp.zeros_like(value_sum)

    def attention_pair(j):
        lanes = pl.ds(pl.multiple_of(j * 128, 128), 128)
        query_pair, grad_pair = query_rot[:, lanes], d_attended[:, lanes]
        total = jnp.zeros((2 * HDIM, window), jnp.float32)
        for side, (key_side, value_side, key_turned) in enumerate(
            ((key_low, value_low, key_low_turned), (key_high, value_high, key_high_turned))
        ):
            probs = softmax_columns(key_side, query_pair, bias[...])
            d_probs = contract_cols(value_side, grad_pair)
            inner = jnp.sum(probs * d_probs, axis=0, keepdims=True)
            d_scores = (probs * (d_probs - inner)).astype(jnp.bfloat16)
            total += plain_dot(key_turned, d_scores)
            key_sum[side] += plain_dot(d_scores, query_pair)
            value_sum[side] += plain_dot(probs.astype(jnp.bfloat16), grad_pair)
        grad_rot = total.T * HDIM**-0.5
        d_query[:, lanes] = (grad_rot * cosine[...] + turn_back(grad_rot * sine[...])).astype(jnp.bfloat16)

    pl.loop(0, width_q // 128)(attention_pair)

    fold = lambda sums: jnp.where(lower, sums[0] + pltpu.roll(sums[1], HDIM, 1), 0.0)
    key_grad, value_grad = fold(key_sum), fold(value_sum)
    key_grad = key_grad * cosine[...] + turn_back(key_grad * sine[...])
    d_pair[...] = jnp.where(lower, key_grad, pltpu.roll(value_grad, HDIM, 1)).astype(jnp.bfloat16)

    block_load.wait()
    block = middle[...] + own_block[...].astype(jnp.float32)
    for i in range(group - 1):
        sums_block[i].wait()
        block += got_two[i].astype(jnp.float32)

    for i in (7, 8, 9, 10):
        kept[i].wait()

    def project_back(rows):
        place_rows = pl.ds(pl.multiple_of(rows * own_rows, own_rows), own_rows)
        grad_rows, pair_rows = d_query[place_rows, :], d_pair[place_rows, :]
        return jnp.concatenate(
            [contract_cols(grad_rows, wq[f]) + contract_cols(pair_rows, wkv[f]) for f in range(KV)], axis=1
        )

    sums_one = {}
    for i in (2, 0, 1):
        sent[i] = project_back(members[i]).astype(jnp.bfloat16)
        sums_one[i] = send(36 + i, sent.at[i], got_one.at[i], peers[i])
    own_one[...] = project_back(member)

    def give(slot, rows, target):
        rows_out[slot] = jnp.where(micro == 0, rows[tok_rows:], rows[:tok_rows]).astype(jnp.bfloat16)
        target[micro] = jnp.where(micro == 0, rows[:tok_rows], rows[tok_rows:])
        return send(39 + slot, rows_out.at[slot], rows_got.at[slot], partner)

    def take(slot, copy, target):
        copy.wait()
        target[1 - micro] = rows_got[slot].astype(jnp.float32)

    give_block = give(0, block, block_out)

    normed_rows = normed
    d_all = jnp.concatenate([d_query[...], d_pair[...]], axis=1)
    late_core_copies = []

    def late_part(x, c):
        for m in range(MB):
            first = ((x * 2 + c) * MB + m) * (group * tok_rows)
            columns = pl.ds(pl.multiple_of(first, group * tok_rows), group * tok_rows)
            rows = normed_rows[:, :, columns].reshape(window, group * tok_rows)
            part = contract_rows(rows, d_all)
            late[x, c, m] = part.astype(jnp.bfloat16).reshape(group, tok_rows, -1)

    for x in range(2):
        late_part(x, 1 - core)
        late_core_copies.append(send(41 + x, late.at[x, 1 - core], late_core.at[x], core_mate))
    for x in range(2):
        late_part(x, core)

    last_unit(0)
    for copy in late_core_copies:
        copy.wait()

    @pl.loop(0, MB * group)
    def _(k):
        m, t = k // group, k % group
        total = late[1 - chip, core, m, t].astype(jnp.float32) + late_core[1 - chip, m, t].astype(jnp.float32)
        late[1 - chip, core, m, t] = total.astype(jnp.bfloat16)

    late_to_chip = send(43, late.at[1 - chip, core], late_chip, chip_mate)

    @pl.when(same_core & jnp.logical_not(same_chip))
    def _():
        out_by_chip.wait_send()

    @pl.when(same_core & same_chip)
    def _():
        out_by_chip.wait_recv()

        @pl.loop(0, MB * group)
        def _(t):
            total = out_part[t].astype(jnp.float32) + out_chip[t].astype(jnp.float32)
            out_part[t] = total.astype(jnp.bfloat16)

        out_by_half.start()

    inputs = xs[...].reshape(own_rows, D).astype(jnp.float32)
    upstream_rows = own_one[...]
    for i in range(group - 1):
        sums_one[i].wait()
        upstream_rows += got_one[i].astype(jnp.float32)
    grad, one_term = norm_back(inputs, rms_scale(inputs), gain_one, upstream_rows)
    give_grad = give(1, grad + d_middle[...], input_grad)
    gain_part[...] = jnp.concatenate([one_term[None], two_term[None], jnp.zeros((6, D), jnp.float32)], axis=0)

    gain_core = send(44, gain_part, gain_got.at[0], core_mate)
    last_unit(1)
    gain_core.wait()
    gain_part[...] = gain_part[...] + gain_got[0]
    gain_chip = send(45, gain_part, gain_got.at[1], chip_mate)

    late_to_chip.wait()

    @pl.loop(0, group)
    def _(t):
        total = late[chip, core, 1 - micro, t].astype(jnp.float32) + late_core[chip, 1 - micro, t].astype(jnp.float32)
        total += late_chip[1 - micro, t].astype(jnp.float32)
        late_chip[1 - micro, t] = total.astype(jnp.bfloat16)

    late_to_half = send(46, late_chip.at[1 - micro], late_half, partner)
    gain_chip.wait()
    gain_part[...] = gain_part[...] + gain_got[1]
    gain_half = send(47, gain_part, gain_got.at[2], partner)

    last_unit(2)
    take(0, give_block, block_out)

    out_here = pltpu.make_async_copy(out_part.at[micro * group + member], out_grad, local_sem.at[24])

    def out_to(i):
        return pltpu.make_async_remote_copy(
            src_ref=out_part.at[micro * group + members[i]],
            dst_ref=out_grad,
            send_sem=send_sem.at[48 + i],
            recv_sem=recv_sem.at[48],
            device_id=peers[i],
            device_id_type=MESH,
        )

    @pl.when(same_core & same_chip)
    def _():
        out_by_half.wait()

        @pl.loop(0, group)
        def _(t):
            total = out_part[micro * group + t].astype(jnp.float32) + out_half[t].astype(jnp.float32)
            out_part[micro * group + t] = total.astype(jnp.bfloat16)

        for i in range(group - 1):
            out_to(i).start()
        out_here.start()

    gain_half.wait()
    gain_part[...] = gain_part[...] + gain_got[2]
    gain_all = [send(51 + i, gain_part, gain_got.at[3 + i], device) for i, device in enumerate(peers)]

    late_to_half.wait()

    @pl.loop(0, group)
    def _(t):
        total = late[chip, core, micro, t].astype(jnp.float32) + late_core[chip, micro, t].astype(jnp.float32)
        total += late_chip[micro, t].astype(jnp.float32) + late_half[t].astype(jnp.float32)
        late_chip[micro, t] = total.astype(jnp.bfloat16)

    own_late = pl.ds(pl.multiple_of(member * d_all.shape[1], 128), d_all.shape[1])
    for i in range(group - 1):
        last_copies.append(send(54 + i, late_chip.at[micro, members[i]], qkv_grad.at[:, own_late], peers[i]))
    here_copies.append(move(25, late_chip.at[micro, member], qkv_grad.at[:, own_late]))
    take(1, give_grad, input_grad)
    for copy in gain_all:
        copy.wait()
    gain_sum[...] = gain_part[...] + gain_got[3] + gain_got[4] + gain_got[5]

    @pl.when(same_core & same_chip)
    def _():
        for i in range(group - 1):
            out_to(i).wait_send()
        out_here.wait()

    @pl.when(jnp.logical_not(same_core & same_chip))
    def _():
        out_to(0).wait_recv()

    for copy in (*last_copies, *here_copies):
        copy.wait()


def back(n_sp, tok_rows, heads, *operands):
    group = n_sp // MB
    own_rows = MB * tok_rows
    window = group * own_rows
    width_q = heads * HDIM
    width_f = FF // group
    width_l = width_q + 2 * HDIM
    low, full = jnp.bfloat16, jnp.float32
    vmem = pl.BlockSpec(memory_space=pltpu.VMEM)
    anywhere = pl.BlockSpec(memory_space=pl.ANY)
    smem = pl.BlockSpec(memory_space=pltpu.SMEM)
    shape = jax.ShapeDtypeStruct
    return pl.pallas_call(
        functools.partial(back_kernel, n_sp),
        out_shape=(
            shape((MB, tok_rows, D), full),
            shape((MB, tok_rows, D), full),
            shape((3, tok_rows, FF), low),
            shape((tok_rows, group * width_l), low),
            shape((tok_rows, D), low),
            shape((8, D), full),
        ),
        in_specs=[anywhere] * 16 + [smem] * 2 + [vmem] * 3,
        out_specs=(vmem, vmem, anywhere, anywhere, anywhere, vmem),
        scratch_shapes=[
            pltpu.VMEM((own_rows, D), low),
            pltpu.VMEM((own_rows, D), low),
            pltpu.VMEM((own_rows, D), full),
            pltpu.VMEM((own_rows, D), full),
            pltpu.VMEM((MB, tok_rows, D), low),
            pltpu.VMEM((own_rows, D), low),
            pltpu.VMEM((group, own_rows, D), low),
            pltpu.VMEM((window, width_q), low),
            pltpu.VMEM((window, 2 * HDIM), low),
            pltpu.VMEM((window, 2 * HDIM), low),
            pltpu.VMEM((window, width_q), low),
            pltpu.VMEM((KV, D // KV, width_q), low),
            pltpu.VMEM((KV, D // KV, 2 * HDIM), low),
            pltpu.VMEM((width_q, D), low),
            pltpu.VMEM((own_rows, D), full),
            pltpu.VMEM((group, own_rows, D), low),
            pltpu.VMEM((window, width_q), low),
            pltpu.VMEM((window, width_q), low),
            pltpu.VMEM((window, 2 * HDIM), low),
            pltpu.VMEM((2, window, 2 * HDIM), full),
            pltpu.VMEM((2, window, 2 * HDIM), full),
            pltpu.VMEM((window, window), full),
            pltpu.VMEM((group - 1, own_rows, D), low),
            pltpu.VMEM((group - 1, own_rows, D), low),
            pltpu.VMEM((group - 1, own_rows, D), low),
            pltpu.VMEM((2, tok_rows, D), low),
            pltpu.VMEM((2, tok_rows, D), low),
            pltpu.VMEM((3, 2, MB, group, tok_rows, width_f), low),
            pltpu.VMEM((3, MB, group, tok_rows, width_f), low),
            pltpu.VMEM((3, group, tok_rows, width_f), low),
            pltpu.VMEM((2, group, tok_rows, width_f), low),
            pltpu.VMEM((2, 2, MB, group, tok_rows, width_l), low),
            pltpu.VMEM((2, MB, group, tok_rows, width_l), low),
            pltpu.VMEM((MB, group, tok_rows, width_l), low),
            pltpu.VMEM((group, tok_rows, width_l), low),
            pltpu.VMEM((MB * group, tok_rows, D), low),
            pltpu.VMEM((MB * group, tok_rows, D), low),
            pltpu.VMEM((MB * group, tok_rows, D), low),
            pltpu.VMEM((group, tok_rows, D), low),
            pltpu.VMEM((8, D), full),
            pltpu.VMEM((6, 8, D), full),
            pltpu.SemaphoreType.DMA((26,)),
            pltpu.SemaphoreType.DMA((57,)),
            pltpu.SemaphoreType.DMA((57,)),
        ],
        compiler_params=pltpu.CompilerParams(
            collective_id=1, has_side_effects=True, vmem_limit_bytes=VMEM_BYTES
        ),
        cost_estimate=pl.CostEstimate(flops=14 * 10**9, bytes_accessed=60 * 10**6, transcendentals=2 * 10**6),
        name="back",
    )(*operands)


def group_body(
    tokens,
    cotangent,
    seq_len,
    slot_order,
    norm1_gain,
    query_weight,
    key_weight,
    value_weight,
    output_weight,
    norm2_gain,
    gate_weight,
    up_weight,
    down_weight,
):
    n_sp = lax.axis_size("sp")
    n_fsdp = lax.axis_size("fsdp")
    group = n_sp // MB
    rank = lax.axis_index("sp")
    shard = lax.axis_index("fsdp")
    micro = rank // group
    member = rank % group
    tok_rows = tokens.shape[1]
    window = n_sp * tok_rows
    own_rows = MB * tok_rows
    inverse = np.float32(ROPE_BASE) ** (np.arange(HDIM // 2, dtype=np.float32) * np.float32(-2.0 / HDIM))
    heads = HEADS // group
    (
        own_tokens,
        upstream_low,
        normed,
        query_rot,
        keys,
        values,
        attended,
        middle,
        normed_two,
        w_query,
        w_kv,
        w_output,
        w_gate,
        w_up,
        w_down,
        gains,
        cosine,
        sine,
    ) = front(
        n_sp, tok_rows, heads,
        tokens, cotangent, seq_len, slot_order, norm1_gain[None], norm2_gain[None],
        jnp.asarray(np.tile(inverse, 4)[None]), key_weight, value_weight,
        query_weight, output_weight, gate_weight, up_weight, down_weight,
    )
    upstream_rows, normed_rows = upstream_low.reshape(window, D), normed_two.reshape(window, D)
    gate_full, up_full, down_full = (w.reshape(D, -1) for w in (w_gate, w_up, w_down))
    gate = plain_dot(normed_rows, gate_full)
    up = plain_dot(normed_rows, up_full)
    d_hidden = plain_dot(upstream_rows, down_full)
    sig = jax.nn.sigmoid(gate)
    silu = gate * sig
    hidden = (silu * up).astype(jnp.bfloat16)
    d_up = (d_hidden * silu).astype(jnp.bfloat16)
    d_gate = (d_hidden * up * sig * (1.0 + gate * (1.0 - sig))).astype(jnp.bfloat16)
    d_two_part = contract_cols(d_gate, gate_full) + contract_cols(d_up, up_full)
    block_part = contract_cols(hidden, down_full)
    gate_part = contract_rows(normed_rows, d_gate).astype(jnp.bfloat16)
    up_part = contract_rows(normed_rows, d_up).astype(jnp.bfloat16)
    down_part = contract_rows(upstream_rows, hidden).astype(jnp.bfloat16)
    by_owner = lambda part: part.reshape(2, 2, MB, group, tok_rows, -1)
    by_member = lambda part: part.reshape(group, own_rows, D).astype(jnp.bfloat16)
    block, d_inputs, ffn_grad, qkv_grad, output_grad, gain_sum = back(
        n_sp, tok_rows, heads,
        by_member(d_two_part), by_member(block_part), by_owner(gate_part), by_owner(up_part), by_owner(down_part),
        middle, own_tokens, upstream_low, normed, query_rot, keys, values, attended,
        w_query, w_kv, w_output, seq_len, slot_order, gains, cosine, sine,
    )
    gain_own = lax.dynamic_slice_in_dim(gain_sum, (shard * n_sp + rank) * tok_rows, tok_rows, 1)

    def part_of(first, width):
        pieces = qkv_grad.reshape(tok_rows, group, -1)[:, :, first : first + width]
        return pieces.reshape(tok_rows, group * width).astype(jnp.float32)

    width_q = heads * HDIM
    return (
        block,
        d_inputs,
        gain_own[0],
        part_of(0, width_q),
        part_of(width_q, HDIM),
        part_of(width_q + HDIM, HDIM),
        output_grad.astype(jnp.float32),
        gain_own[1],
        ffn_grad[0].astype(jnp.float32),
        ffn_grad[1].astype(jnp.float32),
        ffn_grad[2].astype(jnp.float32),
    )


def solution(mesh):
    fits = mesh.shape["fsdp"] == KV and mesh.shape["sp"] == MB * KV
    placed = (
        P(None, ("fsdp", "sp"), None),
        P(None, ("fsdp", "sp"), None),
        P(),
        P(),
        P("fsdp"),
        P("fsdp", None),
        P("fsdp", None),
        P("fsdp", None),
        P("fsdp", None),
        P("fsdp"),
        P("fsdp", None),
        P("fsdp", None),
        P("fsdp", None),
    )
    return jax.shard_map(
        group_body if fits else body,
        mesh=mesh,
        in_specs=placed,
        out_specs=(
            P(None, ("fsdp", "sp"), None),
            P(None, ("fsdp", "sp"), None),
            P(("fsdp", "sp")),
            P(("fsdp", "sp"), None),
            P(("fsdp", "sp"), None),
            P(("fsdp", "sp"), None),
            P(("fsdp", "sp"), None),
            P(("fsdp", "sp")),
            P(("fsdp", "sp"), None),
            P(("fsdp", "sp"), None),
            P(("fsdp", "sp"), None),
        ),
        check_vma=False,
    )
```

```python
import functools

import jax
import jax.numpy as jnp
import numpy as np
from jax import lax
from jax.experimental import pallas as pl
from jax.experimental.pallas import tpu as pltpu
from jax.sharding import PartitionSpec as P

D = 2048
HEADS = 32
KV = 4
HDIM = 64
FF = 5632
MB = 2
MESH = pl.DeviceIdType.MESH
VMEM_BYTES = 60 * 2**20


EPSILON = 1e-05
ROPE_BASE = 10000.0


def plain_dot(left_side, right_side):
    return jnp.dot(left_side, right_side, preferred_element_type=jnp.float32)


def contract_rows(left_side, right_side):
    return lax.dot_general(
        left_side, right_side, (((0,), (0,)), ((), ())), preferred_element_type=jnp.float32
    )


def contract_cols(left_side, right_side):
    return lax.dot_general(
        left_side, right_side, (((1,), (1,)), ((), ())), preferred_element_type=jnp.float32
    )


def window_layout(seq_len, slot_order, window_index, window):
    first_len = seq_len[slot_order[2 * window_index]]
    second_len = seq_len[slot_order[2 * window_index + 1]]
    places = jnp.arange(window, dtype=jnp.int32)
    segment = jnp.where(
        places < first_len, 0, jnp.where(places < first_len + second_len, 1, 2)
    ).astype(jnp.int32)
    anchor = jnp.where(segment == 0, 0, jnp.where(segment == 1, first_len, first_len + second_len))
    return (segment, places - anchor)


def rope_tables(position, head_size):
    half_size = head_size // 2
    inverse = ROPE_BASE ** (-2.0 * jnp.arange(half_size, dtype=jnp.float32) / head_size)
    angles = position.astype(jnp.float32)[:, None] * inverse[None, :]
    angles = jnp.concatenate([angles, angles], axis=1)
    return (jnp.cos(angles)[:, None, :], jnp.sin(angles)[:, None, :])


def apply_rope(vectors, cosine, sine):
    half_size = vectors.shape[-1] // 2
    turned = jnp.concatenate([-vectors[..., half_size:], vectors[..., :half_size]], axis=-1)
    return vectors * cosine + turned * sine


def rope_back(grad_in, cosine, sine):
    half_size = grad_in.shape[-1] // 2
    rotated = grad_in * sine
    return grad_in * cosine + jnp.concatenate(
        [rotated[..., half_size:], -rotated[..., :half_size]], axis=-1
    )


def rms_scale(inputs):
    return lax.rsqrt(jnp.mean(inputs * inputs, axis=-1, keepdims=True) + EPSILON)


def norm_back(inputs, scale_rows, gain_full, upstream):
    through = upstream * gain_full
    gain_term = jnp.sum(upstream * inputs * scale_rows, axis=0)
    grad_in = scale_rows * through - inputs * scale_rows**3 * jnp.mean(
        through * inputs, axis=-1, keepdims=True
    )
    return (grad_in, gain_term)


def score_block(query_block, key_rot, segment, row_start):
    block_rows = query_block.shape[0]
    places = jnp.arange(key_rot.shape[0], dtype=jnp.int32)
    row_place = row_start + jnp.arange(block_rows, dtype=jnp.int32)
    block_segment = lax.dynamic_slice_in_dim(segment, row_start, block_rows, 0)
    allowed = (block_segment[:, None] == segment[None, :]) & (places[None, :] <= row_place[:, None])
    raw_scores = jnp.einsum(
        "qhd,khd->hqk", query_block, key_rot, preferred_element_type=jnp.float32
    ) * query_block.shape[2] ** (-0.5)
    return jnp.where(allowed[None], raw_scores, -1e30)


def attend_forward(query_rot, key_rot, value_heads, segment):
    window = query_rot.shape[0]
    block_rows = min(512, window)

    def step(carry, block_index):
        row_start = block_index * block_rows
        query_block = lax.dynamic_slice_in_dim(query_rot, row_start, block_rows, 0)
        scores = score_block(query_block, key_rot, segment, row_start)
        row_top = jnp.max(scores, axis=-1, keepdims=True)
        weights_exp = jnp.exp(scores - row_top)
        row_total = jnp.sum(weights_exp, axis=-1, keepdims=True)
        probs = (weights_exp / row_total).astype(jnp.bfloat16)
        block_out = jnp.einsum(
            "hqk,khd->qhd", probs, value_heads, preferred_element_type=jnp.float32
        )
        log_total = (row_top + jnp.log(row_total))[:, :, 0].T
        return (carry, (block_out, log_total))

    block_ids = jnp.arange(window // block_rows, dtype=jnp.int32)
    _, (outputs, log_totals) = lax.scan(step, jnp.zeros((), jnp.int32), block_ids)
    return (outputs.reshape(query_rot.shape), log_totals.reshape(window, query_rot.shape[1]))


def attend_backward(query_rot, key_rot, value_heads, grad_heads, log_totals, segment):
    window = query_rot.shape[0]
    block_rows = min(512, window)
    scale_factor = query_rot.shape[2] ** (-0.5)

    def step(carry, block_index):
        key_acc, value_acc = carry
        row_start = block_index * block_rows
        query_block = lax.dynamic_slice_in_dim(query_rot, row_start, block_rows, 0)
        grad_block = lax.dynamic_slice_in_dim(grad_heads, row_start, block_rows, 0)
        total_block = lax.dynamic_slice_in_dim(log_totals, row_start, block_rows, 0)
        scores = score_block(query_block, key_rot, segment, row_start)
        probs = jnp.exp(scores - total_block.T[:, :, None])
        grad_probs = jnp.einsum(
            "qhd,khd->hqk", grad_block, value_heads, preferred_element_type=jnp.float32
        )
        inner_sum = jnp.sum(probs * grad_probs, axis=-1, keepdims=True)
        grad_scores = (probs * (grad_probs - inner_sum)).astype(jnp.bfloat16)
        query_part = (
            jnp.einsum("hqk,khd->qhd", grad_scores, key_rot, preferred_element_type=jnp.float32)
            * scale_factor
        )
        key_acc = (
            key_acc
            + jnp.einsum(
                "hqk,qhd->khd", grad_scores, query_block, preferred_element_type=jnp.float32
            )
            * scale_factor
        )
        value_acc = value_acc + jnp.einsum(
            "hqk,qhd->khd",
            probs.astype(jnp.bfloat16),
            grad_block,
            preferred_element_type=jnp.float32,
        )
        return ((key_acc, value_acc), query_part)

    start_acc = (jnp.zeros(key_rot.shape, jnp.float32), jnp.zeros(value_heads.shape, jnp.float32))
    block_ids = jnp.arange(window // block_rows, dtype=jnp.int32)
    (key_acc, value_acc), query_parts = lax.scan(step, start_acc, block_ids)
    return (query_parts.reshape(query_rot.shape), key_acc, value_acc)


def weight_terms(stored):
    joined = [jnp.concatenate(pieces, axis=0) for pieces in zip(*stored)]
    (
        normed,
        query_low,
        key_low,
        value_low,
        attn_rows,
        middle_low,
        normed_two,
        gate_low,
        up_low,
        upstream_low,
        hidden,
    ) = joined
    return jnp.concatenate(
        [
            contract_rows(normed, query_low),
            contract_rows(normed, key_low),
            contract_rows(normed, value_low),
            contract_rows(attn_rows, middle_low),
            contract_rows(normed_two, gate_low),
            contract_rows(normed_two, up_low),
            contract_rows(upstream_low, hidden),
        ],
        axis=1,
    )


def body(
    tokens,
    cotangent,
    seq_len,
    slot_order,
    norm1_gain,
    query_weight,
    key_weight,
    value_weight,
    output_weight,
    norm2_gain,
    gate_weight,
    up_weight,
    down_weight,
):
    seq_devices = lax.axis_size("sp")
    seq_rank = lax.axis_index("sp")
    shard_rank = lax.axis_index("fsdp")
    tok_rows = tokens.shape[1]
    window = seq_devices * tok_rows
    group_size = HEADS // KV
    kept = []
    outputs = []
    input_grads = []
    gain_sum = jnp.zeros((2, D), jnp.float32)
    grad_shards = None
    for micro_step in range(MB):
        gathered = (
            lax.all_gather(norm1_gain, "fsdp", axis=0, tiled=True),
            lax.all_gather(query_weight, "fsdp", axis=0, tiled=True),
            lax.all_gather(key_weight, "fsdp", axis=0, tiled=True),
            lax.all_gather(value_weight, "fsdp", axis=0, tiled=True),
            lax.all_gather(output_weight, "fsdp", axis=0, tiled=True),
            lax.all_gather(norm2_gain, "fsdp", axis=0, tiled=True),
            lax.all_gather(gate_weight, "fsdp", axis=0, tiled=True),
            lax.all_gather(up_weight, "fsdp", axis=0, tiled=True),
            lax.all_gather(down_weight, "fsdp", axis=0, tiled=True),
        )
        gain_one, w_query, w_key, w_value, w_output, gain_two, w_gate, w_up, w_down = gathered
        gain_one = gain_one.astype(jnp.float32)
        gain_two = gain_two.astype(jnp.float32)
        inputs = tokens[micro_step].astype(jnp.float32)
        window_index = shard_rank * MB + micro_step
        segment, position = window_layout(seq_len, slot_order, window_index, window)
        own_segment = lax.dynamic_slice_in_dim(segment, seq_rank * tok_rows, tok_rows, 0)
        valid_rows = (own_segment < 2).astype(jnp.float32)
        scale_one = rms_scale(inputs)
        normed = (inputs * scale_one * gain_one).astype(jnp.bfloat16)
        query_proj = plain_dot(normed, w_query).astype(jnp.bfloat16).reshape(tok_rows, HEADS, HDIM)
        key_proj = plain_dot(normed, w_key).astype(jnp.bfloat16).reshape(tok_rows, KV, HDIM)
        value_proj = plain_dot(normed, w_value).astype(jnp.bfloat16).reshape(tok_rows, KV, HDIM)
        packed = jnp.concatenate(
            [
                query_proj,
                jnp.repeat(key_proj, group_size, axis=1),
                jnp.repeat(value_proj, group_size, axis=1),
            ],
            axis=2,
        )
        head_side = lax.all_to_all(packed, "sp", split_axis=1, concat_axis=0, tiled=True)
        cosine, sine = rope_tables(position, HDIM)
        query_rot = apply_rope(head_side[:, :, :HDIM].astype(jnp.float32), cosine, sine).astype(
            jnp.bfloat16
        )
        key_rot = apply_rope(
            head_side[:, :, HDIM : 2 * HDIM].astype(jnp.float32), cosine, sine
        ).astype(jnp.bfloat16)
        value_heads = head_side[:, :, 2 * HDIM :]
        attended, log_totals = attend_forward(query_rot, key_rot, value_heads, segment)
        token_side = lax.all_to_all(
            attended.astype(jnp.bfloat16), "sp", split_axis=0, concat_axis=1, tiled=True
        )
        attn_rows = token_side.reshape(tok_rows, D)
        middle = inputs + plain_dot(attn_rows, w_output)
        scale_two = rms_scale(middle)
        normed_two = (middle * scale_two * gain_two).astype(jnp.bfloat16)
        gate_proj = plain_dot(normed_two, w_gate)
        up_proj = plain_dot(normed_two, w_up)
        gate_sig = jax.nn.sigmoid(gate_proj)
        hidden = (gate_proj * gate_sig * up_proj).astype(jnp.bfloat16)
        outputs.append(middle + contract_cols(hidden, w_down))
        upstream = cotangent[micro_step].astype(jnp.float32) * valid_rows[:, None]
        upstream_low = upstream.astype(jnp.bfloat16)
        hidden_grad = plain_dot(upstream_low, w_down)
        up_low = (hidden_grad * gate_proj * gate_sig).astype(jnp.bfloat16)
        gate_low = (hidden_grad * up_proj * gate_sig * (1.0 + gate_proj * (1.0 - gate_sig))).astype(
            jnp.bfloat16
        )
        normed_two_grad = contract_cols(gate_low, w_gate) + contract_cols(up_low, w_up)
        middle_grad, gain_two_term = norm_back(middle, scale_two, gain_two, normed_two_grad)
        middle_grad = middle_grad + upstream
        middle_low = middle_grad.astype(jnp.bfloat16)
        attn_grad = (
            contract_cols(middle_low, w_output).astype(jnp.bfloat16).reshape(tok_rows, HEADS, HDIM)
        )
        grad_heads = lax.all_to_all(attn_grad, "sp", split_axis=1, concat_axis=0, tiled=True)
        query_part, key_acc, value_acc = attend_backward(
            query_rot, key_rot, value_heads, grad_heads, log_totals, segment
        )
        packed_grad = jnp.concatenate(
            [rope_back(query_part, cosine, sine), rope_back(key_acc, cosine, sine), value_acc],
            axis=2,
        )
        grad_tokens = lax.all_to_all(packed_grad, "sp", split_axis=0, concat_axis=1, tiled=True)
        query_low = grad_tokens[:, :, :HDIM].reshape(tok_rows, D).astype(jnp.bfloat16)
        key_low = (
            grad_tokens[:, :, HDIM : 2 * HDIM]
            .reshape(tok_rows, KV, group_size, HDIM)
            .sum(axis=2)
            .reshape(tok_rows, KV * HDIM)
            .astype(jnp.bfloat16)
        )
        value_low = (
            grad_tokens[:, :, 2 * HDIM :]
            .reshape(tok_rows, KV, group_size, HDIM)
            .sum(axis=2)
            .reshape(tok_rows, KV * HDIM)
            .astype(jnp.bfloat16)
        )
        normed_grad = (
            contract_cols(query_low, w_query)
            + contract_cols(key_low, w_key)
            + contract_cols(value_low, w_value)
        )
        inputs_grad, gain_one_term = norm_back(inputs, scale_one, gain_one, normed_grad)
        input_grads.append(inputs_grad + middle_grad)
        gain_sum = gain_sum + jnp.stack([gain_one_term, gain_two_term])
        kept.append(
            (
                normed,
                query_low,
                key_low,
                value_low,
                attn_rows,
                middle_low,
                normed_two,
                gate_low,
                up_low,
                upstream_low,
                hidden,
            )
        )
        grad_shards = None
    grad_shards = lax.psum_scatter(
        weight_terms(kept), ("fsdp", "sp"), scatter_dimension=0, tiled=True
    )
    gain_shards = lax.psum_scatter(gain_sum, ("fsdp", "sp"), scatter_dimension=1, tiled=True)
    kv_width = KV * HDIM
    edges = [
        0,
        D,
        D + kv_width,
        D + 2 * kv_width,
        2 * D + 2 * kv_width,
        2 * D + 2 * kv_width + FF,
        2 * D + 2 * kv_width + 2 * FF,
        2 * D + 2 * kv_width + 3 * FF,
    ]
    pieces = [grad_shards[:, edges[slot] : edges[slot + 1]] for slot in range(7)]
    return (
        jnp.stack(outputs),
        jnp.stack(input_grads),
        gain_shards[0],
        pieces[0],
        pieces[1],
        pieces[2],
        pieces[3],
        gain_shards[1],
        pieces[4],
        pieces[5],
        pieces[6],
    )


def mesh_place(n_sp):
    shard = lax.axis_index("fsdp")
    rank = lax.axis_index("sp")
    group = n_sp // MB
    chip, core = shard // 2, shard % 2
    micro, member = rank // group, rank % group
    high, low = member // 2, member % 2
    base = micro * group
    peers = (
        (shard, base + high * 2 + (1 - low)),
        (shard, base + (1 - high) * 2 + low),
        (shard, base + (1 - high) * 2 + (1 - low)),
    )
    members = (high * 2 + (1 - low), (1 - high) * 2 + low, (1 - high) * 2 + (1 - low))
    partner = (shard, (1 - micro) * group + member)
    core_mate = (chip * 2 + (1 - core), rank)
    chip_mate = ((1 - chip) * 2 + core, rank)
    far_mate = ((1 - chip) * 2 + (1 - core), rank)
    return shard, rank, micro, member, peers, members, partner, core_mate, chip_mate, far_mate


def greet(devices):
    barrier = pltpu.get_barrier_semaphore()
    for device in devices:
        pl.semaphore_signal(barrier, inc=1, device_id=device, device_id_type=MESH)
    pl.semaphore_wait(barrier, len(devices))


def lane_ids(shape):
    return lax.broadcasted_iota(jnp.int32, shape, len(shape) - 1)


def turn(vectors):
    width = vectors.shape[-1]
    ahead = pltpu.roll(vectors, width - HDIM // 2, 1)
    behind = pltpu.roll(vectors, HDIM // 2, 1)
    first = lane_ids(vectors.shape) % HDIM < HDIM // 2
    return jnp.where(first, -ahead, behind)


def turn_back(vectors):
    return -turn(vectors)


def softmax_columns(key_side, query_pair, bias):
    scores = contract_cols(key_side, query_pair) + bias
    weights_exp = jnp.exp(scores - jnp.max(scores, axis=0, keepdims=True))
    return weights_exp * (1.0 / jnp.sum(weights_exp, axis=0, keepdims=True))


def row_places(shape, dim, group, tok_rows):
    ids = lax.broadcasted_iota(jnp.int32, shape, dim)
    own_rows = MB * tok_rows
    return ((ids % own_rows) // tok_rows) * (group * tok_rows) + (ids // own_rows) * tok_rows + ids % tok_rows


def row_positions(window, dim, group, tok_rows, first_len, both_len):
    shape = (window, 1) if dim == 0 else (1, window)
    place = row_places(shape, dim, group, tok_rows)
    anchor = jnp.where(place < first_len, 0, jnp.where(place < both_len, first_len, both_len))
    return place, place - anchor


def pair_bias(window, group, tok_rows, first_len, both_len):
    place, position = row_positions(window, 1, group, tok_rows, first_len, both_len)
    key_place = row_places((window, 1), 0, group, tok_rows)
    return jnp.where((key_place <= place) & (key_place >= place - position), 0.0, -1e30)


def layer_kernel(
    n_sp,
    tokens,
    cotangent,
    seq_len,
    slot_order,
    norm1_gain,
    norm2_gain,
    inverse,
    key_in,
    value_in,
    wq_in,
    wo_in,
    wg_in,
    wu_in,
    wd_in,
    block_out,
    input_grad,
    ffn_grad,
    qkv_grad,
    out_grad,
    gain_sum,
    from_core,
    from_chip,
    from_half,
    out_core,
    out_chip,
    out_half,
    wf,
    wq,
    wkv,
    wo,
    wkv_in,
    gains,
    gains_all,
    cosine,
    sine,
    bias,
    xs,
    gs,
    normed,
    upstream,
    normed_two,
    query_rot,
    keys,
    values,
    attended,
    d_attended,
    d_query,
    d_pair,
    key_sum,
    value_sum,
    middle,
    d_middle,
    own_rest,
    own_block,
    hid,
    sent,
    got,
    got_block,
    got_one,
    rows_out,
    rows_got,
    late_chip,
    late_half,
    out_stage,
    gain_part,
    gain_got,
    local_sem,
    send_sem,
    recv_sem,
):
    place = mesh_place(n_sp)
    shard, rank, micro, member, peers, members, partner, core_mate, chip_mate, far_mate = place
    chip, core = shard // 2, shard % 2
    group = n_sp // MB
    tok_rows = tokens.shape[1]
    own_rows = MB * tok_rows
    window = group * own_rows
    depth = D // KV
    width_q, width_f = wq.shape[1], wf.shape[2]
    width_l = width_q + 2 * HDIM
    half_rows = group * tok_rows
    greet((*peers, partner, core_mate, chip_mate, far_mate))

    def copy_to(index, source, target, device):
        return pltpu.make_async_remote_copy(
            src_ref=source,
            dst_ref=target,
            send_sem=send_sem.at[index],
            recv_sem=recv_sem.at[index],
            device_id=device,
            device_id_type=MESH,
        )

    def send(index, source, target, device):
        copy = copy_to(index, source, target, device)
        copy.start()
        return copy

    def move(index, source, target):
        copy = pltpu.make_async_copy(source, target, local_sem.at[index])
        copy.start()
        return copy

    def row_span(first, size):
        return pl.ds(pl.multiple_of(first, tok_rows), size)

    def lane_span(first, size):
        return pl.ds(pl.multiple_of(first, 128), size)

    swap_x = send(0, tokens.at[1 - micro], xs.at[micro], partner)
    swap_g = send(1, cotangent.at[1 - micro], gs.at[micro], partner)
    own_x = move(0, tokens.at[micro], xs.at[micro])
    own_g = move(1, cotangent.at[micro], gs.at[micro])
    gains[0:1, :] = norm1_gain[...].astype(jnp.float32)
    gains[1:2, :] = norm2_gain[...].astype(jnp.float32)
    gain_sends = [
        send(2 + i, gains, gains_all.at[shard], device) for i, device in enumerate((core_mate, chip_mate, far_mate))
    ]
    own_gain = move(2, gains, gains_all.at[shard])

    own_pair = lane_span(member // 2 * 128, 128)
    key_pair = key_in[:, own_pair].astype(jnp.float32)
    value_pair = value_in[:, own_pair].astype(jnp.float32)
    key_pair = jnp.where(member % 2 == 0, key_pair, pltpu.roll(key_pair, HDIM, 1))
    value_pair = jnp.where(member % 2 == 0, pltpu.roll(value_pair, HDIM, 1), value_pair)
    wkv_in[...] = jnp.where(lane_ids(key_pair.shape) < HDIM, key_pair, value_pair).astype(jnp.bfloat16)

    chip_shard = (1 - chip) * 2 + core
    own_ffn = lane_span(member * width_f, width_f)
    parts = (
        (wq_in.at[:, lane_span(member * width_q, width_q)], wq),
        (wkv_in, wkv),
        (wd_in.at[:, own_ffn], wf.at[0]),
        (wg_in.at[:, own_ffn], wf.at[1]),
        (wu_in.at[:, own_ffn], wf.at[2]),
    )

    def weight_out(i):
        source, target = parts[i]
        rows = row_span(shard * depth, depth)
        over_chip = send(5 + 3 * i, source, target.at[rows], chip_mate)
        over_core = send(6 + 3 * i, source, target.at[rows], core_mate)
        here = move(3 + i, source, target.at[rows])
        return over_chip, over_core, here

    def weight_on(i):
        rows = parts[i][1].at[row_span(chip_shard * depth, depth)]
        return send(7 + 3 * i, rows, rows, core_mate)

    started = {i: weight_out(i) for i in (0, 1)}
    same_chip, same_core = chip == member // 2, core == member % 2
    wo_over_chip = copy_to(20, wo_in, wo, chip_mate)
    wo_over_core = copy_to(21, wo_in, wo, core_mate)
    wo_on = copy_to(22, wo, wo, core_mate)
    wo_here = pltpu.make_async_copy(wo_in, wo, local_sem.at[8])

    @pl.when(same_chip & same_core)
    def _():
        wo_over_chip.start()
        wo_over_core.start()
        wo_here.start()

    for i in (2, 3, 4):
        started[i] = weight_out(i)

    first_len = seq_len[slot_order[2 * (shard * MB + micro)]]
    both_len = first_len + seq_len[slot_order[2 * (shard * MB + micro) + 1]]
    angles = row_positions(window, 0, group, tok_rows, first_len, both_len)[1].astype(jnp.float32) * inverse[...]
    cosine[...] = jnp.cos(angles)
    sine[...] = jnp.sin(angles)
    bias[...] = pair_bias(window, group, tok_rows, first_len, both_len)

    own_gain.wait()
    for copy in gain_sends:
        copy.wait()
    gain_one = jnp.concatenate([gains_all[f, 0:1, :] for f in range(KV)], axis=1)
    gain_two = jnp.concatenate([gains_all[f, 1:2, :] for f in range(KV)], axis=1)
    own_x.wait()
    swap_x.wait()
    inputs = xs[...].reshape(own_rows, D).astype(jnp.float32)
    normed[member] = (inputs * rms_scale(inputs) * gain_one).astype(jnp.bfloat16)
    gather = [send(23 + i, normed.at[member], normed.at[member], device) for i, device in enumerate(peers)]

    own_g.wait()
    swap_g.wait()
    ids = lax.broadcasted_iota(jnp.int32, (own_rows, 1), 0)
    own_place = (ids // tok_rows) * (group * tok_rows) + member * tok_rows + ids % tok_rows
    valid = jnp.where(own_place < both_len, 1.0, 0.0)
    upstream[member] = (gs[...].reshape(own_rows, D).astype(jnp.float32) * valid).astype(jnp.bfloat16)

    on = []
    for i in (0, 1):
        started[i][0].wait()
        on.append(weight_on(i))
    for i in (0, 1):
        started[i][1].wait()
        started[i][2].wait()
    for copy in on:
        copy.wait()

    def project(rows):
        block = normed[rows]
        place_rows = row_span(rows * own_rows, own_rows)
        query = plain_dot(block, wq[...])
        pair = plain_dot(block, wkv[...])
        cos, sin = cosine[place_rows, :], sine[place_rows, :]
        for j in range(width_q // 128):
            lanes = slice(j * 128, (j + 1) * 128)
            head = query[:, lanes].astype(jnp.bfloat16).astype(jnp.float32)
            head = (head * cos + turn(head) * sin).astype(jnp.bfloat16)
            query_rot[place_rows, lanes] = head * HDIM**-0.5
        pair = pair.astype(jnp.bfloat16).astype(jnp.float32)
        turned_key = pair * cos + turn(pair) * sin
        lower = lane_ids(pair.shape) < HDIM
        keys[place_rows, :] = jnp.where(lower, turned_key, pltpu.roll(turned_key, HDIM, 1)).astype(jnp.bfloat16)
        values[place_rows, :] = jnp.where(lower, pltpu.roll(pair, HDIM, 1), pair).astype(jnp.bfloat16)

    project(member)
    for i, copy in enumerate(gather):
        copy.wait()
        project(members[i])
    gather_g = [send(26 + i, upstream.at[member], upstream.at[member], device) for i, device in enumerate(peers)]

    key_twice, value_twice = keys[...], values[...]
    lower = lane_ids(key_twice.shape) < HDIM
    zero = jnp.zeros_like(key_twice)
    key_low, key_high = jnp.where(lower, key_twice, zero), jnp.where(lower, zero, key_twice)
    value_low, value_high = jnp.where(lower, value_twice, zero), jnp.where(lower, zero, value_twice)
    value_low_turned, value_high_turned = value_low.T, value_high.T

    @pl.loop(0, width_q // 128)
    def _(j):
        lanes = lane_span(j * 128, 128)
        pair = query_rot[:, lanes]
        total = plain_dot(value_low_turned, softmax_columns(key_low, pair, bias[...]).astype(jnp.bfloat16))
        total += plain_dot(value_high_turned, softmax_columns(key_high, pair, bias[...]).astype(jnp.bfloat16))
        attended[:, lanes] = total.T.astype(jnp.bfloat16)

    @pl.when(same_chip & same_core)
    def _():
        wo_over_chip.wait_send()
        wo_over_core.wait_send()
        wo_here.wait()

    @pl.when(jnp.logical_not(same_chip) & same_core)
    def _():
        wo_over_chip.wait_recv()
        wo_on.start()
        wo_on.wait_send()

    @pl.when(same_chip & jnp.logical_not(same_core))
    def _():
        wo_over_core.wait_recv()

    @pl.when(jnp.logical_not(same_chip) & jnp.logical_not(same_core))
    def _():
        wo_on.wait_recv()

    def project_out(rows):
        return plain_dot(attended[row_span(rows * own_rows, own_rows), :], wo[...])

    on = []

    def pass_on(i):
        started[i][0].wait()
        on.append(weight_on(i))

    sums = {}
    for i in (2, 0, 1):
        sent[i] = project_out(members[i]).astype(jnp.bfloat16)
        sums[i] = send(29 + i, sent.at[i], got.at[i], peers[i])
    total = inputs + project_out(member)
    pass_on(2)
    for i in (0, 1, 2):
        sums[i].wait()
        total += got[i].astype(jnp.float32)
    middle[...] = total
    normed_two[member] = (total * rms_scale(total) * gain_two).astype(jnp.bfloat16)
    gather_two = [
        send(32 + i, normed_two.at[member], normed_two.at[member], device) for i, device in enumerate(peers)
    ]
    for i in (3, 4):
        pass_on(i)
    for i in (2, 3, 4):
        started[i][1].wait()
        started[i][2].wait()
    for copy in (*on, *gather_g, *gather_two):
        copy.wait()

    @pl.loop(0, group)
    def _(r):
        place_rows = row_span(r * own_rows, own_rows)
        gate = plain_dot(normed_two[r], wf[1])
        up = plain_dot(normed_two[r], wf[2])
        d_hidden = plain_dot(upstream[r], wf[0])
        sig = jax.nn.sigmoid(gate)
        silu = gate * sig
        hid[0, place_rows, :] = (silu * up).astype(jnp.bfloat16)
        hid[1, place_rows, :] = (d_hidden * up * sig * (1.0 + gate * (1.0 - sig))).astype(jnp.bfloat16)
        hid[2, place_rows, :] = (d_hidden * silu).astype(jnp.bfloat16)

    def sum_over_y(index, rows_of, held, landing):
        held[0] = rows_of(members[2]).astype(jnp.bfloat16)
        over = send(index, held.at[0], landing.at[2], peers[0])
        held[1] = rows_of(members[0]).astype(jnp.bfloat16)
        over_y = send(index + 1, held.at[1], landing.at[0], peers[0])
        held[2] = rows_of(members[1]).astype(jnp.bfloat16)
        return over, over_y

    def sum_over_z(index, over, held, landing):
        over.wait()
        held[2] = (held[2].astype(jnp.float32) + landing[2].astype(jnp.float32)).astype(jnp.bfloat16)
        return send(index, held.at[2], landing.at[1], peers[1])

    def sum_of(rows, over_y, over_z, landing):
        over_y.wait()
        over_z.wait()
        return rows + landing[0].astype(jnp.float32) + landing[1].astype(jnp.float32)

    def hid_rows(k, rows):
        return hid[k, row_span(rows * own_rows, own_rows), :]

    base = 35
    block_rows = lambda rows: contract_cols(hid_rows(0, rows), wf[0])
    block_over, block_y = sum_over_y(base, block_rows, got_one, got_block)
    own_block[...] = block_rows(member)

    def weight_part(w, f):
        rows = lane_span(f * depth, depth)
        acts = (upstream if w == 0 else normed_two)[:, :, rows].reshape(window, depth)
        wf[w, rows, :] = contract_rows(acts, hid[w]).astype(jnp.bfloat16)

    core_copies, chip_copies, half_copies, last_copies, here_copies = {}, {}, {}, [], []

    def weight_parts(w):
        for x in range(2):
            weight_part(w, x * 2 + 1 - core)
        if w == 2:
            for x in range(2):
                weight_part(w, x * 2 + core)
        for x in range(2):
            rows = row_span((x * 2 + 1 - core) * depth, depth)
            core_copies[w, x] = send(base + 3 + 2 * w + x, wf.at[w, rows], from_core.at[w, x], core_mate)
        if w != 2:
            for x in range(2):
                weight_part(w, x * 2 + core)

    def slot(x, c, m):
        return (x * 2 + c) * depth + m * half_rows

    def stage_in(index, source, w, first):
        return move(index, source, wf.at[w, row_span(first, half_rows)])

    def add_up(w, first, stages):
        @pl.loop(0, group)
        def _(t):
            total = wf[w, row_span(first + t * tok_rows, tok_rows), :].astype(jnp.float32)
            for stage in stages:
                total += wf[w, row_span(stage + t * tok_rows, tok_rows), :].astype(jnp.float32)
            wf[w, row_span(first + t * tok_rows, tok_rows), :] = total.astype(jnp.bfloat16)

    def core_rows(w, x, m):
        return from_core.at[w, x, row_span(m * half_rows, half_rows)]

    def chip_unit(w, m, index):
        if index == 0:
            core_copies[w, 0].wait()
            core_copies[w, 1].wait()
        first, stage = slot(1 - chip, core, m), slot(1 - chip, 1 - core, m)
        stage_in(9, core_rows(w, 1 - chip, m), w, stage).wait()
        add_up(w, first, (stage,))
        chip_copies[w, index] = send(
            base + 9 + 2 * w + index, wf.at[w, row_span(first, half_rows)], from_chip.at[w, m], chip_mate
        )

    def half_unit(w):
        m = 1 - micro
        first, stage, other = slot(chip, core, m), slot(chip, 1 - core, m), slot(1 - chip, 1 - core, m)
        load = stage_in(9, core_rows(w, chip, m), w, stage)
        chip_copies[w, 0].wait()
        stage_in(10, from_chip.at[w, m], w, other).wait()
        load.wait()
        add_up(w, first, (stage, other))
        half_copies[w] = send(base + 15 + w, wf.at[w, row_span(first, half_rows)], from_half.at[w], partner)

    def last_unit(w):
        first, stage, other = slot(chip, core, micro), slot(chip, 1 - core, micro), slot(1 - chip, 1 - core, micro)
        third = slot(chip, 1 - core, 1 - micro)
        load = stage_in(9, core_rows(w, chip, micro), w, stage)
        chip_copies[w, 1].wait()
        over = stage_in(10, from_chip.at[w, micro], w, other)
        half_copies[w].wait()
        stage_in(11, from_half.at[w], w, third).wait()
        load.wait()
        over.wait()
        add_up(w, first, (stage, other, third))
        for i in range(group - 1):
            source = wf.at[w, row_span(first + members[i] * tok_rows, tok_rows)]
            last_copies.append(send(base + 18 + 3 * w + i, source, ffn_grad.at[w, :, own_ffn], peers[i]))
        source = wf.at[w, row_span(first + member * tok_rows, tok_rows)]
        here_copies.append(move(12 + w, source, ffn_grad.at[w, :, own_ffn]))

    weight_parts(0)
    two_rows = lambda rows: contract_cols(hid_rows(1, rows), wf[1]) + contract_cols(hid_rows(2, rows), wf[2])
    two_over, two_y = sum_over_y(base + 27, two_rows, sent, got)
    own_rest[...] = two_rows(member)
    chip_unit(0, 1 - micro, 0)
    weight_parts(1)
    block_z = sum_over_z(base + 2, block_over, got_one, got_block)
    chip_unit(1, 1 - micro, 0)
    weight_parts(2)
    two_z = sum_over_z(base + 29, two_over, sent, got)
    chip_unit(2, 1 - micro, 0)
    half_unit(0)

    def give(k, rows, target):
        rows_out[k] = jnp.where(micro == 0, rows[tok_rows:], rows[:tok_rows]).astype(jnp.bfloat16)
        target[micro] = jnp.where(micro == 0, rows[:tok_rows], rows[tok_rows:])
        return send(base + 30 + k, rows_out.at[k], rows_got.at[k], partner)

    def take(k, copy, target):
        copy.wait()
        target[1 - micro] = rows_got[k].astype(jnp.float32)

    give_block = give(0, sum_of(middle[...] + own_block[...], block_y, block_z, got_block), block_out)

    d_full = upstream
    middle_rows = middle[...]
    grad, two_term = norm_back(
        middle_rows, rms_scale(middle_rows), gain_two, sum_of(own_rest[...], two_y, two_z, got)
    )
    grad += upstream[member].astype(jnp.float32)
    d_middle[...] = grad
    d_full[member] = grad.astype(jnp.bfloat16)
    to_z = send(base + 32, d_full.at[member], d_full.at[member], peers[1])
    to_y = send(base + 33, d_full.at[member], d_full.at[member], peers[0])

    def attention_grad(rows):
        place_rows = row_span(rows * own_rows, own_rows)
        d_attended[place_rows, :] = contract_cols(d_full[rows], wo[...]).astype(jnp.bfloat16)

    attention_grad(member)
    to_z.wait()
    on_y = send(base + 34, d_full.at[members[1]], d_full.at[members[1]], peers[0])
    attention_grad(members[1])
    half_unit(1)
    to_y.wait()
    attention_grad(members[0])
    on_y.wait()
    attention_grad(members[2])

    out_part = normed_two
    d_rows = d_full[...].reshape(window, D)
    for j in range(group):
        out_part[j] = contract_rows(attended[:, j * 128 : (j + 1) * 128], d_rows).astype(jnp.bfloat16)
    out_by_core = copy_to(base + 35, out_part, out_core, core_mate)
    out_by_chip = copy_to(base + 36, out_part, out_chip, chip_mate)
    half_blocks = group // MB
    out_by_half = copy_to(base + 37, out_part.at[pl.ds((1 - micro) * half_blocks, half_blocks)], out_half, partner)

    def add_blocks(landed, first, count):
        for j in range(count):
            move(15, landed.at[j], out_stage).wait()
            out_part[first + j] = (
                out_part[first + j].astype(jnp.float32) + out_stage[...].astype(jnp.float32)
            ).astype(jnp.bfloat16)

    @pl.when(jnp.logical_not(same_core))
    def _():
        out_by_core.start()

    half_unit(2)
    for w in (0, 1):
        chip_unit(w, micro, 1)

    @pl.when(jnp.logical_not(same_core))
    def _():
        out_by_core.wait_send()

    @pl.when(same_core)
    def _():
        out_by_core.wait_recv()
        add_blocks(out_core, 0, group)

    @pl.when(same_core & jnp.logical_not(same_chip))
    def _():
        out_by_chip.start()

    key_low_turned, key_high_turned = key_low.T, key_high.T
    key_sum[...] = jnp.zeros_like(key_sum)
    value_sum[...] = jnp.zeros_like(value_sum)

    @pl.loop(0, width_q // 128)
    def _(j):
        lanes = lane_span(j * 128, 128)
        query_pair, grad_pair = query_rot[:, lanes], d_attended[:, lanes]
        total = jnp.zeros((2 * HDIM, window), jnp.float32)
        for side, (key_side, value_side, key_turned) in enumerate(
            ((key_low, value_low, key_low_turned), (key_high, value_high, key_high_turned))
        ):
            probs = softmax_columns(key_side, query_pair, bias[...])
            d_probs = contract_cols(value_side, grad_pair)
            inner = jnp.sum(probs * d_probs, axis=0, keepdims=True)
            d_scores = (probs * (d_probs - inner)).astype(jnp.bfloat16)
            total += plain_dot(key_turned, d_scores)
            key_sum[side] += plain_dot(d_scores, query_pair)
            value_sum[side] += plain_dot(probs.astype(jnp.bfloat16), grad_pair)
        grad_rot = total.T * HDIM**-0.5
        d_query[:, lanes] = (grad_rot * cosine[...] + turn_back(grad_rot * sine[...])).astype(jnp.bfloat16)

    fold = lambda sums: jnp.where(lower, sums[0] + pltpu.roll(sums[1], HDIM, 1), 0.0)
    key_grad, value_grad = fold(key_sum), fold(value_sum)
    key_grad = key_grad * cosine[...] + turn_back(key_grad * sine[...])
    d_pair[...] = jnp.where(lower, key_grad, pltpu.roll(value_grad, HDIM, 1)).astype(jnp.bfloat16)

    def one_rows(rows):
        place_rows = row_span(rows * own_rows, own_rows)
        return contract_cols(d_query[place_rows, :], wq[...]) + contract_cols(d_pair[place_rows, :], wkv[...])

    one_over, one_y = sum_over_y(base + 38, one_rows, sent, got_one)
    own_rest[...] = one_rows(member)

    d_all = jnp.concatenate([d_query[...], d_pair[...]], axis=1)

    def late_lanes(c):
        return lane_span(c * width_l, width_l)

    def late_part(x, c):
        for m in range(MB):
            columns = lane_span(((x * 2 + c) * MB + m) * half_rows, half_rows)
            rows = normed[:, :, columns].reshape(window, half_rows)
            hid[x, m * half_rows : (m + 1) * half_rows, late_lanes(c)] = contract_rows(rows, d_all).astype(jnp.bfloat16)

    late_core_copies = []
    for x in range(2):
        late_part(x, 1 - core)
        late_core_copies.append(
            send(base + 41 + x, hid.at[x, :, late_lanes(1 - core)], hid.at[2, :, late_lanes(x)], core_mate)
        )
    one_z = sum_over_z(base + 40, one_over, sent, got_one)
    for x in range(2):
        late_part(x, core)
    for copy in late_core_copies:
        copy.wait()

    def late_add(x, first, count, landed):
        @pl.loop(0, count)
        def _(t):
            rows = row_span(first + t * tok_rows, tok_rows)
            total = hid[x, rows, late_lanes(core)].astype(jnp.float32) + hid[2, rows, late_lanes(x)].astype(jnp.float32)
            for ref, start in landed:
                total += ref[row_span(start + t * tok_rows, tok_rows), :].astype(jnp.float32)
            hid[x, rows, late_lanes(core)] = total.astype(jnp.bfloat16)

    late_add(1 - chip, 0, MB * group, ())
    late_to_chip = send(base + 43, hid.at[1 - chip, :, late_lanes(core)], late_chip, chip_mate)
    chip_unit(2, micro, 1)

    @pl.when(same_core & jnp.logical_not(same_chip))
    def _():
        out_by_chip.wait_send()

    @pl.when(same_core & same_chip)
    def _():
        out_by_chip.wait_recv()
        add_blocks(out_chip, 0, group)
        out_by_half.start()

    inputs = xs[...].reshape(own_rows, D).astype(jnp.float32)
    grad, one_term = norm_back(inputs, rms_scale(inputs), gain_one, sum_of(own_rest[...], one_y, one_z, got_one))
    give_grad = give(1, grad + d_middle[...], input_grad)
    gain_part[...] = jnp.concatenate([one_term[None], two_term[None], jnp.zeros((6, D), jnp.float32)], axis=0)

    gain_core = send(base + 44, gain_part, gain_got.at[0], core_mate)
    last_unit(0)
    gain_core.wait()
    gain_part[...] = gain_part[...] + gain_got[0]
    gain_chip = send(base + 45, gain_part, gain_got.at[1], chip_mate)
    last_unit(1)

    late_to_chip.wait()
    late_add(chip, (1 - micro) * half_rows, group, ((late_chip, (1 - micro) * half_rows),))
    late_to_half = send(
        base + 46, hid.at[chip, row_span((1 - micro) * half_rows, half_rows), late_lanes(core)], late_half, partner
    )
    gain_chip.wait()
    gain_part[...] = gain_part[...] + gain_got[1]
    gain_half = send(base + 47, gain_part, gain_got.at[2], partner)
    take(0, give_block, block_out)

    def out_block(t):
        return out_part.at[micro * half_blocks + t // 2, row_span(t % 2 * tok_rows, tok_rows)]

    out_here = pltpu.make_async_copy(out_block(member), out_grad, local_sem.at[16])

    def out_to(i):
        return pltpu.make_async_remote_copy(
            src_ref=out_block(members[i]),
            dst_ref=out_grad,
            send_sem=send_sem.at[base + 48 + i],
            recv_sem=recv_sem.at[base + 48],
            device_id=peers[i],
            device_id_type=MESH,
        )

    @pl.when(same_core & same_chip)
    def _():
        out_by_half.wait()
        add_blocks(out_half, micro * half_blocks, half_blocks)
        for i in range(group - 1):
            out_to(i).start()
        out_here.start()

    last_unit(2)
    gain_half.wait()
    gain_part[...] = gain_part[...] + gain_got[2]
    gain_all = [send(base + 51 + i, gain_part, gain_got.at[3 + i], device) for i, device in enumerate(peers)]

    late_to_half.wait()
    late_add(chip, micro * half_rows, group, ((late_chip, micro * half_rows), (late_half, 0)))
    own_late = lane_span(member * width_l, width_l)

    def late_rows(t):
        return hid.at[chip, row_span(micro * half_rows + t * tok_rows, tok_rows), late_lanes(core)]

    for i in range(group - 1):
        last_copies.append(send(base + 54 + i, late_rows(members[i]), qkv_grad.at[:, own_late], peers[i]))
    here_copies.append(move(17, late_rows(member), qkv_grad.at[:, own_late]))
    take(1, give_grad, input_grad)
    for copy in gain_all:
        copy.wait()
    gain_sum[...] = gain_part[...] + gain_got[3] + gain_got[4] + gain_got[5]

    @pl.when(same_core & same_chip)
    def _():
        for i in range(group - 1):
            out_to(i).wait_send()
        out_here.wait()

    @pl.when(jnp.logical_not(same_core & same_chip))
    def _():
        out_to(0).wait_recv()

    for copy in (*last_copies, *here_copies):
        copy.wait()


def whole_layer(n_sp, tok_rows, heads, *operands):
    group = n_sp // MB
    own_rows = MB * tok_rows
    window = group * own_rows
    half_rows = group * tok_rows
    width_q = heads * HDIM
    width_f = FF // group
    width_l = width_q + 2 * HDIM
    low, full = jnp.bfloat16, jnp.float32
    vmem = pl.BlockSpec(memory_space=pltpu.VMEM)
    anywhere = pl.BlockSpec(memory_space=pl.ANY)
    smem = pl.BlockSpec(memory_space=pltpu.SMEM)
    shape = jax.ShapeDtypeStruct
    blocks = (group, own_rows, D)
    trio = (group - 1, own_rows, D)
    pair = (MB, tok_rows, D)
    return pl.pallas_call(
        functools.partial(layer_kernel, n_sp),
        out_shape=(
            shape(pair, full),
            shape(pair, full),
            shape((3, tok_rows, FF), low),
            shape((tok_rows, group * width_l), low),
            shape((tok_rows, D), low),
            shape((8, D), full),
            shape((3, 2, MB * half_rows, width_f), low),
            shape((3, MB, half_rows, width_f), low),
            shape((3, half_rows, width_f), low),
            shape(blocks, low),
            shape(blocks, low),
            shape((group // MB, own_rows, D), low),
        ),
        in_specs=[anywhere] * 2 + [smem] * 2 + [vmem] * 5 + [anywhere] * 5,
        out_specs=(vmem, vmem, anywhere, anywhere, anywhere, vmem) + (anywhere,) * 6,
        scratch_shapes=[
            pltpu.VMEM((3, D, width_f), low),
            pltpu.VMEM((D, width_q), low),
            pltpu.VMEM((D, 2 * HDIM), low),
            pltpu.VMEM((width_q, D), low),
            pltpu.VMEM((D // KV, 2 * HDIM), low),
            pltpu.VMEM((8, D // KV), full),
            pltpu.VMEM((KV, 8, D // KV), full),
            pltpu.VMEM((window, 2 * HDIM), full),
            pltpu.VMEM((window, 2 * HDIM), full),
            pltpu.VMEM((window, window), full),
            pltpu.VMEM(pair, low),
            pltpu.VMEM(pair, low),
            pltpu.VMEM(blocks, low),
            pltpu.VMEM(blocks, low),
            pltpu.VMEM(blocks, low),
            pltpu.VMEM((window, width_q), low),
            pltpu.VMEM((window, 2 * HDIM), low),
            pltpu.VMEM((window, 2 * HDIM), low),
            pltpu.VMEM((window, width_q), low),
            pltpu.VMEM((window, width_q), low),
            pltpu.VMEM((window, width_q), low),
            pltpu.VMEM((window, 2 * HDIM), low),
            pltpu.VMEM((2, window, 2 * HDIM), full),
            pltpu.VMEM((2, window, 2 * HDIM), full),
            pltpu.VMEM((own_rows, D), full),
            pltpu.VMEM((own_rows, D), full),
            pltpu.VMEM((own_rows, D), full),
            pltpu.VMEM((own_rows, D), full),
            pltpu.VMEM((3, window, width_f), low),
            pltpu.VMEM(trio, low),
            pltpu.VMEM(trio, low),
            pltpu.VMEM(trio, low),
            pltpu.VMEM(trio, low),
            pltpu.VMEM((2, tok_rows, D), low),
            pltpu.VMEM((2, tok_rows, D), low),
            pltpu.VMEM((MB * half_rows, width_l), low),
            pltpu.VMEM((half_rows, width_l), low),
            pltpu.VMEM((own_rows, D), low),
            pltpu.VMEM((8, D), full),
            pltpu.VMEM((6, 8, D), full),
            pltpu.SemaphoreType.DMA((18,)),
            pltpu.SemaphoreType.DMA((92,)),
            pltpu.SemaphoreType.DMA((92,)),
        ],
        compiler_params=pltpu.CompilerParams(
            collective_id=0, has_side_effects=True, vmem_limit_bytes=VMEM_BYTES
        ),
        cost_estimate=pl.CostEstimate(flops=36 * 10**9, bytes_accessed=100 * 10**6, transcendentals=8 * 10**6),
        name="whole_layer",
    )(*operands)


def group_body(
    tokens,
    cotangent,
    seq_len,
    slot_order,
    norm1_gain,
    query_weight,
    key_weight,
    value_weight,
    output_weight,
    norm2_gain,
    gate_weight,
    up_weight,
    down_weight,
):
    n_sp = lax.axis_size("sp")
    n_fsdp = lax.axis_size("fsdp")
    group = n_sp // MB
    rank = lax.axis_index("sp")
    shard = lax.axis_index("fsdp")
    micro = rank // group
    member = rank % group
    tok_rows = tokens.shape[1]
    window = n_sp * tok_rows
    own_rows = MB * tok_rows
    inverse = np.float32(ROPE_BASE) ** (np.arange(HDIM // 2, dtype=np.float32) * np.float32(-2.0 / HDIM))
    heads = HEADS // group
    block, d_inputs, ffn_grad, qkv_grad, output_grad, gain_sum, *_ = whole_layer(
        n_sp, tok_rows, heads,
        tokens, cotangent, seq_len, slot_order, norm1_gain[None], norm2_gain[None],
        jnp.asarray(np.tile(inverse, 4)[None]), key_weight, value_weight,
        query_weight, output_weight, gate_weight, up_weight, down_weight,
    )
    gain_own = lax.dynamic_slice_in_dim(gain_sum, (shard * n_sp + rank) * tok_rows, tok_rows, 1)

    def part_of(first, width):
        pieces = qkv_grad.reshape(tok_rows, group, -1)[:, :, first : first + width]
        return pieces.reshape(tok_rows, group * width).astype(jnp.float32)

    width_q = heads * HDIM
    return (
        block,
        d_inputs,
        gain_own[0],
        part_of(0, width_q),
        part_of(width_q, HDIM),
        part_of(width_q + HDIM, HDIM),
        output_grad.astype(jnp.float32),
        gain_own[1],
        ffn_grad[1].astype(jnp.float32),
        ffn_grad[2].astype(jnp.float32),
        ffn_grad[0].astype(jnp.float32),
    )


def solution(mesh):
    fits = mesh.shape["fsdp"] == KV and mesh.shape["sp"] == MB * KV
    placed = (
        P(None, ("fsdp", "sp"), None),
        P(None, ("fsdp", "sp"), None),
        P(),
        P(),
        P("fsdp"),
        P("fsdp", None),
        P("fsdp", None),
        P("fsdp", None),
        P("fsdp", None),
        P("fsdp"),
        P("fsdp", None),
        P("fsdp", None),
        P("fsdp", None),
    )
    return jax.shard_map(
        group_body if fits else body,
        mesh=mesh,
        in_specs=placed,
        out_specs=(
            P(None, ("fsdp", "sp"), None),
            P(None, ("fsdp", "sp"), None),
            P(("fsdp", "sp")),
            P(("fsdp", "sp"), None),
            P(("fsdp", "sp"), None),
            P(("fsdp", "sp"), None),
            P(("fsdp", "sp"), None),
            P(("fsdp", "sp")),
            P(("fsdp", "sp"), None),
            P(("fsdp", "sp"), None),
            P(("fsdp", "sp"), None),
        ),
        check_vma=False,
    )
```

```python
import functools

import jax
import jax.numpy as jnp
import numpy as np
from jax import lax
from jax.experimental import pallas as pl
from jax.experimental.pallas import tpu as pltpu
from jax.sharding import PartitionSpec as P

D = 2048
HEADS = 32
KV = 4
HDIM = 64
FF = 5632
MB = 2
MESH = pl.DeviceIdType.MESH
VMEM_BYTES = 60 * 2**20


EPSILON = 1e-05
ROPE_BASE = 10000.0


def plain_dot(left_side, right_side):
    return jnp.dot(left_side, right_side, preferred_element_type=jnp.float32)


def contract_rows(left_side, right_side):
    return lax.dot_general(
        left_side, right_side, (((0,), (0,)), ((), ())), preferred_element_type=jnp.float32
    )


def contract_cols(left_side, right_side):
    return lax.dot_general(
        left_side, right_side, (((1,), (1,)), ((), ())), preferred_element_type=jnp.float32
    )


def window_layout(seq_len, slot_order, window_index, window):
    first_len = seq_len[slot_order[2 * window_index]]
    second_len = seq_len[slot_order[2 * window_index + 1]]
    places = jnp.arange(window, dtype=jnp.int32)
    segment = jnp.where(
        places < first_len, 0, jnp.where(places < first_len + second_len, 1, 2)
    ).astype(jnp.int32)
    anchor = jnp.where(segment == 0, 0, jnp.where(segment == 1, first_len, first_len + second_len))
    return (segment, places - anchor)


def rope_tables(position, head_size):
    half_size = head_size // 2
    inverse = ROPE_BASE ** (-2.0 * jnp.arange(half_size, dtype=jnp.float32) / head_size)
    angles = position.astype(jnp.float32)[:, None] * inverse[None, :]
    angles = jnp.concatenate([angles, angles], axis=1)
    return (jnp.cos(angles)[:, None, :], jnp.sin(angles)[:, None, :])


def apply_rope(vectors, cosine, sine):
    half_size = vectors.shape[-1] // 2
    turned = jnp.concatenate([-vectors[..., half_size:], vectors[..., :half_size]], axis=-1)
    return vectors * cosine + turned * sine


def rope_back(grad_in, cosine, sine):
    half_size = grad_in.shape[-1] // 2
    rotated = grad_in * sine
    return grad_in * cosine + jnp.concatenate(
        [rotated[..., half_size:], -rotated[..., :half_size]], axis=-1
    )


def rms_scale(inputs):
    return lax.rsqrt(jnp.mean(inputs * inputs, axis=-1, keepdims=True) + EPSILON)


def norm_back(inputs, scale_rows, gain_full, upstream):
    through = upstream * gain_full
    gain_term = jnp.sum(upstream * inputs * scale_rows, axis=0)
    grad_in = scale_rows * through - inputs * scale_rows**3 * jnp.mean(
        through * inputs, axis=-1, keepdims=True
    )
    return (grad_in, gain_term)


def score_block(query_block, key_rot, segment, row_start):
    block_rows = query_block.shape[0]
    places = jnp.arange(key_rot.shape[0], dtype=jnp.int32)
    row_place = row_start + jnp.arange(block_rows, dtype=jnp.int32)
    block_segment = lax.dynamic_slice_in_dim(segment, row_start, block_rows, 0)
    allowed = (block_segment[:, None] == segment[None, :]) & (places[None, :] <= row_place[:, None])
    raw_scores = jnp.einsum(
        "qhd,khd->hqk", query_block, key_rot, preferred_element_type=jnp.float32
    ) * query_block.shape[2] ** (-0.5)
    return jnp.where(allowed[None], raw_scores, -1e30)


def attend_forward(query_rot, key_rot, value_heads, segment):
    window = query_rot.shape[0]
    block_rows = min(512, window)

    def step(carry, block_index):
        row_start = block_index * block_rows
        query_block = lax.dynamic_slice_in_dim(query_rot, row_start, block_rows, 0)
        scores = score_block(query_block, key_rot, segment, row_start)
        row_top = jnp.max(scores, axis=-1, keepdims=True)
        weights_exp = jnp.exp(scores - row_top)
        row_total = jnp.sum(weights_exp, axis=-1, keepdims=True)
        probs = (weights_exp / row_total).astype(jnp.bfloat16)
        block_out = jnp.einsum(
            "hqk,khd->qhd", probs, value_heads, preferred_element_type=jnp.float32
        )
        log_total = (row_top + jnp.log(row_total))[:, :, 0].T
        return (carry, (block_out, log_total))

    block_ids = jnp.arange(window // block_rows, dtype=jnp.int32)
    _, (outputs, log_totals) = lax.scan(step, jnp.zeros((), jnp.int32), block_ids)
    return (outputs.reshape(query_rot.shape), log_totals.reshape(window, query_rot.shape[1]))


def attend_backward(query_rot, key_rot, value_heads, grad_heads, log_totals, segment):
    window = query_rot.shape[0]
    block_rows = min(512, window)
    scale_factor = query_rot.shape[2] ** (-0.5)

    def step(carry, block_index):
        key_acc, value_acc = carry
        row_start = block_index * block_rows
        query_block = lax.dynamic_slice_in_dim(query_rot, row_start, block_rows, 0)
        grad_block = lax.dynamic_slice_in_dim(grad_heads, row_start, block_rows, 0)
        total_block = lax.dynamic_slice_in_dim(log_totals, row_start, block_rows, 0)
        scores = score_block(query_block, key_rot, segment, row_start)
        probs = jnp.exp(scores - total_block.T[:, :, None])
        grad_probs = jnp.einsum(
            "qhd,khd->hqk", grad_block, value_heads, preferred_element_type=jnp.float32
        )
        inner_sum = jnp.sum(probs * grad_probs, axis=-1, keepdims=True)
        grad_scores = (probs * (grad_probs - inner_sum)).astype(jnp.bfloat16)
        query_part = (
            jnp.einsum("hqk,khd->qhd", grad_scores, key_rot, preferred_element_type=jnp.float32)
            * scale_factor
        )
        key_acc = (
            key_acc
            + jnp.einsum(
                "hqk,qhd->khd", grad_scores, query_block, preferred_element_type=jnp.float32
            )
            * scale_factor
        )
        value_acc = value_acc + jnp.einsum(
            "hqk,qhd->khd",
            probs.astype(jnp.bfloat16),
            grad_block,
            preferred_element_type=jnp.float32,
        )
        return ((key_acc, value_acc), query_part)

    start_acc = (jnp.zeros(key_rot.shape, jnp.float32), jnp.zeros(value_heads.shape, jnp.float32))
    block_ids = jnp.arange(window // block_rows, dtype=jnp.int32)
    (key_acc, value_acc), query_parts = lax.scan(step, start_acc, block_ids)
    return (query_parts.reshape(query_rot.shape), key_acc, value_acc)


def weight_terms(stored):
    joined = [jnp.concatenate(pieces, axis=0) for pieces in zip(*stored)]
    (
        normed,
        query_low,
        key_low,
        value_low,
        attn_rows,
        middle_low,
        normed_two,
        gate_low,
        up_low,
        upstream_low,
        hidden,
    ) = joined
    return jnp.concatenate(
        [
            contract_rows(normed, query_low),
            contract_rows(normed, key_low),
            contract_rows(normed, value_low),
            contract_rows(attn_rows, middle_low),
            contract_rows(normed_two, gate_low),
            contract_rows(normed_two, up_low),
            contract_rows(upstream_low, hidden),
        ],
        axis=1,
    )


def body(
    tokens,
    cotangent,
    seq_len,
    slot_order,
    norm1_gain,
    query_weight,
    key_weight,
    value_weight,
    output_weight,
    norm2_gain,
    gate_weight,
    up_weight,
    down_weight,
):
    seq_devices = lax.axis_size("sp")
    seq_rank = lax.axis_index("sp")
    shard_rank = lax.axis_index("fsdp")
    tok_rows = tokens.shape[1]
    window = seq_devices * tok_rows
    group_size = HEADS // KV
    kept = []
    outputs = []
    input_grads = []
    gain_sum = jnp.zeros((2, D), jnp.float32)
    grad_shards = None
    for micro_step in range(MB):
        gathered = (
            lax.all_gather(norm1_gain, "fsdp", axis=0, tiled=True),
            lax.all_gather(query_weight, "fsdp", axis=0, tiled=True),
            lax.all_gather(key_weight, "fsdp", axis=0, tiled=True),
            lax.all_gather(value_weight, "fsdp", axis=0, tiled=True),
            lax.all_gather(output_weight, "fsdp", axis=0, tiled=True),
            lax.all_gather(norm2_gain, "fsdp", axis=0, tiled=True),
            lax.all_gather(gate_weight, "fsdp", axis=0, tiled=True),
            lax.all_gather(up_weight, "fsdp", axis=0, tiled=True),
            lax.all_gather(down_weight, "fsdp", axis=0, tiled=True),
        )
        gain_one, w_query, w_key, w_value, w_output, gain_two, w_gate, w_up, w_down = gathered
        gain_one = gain_one.astype(jnp.float32)
        gain_two = gain_two.astype(jnp.float32)
        inputs = tokens[micro_step].astype(jnp.float32)
        window_index = shard_rank * MB + micro_step
        segment, position = window_layout(seq_len, slot_order, window_index, window)
        own_segment = lax.dynamic_slice_in_dim(segment, seq_rank * tok_rows, tok_rows, 0)
        valid_rows = (own_segment < 2).astype(jnp.float32)
        scale_one = rms_scale(inputs)
        normed = (inputs * scale_one * gain_one).astype(jnp.bfloat16)
        query_proj = plain_dot(normed, w_query).astype(jnp.bfloat16).reshape(tok_rows, HEADS, HDIM)
        key_proj = plain_dot(normed, w_key).astype(jnp.bfloat16).reshape(tok_rows, KV, HDIM)
        value_proj = plain_dot(normed, w_value).astype(jnp.bfloat16).reshape(tok_rows, KV, HDIM)
        packed = jnp.concatenate(
            [
                query_proj,
                jnp.repeat(key_proj, group_size, axis=1),
                jnp.repeat(value_proj, group_size, axis=1),
            ],
            axis=2,
        )
        head_side = lax.all_to_all(packed, "sp", split_axis=1, concat_axis=0, tiled=True)
        cosine, sine = rope_tables(position, HDIM)
        query_rot = apply_rope(head_side[:, :, :HDIM].astype(jnp.float32), cosine, sine).astype(
            jnp.bfloat16
        )
        key_rot = apply_rope(
            head_side[:, :, HDIM : 2 * HDIM].astype(jnp.float32), cosine, sine
        ).astype(jnp.bfloat16)
        value_heads = head_side[:, :, 2 * HDIM :]
        attended, log_totals = attend_forward(query_rot, key_rot, value_heads, segment)
        token_side = lax.all_to_all(
            attended.astype(jnp.bfloat16), "sp", split_axis=0, concat_axis=1, tiled=True
        )
        attn_rows = token_side.reshape(tok_rows, D)
        middle = inputs + plain_dot(attn_rows, w_output)
        scale_two = rms_scale(middle)
        normed_two = (middle * scale_two * gain_two).astype(jnp.bfloat16)
        gate_proj = plain_dot(normed_two, w_gate)
        up_proj = plain_dot(normed_two, w_up)
        gate_sig = jax.nn.sigmoid(gate_proj)
        hidden = (gate_proj * gate_sig * up_proj).astype(jnp.bfloat16)
        outputs.append(middle + contract_cols(hidden, w_down))
        upstream = cotangent[micro_step].astype(jnp.float32) * valid_rows[:, None]
        upstream_low = upstream.astype(jnp.bfloat16)
        hidden_grad = plain_dot(upstream_low, w_down)
        up_low = (hidden_grad * gate_proj * gate_sig).astype(jnp.bfloat16)
        gate_low = (hidden_grad * up_proj * gate_sig * (1.0 + gate_proj * (1.0 - gate_sig))).astype(
            jnp.bfloat16
        )
        normed_two_grad = contract_cols(gate_low, w_gate) + contract_cols(up_low, w_up)
        middle_grad, gain_two_term = norm_back(middle, scale_two, gain_two, normed_two_grad)
        middle_grad = middle_grad + upstream
        middle_low = middle_grad.astype(jnp.bfloat16)
        attn_grad = (
            contract_cols(middle_low, w_output).astype(jnp.bfloat16).reshape(tok_rows, HEADS, HDIM)
        )
        grad_heads = lax.all_to_all(attn_grad, "sp", split_axis=1, concat_axis=0, tiled=True)
        query_part, key_acc, value_acc = attend_backward(
            query_rot, key_rot, value_heads, grad_heads, log_totals, segment
        )
        packed_grad = jnp.concatenate(
            [rope_back(query_part, cosine, sine), rope_back(key_acc, cosine, sine), value_acc],
            axis=2,
        )
        grad_tokens = lax.all_to_all(packed_grad, "sp", split_axis=0, concat_axis=1, tiled=True)
        query_low = grad_tokens[:, :, :HDIM].reshape(tok_rows, D).astype(jnp.bfloat16)
        key_low = (
            grad_tokens[:, :, HDIM : 2 * HDIM]
            .reshape(tok_rows, KV, group_size, HDIM)
            .sum(axis=2)
            .reshape(tok_rows, KV * HDIM)
            .astype(jnp.bfloat16)
        )
        value_low = (
            grad_tokens[:, :, 2 * HDIM :]
            .reshape(tok_rows, KV, group_size, HDIM)
            .sum(axis=2)
            .reshape(tok_rows, KV * HDIM)
            .astype(jnp.bfloat16)
        )
        normed_grad = (
            contract_cols(query_low, w_query)
            + contract_cols(key_low, w_key)
            + contract_cols(value_low, w_value)
        )
        inputs_grad, gain_one_term = norm_back(inputs, scale_one, gain_one, normed_grad)
        input_grads.append(inputs_grad + middle_grad)
        gain_sum = gain_sum + jnp.stack([gain_one_term, gain_two_term])
        kept.append(
            (
                normed,
                query_low,
                key_low,
                value_low,
                attn_rows,
                middle_low,
                normed_two,
                gate_low,
                up_low,
                upstream_low,
                hidden,
            )
        )
        grad_shards = None
    grad_shards = lax.psum_scatter(
        weight_terms(kept), ("fsdp", "sp"), scatter_dimension=0, tiled=True
    )
    gain_shards = lax.psum_scatter(gain_sum, ("fsdp", "sp"), scatter_dimension=1, tiled=True)
    kv_width = KV * HDIM
    edges = [
        0,
        D,
        D + kv_width,
        D + 2 * kv_width,
        2 * D + 2 * kv_width,
        2 * D + 2 * kv_width + FF,
        2 * D + 2 * kv_width + 2 * FF,
        2 * D + 2 * kv_width + 3 * FF,
    ]
    pieces = [grad_shards[:, edges[slot] : edges[slot + 1]] for slot in range(7)]
    return (
        jnp.stack(outputs),
        jnp.stack(input_grads),
        gain_shards[0],
        pieces[0],
        pieces[1],
        pieces[2],
        pieces[3],
        gain_shards[1],
        pieces[4],
        pieces[5],
        pieces[6],
    )


def mesh_place(n_sp):
    shard = lax.axis_index("fsdp")
    rank = lax.axis_index("sp")
    group = n_sp // MB
    chip, core = shard // 2, shard % 2
    micro, member = rank // group, rank % group
    high, low = member // 2, member % 2
    base = micro * group
    peers = (
        (shard, base + high * 2 + (1 - low)),
        (shard, base + (1 - high) * 2 + low),
        (shard, base + (1 - high) * 2 + (1 - low)),
    )
    members = (high * 2 + (1 - low), (1 - high) * 2 + low, (1 - high) * 2 + (1 - low))
    partner = (shard, (1 - micro) * group + member)
    core_mate = (chip * 2 + (1 - core), rank)
    chip_mate = ((1 - chip) * 2 + core, rank)
    far_mate = ((1 - chip) * 2 + (1 - core), rank)
    return shard, rank, micro, member, peers, members, partner, core_mate, chip_mate, far_mate


def greet(devices):
    barrier = pltpu.get_barrier_semaphore()
    for device in devices:
        pl.semaphore_signal(barrier, inc=1, device_id=device, device_id_type=MESH)
    pl.semaphore_wait(barrier, len(devices))


def lane_ids(shape):
    return lax.broadcasted_iota(jnp.int32, shape, len(shape) - 1)


def turn(vectors):
    width = vectors.shape[-1]
    ahead = pltpu.roll(vectors, width - HDIM // 2, 1)
    behind = pltpu.roll(vectors, HDIM // 2, 1)
    first = lane_ids(vectors.shape) % HDIM < HDIM // 2
    return jnp.where(first, -ahead, behind)


def turn_back(vectors):
    return -turn(vectors)


def softmax_columns(key_side, query_pair, bias):
    scores = contract_cols(key_side, query_pair) + bias.astype(jnp.float32)
    weights_exp = jnp.exp(scores - jnp.max(scores, axis=0, keepdims=True))
    return weights_exp * (1.0 / jnp.sum(weights_exp, axis=0, keepdims=True))


def row_places(shape, dim, group, tok_rows):
    ids = lax.broadcasted_iota(jnp.int32, shape, dim)
    own_rows = MB * tok_rows
    return ((ids % own_rows) // tok_rows) * (group * tok_rows) + (ids // own_rows) * tok_rows + ids % tok_rows


def row_positions(window, dim, group, tok_rows, first_len, both_len):
    shape = (window, 1) if dim == 0 else (1, window)
    place = row_places(shape, dim, group, tok_rows)
    anchor = jnp.where(place < first_len, 0, jnp.where(place < both_len, first_len, both_len))
    return place, place - anchor


def pair_bias(window, group, tok_rows, first_len, both_len):
    place, position = row_positions(window, 1, group, tok_rows, first_len, both_len)
    key_place = row_places((window, 1), 0, group, tok_rows)
    return jnp.where((key_place <= place) & (key_place >= place - position), 0.0, -1e30)


def layer_kernel(
    n_sp,
    tokens,
    cotangent,
    seq_len,
    slot_order,
    norm1_gain,
    norm2_gain,
    inverse,
    key_in,
    value_in,
    wq_in,
    wo_in,
    wg_in,
    wu_in,
    wd_in,
    block_out,
    input_grad,
    ffn_grad,
    qkv_grad,
    out_grad,
    gain_sum,
    from_core,
    from_chip,
    from_half,
    out_core,
    out_chip,
    out_half,
    wf,
    wq,
    wkv,
    wo,
    wkv_in,
    gains,
    gains_all,
    cosine,
    sine,
    bias,
    xs,
    gs,
    normed,
    upstream,
    normed_two,
    query_rot,
    keys,
    values,
    attended,
    d_attended,
    d_query,
    d_pair,
    key_sum,
    value_sum,
    middle,
    own_rest,
    own_block,
    hid,
    sent,
    sent_block,
    got,
    got_block,
    got_one,
    d_full,
    rows_out,
    rows_got,
    late_chip,
    late_half,
    gain_part,
    gain_got,
    local_sem,
    send_sem,
    recv_sem,
):
    place = mesh_place(n_sp)
    shard, rank, micro, member, peers, members, partner, core_mate, chip_mate, far_mate = place
    chip, core = shard // 2, shard % 2
    group = n_sp // MB
    tok_rows = tokens.shape[1]
    own_rows = MB * tok_rows
    window = group * own_rows
    depth = D // KV
    width_q, width_f = wq.shape[1], wf.shape[2]
    width_l = width_q + 2 * HDIM
    half_rows = group * tok_rows
    others = tuple((shard, (1 - micro) * group + t) for t in members)
    greet((*peers, partner, *others, core_mate, chip_mate, far_mate))

    def copy_to(index, source, target, device):
        return pltpu.make_async_remote_copy(
            src_ref=source,
            dst_ref=target,
            send_sem=send_sem.at[index],
            recv_sem=recv_sem.at[index],
            device_id=device,
            device_id_type=MESH,
        )

    def send(index, source, target, device):
        copy = copy_to(index, source, target, device)
        copy.start()
        return copy

    def move(index, source, target):
        copy = pltpu.make_async_copy(source, target, local_sem.at[index])
        copy.start()
        return copy

    def row_span(first, size):
        return pl.ds(pl.multiple_of(first, tok_rows), size)

    def lane_span(first, size):
        return pl.ds(pl.multiple_of(first, 128), size)

    swap_x = send(0, tokens.at[1 - micro], xs.at[micro], partner)
    own_half = pl.ds(pl.multiple_of(micro * tok_rows, tok_rows), tok_rows)
    swap_g = send(1, cotangent.at[1 - micro], gs.at[own_half], partner)
    own_x = move(0, tokens.at[micro], xs.at[micro])
    own_g = move(1, cotangent.at[micro], gs.at[own_half])
    gains[0:1, :] = norm1_gain[...].astype(jnp.float32)
    gains[1:2, :] = norm2_gain[...].astype(jnp.float32)
    gain_sends = [
        send(2 + i, gains, gains_all.at[shard], device) for i, device in enumerate((core_mate, chip_mate, far_mate))
    ]
    own_gain = move(2, gains, gains_all.at[shard])

    own_pair = lane_span(member // 2 * 128, 128)
    key_pair = key_in[:, own_pair].astype(jnp.float32)
    value_pair = value_in[:, own_pair].astype(jnp.float32)
    key_pair = jnp.where(member % 2 == 0, key_pair, pltpu.roll(key_pair, HDIM, 1))
    value_pair = jnp.where(member % 2 == 0, pltpu.roll(value_pair, HDIM, 1), value_pair)
    wkv_in[...] = jnp.where(lane_ids(key_pair.shape) < HDIM, key_pair, value_pair).astype(jnp.bfloat16)

    chip_shard = (1 - chip) * 2 + core
    own_ffn = lane_span(member * width_f, width_f)
    parts = (
        (wq_in.at[:, lane_span(member * width_q, width_q)], wq),
        (wkv_in, wkv),
        (wd_in.at[:, own_ffn], wf.at[0]),
        (wg_in.at[:, own_ffn], wf.at[1]),
        (wu_in.at[:, own_ffn], wf.at[2]),
    )

    def weight_out(i):
        source, target = parts[i]
        rows = row_span(shard * depth, depth)
        over_chip = send(5 + 3 * i, source, target.at[rows], chip_mate)
        over_core = send(6 + 3 * i, source, target.at[rows], core_mate)
        here = move(3 + i, source, target.at[rows])
        return over_chip, over_core, here

    def weight_on(i):
        rows = parts[i][1].at[row_span(chip_shard * depth, depth)]
        return send(7 + 3 * i, rows, rows, core_mate)

    started = {i: weight_out(i) for i in (0, 1)}
    same_chip, same_core = chip == member // 2, core == member % 2
    wo_over_chip = copy_to(20, wo_in, wo, chip_mate)
    wo_over_core = copy_to(21, wo_in, wo, core_mate)
    wo_on = copy_to(22, wo, wo, core_mate)
    wo_here = pltpu.make_async_copy(wo_in, wo, local_sem.at[8])

    @pl.when(same_chip & same_core)
    def _():
        wo_over_chip.start()
        wo_over_core.start()
        wo_here.start()

    for i in (2, 3, 4):
        started[i] = weight_out(i)

    first_len = seq_len[slot_order[2 * (shard * MB + micro)]]
    both_len = first_len + seq_len[slot_order[2 * (shard * MB + micro) + 1]]
    angles = row_positions(window, 0, group, tok_rows, first_len, both_len)[1].astype(jnp.float32) * inverse[...]
    cosine[...] = jnp.cos(angles)
    sine[...] = jnp.sin(angles)
    bias[...] = pair_bias(window, group, tok_rows, first_len, both_len).astype(jnp.bfloat16)

    own_gain.wait()
    for copy in gain_sends:
        copy.wait()
    gain_one = jnp.concatenate([gains_all[f, 0:1, :] for f in range(KV)], axis=1)
    gain_two = jnp.concatenate([gains_all[f, 1:2, :] for f in range(KV)], axis=1)
    own_x.wait()
    swap_x.wait()
    inputs = xs[...].reshape(own_rows, D).astype(jnp.float32)
    normed[member] = (inputs * rms_scale(inputs) * gain_one).astype(jnp.bfloat16)
    gather = [send(23 + i, normed.at[member], normed.at[member], device) for i, device in enumerate(peers)]

    own_g.wait()
    swap_g.wait()
    ids = lax.broadcasted_iota(jnp.int32, (own_rows, 1), 0)
    own_place = (ids // tok_rows) * (group * tok_rows) + member * tok_rows + ids % tok_rows
    valid = jnp.where(own_place < both_len, 1.0, 0.0)
    upstream[member] = (gs[...].astype(jnp.float32) * valid).astype(jnp.bfloat16)

    on = []
    for i in (0, 1):
        started[i][0].wait()
        on.append(weight_on(i))
    for i in (0, 1):
        started[i][1].wait()
        started[i][2].wait()
    for copy in on:
        copy.wait()

    def project(rows):
        block = normed[rows]
        place_rows = row_span(rows * own_rows, own_rows)
        query = plain_dot(block, wq[...])
        pair = plain_dot(block, wkv[...])
        cos, sin = cosine[place_rows, :], sine[place_rows, :]
        for j in range(width_q // 128):
            lanes = slice(j * 128, (j + 1) * 128)
            head = query[:, lanes].astype(jnp.bfloat16).astype(jnp.float32)
            head = (head * cos + turn(head) * sin).astype(jnp.bfloat16)
            query_rot[place_rows, lanes] = head * HDIM**-0.5
        pair = pair.astype(jnp.bfloat16).astype(jnp.float32)
        turned_key = pair * cos + turn(pair) * sin
        lower = lane_ids(pair.shape) < HDIM
        keys[place_rows, :] = jnp.where(lower, turned_key, pltpu.roll(turned_key, HDIM, 1)).astype(jnp.bfloat16)
        values[place_rows, :] = jnp.where(lower, pltpu.roll(pair, HDIM, 1), pair).astype(jnp.bfloat16)

    project(member)
    for i, copy in enumerate(gather):
        copy.wait()
        project(members[i])
    gather_g = [send(26 + i, upstream.at[member], upstream.at[member], device) for i, device in enumerate(peers)]

    key_twice, value_twice = keys[...], values[...]
    lower = lane_ids(key_twice.shape) < HDIM
    zero = jnp.zeros_like(key_twice)
    key_low, key_high = jnp.where(lower, key_twice, zero), jnp.where(lower, zero, key_twice)
    value_low, value_high = jnp.where(lower, value_twice, zero), jnp.where(lower, zero, value_twice)
    value_low_turned, value_high_turned = value_low.T, value_high.T

    @pl.loop(0, width_q // 128)
    def _(j):
        lanes = lane_span(j * 128, 128)
        pair = query_rot[:, lanes]
        total = plain_dot(value_low_turned, softmax_columns(key_low, pair, bias[...]).astype(jnp.bfloat16))
        total += plain_dot(value_high_turned, softmax_columns(key_high, pair, bias[...]).astype(jnp.bfloat16))
        attended[:, lanes] = total.T.astype(jnp.bfloat16)

    @pl.when(same_chip & same_core)
    def _():
        wo_over_chip.wait_send()
        wo_over_core.wait_send()
        wo_here.wait()

    @pl.when(jnp.logical_not(same_chip) & same_core)
    def _():
        wo_over_chip.wait_recv()
        wo_on.start()
        wo_on.wait_send()

    @pl.when(same_chip & jnp.logical_not(same_core))
    def _():
        wo_over_core.wait_recv()

    @pl.when(jnp.logical_not(same_chip) & jnp.logical_not(same_core))
    def _():
        wo_on.wait_recv()

    def project_out(rows):
        return plain_dot(attended[row_span(rows * own_rows, own_rows), :], wo[...])

    on = []

    def pass_on(i):
        started[i][0].wait()
        on.append(weight_on(i))

    sums = {}
    for i in (2, 0, 1):
        sent[i] = project_out(members[i]).astype(jnp.bfloat16)
        sums[i] = send(29 + i, sent.at[i], got.at[i], peers[i])
    total = inputs + project_out(member)
    pass_on(2)
    for i in (0, 1, 2):
        sums[i].wait()
        total += got[i].astype(jnp.float32)
    middle[...] = total
    normed_two[member] = (total * rms_scale(total) * gain_two).astype(jnp.bfloat16)
    gather_two = [
        send(32 + i, normed_two.at[member], normed_two.at[member], device) for i, device in enumerate(peers)
    ]
    for i in (3, 4):
        pass_on(i)
    for i in (2, 3, 4):
        started[i][1].wait()
        started[i][2].wait()
    for copy in (*on, *gather_g, *gather_two):
        copy.wait()

    @pl.loop(0, group)
    def _(r):
        place_rows = row_span(r * own_rows, own_rows)
        gate = plain_dot(normed_two[r], wf[1])
        up = plain_dot(normed_two[r], wf[2])
        d_hidden = plain_dot(upstream[r], wf[0])
        sig = jax.nn.sigmoid(gate)
        silu = gate * sig
        hid[0, place_rows, :] = (silu * up).astype(jnp.bfloat16)
        hid[1, place_rows, :] = (d_hidden * up * sig * (1.0 + gate * (1.0 - sig))).astype(jnp.bfloat16)
        hid[2, place_rows, :] = (d_hidden * silu).astype(jnp.bfloat16)

    def rows_to_y(index, rows_of, k, held, landing):
        owner, place = ((members[2], 2), (members[0], 0))[k]
        held[k] = rows_of(owner).astype(jnp.bfloat16)
        return send(index, held.at[k], landing.at[place], peers[0])

    def sum_over_z(index, over, held, landing):
        over.wait()
        held[2] = (held[2].astype(jnp.float32) + landing[2].astype(jnp.float32)).astype(jnp.bfloat16)
        return send(index, held.at[2], landing.at[1], peers[1])

    def sum_of(rows, over_y, over_z, landing):
        over_y.wait()
        over_z.wait()
        return rows + landing[0].astype(jnp.float32) + landing[1].astype(jnp.float32)

    def hid_rows(k, rows):
        return hid[k, row_span(rows * own_rows, own_rows), :]

    base = 35
    two_rows = lambda rows: contract_cols(hid_rows(1, rows), wf[1]) + contract_cols(hid_rows(2, rows), wf[2])
    two_over = rows_to_y(base + 27, two_rows, 0, sent, got)
    two_y = rows_to_y(base + 28, two_rows, 1, sent, got)
    block_rows = lambda rows: contract_cols(hid_rows(0, rows), wf[0])
    for k, rows in enumerate((members[2], members[0], members[1])):
        sent_block[k] = block_rows(rows).astype(jnp.bfloat16)
    own_block[...] = (middle[...] + block_rows(member)).reshape(MB, tok_rows, D)

    def weight_part(w, f):
        rows = lane_span(f * depth, depth)
        acts = (upstream if w == 0 else normed_two)[:, :, rows].reshape(window, depth)
        wf[w, rows, :] = contract_rows(acts, hid[w]).astype(jnp.bfloat16)

    core_copies, chip_copies, half_copies, last_copies, here_copies = {}, {}, {}, [], []

    def core_send(w, k):
        x = 1 - chip if k == 0 else chip
        rows = row_span((x * 2 + 1 - core) * depth, depth)
        core_copies[w, k] = send(base + 3 + 2 * w + k, wf.at[w, rows], from_core.at[w, x], core_mate)

    def far_parts(w):
        weight_part(w, (1 - chip) * 2 + 1 - core)
        core_send(w, 0)
        weight_part(w, (1 - chip) * 2 + core)

    def near_parts(w):
        weight_part(w, chip * 2 + 1 - core)
        core_send(w, 1)
        weight_part(w, chip * 2 + core)

    def all_parts(w):
        for f in range(KV):
            weight_part(w, f)
        core_send(w, 0)
        core_send(w, 1)

    def slot(x, c, m):
        return (x * 2 + c) * depth + m * half_rows

    def stage_in(index, source, w, first):
        return move(index, source, wf.at[w, row_span(first, half_rows)])

    def add_up(w, first, stages):
        @pl.loop(0, group)
        def _(t):
            total = wf[w, row_span(first + t * tok_rows, tok_rows), :].astype(jnp.float32)
            for stage in stages:
                total += wf[w, row_span(stage + t * tok_rows, tok_rows), :].astype(jnp.float32)
            wf[w, row_span(first + t * tok_rows, tok_rows), :] = total.astype(jnp.bfloat16)

    def core_rows(w, x, m):
        return from_core.at[w, x, row_span(m * half_rows, half_rows)]

    def chip_unit(w, m, index):
        if index == 0:
            core_copies[w, 0].wait()
        first, stage = slot(1 - chip, core, m), slot(1 - chip, 1 - core, m)
        stage_in(9, core_rows(w, 1 - chip, m), w, stage).wait()
        add_up(w, first, (stage,))
        chip_copies[w, index] = send(
            base + 9 + 2 * w + index, wf.at[w, row_span(first, half_rows)], from_chip.at[w, m], chip_mate
        )

    def half_unit(w):
        m = 1 - micro
        first, stage, other = slot(chip, core, m), slot(chip, 1 - core, m), slot(1 - chip, 1 - core, m)
        core_copies[w, 1].wait()
        load = stage_in(9, core_rows(w, chip, m), w, stage)
        chip_copies[w, 0].wait()
        stage_in(10, from_chip.at[w, m], w, other).wait()
        load.wait()
        add_up(w, first, (stage, other))
        half_copies[w] = send(base + 15 + w, wf.at[w, row_span(first, half_rows)], from_half.at[w], partner)

    def last_unit(w):
        first, stage, other = slot(chip, core, micro), slot(chip, 1 - core, micro), slot(1 - chip, 1 - core, micro)
        third = slot(chip, 1 - core, 1 - micro)
        load = stage_in(9, core_rows(w, chip, micro), w, stage)
        chip_copies[w, 1].wait()
        over = stage_in(10, from_chip.at[w, micro], w, other)
        half_copies[w].wait()
        stage_in(11, from_half.at[w], w, third).wait()
        load.wait()
        over.wait()
        add_up(w, first, (stage, other, third))
        for i in range(group - 1):
            source = wf.at[w, row_span(first + members[i] * tok_rows, tok_rows)]
            last_copies.append(send(base + 18 + 3 * w + i, source, ffn_grad.at[w, :, own_ffn], peers[i]))
        source = wf.at[w, row_span(first + member * tok_rows, tok_rows)]
        here_copies.append(move(12 + w, source, ffn_grad.at[w, :, own_ffn]))

    far_parts(0)
    sent[2] = two_rows(members[1]).astype(jnp.bfloat16)
    two_z = sum_over_z(base + 29, two_over, sent, got)
    chip_unit(0, 1 - micro, 0)
    near_parts(0)
    own_rest[...] = two_rows(member).reshape(MB, tok_rows, D)
    far_parts(1)

    middle_rows = middle[...]
    grad, two_term = norm_back(middle_rows, rms_scale(middle_rows), gain_two, sum_of(own_rest[...].reshape(own_rows, D), two_y, two_z, got))
    grad += upstream[member].astype(jnp.float32)
    middle[...] = grad
    d_full[member] = grad.astype(jnp.bfloat16)
    to_z = send(base + 32, d_full.at[member], d_full.at[member], peers[1])
    to_y = send(base + 33, d_full.at[member], d_full.at[member], peers[0])
    near_parts(1)
    half_unit(0)
    chip_unit(1, 1 - micro, 0)
    all_parts(2)

    def give(k, rows, kept):
        rows_out[k] = jnp.where(micro == 0, rows[tok_rows:], rows[:tok_rows]).astype(jnp.bfloat16)
        kept[micro] = jnp.where(micro == 0, rows[:tok_rows], rows[tok_rows:])
        return send(base + 30 + k, rows_out.at[k], rows_got.at[k], partner)

    def take(k, copy, kept, target):
        copy.wait()
        kept[1 - micro] = rows_got[k].astype(jnp.float32)
        here_copies.append(move(18 + k, kept, target))

    def attention_grad(rows):
        place_rows = row_span(rows * own_rows, own_rows)
        d_attended[place_rows, :] = contract_cols(d_full[rows], wo[...]).astype(jnp.bfloat16)

    to_z.wait()
    on_y = send(base + 34, d_full.at[members[1]], d_full.at[members[1]], peers[0])
    block_over = send(base, sent_block.at[0], got_block.at[2], peers[0])
    block_y = send(base + 1, sent_block.at[1], got_block.at[0], peers[0])
    attention_grad(member)
    attention_grad(members[1])
    to_y.wait()
    attention_grad(members[0])
    chip_unit(2, 1 - micro, 0)
    on_y.wait()
    attention_grad(members[2])
    half_unit(1)

    out_part = normed_two
    d_rows = d_full[...].reshape(window, D)
    for j in range(group):
        out_part[j] = contract_rows(attended[:, j * 128 : (j + 1) * 128], d_rows).astype(jnp.bfloat16)
    out_by_core = copy_to(base + 35, out_part, out_core, core_mate)
    out_by_chip = copy_to(base + 36, out_part, out_chip, chip_mate)
    half_blocks = group // MB
    out_by_half = copy_to(base + 37, out_part.at[pl.ds((1 - micro) * half_blocks, half_blocks)], out_half, partner)

    def add_blocks(landed, first, count):
        for j in range(count):
            move(15, landed.at[j], gs).wait()
            out_part[first + j] = (
                out_part[first + j].astype(jnp.float32) + gs[...].astype(jnp.float32)
            ).astype(jnp.bfloat16)

    @pl.when(jnp.logical_not(same_core))
    def _():
        out_by_core.start()

    for w in (0, 1):
        chip_unit(w, micro, 1)

    key_low_turned, key_high_turned = key_low.T, key_high.T
    key_sum[...] = jnp.zeros_like(key_sum)
    value_sum[...] = jnp.zeros_like(value_sum)

    @pl.loop(0, width_q // 128)
    def _(j):
        lanes = lane_span(j * 128, 128)
        query_pair, grad_pair = query_rot[:, lanes], d_attended[:, lanes]
        total = jnp.zeros((2 * HDIM, window), jnp.float32)
        for side, (key_side, value_side, key_turned) in enumerate(
            ((key_low, value_low, key_low_turned), (key_high, value_high, key_high_turned))
        ):
            probs = softmax_columns(key_side, query_pair, bias[...])
            d_probs = contract_cols(value_side, grad_pair)
            inner = jnp.sum(probs * d_probs, axis=0, keepdims=True)
            d_scores = (probs * (d_probs - inner)).astype(jnp.bfloat16)
            total += plain_dot(key_turned, d_scores)
            key_sum[side] += plain_dot(d_scores, query_pair)
            value_sum[side] += plain_dot(probs.astype(jnp.bfloat16), grad_pair)
        grad_rot = total.T * HDIM**-0.5
        d_query[:, lanes] = (grad_rot * cosine[...] + turn_back(grad_rot * sine[...])).astype(jnp.bfloat16)

    fold = lambda sums: jnp.where(lower, sums[0] + pltpu.roll(sums[1], HDIM, 1), 0.0)
    key_grad, value_grad = fold(key_sum), fold(value_sum)
    key_grad = key_grad * cosine[...] + turn_back(key_grad * sine[...])
    d_pair[...] = jnp.where(lower, key_grad, pltpu.roll(value_grad, HDIM, 1)).astype(jnp.bfloat16)

    def one_rows(rows):
        place_rows = row_span(rows * own_rows, own_rows)
        return contract_cols(d_query[place_rows, :], wq[...]) + contract_cols(d_pair[place_rows, :], wkv[...])

    one_over = rows_to_y(base + 38, one_rows, 0, sent, got_one)
    one_y = rows_to_y(base + 39, one_rows, 1, sent, got_one)
    sent[2] = one_rows(members[1]).astype(jnp.bfloat16)
    own_rest[...] = one_rows(member).reshape(MB, tok_rows, D)
    half_unit(2)

    @pl.when(jnp.logical_not(same_core))
    def _():
        out_by_core.wait_send()

    @pl.when(same_core)
    def _():
        out_by_core.wait_recv()
        add_blocks(out_core, 0, group)

    @pl.when(same_core & jnp.logical_not(same_chip))
    def _():
        out_by_chip.start()

    d_all = jnp.concatenate([d_query[...], d_pair[...]], axis=1)

    def late_lanes(c):
        return lane_span(c * width_l, width_l)

    def late_part(x, c):
        for m in range(MB):
            columns = lane_span(((x * 2 + c) * MB + m) * half_rows, half_rows)
            rows = normed[:, :, columns].reshape(window, half_rows)
            hid[x, m * half_rows : (m + 1) * half_rows, late_lanes(c)] = contract_rows(rows, d_all).astype(jnp.bfloat16)

    late_core_copies = []
    for x in range(2):
        late_part(x, 1 - core)
        late_core_copies.append(
            send(base + 41 + x, hid.at[x, :, late_lanes(1 - core)], hid.at[2, :, late_lanes(x)], core_mate)
        )
    for x in range(2):
        late_part(x, core)
    for copy in late_core_copies:
        copy.wait()

    def late_add(x, first, count, landed):
        @pl.loop(0, count)
        def _(t):
            rows = row_span(first + t * tok_rows, tok_rows)
            total = hid[x, rows, late_lanes(core)].astype(jnp.float32) + hid[2, rows, late_lanes(x)].astype(jnp.float32)
            for ref, start in landed:
                total += ref[row_span(start + t * tok_rows, tok_rows), :].astype(jnp.float32)
            hid[x, rows, late_lanes(core)] = total.astype(jnp.bfloat16)

    late_add(1 - chip, 0, MB * group, ())
    late_to_chip = send(base + 43, hid.at[1 - chip, :, late_lanes(core)], late_chip, chip_mate)
    block_z = sum_over_z(base + 2, block_over, sent_block, got_block)
    one_z = sum_over_z(base + 40, one_over, sent, got_one)
    chip_unit(2, micro, 1)
    block = sum_of(own_block[...].reshape(own_rows, D), block_y, block_z, got_block)
    give_block = give(0, block, own_block)

    @pl.when(same_core & jnp.logical_not(same_chip))
    def _():
        out_by_chip.wait_send()

    @pl.when(same_core & same_chip)
    def _():
        out_by_chip.wait_recv()
        add_blocks(out_chip, 0, group)
        out_by_half.start()

    last_unit(0)
    late_to_chip.wait()
    late_add(chip, (1 - micro) * half_rows, group, ((late_chip, (1 - micro) * half_rows),))
    late_to_half = send(
        base + 46, hid.at[chip, row_span((1 - micro) * half_rows, half_rows), late_lanes(core)], late_half, partner
    )

    inputs = xs[...].reshape(own_rows, D).astype(jnp.float32)
    grad, one_term = norm_back(
        inputs, rms_scale(inputs), gain_one, sum_of(own_rest[...].reshape(own_rows, D), one_y, one_z, got_one)
    )
    give_grad = give(1, grad + middle[...], own_rest)

    for k, term in enumerate((one_term[None], two_term[None])):
        for f in range(KV):
            gain_part[k * KV + f : k * KV + f + 1, :] = term[:, f * depth : (f + 1) * depth]
    gain_first = [
        send(base + 57 + i, gain_part, gain_got.at[i], device)
        for i, device in enumerate((core_mate, chip_mate, far_mate))
    ]
    last_unit(1)
    for copy in gain_first:
        copy.wait()
    gain_part[...] = gain_part[...] + gain_got[0] + gain_got[1] + gain_got[2]
    gain_second = [
        send(base + 60 + i, gain_part, gain_got.at[3 + i], device)
        for i, device in enumerate((*peers, partner, *others))
    ]
    take(0, give_block, own_block, block_out)
    last_unit(2)

    def out_block(t):
        return out_part.at[micro * half_blocks + t // 2, row_span(t % 2 * tok_rows, tok_rows)]

    out_here = pltpu.make_async_copy(out_block(member), out_grad, local_sem.at[16])

    def out_to(i):
        return pltpu.make_async_remote_copy(
            src_ref=out_block(members[i]),
            dst_ref=out_grad,
            send_sem=send_sem.at[base + 48 + i],
            recv_sem=recv_sem.at[base + 48],
            device_id=peers[i],
            device_id_type=MESH,
        )

    @pl.when(same_core & same_chip)
    def _():
        out_by_half.wait()
        add_blocks(out_half, micro * half_blocks, half_blocks)
        for i in range(group - 1):
            out_to(i).start()
        out_here.start()

    late_to_half.wait()
    late_add(chip, micro * half_rows, group, ((late_chip, micro * half_rows), (late_half, 0)))
    own_late = lane_span(member * width_l, width_l)

    def late_rows(t):
        return hid.at[chip, row_span(micro * half_rows + t * tok_rows, tok_rows), late_lanes(core)]

    for i in range(group - 1):
        last_copies.append(send(base + 54 + i, late_rows(members[i]), qkv_grad.at[:, own_late], peers[i]))
    here_copies.append(move(17, late_rows(member), qkv_grad.at[:, own_late]))
    take(1, give_grad, own_rest, input_grad)
    total = gain_part[...]
    for i, copy in enumerate(gain_second):
        copy.wait()
        total += gain_got[3 + i]
    gain_sum[...] = total

    @pl.when(same_core & same_chip)
    def _():
        for i in range(group - 1):
            out_to(i).wait_send()
        out_here.wait()

    @pl.when(jnp.logical_not(same_core & same_chip))
    def _():
        out_to(0).wait_recv()

    for copy in (*last_copies, *here_copies):
        copy.wait()


def whole_layer(n_sp, tok_rows, heads, *operands):
    group = n_sp // MB
    own_rows = MB * tok_rows
    window = group * own_rows
    half_rows = group * tok_rows
    width_q = heads * HDIM
    width_f = FF // group
    width_l = width_q + 2 * HDIM
    low, full = jnp.bfloat16, jnp.float32
    vmem = pl.BlockSpec(memory_space=pltpu.VMEM)
    anywhere = pl.BlockSpec(memory_space=pl.ANY)
    smem = pl.BlockSpec(memory_space=pltpu.SMEM)
    shape = jax.ShapeDtypeStruct
    blocks = (group, own_rows, D)
    trio = (group - 1, own_rows, D)
    pair = (MB, tok_rows, D)
    return pl.pallas_call(
        functools.partial(layer_kernel, n_sp),
        out_shape=(
            shape(pair, full),
            shape(pair, full),
            shape((3, tok_rows, FF), low),
            shape((tok_rows, group * width_l), low),
            shape((tok_rows, D), low),
            shape((2 * KV, D // KV), full),
            shape((3, 2, MB * half_rows, width_f), low),
            shape((3, MB, half_rows, width_f), low),
            shape((3, half_rows, width_f), low),
            shape(blocks, low),
            shape(blocks, low),
            shape((group // MB, own_rows, D), low),
        ),
        in_specs=[anywhere] * 2 + [smem] * 2 + [vmem] * 5 + [anywhere] * 5,
        out_specs=(anywhere,) * 5 + (vmem,) + (anywhere,) * 6,
        scratch_shapes=[
            pltpu.VMEM((3, D, width_f), low),
            pltpu.VMEM((D, width_q), low),
            pltpu.VMEM((D, 2 * HDIM), low),
            pltpu.VMEM((width_q, D), low),
            pltpu.VMEM((D // KV, 2 * HDIM), low),
            pltpu.VMEM((8, D // KV), full),
            pltpu.VMEM((KV, 8, D // KV), full),
            pltpu.VMEM((window, 2 * HDIM), full),
            pltpu.VMEM((window, 2 * HDIM), full),
            pltpu.VMEM((window, window), low),
            pltpu.VMEM(pair, low),
            pltpu.VMEM((own_rows, D), low),
            pltpu.VMEM(blocks, low),
            pltpu.VMEM(blocks, low),
            pltpu.VMEM(blocks, low),
            pltpu.VMEM((window, width_q), low),
            pltpu.VMEM((window, 2 * HDIM), low),
            pltpu.VMEM((window, 2 * HDIM), low),
            pltpu.VMEM((window, width_q), low),
            pltpu.VMEM((window, width_q), low),
            pltpu.VMEM((window, width_q), low),
            pltpu.VMEM((window, 2 * HDIM), low),
            pltpu.VMEM((2, window, 2 * HDIM), full),
            pltpu.VMEM((2, window, 2 * HDIM), full),
            pltpu.VMEM((own_rows, D), full),
            pltpu.VMEM(pair, full),
            pltpu.VMEM(pair, full),
            pltpu.VMEM((3, window, width_f), low),
            pltpu.VMEM(trio, low),
            pltpu.VMEM(trio, low),
            pltpu.VMEM(trio, low),
            pltpu.VMEM(trio, low),
            pltpu.VMEM(trio, low),
            pltpu.VMEM(blocks, low),
            pltpu.VMEM((2, tok_rows, D), low),
            pltpu.VMEM((2, tok_rows, D), low),
            pltpu.VMEM((MB * half_rows, width_l), low),
            pltpu.VMEM((half_rows, width_l), low),
            pltpu.VMEM((2 * KV, D // KV), full),
            pltpu.VMEM((10, 2 * KV, D // KV), full),
            pltpu.SemaphoreType.DMA((20,)),
            pltpu.SemaphoreType.DMA((102,)),
            pltpu.SemaphoreType.DMA((102,)),
        ],
        compiler_params=pltpu.CompilerParams(
            collective_id=0, has_side_effects=True, vmem_limit_bytes=VMEM_BYTES
        ),
        cost_estimate=pl.CostEstimate(flops=36 * 10**9, bytes_accessed=100 * 10**6, transcendentals=8 * 10**6),
        name="whole_layer",
    )(*operands)


def group_body(
    tokens,
    cotangent,
    seq_len,
    slot_order,
    norm1_gain,
    query_weight,
    key_weight,
    value_weight,
    output_weight,
    norm2_gain,
    gate_weight,
    up_weight,
    down_weight,
):
    n_sp = lax.axis_size("sp")
    n_fsdp = lax.axis_size("fsdp")
    group = n_sp // MB
    rank = lax.axis_index("sp")
    shard = lax.axis_index("fsdp")
    micro = rank // group
    member = rank % group
    tok_rows = tokens.shape[1]
    window = n_sp * tok_rows
    own_rows = MB * tok_rows
    inverse = np.float32(ROPE_BASE) ** (np.arange(HDIM // 2, dtype=np.float32) * np.float32(-2.0 / HDIM))
    heads = HEADS // group
    block, d_inputs, ffn_grad, qkv_grad, output_grad, gain_sum, *_ = whole_layer(
        n_sp, tok_rows, heads,
        tokens, cotangent, seq_len, slot_order, norm1_gain[None], norm2_gain[None],
        jnp.asarray(np.tile(inverse, 4)[None]), key_weight, value_weight,
        query_weight, output_weight, gate_weight, up_weight, down_weight,
    )
    gain_own = lax.dynamic_slice_in_dim(gain_sum.reshape(2, D), (shard * n_sp + rank) * tok_rows, tok_rows, 1)

    def part_of(first, width):
        pieces = qkv_grad.reshape(tok_rows, group, -1)[:, :, first : first + width]
        return pieces.reshape(tok_rows, group * width).astype(jnp.float32)

    width_q = heads * HDIM
    return (
        block,
        d_inputs,
        gain_own[0],
        part_of(0, width_q),
        part_of(width_q, HDIM),
        part_of(width_q + HDIM, HDIM),
        output_grad.astype(jnp.float32),
        gain_own[1],
        ffn_grad[1].astype(jnp.float32),
        ffn_grad[2].astype(jnp.float32),
        ffn_grad[0].astype(jnp.float32),
    )


def solution(mesh):
    fits = mesh.shape["fsdp"] == KV and mesh.shape["sp"] == MB * KV
    placed = (
        P(None, ("fsdp", "sp"), None),
        P(None, ("fsdp", "sp"), None),
        P(),
        P(),
        P("fsdp"),
        P("fsdp", None),
        P("fsdp", None),
        P("fsdp", None),
        P("fsdp", None),
        P("fsdp"),
        P("fsdp", None),
        P("fsdp", None),
        P("fsdp", None),
    )
    return jax.shard_map(
        group_body if fits else body,
        mesh=mesh,
        in_specs=placed,
        out_specs=(
            P(None, ("fsdp", "sp"), None),
            P(None, ("fsdp", "sp"), None),
            P(("fsdp", "sp")),
            P(("fsdp", "sp"), None),
            P(("fsdp", "sp"), None),
            P(("fsdp", "sp"), None),
            P(("fsdp", "sp"), None),
            P(("fsdp", "sp")),
            P(("fsdp", "sp"), None),
            P(("fsdp", "sp"), None),
            P(("fsdp", "sp"), None),
        ),
        check_vma=False,
    )
```

```python
import functools

import jax
import jax.numpy as jnp
import numpy as np
from jax import lax
from jax.experimental import pallas as pl
from jax.experimental.pallas import tpu as pltpu
from jax.sharding import PartitionSpec as P

D = 2048
HEADS = 32
KV = 4
HDIM = 64
FF = 5632
MB = 2
MESH = pl.DeviceIdType.MESH
VMEM_BYTES = 60 * 2**20


EPSILON = 1e-05
ROPE_BASE = 10000.0


def plain_dot(left_side, right_side):
    return jnp.dot(left_side, right_side, preferred_element_type=jnp.float32)


def contract_rows(left_side, right_side):
    return lax.dot_general(
        left_side, right_side, (((0,), (0,)), ((), ())), preferred_element_type=jnp.float32
    )


def contract_cols(left_side, right_side):
    return lax.dot_general(
        left_side, right_side, (((1,), (1,)), ((), ())), preferred_element_type=jnp.float32
    )


def window_layout(seq_len, slot_order, window_index, window):
    first_len = seq_len[slot_order[2 * window_index]]
    second_len = seq_len[slot_order[2 * window_index + 1]]
    places = jnp.arange(window, dtype=jnp.int32)
    segment = jnp.where(
        places < first_len, 0, jnp.where(places < first_len + second_len, 1, 2)
    ).astype(jnp.int32)
    anchor = jnp.where(segment == 0, 0, jnp.where(segment == 1, first_len, first_len + second_len))
    return (segment, places - anchor)


def rope_tables(position, head_size):
    half_size = head_size // 2
    inverse = ROPE_BASE ** (-2.0 * jnp.arange(half_size, dtype=jnp.float32) / head_size)
    angles = position.astype(jnp.float32)[:, None] * inverse[None, :]
    angles = jnp.concatenate([angles, angles], axis=1)
    return (jnp.cos(angles)[:, None, :], jnp.sin(angles)[:, None, :])


def apply_rope(vectors, cosine, sine):
    half_size = vectors.shape[-1] // 2
    turned = jnp.concatenate([-vectors[..., half_size:], vectors[..., :half_size]], axis=-1)
    return vectors * cosine + turned * sine


def rope_back(grad_in, cosine, sine):
    half_size = grad_in.shape[-1] // 2
    rotated = grad_in * sine
    return grad_in * cosine + jnp.concatenate(
        [rotated[..., half_size:], -rotated[..., :half_size]], axis=-1
    )


def rms_scale(inputs):
    return lax.rsqrt(jnp.mean(inputs * inputs, axis=-1, keepdims=True) + EPSILON)


def norm_back(inputs, scale_rows, gain_full, upstream):
    through = upstream * gain_full
    gain_term = jnp.sum(upstream * inputs * scale_rows, axis=0)
    grad_in = scale_rows * through - inputs * scale_rows**3 * jnp.mean(
        through * inputs, axis=-1, keepdims=True
    )
    return (grad_in, gain_term)


def score_block(query_block, key_rot, segment, row_start):
    block_rows = query_block.shape[0]
    places = jnp.arange(key_rot.shape[0], dtype=jnp.int32)
    row_place = row_start + jnp.arange(block_rows, dtype=jnp.int32)
    block_segment = lax.dynamic_slice_in_dim(segment, row_start, block_rows, 0)
    allowed = (block_segment[:, None] == segment[None, :]) & (places[None, :] <= row_place[:, None])
    raw_scores = jnp.einsum(
        "qhd,khd->hqk", query_block, key_rot, preferred_element_type=jnp.float32
    ) * query_block.shape[2] ** (-0.5)
    return jnp.where(allowed[None], raw_scores, -1e30)


def attend_forward(query_rot, key_rot, value_heads, segment):
    window = query_rot.shape[0]
    block_rows = min(512, window)

    def step(carry, block_index):
        row_start = block_index * block_rows
        query_block = lax.dynamic_slice_in_dim(query_rot, row_start, block_rows, 0)
        scores = score_block(query_block, key_rot, segment, row_start)
        row_top = jnp.max(scores, axis=-1, keepdims=True)
        weights_exp = jnp.exp(scores - row_top)
        row_total = jnp.sum(weights_exp, axis=-1, keepdims=True)
        probs = (weights_exp / row_total).astype(jnp.bfloat16)
        block_out = jnp.einsum(
            "hqk,khd->qhd", probs, value_heads, preferred_element_type=jnp.float32
        )
        log_total = (row_top + jnp.log(row_total))[:, :, 0].T
        return (carry, (block_out, log_total))

    block_ids = jnp.arange(window // block_rows, dtype=jnp.int32)
    _, (outputs, log_totals) = lax.scan(step, jnp.zeros((), jnp.int32), block_ids)
    return (outputs.reshape(query_rot.shape), log_totals.reshape(window, query_rot.shape[1]))


def attend_backward(query_rot, key_rot, value_heads, grad_heads, log_totals, segment):
    window = query_rot.shape[0]
    block_rows = min(512, window)
    scale_factor = query_rot.shape[2] ** (-0.5)

    def step(carry, block_index):
        key_acc, value_acc = carry
        row_start = block_index * block_rows
        query_block = lax.dynamic_slice_in_dim(query_rot, row_start, block_rows, 0)
        grad_block = lax.dynamic_slice_in_dim(grad_heads, row_start, block_rows, 0)
        total_block = lax.dynamic_slice_in_dim(log_totals, row_start, block_rows, 0)
        scores = score_block(query_block, key_rot, segment, row_start)
        probs = jnp.exp(scores - total_block.T[:, :, None])
        grad_probs = jnp.einsum(
            "qhd,khd->hqk", grad_block, value_heads, preferred_element_type=jnp.float32
        )
        inner_sum = jnp.sum(probs * grad_probs, axis=-1, keepdims=True)
        grad_scores = (probs * (grad_probs - inner_sum)).astype(jnp.bfloat16)
        query_part = (
            jnp.einsum("hqk,khd->qhd", grad_scores, key_rot, preferred_element_type=jnp.float32)
            * scale_factor
        )
        key_acc = (
            key_acc
            + jnp.einsum(
                "hqk,qhd->khd", grad_scores, query_block, preferred_element_type=jnp.float32
            )
            * scale_factor
        )
        value_acc = value_acc + jnp.einsum(
            "hqk,qhd->khd",
            probs.astype(jnp.bfloat16),
            grad_block,
            preferred_element_type=jnp.float32,
        )
        return ((key_acc, value_acc), query_part)

    start_acc = (jnp.zeros(key_rot.shape, jnp.float32), jnp.zeros(value_heads.shape, jnp.float32))
    block_ids = jnp.arange(window // block_rows, dtype=jnp.int32)
    (key_acc, value_acc), query_parts = lax.scan(step, start_acc, block_ids)
    return (query_parts.reshape(query_rot.shape), key_acc, value_acc)


def weight_terms(stored):
    joined = [jnp.concatenate(pieces, axis=0) for pieces in zip(*stored)]
    (
        normed,
        query_low,
        key_low,
        value_low,
        attn_rows,
        middle_low,
        normed_two,
        gate_low,
        up_low,
        upstream_low,
        hidden,
    ) = joined
    return jnp.concatenate(
        [
            contract_rows(normed, query_low),
            contract_rows(normed, key_low),
            contract_rows(normed, value_low),
            contract_rows(attn_rows, middle_low),
            contract_rows(normed_two, gate_low),
            contract_rows(normed_two, up_low),
            contract_rows(upstream_low, hidden),
        ],
        axis=1,
    )


def body(
    tokens,
    cotangent,
    seq_len,
    slot_order,
    norm1_gain,
    query_weight,
    key_weight,
    value_weight,
    output_weight,
    norm2_gain,
    gate_weight,
    up_weight,
    down_weight,
):
    seq_devices = lax.axis_size("sp")
    seq_rank = lax.axis_index("sp")
    shard_rank = lax.axis_index("fsdp")
    tok_rows = tokens.shape[1]
    window = seq_devices * tok_rows
    group_size = HEADS // KV
    kept = []
    outputs = []
    input_grads = []
    gain_sum = jnp.zeros((2, D), jnp.float32)
    grad_shards = None
    for micro_step in range(MB):
        gathered = (
            lax.all_gather(norm1_gain, "fsdp", axis=0, tiled=True),
            lax.all_gather(query_weight, "fsdp", axis=0, tiled=True),
            lax.all_gather(key_weight, "fsdp", axis=0, tiled=True),
            lax.all_gather(value_weight, "fsdp", axis=0, tiled=True),
            lax.all_gather(output_weight, "fsdp", axis=0, tiled=True),
            lax.all_gather(norm2_gain, "fsdp", axis=0, tiled=True),
            lax.all_gather(gate_weight, "fsdp", axis=0, tiled=True),
            lax.all_gather(up_weight, "fsdp", axis=0, tiled=True),
            lax.all_gather(down_weight, "fsdp", axis=0, tiled=True),
        )
        gain_one, w_query, w_key, w_value, w_output, gain_two, w_gate, w_up, w_down = gathered
        gain_one = gain_one.astype(jnp.float32)
        gain_two = gain_two.astype(jnp.float32)
        inputs = tokens[micro_step].astype(jnp.float32)
        window_index = shard_rank * MB + micro_step
        segment, position = window_layout(seq_len, slot_order, window_index, window)
        own_segment = lax.dynamic_slice_in_dim(segment, seq_rank * tok_rows, tok_rows, 0)
        valid_rows = (own_segment < 2).astype(jnp.float32)
        scale_one = rms_scale(inputs)
        normed = (inputs * scale_one * gain_one).astype(jnp.bfloat16)
        query_proj = plain_dot(normed, w_query).astype(jnp.bfloat16).reshape(tok_rows, HEADS, HDIM)
        key_proj = plain_dot(normed, w_key).astype(jnp.bfloat16).reshape(tok_rows, KV, HDIM)
        value_proj = plain_dot(normed, w_value).astype(jnp.bfloat16).reshape(tok_rows, KV, HDIM)
        packed = jnp.concatenate(
            [
                query_proj,
                jnp.repeat(key_proj, group_size, axis=1),
                jnp.repeat(value_proj, group_size, axis=1),
            ],
            axis=2,
        )
        head_side = lax.all_to_all(packed, "sp", split_axis=1, concat_axis=0, tiled=True)
        cosine, sine = rope_tables(position, HDIM)
        query_rot = apply_rope(head_side[:, :, :HDIM].astype(jnp.float32), cosine, sine).astype(
            jnp.bfloat16
        )
        key_rot = apply_rope(
            head_side[:, :, HDIM : 2 * HDIM].astype(jnp.float32), cosine, sine
        ).astype(jnp.bfloat16)
        value_heads = head_side[:, :, 2 * HDIM :]
        attended, log_totals = attend_forward(query_rot, key_rot, value_heads, segment)
        token_side = lax.all_to_all(
            attended.astype(jnp.bfloat16), "sp", split_axis=0, concat_axis=1, tiled=True
        )
        attn_rows = token_side.reshape(tok_rows, D)
        middle = inputs + plain_dot(attn_rows, w_output)
        scale_two = rms_scale(middle)
        normed_two = (middle * scale_two * gain_two).astype(jnp.bfloat16)
        gate_proj = plain_dot(normed_two, w_gate)
        up_proj = plain_dot(normed_two, w_up)
        gate_sig = jax.nn.sigmoid(gate_proj)
        hidden = (gate_proj * gate_sig * up_proj).astype(jnp.bfloat16)
        outputs.append(middle + contract_cols(hidden, w_down))
        upstream = cotangent[micro_step].astype(jnp.float32) * valid_rows[:, None]
        upstream_low = upstream.astype(jnp.bfloat16)
        hidden_grad = plain_dot(upstream_low, w_down)
        up_low = (hidden_grad * gate_proj * gate_sig).astype(jnp.bfloat16)
        gate_low = (hidden_grad * up_proj * gate_sig * (1.0 + gate_proj * (1.0 - gate_sig))).astype(
            jnp.bfloat16
        )
        normed_two_grad = contract_cols(gate_low, w_gate) + contract_cols(up_low, w_up)
        middle_grad, gain_two_term = norm_back(middle, scale_two, gain_two, normed_two_grad)
        middle_grad = middle_grad + upstream
        middle_low = middle_grad.astype(jnp.bfloat16)
        attn_grad = (
            contract_cols(middle_low, w_output).astype(jnp.bfloat16).reshape(tok_rows, HEADS, HDIM)
        )
        grad_heads = lax.all_to_all(attn_grad, "sp", split_axis=1, concat_axis=0, tiled=True)
        query_part, key_acc, value_acc = attend_backward(
            query_rot, key_rot, value_heads, grad_heads, log_totals, segment
        )
        packed_grad = jnp.concatenate(
            [rope_back(query_part, cosine, sine), rope_back(key_acc, cosine, sine), value_acc],
            axis=2,
        )
        grad_tokens = lax.all_to_all(packed_grad, "sp", split_axis=0, concat_axis=1, tiled=True)
        query_low = grad_tokens[:, :, :HDIM].reshape(tok_rows, D).astype(jnp.bfloat16)
        key_low = (
            grad_tokens[:, :, HDIM : 2 * HDIM]
            .reshape(tok_rows, KV, group_size, HDIM)
            .sum(axis=2)
            .reshape(tok_rows, KV * HDIM)
            .astype(jnp.bfloat16)
        )
        value_low = (
            grad_tokens[:, :, 2 * HDIM :]
            .reshape(tok_rows, KV, group_size, HDIM)
            .sum(axis=2)
            .reshape(tok_rows, KV * HDIM)
            .astype(jnp.bfloat16)
        )
        normed_grad = (
            contract_cols(query_low, w_query)
            + contract_cols(key_low, w_key)
            + contract_cols(value_low, w_value)
        )
        inputs_grad, gain_one_term = norm_back(inputs, scale_one, gain_one, normed_grad)
        input_grads.append(inputs_grad + middle_grad)
        gain_sum = gain_sum + jnp.stack([gain_one_term, gain_two_term])
        kept.append(
            (
                normed,
                query_low,
                key_low,
                value_low,
                attn_rows,
                middle_low,
                normed_two,
                gate_low,
                up_low,
                upstream_low,
                hidden,
            )
        )
        grad_shards = None
    grad_shards = lax.psum_scatter(
        weight_terms(kept), ("fsdp", "sp"), scatter_dimension=0, tiled=True
    )
    gain_shards = lax.psum_scatter(gain_sum, ("fsdp", "sp"), scatter_dimension=1, tiled=True)
    kv_width = KV * HDIM
    edges = [
        0,
        D,
        D + kv_width,
        D + 2 * kv_width,
        2 * D + 2 * kv_width,
        2 * D + 2 * kv_width + FF,
        2 * D + 2 * kv_width + 2 * FF,
        2 * D + 2 * kv_width + 3 * FF,
    ]
    pieces = [grad_shards[:, edges[slot] : edges[slot + 1]] for slot in range(7)]
    return (
        jnp.stack(outputs),
        jnp.stack(input_grads),
        gain_shards[0],
        pieces[0],
        pieces[1],
        pieces[2],
        pieces[3],
        gain_shards[1],
        pieces[4],
        pieces[5],
        pieces[6],
    )


def mesh_place(n_sp):
    shard = lax.axis_index("fsdp")
    rank = lax.axis_index("sp")
    group = n_sp // MB
    chip, core = shard // 2, shard % 2
    micro, member = rank // group, rank % group
    high, low = member // 2, member % 2
    base = micro * group
    peers = (
        (shard, base + high * 2 + (1 - low)),
        (shard, base + (1 - high) * 2 + low),
        (shard, base + (1 - high) * 2 + (1 - low)),
    )
    members = (high * 2 + (1 - low), (1 - high) * 2 + low, (1 - high) * 2 + (1 - low))
    partner = (shard, (1 - micro) * group + member)
    core_mate = (chip * 2 + (1 - core), rank)
    chip_mate = ((1 - chip) * 2 + core, rank)
    far_mate = ((1 - chip) * 2 + (1 - core), rank)
    return shard, rank, micro, member, peers, members, partner, core_mate, chip_mate, far_mate


def greet(devices):
    barrier = pltpu.get_barrier_semaphore()
    for device in devices:
        pl.semaphore_signal(barrier, inc=1, device_id=device, device_id_type=MESH)
    pl.semaphore_wait(barrier, len(devices))


def lane_ids(shape):
    return lax.broadcasted_iota(jnp.int32, shape, len(shape) - 1)


def turn(vectors):
    width = vectors.shape[-1]
    ahead = pltpu.roll(vectors, width - HDIM // 2, 1)
    behind = pltpu.roll(vectors, HDIM // 2, 1)
    first = lane_ids(vectors.shape) % HDIM < HDIM // 2
    return jnp.where(first, -ahead, behind)


def turn_back(vectors):
    return -turn(vectors)


def softmax_columns(key_side, query_pair, bias):
    scores = contract_cols(key_side, query_pair) + bias.astype(jnp.float32)
    weights_exp = jnp.exp(scores - jnp.max(scores, axis=0, keepdims=True))
    return weights_exp * (1.0 / jnp.sum(weights_exp, axis=0, keepdims=True))


def row_places(shape, dim, group, tok_rows):
    ids = lax.broadcasted_iota(jnp.int32, shape, dim)
    own_rows = MB * tok_rows
    return ((ids % own_rows) // tok_rows) * (group * tok_rows) + (ids // own_rows) * tok_rows + ids % tok_rows


def row_positions(window, dim, group, tok_rows, first_len, both_len):
    shape = (window, 1) if dim == 0 else (1, window)
    place = row_places(shape, dim, group, tok_rows)
    anchor = jnp.where(place < first_len, 0, jnp.where(place < both_len, first_len, both_len))
    return place, place - anchor


def pair_bias(window, group, tok_rows, first_len, both_len):
    place, position = row_positions(window, 1, group, tok_rows, first_len, both_len)
    key_place = row_places((window, 1), 0, group, tok_rows)
    return jnp.where((key_place <= place) & (key_place >= place - position), 0.0, -1e30)


def layer_kernel(
    n_sp,
    tokens,
    cotangent,
    seq_len,
    slot_order,
    norm1_gain,
    norm2_gain,
    inverse,
    key_in,
    value_in,
    wq_in,
    wo_in,
    wg_in,
    wu_in,
    wd_in,
    block_out,
    input_grad,
    ffn_grad,
    qkv_grad,
    out_grad,
    gain_sum,
    from_core,
    from_chip,
    from_half,
    out_core,
    out_chip,
    out_half,
    wf,
    wq,
    wkv,
    wo,
    wkv_in,
    gains,
    gains_all,
    cosine,
    sine,
    bias,
    xs,
    gs,
    normed,
    upstream,
    normed_two,
    query_rot,
    keys,
    values,
    attended,
    d_attended,
    d_query,
    d_pair,
    key_sum,
    value_sum,
    middle,
    own_rest,
    own_block,
    hid,
    sent,
    sent_block,
    got,
    got_block,
    got_one,
    d_full,
    rows_out,
    rows_got,
    late_chip,
    late_half,
    gain_part,
    gain_got,
    local_sem,
    send_sem,
    recv_sem,
):
    place = mesh_place(n_sp)
    shard, rank, micro, member, peers, members, partner, core_mate, chip_mate, far_mate = place
    chip, core = shard // 2, shard % 2
    group = n_sp // MB
    tok_rows = tokens.shape[1]
    own_rows = MB * tok_rows
    window = group * own_rows
    depth = D // KV
    width_q, width_f = wq.shape[1], wf.shape[2]
    width_l = width_q + 2 * HDIM
    half_rows = group * tok_rows
    others = tuple((shard, (1 - micro) * group + t) for t in members)
    greet((*peers, partner, *others, core_mate, chip_mate, far_mate))

    def copy_to(index, source, target, device):
        return pltpu.make_async_remote_copy(
            src_ref=source,
            dst_ref=target,
            send_sem=send_sem.at[index],
            recv_sem=recv_sem.at[index],
            device_id=device,
            device_id_type=MESH,
        )

    def send(index, source, target, device):
        copy = copy_to(index, source, target, device)
        copy.start()
        return copy

    def move(index, source, target):
        copy = pltpu.make_async_copy(source, target, local_sem.at[index])
        copy.start()
        return copy

    def row_span(first, size):
        return pl.ds(pl.multiple_of(first, tok_rows), size)

    def lane_span(first, size):
        return pl.ds(pl.multiple_of(first, 128), size)

    swap_x = send(0, tokens.at[1 - micro], xs.at[micro], partner)
    own_half = pl.ds(pl.multiple_of(micro * tok_rows, tok_rows), tok_rows)
    swap_g = send(1, cotangent.at[1 - micro], gs.at[own_half], partner)
    own_x = move(0, tokens.at[micro], xs.at[micro])
    own_g = move(1, cotangent.at[micro], gs.at[own_half])
    gains[0:1, :] = norm1_gain[...].astype(jnp.float32)
    gains[1:2, :] = norm2_gain[...].astype(jnp.float32)
    gain_sends = [
        send(2 + i, gains, gains_all.at[shard], device) for i, device in enumerate((core_mate, chip_mate, far_mate))
    ]
    own_gain = move(2, gains, gains_all.at[shard])

    own_pair = lane_span(member // 2 * 128, 128)
    key_pair = key_in[:, own_pair].astype(jnp.float32)
    value_pair = value_in[:, own_pair].astype(jnp.float32)
    key_pair = jnp.where(member % 2 == 0, key_pair, pltpu.roll(key_pair, HDIM, 1))
    value_pair = jnp.where(member % 2 == 0, pltpu.roll(value_pair, HDIM, 1), value_pair)
    wkv_in[...] = jnp.where(lane_ids(key_pair.shape) < HDIM, key_pair, value_pair).astype(jnp.bfloat16)

    chip_shard = (1 - chip) * 2 + core
    own_ffn = lane_span(member * width_f, width_f)
    parts = (
        (wq_in.at[:, lane_span(member * width_q, width_q)], wq),
        (wkv_in, wkv),
    )

    def weight_out(i):
        source, target = parts[i]
        rows = row_span(shard * depth, depth)
        over_chip = send(5 + 3 * i, source, target.at[rows], chip_mate)
        over_core = send(6 + 3 * i, source, target.at[rows], core_mate)
        here = move(3 + i, source, target.at[rows])
        return over_chip, over_core, here

    def weight_on(i):
        rows = parts[i][1].at[row_span(chip_shard * depth, depth)]
        return send(7 + 3 * i, rows, rows, core_mate)

    started = {i: weight_out(i) for i in (0, 1)}
    same_chip, same_core = chip == member // 2, core == member % 2
    wo_half = width_q // 2
    wo_mine = row_span((core + member % 2) % 2 * wo_half, wo_half)
    wo_over_core = copy_to(21, wo_in, wo, core_mate)
    wo_first = copy_to(20, wo_in.at[wo_mine], wo.at[wo_mine], chip_mate)
    wo_second = copy_to(20, wo.at[wo_mine], wo.at[wo_mine], chip_mate)
    wo_on = copy_to(22, wo.at[wo_mine], wo.at[wo_mine], core_mate)
    wo_here = pltpu.make_async_copy(wo_in, wo, local_sem.at[8])

    @pl.when(same_chip & same_core)
    def _():
        wo_over_core.start()
        wo_first.start()
        wo_here.start()

    @pl.when(same_chip & jnp.logical_not(same_core))
    def _():
        wo_over_core.wait_recv()
        wo_second.start()

    ffn_in = (wd_in, wg_in, wu_in)
    quarter = depth // 4

    def ffn_rows(w, shard_of, first, size):
        return wf.at[w, row_span(shard_of * depth + first, size)]

    quarters, rests, mates, heres, handed, ons = [], [], [], [], [], []
    for w in range(3):
        for copies, first, size, index in ((quarters, micro * quarter, quarter, 102), (rests, 2 * quarter, 2 * quarter, 105)):
            source = ffn_in[w].at[row_span(first, size), own_ffn]
            copies.append(send(index + w, source, ffn_rows(w, shard, first, size), chip_mate))
        mates.append(send(108 + w, ffn_in[w].at[:, own_ffn], ffn_rows(w, shard, 0, depth), core_mate))
        heres.append(move(5 + w, ffn_in[w].at[:, own_ffn], ffn_rows(w, shard, 0, depth)))

    def hand_on(w):
        quarters[w].wait()
        rows = ffn_rows(w, chip_shard, micro * quarter, quarter)
        handed.append(send(111 + w, rows, rows, partner))

    def core_on(w):
        rests[w].wait()
        handed[w].wait()
        rows = ffn_rows(w, chip_shard, 0, depth)
        ons.append(send(114 + w, rows, rows, core_mate))

    first_len = seq_len[slot_order[2 * (shard * MB + micro)]]
    both_len = first_len + seq_len[slot_order[2 * (shard * MB + micro) + 1]]
    angles = row_positions(window, 0, group, tok_rows, first_len, both_len)[1].astype(jnp.float32) * inverse[...]
    cosine[...] = jnp.cos(angles)
    sine[...] = jnp.sin(angles)
    bias[...] = pair_bias(window, group, tok_rows, first_len, both_len).astype(jnp.bfloat16)

    own_gain.wait()
    for copy in gain_sends:
        copy.wait()
    gain_one = jnp.concatenate([gains_all[f, 0:1, :] for f in range(KV)], axis=1)
    gain_two = jnp.concatenate([gains_all[f, 1:2, :] for f in range(KV)], axis=1)
    own_x.wait()
    swap_x.wait()
    inputs = xs[...].reshape(own_rows, D).astype(jnp.float32)
    normed[member] = (inputs * rms_scale(inputs) * gain_one).astype(jnp.bfloat16)


    def block_to(index, ref, block, device):
        return send(index, ref.at[block], ref.at[block], device)

    first_half, second_half = pl.ds(0, tok_rows), pl.ds(tok_rows, tok_rows)

    def half_to(index, ref, block, rows, device):
        return send(index, ref.at[block, rows], ref.at[block, rows], device)

    def gather_start(index, ref):
        return (
            half_to(index, ref, member, first_half, peers[1]),
            half_to(index + 1, ref, member, second_half, peers[0]),
            half_to(index + 2, ref, member, second_half, peers[1]),
            half_to(index + 3, ref, member, first_half, peers[0]),
        )

    def gather_on(index, ref, parts):
        parts[0].wait()
        on_y = half_to(index + 4, ref, members[1], first_half, peers[0])
        parts[1].wait()
        return on_y, half_to(index + 5, ref, members[0], second_half, peers[1])

    one_parts = gather_start(117, normed)

    own_g.wait()
    swap_g.wait()
    ids = lax.broadcasted_iota(jnp.int32, (own_rows, 1), 0)
    own_place = (ids // tok_rows) * (group * tok_rows) + member * tok_rows + ids % tok_rows
    valid = jnp.where(own_place < both_len, 1.0, 0.0)
    upstream[member] = (gs[...].astype(jnp.float32) * valid).astype(jnp.bfloat16)

    def weights_one():
        on = []
        for i in (0, 1):
            started[i][0].wait()
            on.append(weight_on(i))
        for i in (0, 1):
            started[i][1].wait()
            started[i][2].wait()
        for copy in on:
            copy.wait()

    def project(rows):
        block = normed[rows]
        place_rows = row_span(rows * own_rows, own_rows)
        query = plain_dot(block, wq[...])
        pair = plain_dot(block, wkv[...])
        cos, sin = cosine[place_rows, :], sine[place_rows, :]
        for j in range(width_q // 128):
            lanes = slice(j * 128, (j + 1) * 128)
            head = query[:, lanes].astype(jnp.bfloat16).astype(jnp.float32)
            head = (head * cos + turn(head) * sin).astype(jnp.bfloat16)
            query_rot[place_rows, lanes] = head * HDIM**-0.5
        pair = pair.astype(jnp.bfloat16).astype(jnp.float32)
        turned_key = pair * cos + turn(pair) * sin
        lower = lane_ids(pair.shape) < HDIM
        keys[place_rows, :] = jnp.where(lower, turned_key, pltpu.roll(turned_key, HDIM, 1)).astype(jnp.bfloat16)
        values[place_rows, :] = jnp.where(lower, pltpu.roll(pair, HDIM, 1), pair).astype(jnp.bfloat16)

    one_ons = gather_on(117, normed, one_parts)
    g_over_z = block_to(26, upstream, member, peers[1])
    g_over_y = block_to(27, upstream, member, peers[0])
    weights_one()
    project(member)
    one_parts[2].wait()
    project(members[1])
    one_parts[3].wait()
    project(members[0])
    for copy in one_ons:
        copy.wait()
    project(members[2])

    key_twice, value_twice = keys[...], values[...]
    lower = lane_ids(key_twice.shape) < HDIM
    zero = jnp.zeros_like(key_twice)
    key_low, key_high = jnp.where(lower, key_twice, zero), jnp.where(lower, zero, key_twice)
    value_low, value_high = jnp.where(lower, value_twice, zero), jnp.where(lower, zero, value_twice)
    value_low_turned, value_high_turned = value_low.T, value_high.T

    @pl.loop(0, width_q // 128)
    def _(j):
        lanes = lane_span(j * 128, 128)
        pair = query_rot[:, lanes]
        total = plain_dot(value_low_turned, softmax_columns(key_low, pair, bias[...]).astype(jnp.bfloat16))
        total += plain_dot(value_high_turned, softmax_columns(key_high, pair, bias[...]).astype(jnp.bfloat16))
        attended[:, lanes] = total.T.astype(jnp.bfloat16)

    @pl.when(same_chip & same_core)
    def _():
        wo_first.wait_send()
        wo_over_core.wait_send()
        wo_here.wait()

    @pl.when(same_chip & jnp.logical_not(same_core))
    def _():
        wo_second.wait_send()

    @pl.when(jnp.logical_not(same_chip))
    def _():
        wo_first.wait_recv()
        wo_on.start()
        wo_on.wait()

    def project_out(rows):
        return plain_dot(attended[row_span(rows * own_rows, own_rows), :], wo[...])

    def rows_to_y(index, rows_of, k, held, landing):
        owner, place = ((members[2], 2), (members[0], 0))[k]
        held[k] = rows_of(owner).astype(jnp.bfloat16)
        return send(index, held.at[k], landing.at[place], peers[0])

    def sum_over_z(index, over, held, landing):
        over.wait()
        held[2] = (held[2].astype(jnp.float32) + landing[2].astype(jnp.float32)).astype(jnp.bfloat16)
        return send(index, held.at[2], landing.at[1], peers[1])

    def sum_of(rows, over_y, over_z, landing):
        over_y.wait()
        over_z.wait()
        return rows + landing[0].astype(jnp.float32) + landing[1].astype(jnp.float32)

    mid_over = rows_to_y(29, project_out, 0, sent, got)
    mid_y = rows_to_y(30, project_out, 1, sent, got)
    sent[2] = project_out(members[1]).astype(jnp.bfloat16)
    mid_own = inputs + project_out(member)
    mid_z = sum_over_z(31, mid_over, sent, got)
    hand_on(0)
    total = sum_of(mid_own, mid_y, mid_z, got)
    middle[...] = total
    normed_two[member] = (total * rms_scale(total) * gain_two).astype(jnp.bfloat16)
    two_parts = gather_start(123, normed_two)
    two_ons = gather_on(123, normed_two, two_parts)
    g_over_z.wait()
    g_on_y = block_to(28, upstream, members[1], peers[0])
    hand_on(1)
    core_on(0)
    hand_on(2)
    core_on(1)
    core_on(2)
    for copy in (*mates, *heres, *ons, g_over_y, g_on_y, *two_parts[2:], *two_ons):
        copy.wait()

    @pl.loop(0, group)
    def _(r):
        place_rows = row_span(r * own_rows, own_rows)
        gate = plain_dot(normed_two[r], wf[1])
        up = plain_dot(normed_two[r], wf[2])
        d_hidden = plain_dot(upstream[r], wf[0])
        sig = jax.nn.sigmoid(gate)
        silu = gate * sig
        hid[0, place_rows, :] = (silu * up).astype(jnp.bfloat16)
        hid[1, place_rows, :] = (d_hidden * up * sig * (1.0 + gate * (1.0 - sig))).astype(jnp.bfloat16)
        hid[2, place_rows, :] = (d_hidden * silu).astype(jnp.bfloat16)

    def hid_rows(k, rows):
        return hid[k, row_span(rows * own_rows, own_rows), :]

    base = 35
    two_rows = lambda rows: contract_cols(hid_rows(1, rows), wf[1]) + contract_cols(hid_rows(2, rows), wf[2])
    two_over = rows_to_y(base + 27, two_rows, 0, sent, got)
    two_y = rows_to_y(base + 28, two_rows, 1, sent, got)
    block_rows = lambda rows: contract_cols(hid_rows(0, rows), wf[0])
    for k, rows in enumerate((members[2], members[0], members[1])):
        sent_block[k] = block_rows(rows).astype(jnp.bfloat16)
    own_block[...] = (middle[...] + block_rows(member)).reshape(MB, tok_rows, D)

    def weight_part(w, f):
        rows = lane_span(f * depth, depth)
        acts = (upstream if w == 0 else normed_two)[:, :, rows].reshape(window, depth)
        wf[w, rows, :] = contract_rows(acts, hid[w]).astype(jnp.bfloat16)

    core_copies, chip_copies, half_copies, last_copies, here_copies = {}, {}, {}, [], []

    def core_send(w, k):
        x = 1 - chip if k == 0 else chip
        rows = row_span((x * 2 + 1 - core) * depth, depth)
        core_copies[w, k] = send(base + 3 + 2 * w + k, wf.at[w, rows], from_core.at[w, x], core_mate)

    def far_parts(w):
        weight_part(w, (1 - chip) * 2 + 1 - core)
        core_send(w, 0)
        weight_part(w, (1 - chip) * 2 + core)

    def near_parts(w):
        weight_part(w, chip * 2 + 1 - core)
        core_send(w, 1)
        weight_part(w, chip * 2 + core)

    def all_parts(w):
        for f in range(KV):
            weight_part(w, f)
        core_send(w, 0)
        core_send(w, 1)

    def slot(x, c, m):
        return (x * 2 + c) * depth + m * half_rows

    def stage_in(index, source, w, first):
        return move(index, source, wf.at[w, row_span(first, half_rows)])

    def add_up(w, first, stages):
        @pl.loop(0, group)
        def _(t):
            total = wf[w, row_span(first + t * tok_rows, tok_rows), :].astype(jnp.float32)
            for stage in stages:
                total += wf[w, row_span(stage + t * tok_rows, tok_rows), :].astype(jnp.float32)
            wf[w, row_span(first + t * tok_rows, tok_rows), :] = total.astype(jnp.bfloat16)

    def core_rows(w, x, m):
        return from_core.at[w, x, row_span(m * half_rows, half_rows)]

    def chip_unit(w, m, index):
        if index == 0:
            core_copies[w, 0].wait()
        first, stage = slot(1 - chip, core, m), slot(1 - chip, 1 - core, m)
        stage_in(9, core_rows(w, 1 - chip, m), w, stage).wait()
        add_up(w, first, (stage,))
        chip_copies[w, index] = send(
            base + 9 + 2 * w + index, wf.at[w, row_span(first, half_rows)], from_chip.at[w, m], chip_mate
        )

    def half_unit(w):
        m = 1 - micro
        first, stage, other = slot(chip, core, m), slot(chip, 1 - core, m), slot(1 - chip, 1 - core, m)
        core_copies[w, 1].wait()
        load = stage_in(9, core_rows(w, chip, m), w, stage)
        chip_copies[w, 0].wait()
        stage_in(10, from_chip.at[w, m], w, other).wait()
        load.wait()
        add_up(w, first, (stage, other))
        half_copies[w] = send(base + 15 + w, wf.at[w, row_span(first, half_rows)], from_half.at[w], partner)

    def last_unit(w):
        first, stage, other = slot(chip, core, micro), slot(chip, 1 - core, micro), slot(1 - chip, 1 - core, micro)
        third = slot(chip, 1 - core, 1 - micro)
        load = stage_in(9, core_rows(w, chip, micro), w, stage)
        chip_copies[w, 1].wait()
        over = stage_in(10, from_chip.at[w, micro], w, other)
        half_copies[w].wait()
        stage_in(11, from_half.at[w], w, third).wait()
        load.wait()
        over.wait()
        add_up(w, first, (stage, other, third))
        for i in range(group - 1):
            source = wf.at[w, row_span(first + members[i] * tok_rows, tok_rows)]
            last_copies.append(send(base + 18 + 3 * w + i, source, ffn_grad.at[w, :, own_ffn], peers[i]))
        source = wf.at[w, row_span(first + member * tok_rows, tok_rows)]
        here_copies.append(move(12 + w, source, ffn_grad.at[w, :, own_ffn]))

    far_parts(0)
    sent[2] = two_rows(members[1]).astype(jnp.bfloat16)
    two_z = sum_over_z(base + 29, two_over, sent, got)
    chip_unit(0, 1 - micro, 0)
    near_parts(0)
    own_rest[...] = two_rows(member).reshape(MB, tok_rows, D)
    far_parts(1)

    middle_rows = middle[...]
    grad, two_term = norm_back(middle_rows, rms_scale(middle_rows), gain_two, sum_of(own_rest[...].reshape(own_rows, D), two_y, two_z, got))
    grad += upstream[member].astype(jnp.float32)
    middle[...] = grad
    d_full[member] = grad.astype(jnp.bfloat16)
    to_z = send(base + 32, d_full.at[member], d_full.at[member], peers[1])
    to_y = send(base + 33, d_full.at[member], d_full.at[member], peers[0])
    near_parts(1)
    half_unit(0)
    chip_unit(1, 1 - micro, 0)
    all_parts(2)

    def give(k, rows, kept):
        rows_out[k] = jnp.where(micro == 0, rows[tok_rows:], rows[:tok_rows]).astype(jnp.bfloat16)
        kept[micro] = jnp.where(micro == 0, rows[:tok_rows], rows[tok_rows:])
        return send(base + 30 + k, rows_out.at[k], rows_got.at[k], partner)

    def take(k, copy, kept, target):
        copy.wait()
        kept[1 - micro] = rows_got[k].astype(jnp.float32)
        here_copies.append(move(18 + k, kept, target))

    def attention_grad(rows):
        place_rows = row_span(rows * own_rows, own_rows)
        d_attended[place_rows, :] = contract_cols(d_full[rows], wo[...]).astype(jnp.bfloat16)

    to_z.wait()
    on_y = send(base + 34, d_full.at[members[1]], d_full.at[members[1]], peers[0])
    block_over = send(base, sent_block.at[0], got_block.at[2], peers[0])
    block_y = send(base + 1, sent_block.at[1], got_block.at[0], peers[0])
    attention_grad(member)
    attention_grad(members[1])
    to_y.wait()
    attention_grad(members[0])
    chip_unit(2, 1 - micro, 0)
    on_y.wait()
    attention_grad(members[2])
    half_unit(1)

    out_part = normed_two
    d_rows = d_full[...].reshape(window, D)
    for j in range(group):
        out_part[j] = contract_rows(attended[:, j * 128 : (j + 1) * 128], d_rows).astype(jnp.bfloat16)
    out_by_core = copy_to(base + 35, out_part, out_core, core_mate)
    out_by_chip = copy_to(base + 36, out_part, out_chip, chip_mate)
    half_blocks = group // MB
    out_by_half = copy_to(base + 37, out_part.at[pl.ds((1 - micro) * half_blocks, half_blocks)], out_half, partner)

    def add_blocks(landed, first, count):
        for j in range(count):
            move(15, landed.at[j], gs).wait()
            out_part[first + j] = (
                out_part[first + j].astype(jnp.float32) + gs[...].astype(jnp.float32)
            ).astype(jnp.bfloat16)

    @pl.when(jnp.logical_not(same_core))
    def _():
        out_by_core.start()

    for w in (0, 1):
        chip_unit(w, micro, 1)

    key_low_turned, key_high_turned = key_low.T, key_high.T
    key_sum[...] = jnp.zeros_like(key_sum)
    value_sum[...] = jnp.zeros_like(value_sum)

    @pl.loop(0, width_q // 128)
    def _(j):
        lanes = lane_span(j * 128, 128)
        query_pair, grad_pair = query_rot[:, lanes], d_attended[:, lanes]
        total = jnp.zeros((2 * HDIM, window), jnp.float32)
        for side, (key_side, value_side, key_turned) in enumerate(
            ((key_low, value_low, key_low_turned), (key_high, value_high, key_high_turned))
        ):
            probs = softmax_columns(key_side, query_pair, bias[...])
            d_probs = contract_cols(value_side, grad_pair)
            inner = jnp.sum(probs * d_probs, axis=0, keepdims=True)
            d_scores = (probs * (d_probs - inner)).astype(jnp.bfloat16)
            total += plain_dot(key_turned, d_scores)
            key_sum[side] += plain_dot(d_scores, query_pair)
            value_sum[side] += plain_dot(probs.astype(jnp.bfloat16), grad_pair)
        grad_rot = total.T * HDIM**-0.5
        d_query[:, lanes] = (grad_rot * cosine[...] + turn_back(grad_rot * sine[...])).astype(jnp.bfloat16)

    fold = lambda sums: jnp.where(lower, sums[0] + pltpu.roll(sums[1], HDIM, 1), 0.0)
    key_grad, value_grad = fold(key_sum), fold(value_sum)
    key_grad = key_grad * cosine[...] + turn_back(key_grad * sine[...])
    d_pair[...] = jnp.where(lower, key_grad, pltpu.roll(value_grad, HDIM, 1)).astype(jnp.bfloat16)

    def one_rows(rows):
        place_rows = row_span(rows * own_rows, own_rows)
        return contract_cols(d_query[place_rows, :], wq[...]) + contract_cols(d_pair[place_rows, :], wkv[...])

    one_over = rows_to_y(base + 38, one_rows, 0, sent, got_one)
    one_y = rows_to_y(base + 39, one_rows, 1, sent, got_one)
    sent[2] = one_rows(members[1]).astype(jnp.bfloat16)
    own_rest[...] = one_rows(member).reshape(MB, tok_rows, D)
    half_unit(2)

    @pl.when(jnp.logical_not(same_core))
    def _():
        out_by_core.wait_send()

    @pl.when(same_core)
    def _():
        out_by_core.wait_recv()
        add_blocks(out_core, 0, group)

    @pl.when(same_core & jnp.logical_not(same_chip))
    def _():
        out_by_chip.start()

    d_all = jnp.concatenate([d_query[...], d_pair[...]], axis=1)

    def late_lanes(c):
        return lane_span(c * width_l, width_l)

    def late_part(x, c):
        for m in range(MB):
            columns = lane_span(((x * 2 + c) * MB + m) * half_rows, half_rows)
            rows = normed[:, :, columns].reshape(window, half_rows)
            hid[x, m * half_rows : (m + 1) * half_rows, late_lanes(c)] = contract_rows(rows, d_all).astype(jnp.bfloat16)

    late_core_copies = []
    for x in range(2):
        late_part(x, 1 - core)
        late_core_copies.append(
            send(base + 41 + x, hid.at[x, :, late_lanes(1 - core)], hid.at[2, :, late_lanes(x)], core_mate)
        )
    for x in range(2):
        late_part(x, core)
    for copy in late_core_copies:
        copy.wait()

    def late_add(x, first, count, landed):
        @pl.loop(0, count)
        def _(t):
            rows = row_span(first + t * tok_rows, tok_rows)
            total = hid[x, rows, late_lanes(core)].astype(jnp.float32) + hid[2, rows, late_lanes(x)].astype(jnp.float32)
            for ref, start in landed:
                total += ref[row_span(start + t * tok_rows, tok_rows), :].astype(jnp.float32)
            hid[x, rows, late_lanes(core)] = total.astype(jnp.bfloat16)

    late_add(1 - chip, 0, MB * group, ())
    late_to_chip = send(base + 43, hid.at[1 - chip, :, late_lanes(core)], late_chip, chip_mate)
    block_z = sum_over_z(base + 2, block_over, sent_block, got_block)
    one_z = sum_over_z(base + 40, one_over, sent, got_one)
    chip_unit(2, micro, 1)
    block = sum_of(own_block[...].reshape(own_rows, D), block_y, block_z, got_block)
    give_block = give(0, block, own_block)

    @pl.when(same_core & jnp.logical_not(same_chip))
    def _():
        out_by_chip.wait_send()

    @pl.when(same_core & same_chip)
    def _():
        out_by_chip.wait_recv()
        add_blocks(out_chip, 0, group)
        out_by_half.start()

    last_unit(0)
    late_to_chip.wait()
    late_add(chip, (1 - micro) * half_rows, group, ((late_chip, (1 - micro) * half_rows),))
    late_to_half = send(
        base + 46, hid.at[chip, row_span((1 - micro) * half_rows, half_rows), late_lanes(core)], late_half, partner
    )

    inputs = xs[...].reshape(own_rows, D).astype(jnp.float32)
    grad, one_term = norm_back(
        inputs, rms_scale(inputs), gain_one, sum_of(own_rest[...].reshape(own_rows, D), one_y, one_z, got_one)
    )
    give_grad = give(1, grad + middle[...], own_rest)

    for k, term in enumerate((one_term[None], two_term[None])):
        for f in range(KV):
            gain_part[k * KV + f : k * KV + f + 1, :] = term[:, f * depth : (f + 1) * depth]
    gain_first = [
        send(base + 57 + i, gain_part, gain_got.at[i], device)
        for i, device in enumerate((core_mate, chip_mate, far_mate))
    ]
    last_unit(1)
    for copy in gain_first:
        copy.wait()
    gain_part[...] = gain_part[...] + gain_got[0] + gain_got[1] + gain_got[2]
    gain_second = [
        send(base + 60 + i, gain_part, gain_got.at[3 + i], device)
        for i, device in enumerate((*peers, partner, *others))
    ]
    take(0, give_block, own_block, block_out)
    last_unit(2)

    def out_block(t):
        return out_part.at[micro * half_blocks + t // 2, row_span(t % 2 * tok_rows, tok_rows)]

    out_here = pltpu.make_async_copy(out_block(member), out_grad, local_sem.at[16])

    def out_to(i):
        return pltpu.make_async_remote_copy(
            src_ref=out_block(members[i]),
            dst_ref=out_grad,
            send_sem=send_sem.at[base + 48 + i],
            recv_sem=recv_sem.at[base + 48],
            device_id=peers[i],
            device_id_type=MESH,
        )

    @pl.when(same_core & same_chip)
    def _():
        out_by_half.wait()
        add_blocks(out_half, micro * half_blocks, half_blocks)
        for i in range(group - 1):
            out_to(i).start()
        out_here.start()

    late_to_half.wait()
    late_add(chip, micro * half_rows, group, ((late_chip, micro * half_rows), (late_half, 0)))
    own_late = lane_span(member * width_l, width_l)

    def late_rows(t):
        return hid.at[chip, row_span(micro * half_rows + t * tok_rows, tok_rows), late_lanes(core)]

    for i in range(group - 1):
        last_copies.append(send(base + 54 + i, late_rows(members[i]), qkv_grad.at[:, own_late], peers[i]))
    here_copies.append(move(17, late_rows(member), qkv_grad.at[:, own_late]))
    take(1, give_grad, own_rest, input_grad)
    total = gain_part[...]
    for i, copy in enumerate(gain_second):
        copy.wait()
        total += gain_got[3 + i]
    gain_sum[...] = total

    @pl.when(same_core & same_chip)
    def _():
        for i in range(group - 1):
            out_to(i).wait_send()
        out_here.wait()

    @pl.when(jnp.logical_not(same_core & same_chip))
    def _():
        out_to(0).wait_recv()

    for copy in (*last_copies, *here_copies):
        copy.wait()


def whole_layer(n_sp, tok_rows, heads, *operands):
    group = n_sp // MB
    own_rows = MB * tok_rows
    window = group * own_rows
    half_rows = group * tok_rows
    width_q = heads * HDIM
    width_f = FF // group
    width_l = width_q + 2 * HDIM
    low, full = jnp.bfloat16, jnp.float32
    vmem = pl.BlockSpec(memory_space=pltpu.VMEM)
    anywhere = pl.BlockSpec(memory_space=pl.ANY)
    smem = pl.BlockSpec(memory_space=pltpu.SMEM)
    shape = jax.ShapeDtypeStruct
    blocks = (group, own_rows, D)
    trio = (group - 1, own_rows, D)
    pair = (MB, tok_rows, D)
    return pl.pallas_call(
        functools.partial(layer_kernel, n_sp),
        out_shape=(
            shape(pair, full),
            shape(pair, full),
            shape((3, tok_rows, FF), low),
            shape((tok_rows, group * width_l), low),
            shape((tok_rows, D), low),
            shape((2 * KV, D // KV), full),
            shape((3, 2, MB * half_rows, width_f), low),
            shape((3, MB, half_rows, width_f), low),
            shape((3, half_rows, width_f), low),
            shape(blocks, low),
            shape(blocks, low),
            shape((group // MB, own_rows, D), low),
        ),
        in_specs=[anywhere] * 2 + [smem] * 2 + [vmem] * 5 + [anywhere] * 5,
        out_specs=(anywhere,) * 5 + (vmem,) + (anywhere,) * 6,
        scratch_shapes=[
            pltpu.VMEM((3, D, width_f), low),
            pltpu.VMEM((D, width_q), low),
            pltpu.VMEM((D, 2 * HDIM), low),
            pltpu.VMEM((width_q, D), low),
            pltpu.VMEM((D // KV, 2 * HDIM), low),
            pltpu.VMEM((8, D // KV), full),
            pltpu.VMEM((KV, 8, D // KV), full),
            pltpu.VMEM((window, 2 * HDIM), full),
            pltpu.VMEM((window, 2 * HDIM), full),
            pltpu.VMEM((window, window), low),
            pltpu.VMEM(pair, low),
            pltpu.VMEM((own_rows, D), low),
            pltpu.VMEM(blocks, low),
            pltpu.VMEM(blocks, low),
            pltpu.VMEM(blocks, low),
            pltpu.VMEM((window, width_q), low),
            pltpu.VMEM((window, 2 * HDIM), low),
            pltpu.VMEM((window, 2 * HDIM), low),
            pltpu.VMEM((window, width_q), low),
            pltpu.VMEM((window, width_q), low),
            pltpu.VMEM((window, width_q), low),
            pltpu.VMEM((window, 2 * HDIM), low),
            pltpu.VMEM((2, window, 2 * HDIM), full),
            pltpu.VMEM((2, window, 2 * HDIM), full),
            pltpu.VMEM((own_rows, D), full),
            pltpu.VMEM(pair, full),
            pltpu.VMEM(pair, full),
            pltpu.VMEM((3, window, width_f), low),
            pltpu.VMEM(trio, low),
            pltpu.VMEM(trio, low),
            pltpu.VMEM(trio, low),
            pltpu.VMEM(trio, low),
            pltpu.VMEM(trio, low),
            pltpu.VMEM(blocks, low),
            pltpu.VMEM((2, tok_rows, D), low),
            pltpu.VMEM((2, tok_rows, D), low),
            pltpu.VMEM((MB * half_rows, width_l), low),
            pltpu.VMEM((half_rows, width_l), low),
            pltpu.VMEM((2 * KV, D // KV), full),
            pltpu.VMEM((10, 2 * KV, D // KV), full),
            pltpu.SemaphoreType.DMA((20,)),
            pltpu.SemaphoreType.DMA((129,)),
            pltpu.SemaphoreType.DMA((129,)),
        ],
        compiler_params=pltpu.CompilerParams(
            collective_id=0, has_side_effects=True, vmem_limit_bytes=VMEM_BYTES
        ),
        cost_estimate=pl.CostEstimate(flops=36 * 10**9, bytes_accessed=100 * 10**6, transcendentals=8 * 10**6),
        name="whole_layer",
    )(*operands)


def group_body(
    tokens,
    cotangent,
    seq_len,
    slot_order,
    norm1_gain,
    query_weight,
    key_weight,
    value_weight,
    output_weight,
    norm2_gain,
    gate_weight,
    up_weight,
    down_weight,
):
    n_sp = lax.axis_size("sp")
    n_fsdp = lax.axis_size("fsdp")
    group = n_sp // MB
    rank = lax.axis_index("sp")
    shard = lax.axis_index("fsdp")
    micro = rank // group
    member = rank % group
    tok_rows = tokens.shape[1]
    window = n_sp * tok_rows
    own_rows = MB * tok_rows
    inverse = np.float32(ROPE_BASE) ** (np.arange(HDIM // 2, dtype=np.float32) * np.float32(-2.0 / HDIM))
    heads = HEADS // group
    block, d_inputs, ffn_grad, qkv_grad, output_grad, gain_sum, *_ = whole_layer(
        n_sp, tok_rows, heads,
        tokens, cotangent, seq_len, slot_order, norm1_gain[None], norm2_gain[None],
        jnp.asarray(np.tile(inverse, 4)[None]), key_weight, value_weight,
        query_weight, output_weight, gate_weight, up_weight, down_weight,
    )
    gain_own = lax.dynamic_slice_in_dim(gain_sum.reshape(2, D), (shard * n_sp + rank) * tok_rows, tok_rows, 1)

    def part_of(first, width):
        pieces = qkv_grad.reshape(tok_rows, group, -1)[:, :, first : first + width]
        return pieces.reshape(tok_rows, group * width).astype(jnp.float32)

    width_q = heads * HDIM
    return (
        block,
        d_inputs,
        gain_own[0],
        part_of(0, width_q),
        part_of(width_q, HDIM),
        part_of(width_q + HDIM, HDIM),
        output_grad.astype(jnp.float32),
        gain_own[1],
        ffn_grad[1].astype(jnp.float32),
        ffn_grad[2].astype(jnp.float32),
        ffn_grad[0].astype(jnp.float32),
    )


def solution(mesh):
    fits = mesh.shape["fsdp"] == KV and mesh.shape["sp"] == MB * KV
    placed = (
        P(None, ("fsdp", "sp"), None),
        P(None, ("fsdp", "sp"), None),
        P(),
        P(),
        P("fsdp"),
        P("fsdp", None),
        P("fsdp", None),
        P("fsdp", None),
        P("fsdp", None),
        P("fsdp"),
        P("fsdp", None),
        P("fsdp", None),
        P("fsdp", None),
    )
    return jax.shard_map(
        group_body if fits else body,
        mesh=mesh,
        in_specs=placed,
        out_specs=(
            P(None, ("fsdp", "sp"), None),
            P(None, ("fsdp", "sp"), None),
            P(("fsdp", "sp")),
            P(("fsdp", "sp"), None),
            P(("fsdp", "sp"), None),
            P(("fsdp", "sp"), None),
            P(("fsdp", "sp"), None),
            P(("fsdp", "sp")),
            P(("fsdp", "sp"), None),
            P(("fsdp", "sp"), None),
            P(("fsdp", "sp"), None),
        ),
        check_vma=False,
    )
```

```python
import functools

import jax
import jax.numpy as jnp
import numpy as np
from jax import lax
from jax.experimental import pallas as pl
from jax.experimental.pallas import tpu as pltpu
from jax.sharding import PartitionSpec as P

D = 2048
HEADS = 32
KV = 4
HDIM = 64
FF = 5632
MB = 2
MESH = pl.DeviceIdType.MESH
VMEM_BYTES = 60 * 2**20


EPSILON = 1e-05
ROPE_BASE = 10000.0


def plain_dot(left_side, right_side):
    return jnp.dot(left_side, right_side, preferred_element_type=jnp.float32)


def contract_rows(left_side, right_side):
    return lax.dot_general(
        left_side, right_side, (((0,), (0,)), ((), ())), preferred_element_type=jnp.float32
    )


def contract_cols(left_side, right_side):
    return lax.dot_general(
        left_side, right_side, (((1,), (1,)), ((), ())), preferred_element_type=jnp.float32
    )


def window_layout(seq_len, slot_order, window_index, window):
    first_len = seq_len[slot_order[2 * window_index]]
    second_len = seq_len[slot_order[2 * window_index + 1]]
    places = jnp.arange(window, dtype=jnp.int32)
    segment = jnp.where(
        places < first_len, 0, jnp.where(places < first_len + second_len, 1, 2)
    ).astype(jnp.int32)
    anchor = jnp.where(segment == 0, 0, jnp.where(segment == 1, first_len, first_len + second_len))
    return (segment, places - anchor)


def rope_tables(position, head_size):
    half_size = head_size // 2
    inverse = ROPE_BASE ** (-2.0 * jnp.arange(half_size, dtype=jnp.float32) / head_size)
    angles = position.astype(jnp.float32)[:, None] * inverse[None, :]
    angles = jnp.concatenate([angles, angles], axis=1)
    return (jnp.cos(angles)[:, None, :], jnp.sin(angles)[:, None, :])


def apply_rope(vectors, cosine, sine):
    half_size = vectors.shape[-1] // 2
    turned = jnp.concatenate([-vectors[..., half_size:], vectors[..., :half_size]], axis=-1)
    return vectors * cosine + turned * sine


def rope_back(grad_in, cosine, sine):
    half_size = grad_in.shape[-1] // 2
    rotated = grad_in * sine
    return grad_in * cosine + jnp.concatenate(
        [rotated[..., half_size:], -rotated[..., :half_size]], axis=-1
    )


def rms_scale(inputs):
    return lax.rsqrt(jnp.mean(inputs * inputs, axis=-1, keepdims=True) + EPSILON)


def norm_back(inputs, scale_rows, gain_full, upstream):
    through = upstream * gain_full
    gain_term = jnp.sum(upstream * inputs * scale_rows, axis=0)
    grad_in = scale_rows * through - inputs * scale_rows**3 * jnp.mean(
        through * inputs, axis=-1, keepdims=True
    )
    return (grad_in, gain_term)


def score_block(query_block, key_rot, segment, row_start):
    block_rows = query_block.shape[0]
    places = jnp.arange(key_rot.shape[0], dtype=jnp.int32)
    row_place = row_start + jnp.arange(block_rows, dtype=jnp.int32)
    block_segment = lax.dynamic_slice_in_dim(segment, row_start, block_rows, 0)
    allowed = (block_segment[:, None] == segment[None, :]) & (places[None, :] <= row_place[:, None])
    raw_scores = jnp.einsum(
        "qhd,khd->hqk", query_block, key_rot, preferred_element_type=jnp.float32
    ) * query_block.shape[2] ** (-0.5)
    return jnp.where(allowed[None], raw_scores, -1e30)


def attend_forward(query_rot, key_rot, value_heads, segment):
    window = query_rot.shape[0]
    block_rows = min(512, window)

    def step(carry, block_index):
        row_start = block_index * block_rows
        query_block = lax.dynamic_slice_in_dim(query_rot, row_start, block_rows, 0)
        scores = score_block(query_block, key_rot, segment, row_start)
        row_top = jnp.max(scores, axis=-1, keepdims=True)
        weights_exp = jnp.exp(scores - row_top)
        row_total = jnp.sum(weights_exp, axis=-1, keepdims=True)
        probs = (weights_exp / row_total).astype(jnp.bfloat16)
        block_out = jnp.einsum(
            "hqk,khd->qhd", probs, value_heads, preferred_element_type=jnp.float32
        )
        log_total = (row_top + jnp.log(row_total))[:, :, 0].T
        return (carry, (block_out, log_total))

    block_ids = jnp.arange(window // block_rows, dtype=jnp.int32)
    _, (outputs, log_totals) = lax.scan(step, jnp.zeros((), jnp.int32), block_ids)
    return (outputs.reshape(query_rot.shape), log_totals.reshape(window, query_rot.shape[1]))


def attend_backward(query_rot, key_rot, value_heads, grad_heads, log_totals, segment):
    window = query_rot.shape[0]
    block_rows = min(512, window)
    scale_factor = query_rot.shape[2] ** (-0.5)

    def step(carry, block_index):
        key_acc, value_acc = carry
        row_start = block_index * block_rows
        query_block = lax.dynamic_slice_in_dim(query_rot, row_start, block_rows, 0)
        grad_block = lax.dynamic_slice_in_dim(grad_heads, row_start, block_rows, 0)
        total_block = lax.dynamic_slice_in_dim(log_totals, row_start, block_rows, 0)
        scores = score_block(query_block, key_rot, segment, row_start)
        probs = jnp.exp(scores - total_block.T[:, :, None])
        grad_probs = jnp.einsum(
            "qhd,khd->hqk", grad_block, value_heads, preferred_element_type=jnp.float32
        )
        inner_sum = jnp.sum(probs * grad_probs, axis=-1, keepdims=True)
        grad_scores = (probs * (grad_probs - inner_sum)).astype(jnp.bfloat16)
        query_part = (
            jnp.einsum("hqk,khd->qhd", grad_scores, key_rot, preferred_element_type=jnp.float32)
            * scale_factor
        )
        key_acc = (
            key_acc
            + jnp.einsum(
                "hqk,qhd->khd", grad_scores, query_block, preferred_element_type=jnp.float32
            )
            * scale_factor
        )
        value_acc = value_acc + jnp.einsum(
            "hqk,qhd->khd",
            probs.astype(jnp.bfloat16),
            grad_block,
            preferred_element_type=jnp.float32,
        )
        return ((key_acc, value_acc), query_part)

    start_acc = (jnp.zeros(key_rot.shape, jnp.float32), jnp.zeros(value_heads.shape, jnp.float32))
    block_ids = jnp.arange(window // block_rows, dtype=jnp.int32)
    (key_acc, value_acc), query_parts = lax.scan(step, start_acc, block_ids)
    return (query_parts.reshape(query_rot.shape), key_acc, value_acc)


def weight_terms(stored):
    joined = [jnp.concatenate(pieces, axis=0) for pieces in zip(*stored)]
    (
        normed,
        query_low,
        key_low,
        value_low,
        attn_rows,
        middle_low,
        normed_two,
        gate_low,
        up_low,
        upstream_low,
        hidden,
    ) = joined
    return jnp.concatenate(
        [
            contract_rows(normed, query_low),
            contract_rows(normed, key_low),
            contract_rows(normed, value_low),
            contract_rows(attn_rows, middle_low),
            contract_rows(normed_two, gate_low),
            contract_rows(normed_two, up_low),
            contract_rows(upstream_low, hidden),
        ],
        axis=1,
    )


def body(
    tokens,
    cotangent,
    seq_len,
    slot_order,
    norm1_gain,
    query_weight,
    key_weight,
    value_weight,
    output_weight,
    norm2_gain,
    gate_weight,
    up_weight,
    down_weight,
):
    seq_devices = lax.axis_size("sp")
    seq_rank = lax.axis_index("sp")
    shard_rank = lax.axis_index("fsdp")
    tok_rows = tokens.shape[1]
    window = seq_devices * tok_rows
    group_size = HEADS // KV
    kept = []
    outputs = []
    input_grads = []
    gain_sum = jnp.zeros((2, D), jnp.float32)
    grad_shards = None
    for micro_step in range(MB):
        gathered = (
            lax.all_gather(norm1_gain, "fsdp", axis=0, tiled=True),
            lax.all_gather(query_weight, "fsdp", axis=0, tiled=True),
            lax.all_gather(key_weight, "fsdp", axis=0, tiled=True),
            lax.all_gather(value_weight, "fsdp", axis=0, tiled=True),
            lax.all_gather(output_weight, "fsdp", axis=0, tiled=True),
            lax.all_gather(norm2_gain, "fsdp", axis=0, tiled=True),
            lax.all_gather(gate_weight, "fsdp", axis=0, tiled=True),
            lax.all_gather(up_weight, "fsdp", axis=0, tiled=True),
            lax.all_gather(down_weight, "fsdp", axis=0, tiled=True),
        )
        gain_one, w_query, w_key, w_value, w_output, gain_two, w_gate, w_up, w_down = gathered
        gain_one = gain_one.astype(jnp.float32)
        gain_two = gain_two.astype(jnp.float32)
        inputs = tokens[micro_step].astype(jnp.float32)
        window_index = shard_rank * MB + micro_step
        segment, position = window_layout(seq_len, slot_order, window_index, window)
        own_segment = lax.dynamic_slice_in_dim(segment, seq_rank * tok_rows, tok_rows, 0)
        valid_rows = (own_segment < 2).astype(jnp.float32)
        scale_one = rms_scale(inputs)
        normed = (inputs * scale_one * gain_one).astype(jnp.bfloat16)
        query_proj = plain_dot(normed, w_query).astype(jnp.bfloat16).reshape(tok_rows, HEADS, HDIM)
        key_proj = plain_dot(normed, w_key).astype(jnp.bfloat16).reshape(tok_rows, KV, HDIM)
        value_proj = plain_dot(normed, w_value).astype(jnp.bfloat16).reshape(tok_rows, KV, HDIM)
        packed = jnp.concatenate(
            [
                query_proj,
                jnp.repeat(key_proj, group_size, axis=1),
                jnp.repeat(value_proj, group_size, axis=1),
            ],
            axis=2,
        )
        head_side = lax.all_to_all(packed, "sp", split_axis=1, concat_axis=0, tiled=True)
        cosine, sine = rope_tables(position, HDIM)
        query_rot = apply_rope(head_side[:, :, :HDIM].astype(jnp.float32), cosine, sine).astype(
            jnp.bfloat16
        )
        key_rot = apply_rope(
            head_side[:, :, HDIM : 2 * HDIM].astype(jnp.float32), cosine, sine
        ).astype(jnp.bfloat16)
        value_heads = head_side[:, :, 2 * HDIM :]
        attended, log_totals = attend_forward(query_rot, key_rot, value_heads, segment)
        token_side = lax.all_to_all(
            attended.astype(jnp.bfloat16), "sp", split_axis=0, concat_axis=1, tiled=True
        )
        attn_rows = token_side.reshape(tok_rows, D)
        middle = inputs + plain_dot(attn_rows, w_output)
        scale_two = rms_scale(middle)
        normed_two = (middle * scale_two * gain_two).astype(jnp.bfloat16)
        gate_proj = plain_dot(normed_two, w_gate)
        up_proj = plain_dot(normed_two, w_up)
        gate_sig = jax.nn.sigmoid(gate_proj)
        hidden = (gate_proj * gate_sig * up_proj).astype(jnp.bfloat16)
        outputs.append(middle + contract_cols(hidden, w_down))
        upstream = cotangent[micro_step].astype(jnp.float32) * valid_rows[:, None]
        upstream_low = upstream.astype(jnp.bfloat16)
        hidden_grad = plain_dot(upstream_low, w_down)
        up_low = (hidden_grad * gate_proj * gate_sig).astype(jnp.bfloat16)
        gate_low = (hidden_grad * up_proj * gate_sig * (1.0 + gate_proj * (1.0 - gate_sig))).astype(
            jnp.bfloat16
        )
        normed_two_grad = contract_cols(gate_low, w_gate) + contract_cols(up_low, w_up)
        middle_grad, gain_two_term = norm_back(middle, scale_two, gain_two, normed_two_grad)
        middle_grad = middle_grad + upstream
        middle_low = middle_grad.astype(jnp.bfloat16)
        attn_grad = (
            contract_cols(middle_low, w_output).astype(jnp.bfloat16).reshape(tok_rows, HEADS, HDIM)
        )
        grad_heads = lax.all_to_all(attn_grad, "sp", split_axis=1, concat_axis=0, tiled=True)
        query_part, key_acc, value_acc = attend_backward(
            query_rot, key_rot, value_heads, grad_heads, log_totals, segment
        )
        packed_grad = jnp.concatenate(
            [rope_back(query_part, cosine, sine), rope_back(key_acc, cosine, sine), value_acc],
            axis=2,
        )
        grad_tokens = lax.all_to_all(packed_grad, "sp", split_axis=0, concat_axis=1, tiled=True)
        query_low = grad_tokens[:, :, :HDIM].reshape(tok_rows, D).astype(jnp.bfloat16)
        key_low = (
            grad_tokens[:, :, HDIM : 2 * HDIM]
            .reshape(tok_rows, KV, group_size, HDIM)
            .sum(axis=2)
            .reshape(tok_rows, KV * HDIM)
            .astype(jnp.bfloat16)
        )
        value_low = (
            grad_tokens[:, :, 2 * HDIM :]
            .reshape(tok_rows, KV, group_size, HDIM)
            .sum(axis=2)
            .reshape(tok_rows, KV * HDIM)
            .astype(jnp.bfloat16)
        )
        normed_grad = (
            contract_cols(query_low, w_query)
            + contract_cols(key_low, w_key)
            + contract_cols(value_low, w_value)
        )
        inputs_grad, gain_one_term = norm_back(inputs, scale_one, gain_one, normed_grad)
        input_grads.append(inputs_grad + middle_grad)
        gain_sum = gain_sum + jnp.stack([gain_one_term, gain_two_term])
        kept.append(
            (
                normed,
                query_low,
                key_low,
                value_low,
                attn_rows,
                middle_low,
                normed_two,
                gate_low,
                up_low,
                upstream_low,
                hidden,
            )
        )
        grad_shards = None
    grad_shards = lax.psum_scatter(
        weight_terms(kept), ("fsdp", "sp"), scatter_dimension=0, tiled=True
    )
    gain_shards = lax.psum_scatter(gain_sum, ("fsdp", "sp"), scatter_dimension=1, tiled=True)
    kv_width = KV * HDIM
    edges = [
        0,
        D,
        D + kv_width,
        D + 2 * kv_width,
        2 * D + 2 * kv_width,
        2 * D + 2 * kv_width + FF,
        2 * D + 2 * kv_width + 2 * FF,
        2 * D + 2 * kv_width + 3 * FF,
    ]
    pieces = [grad_shards[:, edges[slot] : edges[slot + 1]] for slot in range(7)]
    return (
        jnp.stack(outputs),
        jnp.stack(input_grads),
        gain_shards[0],
        pieces[0],
        pieces[1],
        pieces[2],
        pieces[3],
        gain_shards[1],
        pieces[4],
        pieces[5],
        pieces[6],
    )


def mesh_place(n_sp):
    shard = lax.axis_index("fsdp")
    rank = lax.axis_index("sp")
    group = n_sp // MB
    chip, core = shard // 2, shard % 2
    micro, member = rank // group, rank % group
    high, low = member // 2, member % 2
    base = micro * group
    peers = (
        (shard, base + high * 2 + (1 - low)),
        (shard, base + (1 - high) * 2 + low),
        (shard, base + (1 - high) * 2 + (1 - low)),
    )
    members = (high * 2 + (1 - low), (1 - high) * 2 + low, (1 - high) * 2 + (1 - low))
    partner = (shard, (1 - micro) * group + member)
    core_mate = (chip * 2 + (1 - core), rank)
    chip_mate = ((1 - chip) * 2 + core, rank)
    far_mate = ((1 - chip) * 2 + (1 - core), rank)
    return shard, rank, micro, member, peers, members, partner, core_mate, chip_mate, far_mate


def greet(devices):
    barrier = pltpu.get_barrier_semaphore()
    for device in devices:
        pl.semaphore_signal(barrier, inc=1, device_id=device, device_id_type=MESH)
    pl.semaphore_wait(barrier, len(devices))


def lane_ids(shape):
    return lax.broadcasted_iota(jnp.int32, shape, len(shape) - 1)


def turn(vectors):
    width = vectors.shape[-1]
    ahead = pltpu.roll(vectors, width - HDIM // 2, 1)
    behind = pltpu.roll(vectors, HDIM // 2, 1)
    first = lane_ids(vectors.shape) % HDIM < HDIM // 2
    return jnp.where(first, -ahead, behind)


def turn_back(vectors):
    return -turn(vectors)


def softmax_columns(key_side, query_pair, bias):
    scores = contract_cols(key_side, query_pair) + bias.astype(jnp.float32)
    weights_exp = jnp.exp(scores - jnp.max(scores, axis=0, keepdims=True))
    return weights_exp * (1.0 / jnp.sum(weights_exp, axis=0, keepdims=True))


def row_places(shape, dim, group, tok_rows):
    ids = lax.broadcasted_iota(jnp.int32, shape, dim)
    own_rows = MB * tok_rows
    return ((ids % own_rows) // tok_rows) * (group * tok_rows) + (ids // own_rows) * tok_rows + ids % tok_rows


def row_positions(window, dim, group, tok_rows, first_len, both_len):
    shape = (window, 1) if dim == 0 else (1, window)
    place = row_places(shape, dim, group, tok_rows)
    anchor = jnp.where(place < first_len, 0, jnp.where(place < both_len, first_len, both_len))
    return place, place - anchor


def pair_bias(window, group, tok_rows, first_len, both_len):
    place, position = row_positions(window, 1, group, tok_rows, first_len, both_len)
    key_place = row_places((window, 1), 0, group, tok_rows)
    return jnp.where((key_place <= place) & (key_place >= place - position), 0.0, -1e30)


def layer_kernel(
    n_sp,
    tokens,
    cotangent,
    seq_len,
    slot_order,
    norm1_gain,
    norm2_gain,
    inverse,
    key_in,
    value_in,
    wq_in,
    wo_in,
    wg_in,
    wu_in,
    wd_in,
    block_out,
    input_grad,
    ffn_grad,
    qkv_grad,
    out_grad,
    gain_sum,
    from_core,
    from_chip,
    from_half,
    out_core,
    out_chip,
    out_half,
    wf,
    wq,
    wkv,
    wo,
    wkv_in,
    gains,
    gains_all,
    cosine,
    sine,
    bias,
    xs,
    gs,
    normed,
    upstream,
    normed_two,
    query_rot,
    keys,
    values,
    attended,
    d_attended,
    d_query,
    d_pair,
    key_sum,
    value_sum,
    middle,
    own_rest,
    own_block,
    hid,
    sent,
    sent_block,
    got,
    got_block,
    got_one,
    d_full,
    rows_out,
    rows_got,
    late_chip,
    late_half,
    gain_part,
    gain_got,
    local_sem,
    send_sem,
    recv_sem,
):
    place = mesh_place(n_sp)
    shard, rank, micro, member, peers, members, partner, core_mate, chip_mate, far_mate = place
    chip, core = shard // 2, shard % 2
    group = n_sp // MB
    tok_rows = tokens.shape[1]
    own_rows = MB * tok_rows
    window = group * own_rows
    depth = D // KV
    width_q, width_f = wq.shape[1], wf.shape[2]
    width_l = width_q + 2 * HDIM
    half_rows = group * tok_rows
    others = tuple((shard, (1 - micro) * group + t) for t in members)
    greet((*peers, partner, *others, core_mate, chip_mate, far_mate))

    def copy_to(index, source, target, device):
        return pltpu.make_async_remote_copy(
            src_ref=source,
            dst_ref=target,
            send_sem=send_sem.at[index],
            recv_sem=recv_sem.at[index],
            device_id=device,
            device_id_type=MESH,
        )

    def send(index, source, target, device):
        copy = copy_to(index, source, target, device)
        copy.start()
        return copy

    def move(index, source, target):
        copy = pltpu.make_async_copy(source, target, local_sem.at[index])
        copy.start()
        return copy

    def row_span(first, size):
        return pl.ds(pl.multiple_of(first, tok_rows), size)

    def lane_span(first, size):
        return pl.ds(pl.multiple_of(first, 128), size)

    swap_x = send(0, tokens.at[1 - micro], xs.at[micro], partner)
    own_half = pl.ds(pl.multiple_of(micro * tok_rows, tok_rows), tok_rows)
    swap_g = send(1, cotangent.at[1 - micro], gs.at[own_half], partner)
    own_x = move(0, tokens.at[micro], xs.at[micro])
    own_g = move(1, cotangent.at[micro], gs.at[own_half])
    gains[0:1, :] = norm1_gain[...].astype(jnp.float32)
    gains[1:2, :] = norm2_gain[...].astype(jnp.float32)
    gain_sends = [
        send(2 + i, gains, gains_all.at[shard], device) for i, device in enumerate((core_mate, chip_mate, far_mate))
    ]
    own_gain = move(2, gains, gains_all.at[shard])

    own_pair = lane_span(member // 2 * 128, 128)
    key_pair = key_in[:, own_pair].astype(jnp.float32)
    value_pair = value_in[:, own_pair].astype(jnp.float32)
    key_pair = jnp.where(member % 2 == 0, key_pair, pltpu.roll(key_pair, HDIM, 1))
    value_pair = jnp.where(member % 2 == 0, pltpu.roll(value_pair, HDIM, 1), value_pair)
    wkv_in[...] = jnp.where(lane_ids(key_pair.shape) < HDIM, key_pair, value_pair).astype(jnp.bfloat16)

    chip_shard = (1 - chip) * 2 + core
    own_ffn = lane_span(member * width_f, width_f)
    parts = (
        (wq_in.at[:, lane_span(member * width_q, width_q)], wq),
        (wkv_in, wkv),
    )

    def weight_out(i):
        source, target = parts[i]
        rows = row_span(shard * depth, depth)
        over_chip = send(5 + 3 * i, source, target.at[rows], chip_mate)
        over_core = send(6 + 3 * i, source, target.at[rows], core_mate)
        here = move(3 + i, source, target.at[rows])
        return over_chip, over_core, here

    def weight_on(i):
        rows = parts[i][1].at[row_span(chip_shard * depth, depth)]
        return send(7 + 3 * i, rows, rows, core_mate)

    started = {i: weight_out(i) for i in (0, 1)}
    same_chip, same_core = chip == member // 2, core == member % 2
    wo_half = width_q // 2
    wo_mine = row_span((core + member % 2) % 2 * wo_half, wo_half)
    wo_over_core = copy_to(21, wo_in, wo, core_mate)
    wo_first = copy_to(20, wo_in.at[wo_mine], wo.at[wo_mine], chip_mate)
    wo_second = copy_to(20, wo.at[wo_mine], wo.at[wo_mine], chip_mate)
    wo_on = copy_to(22, wo.at[wo_mine], wo.at[wo_mine], core_mate)
    wo_here = pltpu.make_async_copy(wo_in, wo, local_sem.at[8])

    @pl.when(same_chip & same_core)
    def _():
        wo_over_core.start()
        wo_first.start()
        wo_here.start()

    @pl.when(same_chip & jnp.logical_not(same_core))
    def _():
        wo_over_core.wait_recv()
        wo_second.start()

    ffn_in = (wd_in, wg_in, wu_in)
    quarter = depth // 4

    def ffn_rows(w, shard_of, first, size):
        return wf.at[w, row_span(shard_of * depth + first, size)]

    quarters, rests, mates, heres, handed, ons = [], [], [], [], [], []
    for w in range(3):
        for copies, first, size, index in ((quarters, micro * quarter, quarter, 102), (rests, 2 * quarter, 2 * quarter, 105)):
            source = ffn_in[w].at[row_span(first, size), own_ffn]
            copies.append(send(index + w, source, ffn_rows(w, shard, first, size), chip_mate))
        mates.append(send(108 + w, ffn_in[w].at[:, own_ffn], ffn_rows(w, shard, 0, depth), core_mate))
        heres.append(move(5 + w, ffn_in[w].at[:, own_ffn], ffn_rows(w, shard, 0, depth)))

    def hand_on(w):
        quarters[w].wait()
        rows = ffn_rows(w, chip_shard, micro * quarter, quarter)
        handed.append(send(111 + w, rows, rows, partner))

    def core_on(w):
        rests[w].wait()
        handed[w].wait()
        rows = ffn_rows(w, chip_shard, 0, depth)
        ons.append(send(114 + w, rows, rows, core_mate))

    first_len = seq_len[slot_order[2 * (shard * MB + micro)]]
    both_len = first_len + seq_len[slot_order[2 * (shard * MB + micro) + 1]]
    angles = row_positions(window, 0, group, tok_rows, first_len, both_len)[1].astype(jnp.float32) * inverse[...]
    cosine[...] = jnp.cos(angles)
    sine[...] = jnp.sin(angles)
    bias[...] = pair_bias(window, group, tok_rows, first_len, both_len).astype(jnp.bfloat16)

    own_gain.wait()
    for copy in gain_sends:
        copy.wait()
    gain_one = jnp.concatenate([gains_all[f, 0:1, :] for f in range(KV)], axis=1)
    gain_two = jnp.concatenate([gains_all[f, 1:2, :] for f in range(KV)], axis=1)
    own_x.wait()
    swap_x.wait()
    inputs = xs[...].reshape(own_rows, D).astype(jnp.float32)
    normed[member] = (inputs * rms_scale(inputs) * gain_one).astype(jnp.bfloat16)


    def block_to(index, ref, block, device):
        return send(index, ref.at[block], ref.at[block], device)

    first_half, second_half = pl.ds(0, tok_rows), pl.ds(tok_rows, tok_rows)

    def half_to(index, ref, block, rows, device):
        return send(index, ref.at[block, rows], ref.at[block, rows], device)

    def gather_start(index, ref):
        return (
            half_to(index, ref, member, first_half, peers[1]),
            half_to(index + 1, ref, member, second_half, peers[0]),
            half_to(index + 2, ref, member, second_half, peers[1]),
            half_to(index + 3, ref, member, first_half, peers[0]),
        )

    def gather_on(index, ref, parts):
        parts[0].wait()
        on_y = half_to(index + 4, ref, members[1], first_half, peers[0])
        parts[1].wait()
        return on_y, half_to(index + 5, ref, members[0], second_half, peers[1])

    one_parts = gather_start(117, normed)

    own_g.wait()
    swap_g.wait()
    ids = lax.broadcasted_iota(jnp.int32, (own_rows, 1), 0)
    own_place = (ids // tok_rows) * (group * tok_rows) + member * tok_rows + ids % tok_rows
    valid = jnp.where(own_place < both_len, 1.0, 0.0)
    upstream[member] = (gs[...].astype(jnp.float32) * valid).astype(jnp.bfloat16)

    def weights_one():
        on = []
        for i in (0, 1):
            started[i][0].wait()
            on.append(weight_on(i))
        for i in (0, 1):
            started[i][1].wait()
            started[i][2].wait()
        for copy in on:
            copy.wait()

    def project(rows):
        block = normed[rows]
        place_rows = row_span(rows * own_rows, own_rows)
        query = plain_dot(block, wq[...])
        pair = plain_dot(block, wkv[...])
        cos, sin = cosine[place_rows, :], sine[place_rows, :]
        for j in range(width_q // 128):
            lanes = slice(j * 128, (j + 1) * 128)
            head = query[:, lanes].astype(jnp.bfloat16).astype(jnp.float32)
            head = (head * cos + turn(head) * sin).astype(jnp.bfloat16)
            query_rot[place_rows, lanes] = head * HDIM**-0.5
        pair = pair.astype(jnp.bfloat16).astype(jnp.float32)
        turned_key = pair * cos + turn(pair) * sin
        lower = lane_ids(pair.shape) < HDIM
        keys[place_rows, :] = jnp.where(lower, turned_key, pltpu.roll(turned_key, HDIM, 1)).astype(jnp.bfloat16)
        values[place_rows, :] = jnp.where(lower, pltpu.roll(pair, HDIM, 1), pair).astype(jnp.bfloat16)

    one_ons = gather_on(117, normed, one_parts)
    g_over_z = block_to(26, upstream, member, peers[1])
    g_over_y = block_to(27, upstream, member, peers[0])
    weights_one()
    project(member)
    one_parts[2].wait()
    project(members[1])
    one_parts[3].wait()
    project(members[0])
    for copy in one_ons:
        copy.wait()
    project(members[2])

    key_twice, value_twice = keys[...], values[...]
    lower = lane_ids(key_twice.shape) < HDIM
    zero = jnp.zeros_like(key_twice)
    key_low, key_high = jnp.where(lower, key_twice, zero), jnp.where(lower, zero, key_twice)
    value_low, value_high = jnp.where(lower, value_twice, zero), jnp.where(lower, zero, value_twice)
    value_low_turned, value_high_turned = value_low.T, value_high.T

    @pl.loop(0, width_q // 128)
    def _(j):
        lanes = lane_span(j * 128, 128)
        pair = query_rot[:, lanes]
        total = plain_dot(value_low_turned, softmax_columns(key_low, pair, bias[...]).astype(jnp.bfloat16))
        total += plain_dot(value_high_turned, softmax_columns(key_high, pair, bias[...]).astype(jnp.bfloat16))
        attended[:, lanes] = total.T.astype(jnp.bfloat16)

    @pl.when(same_chip & same_core)
    def _():
        wo_first.wait_send()
        wo_over_core.wait_send()
        wo_here.wait()

    @pl.when(same_chip & jnp.logical_not(same_core))
    def _():
        wo_second.wait_send()

    @pl.when(jnp.logical_not(same_chip))
    def _():
        wo_first.wait_recv()
        wo_on.start()
        wo_on.wait()

    def project_out(rows):
        return plain_dot(attended[row_span(rows * own_rows, own_rows), :], wo[...])

    def rows_to_y(index, rows_of, k, held, landing):
        owner, place = ((members[2], 2), (members[0], 0))[k]
        held[k] = rows_of(owner).astype(jnp.bfloat16)
        return send(index, held.at[k], landing.at[place], peers[0])

    def sum_over_z(index, over, held, landing):
        over.wait()
        held[2] = (held[2].astype(jnp.float32) + landing[2].astype(jnp.float32)).astype(jnp.bfloat16)
        return send(index, held.at[2], landing.at[1], peers[1])

    def sum_of(rows, over_y, over_z, landing):
        over_y.wait()
        over_z.wait()
        return rows + landing[0].astype(jnp.float32) + landing[1].astype(jnp.float32)

    mid_over = rows_to_y(29, project_out, 0, sent, got)
    mid_y = rows_to_y(30, project_out, 1, sent, got)
    sent[2] = project_out(members[1]).astype(jnp.bfloat16)
    mid_own = inputs + project_out(member)
    mid_z = sum_over_z(31, mid_over, sent, got)
    hand_on(0)
    total = sum_of(mid_own, mid_y, mid_z, got)
    middle[...] = total
    normed_two[member] = (total * rms_scale(total) * gain_two).astype(jnp.bfloat16)
    two_parts = gather_start(123, normed_two)
    two_ons = gather_on(123, normed_two, two_parts)
    g_over_z.wait()
    g_on_y = block_to(28, upstream, members[1], peers[0])
    hand_on(1)
    core_on(0)
    hand_on(2)
    core_on(1)
    core_on(2)
    for copy in (*mates, *heres, *ons, g_over_y, g_on_y, *two_parts[2:], *two_ons):
        copy.wait()

    @pl.loop(0, group)
    def _(r):
        place_rows = row_span(r * own_rows, own_rows)
        gate = plain_dot(normed_two[r], wf[1])
        up = plain_dot(normed_two[r], wf[2])
        d_hidden = plain_dot(upstream[r], wf[0])
        sig = jax.nn.sigmoid(gate)
        silu = gate * sig
        hid[0, place_rows, :] = (silu * up).astype(jnp.bfloat16)
        hid[1, place_rows, :] = (d_hidden * up * sig * (1.0 + gate * (1.0 - sig))).astype(jnp.bfloat16)
        hid[2, place_rows, :] = (d_hidden * silu).astype(jnp.bfloat16)

    def hid_rows(k, rows):
        return hid[k, row_span(rows * own_rows, own_rows), :]

    base = 35
    two_rows = lambda rows: contract_cols(hid_rows(1, rows), wf[1]) + contract_cols(hid_rows(2, rows), wf[2])
    two_over = rows_to_y(base + 27, two_rows, 0, sent, got)
    two_y = rows_to_y(base + 28, two_rows, 1, sent, got)
    block_rows = lambda rows: contract_cols(hid_rows(0, rows), wf[0])
    for k, rows in enumerate((members[2], members[0], members[1])):
        sent_block[k] = block_rows(rows).astype(jnp.bfloat16)
    own_block[...] = (middle[...] + block_rows(member)).reshape(MB, tok_rows, D)

    def weight_part(w, f):
        rows = lane_span(f * depth, depth)
        acts = (upstream if w == 0 else normed_two)[:, :, rows].reshape(window, depth)
        wf[w, rows, :] = contract_rows(acts, hid[w]).astype(jnp.bfloat16)

    core_copies, chip_copies, half_copies, last_copies, here_copies = {}, {}, {}, [], []

    def core_send(w, k):
        x = 1 - chip if k == 0 else chip
        rows = row_span((x * 2 + 1 - core) * depth, depth)
        core_copies[w, k] = send(base + 3 + 2 * w + k, wf.at[w, rows], from_core.at[w, x], core_mate)

    def far_parts(w):
        weight_part(w, (1 - chip) * 2 + 1 - core)
        core_send(w, 0)
        weight_part(w, (1 - chip) * 2 + core)

    def near_parts(w):
        weight_part(w, chip * 2 + 1 - core)
        core_send(w, 1)
        weight_part(w, chip * 2 + core)

    def all_parts(w):
        for f in range(KV):
            weight_part(w, f)
        core_send(w, 0)
        core_send(w, 1)

    def slot(x, c, m):
        return (x * 2 + c) * depth + m * half_rows

    def stage_in(index, source, w, first):
        return move(index, source, wf.at[w, row_span(first, half_rows)])

    def add_up(w, first, stages):
        @pl.loop(0, group)
        def _(t):
            total = wf[w, row_span(first + t * tok_rows, tok_rows), :].astype(jnp.float32)
            for stage in stages:
                total += wf[w, row_span(stage + t * tok_rows, tok_rows), :].astype(jnp.float32)
            wf[w, row_span(first + t * tok_rows, tok_rows), :] = total.astype(jnp.bfloat16)

    def core_rows(w, x, m):
        return from_core.at[w, x, row_span(m * half_rows, half_rows)]

    def chip_unit(w, m, index):
        if index == 0:
            core_copies[w, 0].wait()
        first, stage = slot(1 - chip, core, m), slot(1 - chip, 1 - core, m)
        stage_in(9, core_rows(w, 1 - chip, m), w, stage).wait()
        add_up(w, first, (stage,))
        chip_copies[w, index] = send(
            base + 9 + 2 * w + index, wf.at[w, row_span(first, half_rows)], from_chip.at[w, m], chip_mate
        )

    def half_unit(w):
        m = 1 - micro
        first, stage, other = slot(chip, core, m), slot(chip, 1 - core, m), slot(1 - chip, 1 - core, m)
        core_copies[w, 1].wait()
        load = stage_in(9, core_rows(w, chip, m), w, stage)
        chip_copies[w, 0].wait()
        stage_in(10, from_chip.at[w, m], w, other).wait()
        load.wait()
        add_up(w, first, (stage, other))
        half_copies[w] = send(base + 15 + w, wf.at[w, row_span(first, half_rows)], from_half.at[w], partner)

    def last_unit(w):
        first, stage, other = slot(chip, core, micro), slot(chip, 1 - core, micro), slot(1 - chip, 1 - core, micro)
        third = slot(chip, 1 - core, 1 - micro)
        load = stage_in(9, core_rows(w, chip, micro), w, stage)
        chip_copies[w, 1].wait()
        over = stage_in(10, from_chip.at[w, micro], w, other)
        half_copies[w].wait()
        stage_in(11, from_half.at[w], w, third).wait()
        load.wait()
        over.wait()
        add_up(w, first, (stage, other, third))
        for i in range(group - 1):
            source = wf.at[w, row_span(first + members[i] * tok_rows, tok_rows)]
            last_copies.append(send(base + 18 + 3 * w + i, source, ffn_grad.at[w, :, own_ffn], peers[i]))
        source = wf.at[w, row_span(first + member * tok_rows, tok_rows)]
        here_copies.append(move(12 + w, source, ffn_grad.at[w, :, own_ffn]))

    far_parts(0)
    sent[2] = two_rows(members[1]).astype(jnp.bfloat16)
    two_z = sum_over_z(base + 29, two_over, sent, got)
    chip_unit(0, 1 - micro, 0)
    near_parts(0)
    own_rest[...] = two_rows(member).reshape(MB, tok_rows, D)
    far_parts(1)

    middle_rows = middle[...]
    grad, two_term = norm_back(middle_rows, rms_scale(middle_rows), gain_two, sum_of(own_rest[...].reshape(own_rows, D), two_y, two_z, got))
    grad += upstream[member].astype(jnp.float32)
    middle[...] = grad
    d_full[member] = grad.astype(jnp.bfloat16)
    to_z = send(base + 32, d_full.at[member], d_full.at[member], peers[1])
    to_y = send(base + 33, d_full.at[member], d_full.at[member], peers[0])
    near_parts(1)
    half_unit(0)
    chip_unit(1, 1 - micro, 0)
    all_parts(2)

    def give(k, rows, kept):
        rows_out[k] = jnp.where(micro == 0, rows[tok_rows:], rows[:tok_rows]).astype(jnp.bfloat16)
        kept[micro] = jnp.where(micro == 0, rows[:tok_rows], rows[tok_rows:])
        return send(base + 30 + k, rows_out.at[k], rows_got.at[k], partner)

    def take(k, copy, kept, target):
        copy.wait()
        kept[1 - micro] = rows_got[k].astype(jnp.float32)
        here_copies.append(move(18 + k, kept, target))

    def attention_grad(rows):
        place_rows = row_span(rows * own_rows, own_rows)
        d_attended[place_rows, :] = contract_cols(d_full[rows], wo[...]).astype(jnp.bfloat16)

    to_z.wait()
    on_y = send(base + 34, d_full.at[members[1]], d_full.at[members[1]], peers[0])
    block_over = send(base, sent_block.at[0], got_block.at[2], peers[0])
    block_y = send(base + 1, sent_block.at[1], got_block.at[0], peers[0])
    attention_grad(member)
    attention_grad(members[1])
    to_y.wait()
    attention_grad(members[0])
    chip_unit(2, 1 - micro, 0)
    on_y.wait()
    attention_grad(members[2])
    half_unit(1)

    out_part = normed_two
    d_rows = d_full[...].reshape(window, D)
    for j in range(group):
        out_part[j] = contract_rows(attended[:, j * 128 : (j + 1) * 128], d_rows).astype(jnp.bfloat16)
    out_by_core = copy_to(base + 35, out_part, out_core, core_mate)
    out_by_chip = copy_to(base + 36, out_part, out_chip, chip_mate)
    half_blocks = group // MB
    out_by_half = copy_to(base + 37, out_part.at[pl.ds((1 - micro) * half_blocks, half_blocks)], out_half, partner)

    def add_blocks(landed, first, count):
        for j in range(count):
            move(15, landed.at[j], gs).wait()
            out_part[first + j] = (
                out_part[first + j].astype(jnp.float32) + gs[...].astype(jnp.float32)
            ).astype(jnp.bfloat16)

    @pl.when(jnp.logical_not(same_core))
    def _():
        out_by_core.start()

    for w in (0, 1):
        chip_unit(w, micro, 1)

    key_low_turned, key_high_turned = key_low.T, key_high.T
    key_sum[...] = jnp.zeros_like(key_sum)
    value_sum[...] = jnp.zeros_like(value_sum)

    @pl.loop(0, width_q // 128)
    def _(j):
        lanes = lane_span(j * 128, 128)
        query_pair, grad_pair = query_rot[:, lanes], d_attended[:, lanes]
        total = jnp.zeros((2 * HDIM, window), jnp.float32)
        for side, (key_side, value_side, key_turned) in enumerate(
            ((key_low, value_low, key_low_turned), (key_high, value_high, key_high_turned))
        ):
            probs = softmax_columns(key_side, query_pair, bias[...])
            d_probs = contract_cols(value_side, grad_pair)
            inner = jnp.sum(probs * d_probs, axis=0, keepdims=True)
            d_scores = (probs * (d_probs - inner)).astype(jnp.bfloat16)
            total += plain_dot(key_turned, d_scores)
            key_sum[side] += plain_dot(d_scores, query_pair)
            value_sum[side] += plain_dot(probs.astype(jnp.bfloat16), grad_pair)
        grad_rot = total.T * HDIM**-0.5
        d_query[:, lanes] = (grad_rot * cosine[...] + turn_back(grad_rot * sine[...])).astype(jnp.bfloat16)

    fold = lambda sums: jnp.where(lower, sums[0] + pltpu.roll(sums[1], HDIM, 1), 0.0)
    key_grad, value_grad = fold(key_sum), fold(value_sum)
    key_grad = key_grad * cosine[...] + turn_back(key_grad * sine[...])
    d_pair[...] = jnp.where(lower, key_grad, pltpu.roll(value_grad, HDIM, 1)).astype(jnp.bfloat16)

    def one_rows(rows):
        place_rows = row_span(rows * own_rows, own_rows)
        return contract_cols(d_query[place_rows, :], wq[...]) + contract_cols(d_pair[place_rows, :], wkv[...])

    block_z = sum_over_z(base + 2, block_over, sent_block, got_block)
    one_over = rows_to_y(base + 38, one_rows, 0, sent, got_one)
    one_y = rows_to_y(base + 39, one_rows, 1, sent, got_one)
    sent[2] = one_rows(members[1]).astype(jnp.bfloat16)
    own_rest[...] = one_rows(member).reshape(MB, tok_rows, D)
    half_unit(2)

    @pl.when(jnp.logical_not(same_core))
    def _():
        out_by_core.wait_send()

    @pl.when(same_core)
    def _():
        out_by_core.wait_recv()
        add_blocks(out_core, 0, group)

    @pl.when(same_core & jnp.logical_not(same_chip))
    def _():
        out_by_chip.start()

    d_all = jnp.concatenate([d_query[...], d_pair[...]], axis=1)

    def late_lanes(c):
        return lane_span(c * width_l, width_l)

    def late_part(x, c):
        for m in range(MB):
            columns = lane_span(((x * 2 + c) * MB + m) * half_rows, half_rows)
            rows = normed[:, :, columns].reshape(window, half_rows)
            hid[x, m * half_rows : (m + 1) * half_rows, late_lanes(c)] = contract_rows(rows, d_all).astype(jnp.bfloat16)

    late_core_copies = []
    for x in range(2):
        late_part(x, 1 - core)
        late_core_copies.append(
            send(base + 41 + x, hid.at[x, :, late_lanes(1 - core)], hid.at[2, :, late_lanes(x)], core_mate)
        )
    for x in range(2):
        late_part(x, core)
    for copy in late_core_copies:
        copy.wait()

    def late_add(x, first, count, landed):
        @pl.loop(0, count)
        def _(t):
            rows = row_span(first + t * tok_rows, tok_rows)
            total = hid[x, rows, late_lanes(core)].astype(jnp.float32) + hid[2, rows, late_lanes(x)].astype(jnp.float32)
            for ref, start in landed:
                total += ref[row_span(start + t * tok_rows, tok_rows), :].astype(jnp.float32)
            hid[x, rows, late_lanes(core)] = total.astype(jnp.bfloat16)

    late_add(1 - chip, 0, MB * group, ())
    late_to_chip = send(base + 43, hid.at[1 - chip, :, late_lanes(core)], late_chip, chip_mate)
    chip_unit(2, micro, 1)
    one_z = sum_over_z(base + 40, one_over, sent, got_one)
    block = sum_of(own_block[...].reshape(own_rows, D), block_y, block_z, got_block)
    give_block = give(0, block, own_block)

    @pl.when(same_core & jnp.logical_not(same_chip))
    def _():
        out_by_chip.wait_send()

    @pl.when(same_core & same_chip)
    def _():
        out_by_chip.wait_recv()
        add_blocks(out_chip, 0, group)
        out_by_half.start()

    last_unit(0)
    late_to_chip.wait()
    late_add(chip, (1 - micro) * half_rows, group, ((late_chip, (1 - micro) * half_rows),))
    late_to_half = send(
        base + 46, hid.at[chip, row_span((1 - micro) * half_rows, half_rows), late_lanes(core)], late_half, partner
    )

    inputs = xs[...].reshape(own_rows, D).astype(jnp.float32)
    grad, one_term = norm_back(
        inputs, rms_scale(inputs), gain_one, sum_of(own_rest[...].reshape(own_rows, D), one_y, one_z, got_one)
    )
    give_grad = give(1, grad + middle[...], own_rest)

    for k, term in enumerate((one_term[None], two_term[None])):
        for f in range(KV):
            gain_part[k * KV + f : k * KV + f + 1, :] = term[:, f * depth : (f + 1) * depth]
    gain_first = [
        send(base + 57 + i, gain_part, gain_got.at[i], device)
        for i, device in enumerate((core_mate, chip_mate, far_mate))
    ]
    last_unit(1)
    for copy in gain_first:
        copy.wait()
    gain_part[...] = gain_part[...] + gain_got[0] + gain_got[1] + gain_got[2]
    gain_second = [
        send(base + 60 + i, gain_part, gain_got.at[3 + i], device)
        for i, device in enumerate((*peers, partner, *others))
    ]
    take(0, give_block, own_block, block_out)
    last_unit(2)

    def out_block(t):
        return out_part.at[micro * half_blocks + t // 2, row_span(t % 2 * tok_rows, tok_rows)]

    out_here = pltpu.make_async_copy(out_block(member), out_grad, local_sem.at[16])

    def out_to(i):
        return pltpu.make_async_remote_copy(
            src_ref=out_block(members[i]),
            dst_ref=out_grad,
            send_sem=send_sem.at[base + 48 + i],
            recv_sem=recv_sem.at[base + 48],
            device_id=peers[i],
            device_id_type=MESH,
        )

    @pl.when(same_core & same_chip)
    def _():
        out_by_half.wait()
        add_blocks(out_half, micro * half_blocks, half_blocks)
        for i in range(group - 1):
            out_to(i).start()
        out_here.start()

    late_to_half.wait()
    late_add(chip, micro * half_rows, group, ((late_chip, micro * half_rows), (late_half, 0)))
    own_late = lane_span(member * width_l, width_l)

    def late_rows(t):
        return hid.at[chip, row_span(micro * half_rows + t * tok_rows, tok_rows), late_lanes(core)]

    for i in range(group - 1):
        last_copies.append(send(base + 54 + i, late_rows(members[i]), qkv_grad.at[:, own_late], peers[i]))
    here_copies.append(move(17, late_rows(member), qkv_grad.at[:, own_late]))
    take(1, give_grad, own_rest, input_grad)
    total = gain_part[...]
    for i, copy in enumerate(gain_second):
        copy.wait()
        total += gain_got[3 + i]
    gain_sum[...] = total

    @pl.when(same_core & same_chip)
    def _():
        for i in range(group - 1):
            out_to(i).wait_send()
        out_here.wait()

    @pl.when(jnp.logical_not(same_core & same_chip))
    def _():
        out_to(0).wait_recv()

    for copy in (*last_copies, *here_copies):
        copy.wait()


def whole_layer(n_sp, tok_rows, heads, *operands):
    group = n_sp // MB
    own_rows = MB * tok_rows
    window = group * own_rows
    half_rows = group * tok_rows
    width_q = heads * HDIM
    width_f = FF // group
    width_l = width_q + 2 * HDIM
    low, full = jnp.bfloat16, jnp.float32
    vmem = pl.BlockSpec(memory_space=pltpu.VMEM)
    anywhere = pl.BlockSpec(memory_space=pl.ANY)
    smem = pl.BlockSpec(memory_space=pltpu.SMEM)
    shape = jax.ShapeDtypeStruct
    blocks = (group, own_rows, D)
    trio = (group - 1, own_rows, D)
    pair = (MB, tok_rows, D)
    return pl.pallas_call(
        functools.partial(layer_kernel, n_sp),
        out_shape=(
            shape(pair, full),
            shape(pair, full),
            shape((3, tok_rows, FF), low),
            shape((tok_rows, group * width_l), low),
            shape((tok_rows, D), low),
            shape((2 * KV, D // KV), full),
            shape((3, 2, MB * half_rows, width_f), low),
            shape((3, MB, half_rows, width_f), low),
            shape((3, half_rows, width_f), low),
            shape(blocks, low),
            shape(blocks, low),
            shape((group // MB, own_rows, D), low),
        ),
        in_specs=[anywhere] * 2 + [smem] * 2 + [vmem] * 5 + [anywhere] * 5,
        out_specs=(anywhere,) * 5 + (vmem,) + (anywhere,) * 6,
        scratch_shapes=[
            pltpu.VMEM((3, D, width_f), low),
            pltpu.VMEM((D, width_q), low),
            pltpu.VMEM((D, 2 * HDIM), low),
            pltpu.VMEM((width_q, D), low),
            pltpu.VMEM((D // KV, 2 * HDIM), low),
            pltpu.VMEM((8, D // KV), full),
            pltpu.VMEM((KV, 8, D // KV), full),
            pltpu.VMEM((window, 2 * HDIM), full),
            pltpu.VMEM((window, 2 * HDIM), full),
            pltpu.VMEM((window, window), low),
            pltpu.VMEM(pair, low),
            pltpu.VMEM((own_rows, D), low),
            pltpu.VMEM(blocks, low),
            pltpu.VMEM(blocks, low),
            pltpu.VMEM(blocks, low),
            pltpu.VMEM((window, width_q), low),
            pltpu.VMEM((window, 2 * HDIM), low),
            pltpu.VMEM((window, 2 * HDIM), low),
            pltpu.VMEM((window, width_q), low),
            pltpu.VMEM((window, width_q), low),
            pltpu.VMEM((window, width_q), low),
            pltpu.VMEM((window, 2 * HDIM), low),
            pltpu.VMEM((2, window, 2 * HDIM), full),
            pltpu.VMEM((2, window, 2 * HDIM), full),
            pltpu.VMEM((own_rows, D), full),
            pltpu.VMEM(pair, full),
            pltpu.VMEM(pair, full),
            pltpu.VMEM((3, window, width_f), low),
            pltpu.VMEM(trio, low),
            pltpu.VMEM(trio, low),
            pltpu.VMEM(trio, low),
            pltpu.VMEM(trio, low),
            pltpu.VMEM(trio, low),
            pltpu.VMEM(blocks, low),
            pltpu.VMEM((2, tok_rows, D), low),
            pltpu.VMEM((2, tok_rows, D), low),
            pltpu.VMEM((MB * half_rows, width_l), low),
            pltpu.VMEM((half_rows, width_l), low),
            pltpu.VMEM((2 * KV, D // KV), full),
            pltpu.VMEM((10, 2 * KV, D // KV), full),
            pltpu.SemaphoreType.DMA((20,)),
            pltpu.SemaphoreType.DMA((129,)),
            pltpu.SemaphoreType.DMA((129,)),
        ],
        compiler_params=pltpu.CompilerParams(
            collective_id=0, has_side_effects=True, vmem_limit_bytes=VMEM_BYTES
        ),
        cost_estimate=pl.CostEstimate(flops=36 * 10**9, bytes_accessed=100 * 10**6, transcendentals=8 * 10**6),
        name="whole_layer",
    )(*operands)


def group_body(
    tokens,
    cotangent,
    seq_len,
    slot_order,
    norm1_gain,
    query_weight,
    key_weight,
    value_weight,
    output_weight,
    norm2_gain,
    gate_weight,
    up_weight,
    down_weight,
):
    n_sp = lax.axis_size("sp")
    n_fsdp = lax.axis_size("fsdp")
    group = n_sp // MB
    rank = lax.axis_index("sp")
    shard = lax.axis_index("fsdp")
    micro = rank // group
    member = rank % group
    tok_rows = tokens.shape[1]
    window = n_sp * tok_rows
    own_rows = MB * tok_rows
    inverse = np.float32(ROPE_BASE) ** (np.arange(HDIM // 2, dtype=np.float32) * np.float32(-2.0 / HDIM))
    heads = HEADS // group
    block, d_inputs, ffn_grad, qkv_grad, output_grad, gain_sum, *_ = whole_layer(
        n_sp, tok_rows, heads,
        tokens, cotangent, seq_len, slot_order, norm1_gain[None], norm2_gain[None],
        jnp.asarray(np.tile(inverse, 4)[None]), key_weight, value_weight,
        query_weight, output_weight, gate_weight, up_weight, down_weight,
    )
    gain_own = lax.dynamic_slice_in_dim(gain_sum.reshape(2, D), (shard * n_sp + rank) * tok_rows, tok_rows, 1)

    def part_of(first, width):
        pieces = qkv_grad.reshape(tok_rows, group, -1)[:, :, first : first + width]
        return pieces.reshape(tok_rows, group * width).astype(jnp.float32)

    width_q = heads * HDIM
    return (
        block,
        d_inputs,
        gain_own[0],
        part_of(0, width_q),
        part_of(width_q, HDIM),
        part_of(width_q + HDIM, HDIM),
        output_grad.astype(jnp.float32),
        gain_own[1],
        ffn_grad[1].astype(jnp.float32),
        ffn_grad[2].astype(jnp.float32),
        ffn_grad[0].astype(jnp.float32),
    )


def solution(mesh):
    fits = mesh.shape["fsdp"] == KV and mesh.shape["sp"] == MB * KV
    placed = (
        P(None, ("fsdp", "sp"), None),
        P(None, ("fsdp", "sp"), None),
        P(),
        P(),
        P("fsdp"),
        P("fsdp", None),
        P("fsdp", None),
        P("fsdp", None),
        P("fsdp", None),
        P("fsdp"),
        P("fsdp", None),
        P("fsdp", None),
        P("fsdp", None),
    )
    return jax.shard_map(
        group_body if fits else body,
        mesh=mesh,
        in_specs=placed,
        out_specs=(
            P(None, ("fsdp", "sp"), None),
            P(None, ("fsdp", "sp"), None),
            P(("fsdp", "sp")),
            P(("fsdp", "sp"), None),
            P(("fsdp", "sp"), None),
            P(("fsdp", "sp"), None),
            P(("fsdp", "sp"), None),
            P(("fsdp", "sp")),
            P(("fsdp", "sp"), None),
            P(("fsdp", "sp"), None),
            P(("fsdp", "sp"), None),
        ),
        check_vma=False,
    )
```
